32 devices in a mesh: section: 4 (over z), tensor: 8 (over y, x, core).
Axes of the slice: x: 2, y: 2, z: 4, core: 2. Of those that a mesh axis runs over, the one named last changes fastest.
Arguments:
- text: bfloat16 [4, 256, 8192], P('section', 'tensor'), may hold values from -6 to 6
- features: bfloat16 [192, 8192], P(None, 'tensor'), may hold values from -6 to 6
- in_gain: bfloat16 [4, 8192], P('section'), may hold values from 0.5 to 1.5
- w_query: bfloat16 [4, 8192, 4096], P('section', None, 'tensor'), may hold values from -0.0625 to 0.0625
- q_gain: bfloat16 [4, 128], P('section'), may hold values from 0.099609375 to 1.8984375
- w_key_value: bfloat16 [4, 8192, 2048], P('section', 'tensor'), may hold values from -0.0625 to 0.0625
- k_gain: bfloat16 [4, 128], P('section'), may hold values from 0.099609375 to 1.8984375
- tile_count: int32 [2], replicated, may hold values from 1 to 4, as said below
- image_start: int32 [2], replicated, may hold values from 1 to 127
- grad_out: bfloat16 [4, 256, 4096], P('section', None, 'tensor'), may hold values from -6 to 6
Outputs:
- attended: bfloat16 [4, 256, 4096], P('section', None, 'tensor')
- feature_grad: float32 [192, 8192], P('section', 'tensor')
The draws below stay inside these ranges and needn't reach their ends.
Inputs may be any that keep to these rules, and one draw needn't show every extreme that they name: `tile_count`: some sample has 4 tiles.
All inputs are finite; a program needn't handle non-finite values.
Results may differ from the reference program's by a relative error of at most 0.0089.
Values may be sent and summed in bfloat16 or wider, within the bound.
No kernel may reach another device: no remote copies, remote signals or barrier semaphores. Data moves between devices by JAX's collectives and lax.ppermute only.
A program may use at most 64 MiB of HBM per device.

```python
import jax
import jax.numpy as jnp
from jax import lax

D = 8192
HEADS = 32
KV_HEADS = 8
HEAD_DIM = 128
TILES = 4
TILE_LEN = 24
TXT_TOK = 128
MB = 2
LAYERS = 4
ROWS = 256
IMG_ALL = 192
N_TENSOR = 8


def draw_tile_count(key, part):
    counts = jax.random.randint(key, (MB,), 1, TILES + 1)
    chosen = jax.random.randint(jax.random.fold_in(key, 7), (), 0, MB)
    return jnp.where(jnp.arange(MB) == chosen, TILES, counts).astype(jnp.int32)


def levels(key, extent, cuts, low, largest):
    level, own = 1.0, jax.random.fold_in(key, 6)
    for axis_at, shards_of in cuts:
        steps = jnp.exp(jax.random.uniform(jax.random.fold_in(own, axis_at), (shards_of,), jnp.float32, low / len(cuts), largest / len(cuts)))
        level = level * jnp.repeat(steps, extent[axis_at] // shards_of).reshape([-1 if axis == axis_at else 1 for axis in range(len(extent))])
    return level


def bell_draw(stream_key, dims, deviation, reach, cuts=(), held_as=jnp.bfloat16):
    entries = jax.random.normal(stream_key, dims, jnp.float32) * deviation
    if len(cuts) > 0:
        entries = levels(stream_key, dims, cuts, -0.22, 0.18) * entries
    return jnp.clip(entries, min=-reach, max=reach).astype(held_as)


def setup_inputs(seed: int = 0) -> dict:
    streams_of = jax.random.split(jax.random.key(seed), 11)
    return {
        "text": bell_draw(streams_of[0], (LAYERS, ROWS, D), 1.0, 6.0, ((0, 4), (1, 8))),
        "features": bell_draw(streams_of[1], (IMG_ALL, D), 1.0, 6.0, ((1, 8),)),
        "in_gain": jnp.clip(1.0 + 0.1 * jax.random.normal(streams_of[2], (LAYERS, D), jnp.float32), 0.5, 1.5).astype(jnp.bfloat16),
        "w_query": bell_draw(streams_of[3], (LAYERS, D, HEADS * HEAD_DIM), D ** -0.5, 0.0625, ((0, 4), (2, 8))),
        "q_gain": jnp.clip(1.0 + 0.18 * jax.random.normal(streams_of[4], (LAYERS, HEAD_DIM), jnp.float32), 0.099609375, 1.8984375).astype(jnp.bfloat16),
        "w_key_value": bell_draw(streams_of[5], (LAYERS, D, 2 * KV_HEADS * HEAD_DIM), D ** -0.5, 0.0625, ((0, 4), (1, 8))),
        "k_gain": jnp.clip(1.0 + 0.18 * jax.random.normal(streams_of[6], (LAYERS, HEAD_DIM), jnp.float32), 0.099609375, 1.8984375).astype(jnp.bfloat16),
        "tile_count": draw_tile_count(jax.random.fold_in(streams_of[10], 71), 0),
        "image_start": jax.random.randint(streams_of[8], (MB,), 1, TXT_TOK).astype(jnp.int32),
        "grad_out": bell_draw(streams_of[9], (LAYERS, ROWS, HEADS * HEAD_DIM), 1.0, 6.0, ((0, 4), (2, 8))),
    }


eps = 1e-05

def rms_scale(values, norm_gain):
    inverse = lax.rsqrt(lax.optimization_barrier(jnp.mean(values * values, axis=-1, keepdims=True)) + eps)
    return values * inverse * norm_gain

def rounded(values):
    return lax.optimization_barrier(values.astype(jnp.bfloat16)).astype(jnp.float32)

def reference(text, features, in_gain, w_query, q_gain, w_key_value, k_gain, tile_count, image_start, grad_out):
    score_scale = HEAD_DIM ** (-0.5)
    group_size = HEADS // KV_HEADS
    block_size = HEADS // N_TENSOR
    per_kv = N_TENSOR // KV_HEADS
    image_slots = TILES * TILE_LEN
    key_live = jnp.arange(image_slots, dtype=jnp.int32)[None, :] < (tile_count * TILE_LEN)[:, None]
    row_live = (jnp.arange(TXT_TOK, dtype=jnp.int32)[None, :] >= image_start[:, None]).astype(jnp.float32)
    row_mask = row_live[:, :, None, None]

    def layer(carry, inputs):
        hidden, layer_gain, weight_q, query_gain, weight_kv, key_gain, upstream_in = inputs
        normed = rms_scale(hidden.astype(jnp.float32), layer_gain.astype(jnp.float32)).astype(jnp.bfloat16)
        raw_q = jnp.dot(normed, weight_q, preferred_element_type=jnp.float32)
        queries = rounded(rms_scale(raw_q.reshape(MB, TXT_TOK, HEADS, HEAD_DIM), query_gain.astype(jnp.float32)))
        kv_full = jnp.dot(features, weight_kv, preferred_element_type=jnp.float32)
        key_raw = kv_full[:, :KV_HEADS * HEAD_DIM].reshape(MB, image_slots, KV_HEADS, HEAD_DIM)
        values = rounded(kv_full[:, KV_HEADS * HEAD_DIM:].reshape(MB, image_slots, KV_HEADS, HEAD_DIM))
        inverse = lax.rsqrt(lax.optimization_barrier(jnp.mean(key_raw * key_raw, axis=-1, keepdims=True)) + eps)
        key_hat = key_raw * inverse
        key_scale = key_gain.astype(jnp.float32)
        normed_keys = rounded(key_hat * key_scale)
        keys_h = jnp.repeat(normed_keys, group_size, axis=2)
        values_h = jnp.repeat(values, group_size, axis=2)
        scores = jnp.einsum('bthd,bjhd->bhtj', queries, keys_h) * score_scale
        exponent = jnp.where(key_live[:, None, None, :], jnp.exp(scores), 0.0)
        probs = exponent / lax.optimization_barrier(jnp.sum(exponent, axis=-1, keepdims=True))
        weights = rounded(probs)
        head_out = jnp.einsum('bhtj,bjhd->bthd', weights, values_h) * row_mask
        attended = head_out.reshape(ROWS, HEADS * HEAD_DIM).astype(jnp.bfloat16)
        upstream = upstream_in.astype(jnp.float32).reshape(MB, TXT_TOK, HEADS, HEAD_DIM) * row_mask
        d_weights = jnp.einsum('bthd,bjhd->bhtj', upstream, values_h)
        d_scores = rounded(probs * (d_weights - lax.optimization_barrier(jnp.sum(probs * d_weights, axis=-1, keepdims=True))) * score_scale)
        d_keys = jnp.einsum('bhtj,bthd->bjhd', d_scores, queries)
        d_values = jnp.einsum('bhtj,bthd->bjhd', weights, upstream)
        d_keys = d_keys.reshape(MB, image_slots, N_TENSOR, block_size, HEAD_DIM).sum(axis=3)
        d_values = d_values.reshape(MB, image_slots, N_TENSOR, block_size, HEAD_DIM).sum(axis=3)
        hat_blocks = jnp.repeat(key_hat, per_kv, axis=2)
        inverse_blocks = jnp.repeat(inverse, per_kv, axis=2)
        scaled = d_keys * key_scale
        d_raw = inverse_blocks * (scaled - hat_blocks * lax.optimization_barrier(jnp.mean(hat_blocks * scaled, axis=-1, keepdims=True)))
        d_raw = rounded(d_raw)
        d_values = rounded(d_values)
        key_sum = d_raw.reshape(MB, image_slots, KV_HEADS, per_kv, HEAD_DIM).sum(axis=3)
        value_sum = d_values.reshape(MB, image_slots, KV_HEADS, per_kv, HEAD_DIM).sum(axis=3)
        d_kv = jnp.concatenate([key_sum.reshape(IMG_ALL, KV_HEADS * HEAD_DIM), value_sum.reshape(IMG_ALL, KV_HEADS * HEAD_DIM)], axis=-1).astype(jnp.bfloat16)
        d_feat = lax.dot_general(d_kv, weight_kv, (((1,), (1,)), ((), ())), preferred_element_type=jnp.float32)
        return (carry + d_feat, attended)
    zeros_start = jnp.zeros((IMG_ALL, D), jnp.float32)
    summed_grad, attended = lax.scan(layer, zeros_start, (text, in_gain, w_query, q_gain, w_key_value, k_gain, grad_out))
    return (attended, summed_grad)
```

```python
import functools

import jax
import jax.numpy as jnp
from jax import lax
from jax.experimental import pallas as pl
from jax.experimental.pallas import tpu as pltpu
from jax.sharding import PartitionSpec as P

KV_HEADS = 8
HEAD_DIM = 128
TILES = 4
TILE_LEN = 24
TXT_TOK = 128
MB = 2
TEXT_CHUNKS = 4

eps = 1e-05

F32 = jnp.float32
BF16 = jnp.bfloat16
MIB = 1 << 20


def whole(memory=pltpu.VMEM):
    return pl.BlockSpec(memory_space=memory)


def dot_nn(a, b):
    return jnp.dot(a, b, preferred_element_type=F32)


def dot_nt(a, b):
    return lax.dot_general(a, b, (((1,), (1,)), ((), ())), preferred_element_type=F32)


def dot_tn(a, b):
    return lax.dot_general(a, b, (((0,), (0,)), ((), ())), preferred_element_type=F32)


def params(mib):
    return pltpu.CompilerParams(vmem_limit_bytes=mib * MIB)


def cost(flops, size):
    return pl.CostEstimate(flops=flops, bytes_accessed=size, transcendentals=0)


def norm_kernel(text_ref, gain_ref, *out_refs):
    width = out_refs[0].shape[1]
    total = 0.0
    for c in range(len(out_refs)):
        x = text_ref[0, :, c * width : (c + 1) * width].astype(F32)
        total = total + jnp.sum(x * x, axis=-1, keepdims=True)
    inverse = lax.rsqrt(total / text_ref.shape[2] + eps)
    for c in range(len(out_refs)):
        cols = slice(c * width, (c + 1) * width)
        x = text_ref[0, :, cols].astype(F32)
        gain = gain_ref[:, cols].astype(F32)
        out_refs[c][...] = (x * inverse * gain).astype(BF16)


def norm_rows(text, gain, chunks):
    rows, depth = text.shape[1:]
    return pl.pallas_call(
        norm_kernel,
        out_shape=[jax.ShapeDtypeStruct((rows, depth // chunks), BF16)] * chunks,
        in_specs=[whole(), whole()],
        out_specs=[whole()] * chunks,
        compiler_params=params(16),
        cost_estimate=cost(rows * depth * 6, rows * depth * 4),
        name="input_norm",
    )(text, gain)


def kv_send_kernel(pos_ref, feat_ref, wk_ref, wv_ref, out_ref):
    weight = jnp.concatenate([wk_ref[0], wv_ref[0]], axis=1)
    out_ref[0] = dot_nn(feat_ref[...], weight)


def kv_keep_kernel(pos_ref, feat_ref, wk_ref, wv_ref, other_ref, *out_refs):
    weight = jnp.concatenate([wk_ref[0], wv_ref[0]], axis=1)
    total = dot_nn(feat_ref[...], weight) + other_ref[0]
    for j, out_ref in enumerate(out_refs):

        @pl.when(pl.program_id(0) == j)
        def _():
            out_ref[...] = total.astype(out_ref.dtype)


def kv_partial(pos, features, weight, count, other=None):
    rows, depth = features.shape
    pairs = count // 2
    per_kv = count // KV_HEADS
    odd = 1 if other is None else 0

    def head_of(j, pos_ref):
        return lax.div(lax.bitwise_xor(pos_ref[0], 2 * j + odd), per_kv)

    block = (1, depth, HEAD_DIM)
    in_specs = [
        pl.BlockSpec((rows, depth), lambda j, pos_ref: (0, 0)),
        pl.BlockSpec(block, lambda j, pos_ref: (0, 0, head_of(j, pos_ref))),
        pl.BlockSpec(block, lambda j, pos_ref: (0, 0, KV_HEADS + head_of(j, pos_ref))),
    ]
    piece = pl.BlockSpec((1, rows, 2 * HEAD_DIM), lambda j, pos_ref: (j, 0, 0))
    operands = [pos, features, weight, weight]
    if other is None:
        kernel, name = kv_send_kernel, "kv_partial_other_core"
        out_specs = piece
        out_shape = jax.ShapeDtypeStruct((pairs, rows, 2 * HEAD_DIM), F32)
    else:
        kernel, name = kv_keep_kernel, "kv_partial_own_core"
        in_specs.append(piece)
        operands.append(other)
        flat = pl.BlockSpec((rows, 2 * HEAD_DIM), lambda j, pos_ref: (0, 0))
        out_specs = [flat] * pairs
        out_shape = [
            jax.ShapeDtypeStruct((rows, 2 * HEAD_DIM), F32 if j == 0 else BF16)
            for j in range(pairs)
        ]
    return pl.pallas_call(
        kernel,
        grid_spec=pltpu.PrefetchScalarGridSpec(
            num_scalar_prefetch=1, grid=(pairs,), in_specs=in_specs, out_specs=out_specs
        ),
        out_shape=out_shape,
        compiler_params=params(24),
        cost_estimate=cost(
            4 * pairs * rows * depth * HEAD_DIM, 4 * pairs * (depth + rows) * HEAD_DIM
        ),
        name=name,
    )(*operands)


def project_kernel(count, first, pos_ref, *refs):
    blocks, refs = refs[:count], refs[count:]
    if first:
        weight_ref, out_ref, held = refs
    else:
        weight_ref, before_ref, out_ref, held = refs
    step = pl.program_id(0)
    rows = blocks[0].shape[0]
    span = held.shape[2]

    @pl.when(step == 0)
    def _():
        for p, block in enumerate(blocks):
            at = pl.multiple_of(lax.bitwise_xor(pos_ref[0], p) * rows, rows)
            for s in range(held.shape[0]):
                part = block[:, s * span : (s + 1) * span]
                held[s, pl.ds(at, rows), :] = part.astype(held.dtype)
        if first:
            out_ref[...] = jnp.zeros_like(out_ref)
        else:
            out_ref[...] = before_ref[...]

    out_ref[...] += dot_nn(held[step].astype(BF16), weight_ref[0])


def project(pos, blocks, weight, before, chunk, chunks):
    count = len(blocks)
    rows, width = blocks[0].shape
    heads_width = weight.shape[2]
    steps = 2
    span = width // steps
    held = BF16 if rows % 16 == 0 else F32
    fixed = lambda i, pos_ref: (0, 0)
    in_specs = [pl.BlockSpec((rows, width), fixed)] * count
    in_specs.append(
        pl.BlockSpec(
            (1, span, heads_width), lambda i, pos_ref: (0, chunk * steps + i, 0)
        )
    )
    operands = [pos, *blocks, weight]
    if before is not None:
        in_specs.append(pl.BlockSpec((rows * count, heads_width), fixed))
        operands.append(before)
    return pl.pallas_call(
        functools.partial(project_kernel, count, before is None),
        grid_spec=pltpu.PrefetchScalarGridSpec(
            num_scalar_prefetch=1,
            grid=(steps,),
            in_specs=in_specs,
            out_specs=pl.BlockSpec((rows * count, heads_width), fixed),
            scratch_shapes=[pltpu.VMEM((steps, rows * count, span), held)],
        ),
        out_shape=jax.ShapeDtypeStruct((rows * count, heads_width), F32),
        compiler_params=params(24),
        cost_estimate=cost(
            2 * rows * count * width * heads_width, 2 * width * (rows * count + heads_width)
        ),
        name="query_projection",
    )(*operands)


def attention_kernel(
    count_ref, start_ref, query_ref, grad_ref, q_gain_ref, k_gain_ref, own_ref, *refs
):
    parts, (attended_ref, block_ref) = refs[:-2], refs[-2:]
    heads = query_ref.shape[1] // HEAD_DIM
    slots = TILES * TILE_LEN
    scale = HEAD_DIM ** (-0.5)
    q_gain = q_gain_ref[...].astype(F32)
    k_gain = k_gain_ref[...].astype(F32)
    kv = own_ref[...]
    for part in parts:
        kv = kv + part[...].astype(F32)
    key_raw = kv[:, :HEAD_DIM]
    values = kv[:, HEAD_DIM:].astype(BF16)
    inverse = lax.rsqrt(jnp.mean(key_raw * key_raw, axis=-1, keepdims=True) + eps)
    key_hat = key_raw * inverse
    keys = (key_hat * k_gain).astype(BF16)
    for b in range(MB):
        img = slice(b * slots, (b + 1) * slots)
        txt = slice(b * TXT_TOK, (b + 1) * TXT_TOK)
        keys_b, values_b = keys[img], values[img]
        live = lax.broadcasted_iota(jnp.int32, (1, slots), 1) < count_ref[b] * TILE_LEN
        row_live = lax.broadcasted_iota(jnp.int32, (TXT_TOK, 1), 0) >= start_ref[b]
        queries, upstream = [], []
        for h in range(heads):
            cols = slice(h * HEAD_DIM, (h + 1) * HEAD_DIM)
            raw = query_ref[txt, cols]
            q_inverse = lax.rsqrt(jnp.mean(raw * raw, axis=-1, keepdims=True) + eps)
            queries.append((raw * q_inverse * q_gain).astype(BF16))
            upstream.append(
                jnp.where(row_live, grad_ref[0, txt, cols].astype(F32), 0.0).astype(BF16)
            )
        queries = jnp.concatenate(queries, axis=0)
        upstream = jnp.concatenate(upstream, axis=0)
        scores = dot_nt(queries, keys_b) * scale
        exponent = jnp.where(live, jnp.exp(scores), 0.0)
        probs = exponent * (1.0 / jnp.sum(exponent, axis=-1, keepdims=True))
        weights = probs.astype(BF16)
        head_out = dot_nn(weights, values_b)
        for h in range(heads):
            cols = slice(h * HEAD_DIM, (h + 1) * HEAD_DIM)
            one = head_out[h * TXT_TOK : (h + 1) * TXT_TOK]
            attended_ref[0, txt, cols] = jnp.where(row_live, one, 0.0).astype(BF16)
        d_weights = dot_nt(upstream, values_b)
        inner = jnp.sum(probs * d_weights, axis=-1, keepdims=True)
        d_scores = (probs * (d_weights - inner) * scale).astype(BF16)
        d_keys = dot_tn(d_scores, queries)
        d_values = dot_tn(weights, upstream)
        scaled = d_keys * k_gain
        hat_b = key_hat[img]
        d_raw = inverse[img] * (
            scaled - hat_b * jnp.mean(hat_b * scaled, axis=-1, keepdims=True)
        )
        block_ref[img, :HEAD_DIM] = d_raw.astype(BF16)
        block_ref[img, HEAD_DIM:] = d_values.astype(BF16)


def attention(tile_count, image_start, raw_q, grad_out, q_gain, k_gain, own, parts):
    image_rows = own.shape[0]
    return pl.pallas_call(
        attention_kernel,
        in_specs=[whole(pltpu.SMEM)] * 2 + [whole()] * (5 + len(parts)),
        out_specs=[whole()] * 2,
        out_shape=[
            jax.ShapeDtypeStruct(grad_out.shape, BF16),
            jax.ShapeDtypeStruct((image_rows, 2 * HEAD_DIM), BF16),
        ],
        compiler_params=params(24),
        cost_estimate=cost(10 * raw_q.size * TILES * TILE_LEN, 8 * raw_q.size),
        name="attention",
    )(tile_count, image_start, raw_q, grad_out, q_gain, k_gain, own, *parts)


def grad_kernel(count, sections, pos_ref, *refs):
    per_kv = count // KV_HEADS
    blocks, weight_ref = refs[:count], refs[count]
    out_refs = refs[count + 1 : count + 1 + sections]
    d_kv, total = refs[count + 1 + sections : count + 3 + sections]
    rows = out_refs[0].shape[0]

    @pl.when(pl.program_id(0) == 0)
    def _():
        if per_kv > 1:
            sums = refs[-1]
            sums[...] = jnp.zeros_like(sums)
        for p, block in enumerate(blocks):
            head = lax.div(lax.bitwise_xor(pos_ref[0], p), per_kv)
            for half in range(2):
                at = pl.multiple_of((half * KV_HEADS + head) * HEAD_DIM, HEAD_DIM)
                part = block[:, half * HEAD_DIM : (half + 1) * HEAD_DIM]
                if per_kv > 1:
                    sums[:, pl.ds(at, HEAD_DIM)] += part.astype(F32)
                else:
                    d_kv[:, pl.ds(at, HEAD_DIM)] = part
        if per_kv > 1:
            d_kv[...] = sums[...].astype(BF16)

    total[...] = dot_nt(d_kv[...], weight_ref[0])
    for k, out_ref in enumerate(out_refs):
        to = lax.rem(pos_ref[1] + k, sections)
        part = total[pl.ds(pl.multiple_of(to * rows, rows), rows), :]
        out_ref[...] = part.astype(out_ref.dtype)


def feature_pieces(pos, blocks, weight, sections):
    count = len(blocks)
    image_rows = blocks[0].shape[0]
    width, depth = weight.shape[1:]
    rows = image_rows // sections
    steps = max(1, width // 256)
    span = width // steps
    fixed = lambda i, pos_ref: (0, 0)
    scratch = [pltpu.VMEM((image_rows, depth), BF16), pltpu.VMEM((image_rows, span), F32)]
    if count > KV_HEADS:
        scratch.append(pltpu.VMEM((image_rows, depth), F32))
    return pl.pallas_call(
        functools.partial(grad_kernel, count, sections),
        grid_spec=pltpu.PrefetchScalarGridSpec(
            num_scalar_prefetch=1,
            grid=(steps,),
            in_specs=[pl.BlockSpec(blocks[0].shape, fixed)] * count
            + [pl.BlockSpec((1, span, depth), lambda i, pos_ref: (0, i, 0))],
            out_specs=[pl.BlockSpec((rows, span), lambda i, pos_ref: (0, i))] * sections,
            scratch_shapes=scratch,
        ),
        out_shape=[
            jax.ShapeDtypeStruct((rows, width), F32 if k == 0 else BF16)
            for k in range(sections)
        ],
        compiler_params=params(24),
        cost_estimate=cost(2 * image_rows * width * depth, 2 * width * depth),
        name="feature_grad",
    )(pos, *blocks, weight)


def shards(
    text, features, in_gain, w_query, q_gain, w_key_value, k_gain, tile_count, image_start, grad_out
):
    count = lax.axis_size("tensor")
    sections = lax.axis_size("section")
    pos = jnp.stack([lax.axis_index("tensor"), lax.axis_index("section")]).astype(jnp.int32)

    def swap(x, distance):
        return lax.ppermute(x, "tensor", [(i, i ^ distance) for i in range(count)])

    def gather(x):
        out = [None] * count
        for j in range(0, count, 2):
            out[j] = x if j == 0 else swap(x, j)
        for j in range(0, count, 2):
            out[j + 1] = swap(out[j], 1)
        return out

    normed = norm_rows(text, in_gain, TEXT_CHUNKS)
    gathered = [gather(piece) for piece in normed]

    other = swap(kv_partial(pos, features, w_key_value, count), 1)
    own, *outgoing = kv_partial(pos, features, w_key_value, count, other)
    parts = [swap(x, 2 * (j + 1)) for j, x in enumerate(outgoing)]

    raw_q = None
    for c in range(TEXT_CHUNKS):
        raw_q = project(pos, gathered[c], w_query, raw_q, c, TEXT_CHUNKS)

    attended, block = attention(
        tile_count, image_start, raw_q, grad_out, q_gain, k_gain, own, parts
    )

    kept, *leaving = feature_pieces(pos, gather(block), w_key_value, sections)
    feature_grad = kept
    for k, x in enumerate(leaving):
        perm = [(i, (i + k + 1) % sections) for i in range(sections)]
        feature_grad = feature_grad + lax.ppermute(x, "section", perm).astype(F32)
    return (attended, feature_grad)


def solution(mesh):
    return jax.shard_map(
        shards,
        mesh=mesh,
        in_specs=(
            P("section", "tensor", None),
            P(None, "tensor"),
            P("section", None),
            P("section", None, "tensor"),
            P("section", None),
            P("section", "tensor", None),
            P("section", None),
            P(),
            P(),
            P("section", None, "tensor"),
        ),
        out_specs=(P("section", None, "tensor"), P("section", "tensor")),
        check_vma=False,
    )
```

```python
import functools

import jax
import jax.numpy as jnp
from jax import lax
from jax.experimental import pallas as pl
from jax.experimental.pallas import tpu as pltpu
from jax.sharding import PartitionSpec as P

KV_HEADS = 8
HEAD_DIM = 128
TILES = 4
TILE_LEN = 24
TXT_TOK = 128
MB = 2

eps = 1e-05

F32 = jnp.float32
BF16 = jnp.bfloat16
MIB = 1 << 20


def whole(memory=pltpu.VMEM):
    return pl.BlockSpec(memory_space=memory)


def dot_nn(a, b):
    return jnp.dot(a, b, preferred_element_type=F32)


def dot_nt(a, b):
    return lax.dot_general(a, b, (((1,), (1,)), ((), ())), preferred_element_type=F32)


def dot_tn(a, b):
    return lax.dot_general(a, b, (((0,), (0,)), ((), ())), preferred_element_type=F32)


def params(mib):
    return pltpu.CompilerParams(vmem_limit_bytes=mib * MIB)


def cost(flops, size):
    return pl.CostEstimate(flops=flops, bytes_accessed=size, transcendentals=0)


def norm_kernel(text_hbm, gain_hbm, out_ref, text_ref, gain_ref, sems):
    copies = [
        pltpu.make_async_copy(text_hbm, text_ref, sems.at[0]),
        pltpu.make_async_copy(gain_hbm, gain_ref, sems.at[1]),
    ]
    for copy in copies:
        copy.start()
    for copy in copies:
        copy.wait()
    depth = out_ref.shape[1]
    width = min(2048, depth)
    total = 0.0
    for c in range(0, depth, width):
        x = text_ref[0, :, c : c + width].astype(F32)
        total = total + jnp.sum(x * x, axis=-1, keepdims=True)
    inverse = lax.rsqrt(total / depth + eps)
    for c in range(0, depth, width):
        x = text_ref[0, :, c : c + width].astype(F32)
        gain = gain_ref[:, c : c + width].astype(F32)
        out_ref[:, c : c + width] = (x * inverse * gain).astype(BF16)


def norm_rows(text, gain):
    rows, depth = text.shape[1:]
    return pl.pallas_call(
        norm_kernel,
        out_shape=jax.ShapeDtypeStruct((rows, depth), BF16),
        in_specs=[whole(pl.ANY)] * 2,
        out_specs=whole(),
        scratch_shapes=[
            pltpu.VMEM(text.shape, BF16),
            pltpu.VMEM(gain.shape, BF16),
            pltpu.SemaphoreType.DMA((2,)),
        ],
        compiler_params=params(60),
        cost_estimate=cost(rows * depth * 6, rows * depth * 4),
        name="input_norm",
    )(text, gain)


def kv_kernel(per_kv, pairs, odd, pos_ref, feat_ref, weight_ref, *refs):
    features = feat_ref[...]
    for j in range(pairs):
        head = lax.div(lax.bitwise_xor(pos_ref[0], 2 * j + odd), per_kv)
        cols = [
            pl.ds(pl.multiple_of((half * KV_HEADS + head) * HEAD_DIM, HEAD_DIM), HEAD_DIM)
            for half in range(2)
        ]
        weight = jnp.concatenate([weight_ref[0, :, c] for c in cols], axis=1)
        total = dot_nn(features, weight)
        if odd:
            refs[-1][j] = total
        else:
            out_ref = refs[1 + j]
            out_ref[...] = (total + refs[0][j]).astype(out_ref.dtype)


def kv_partial(pos, features, weight, count, other=None, after=()):
    rows, depth = features.shape
    pairs = count // 2
    odd = 1 if other is None else 0
    in_specs = [whole(pltpu.SMEM), whole(), whole()]
    if odd:
        extra = list(after)
        in_specs += [whole(pl.ANY)] * len(extra)
        out_shape = jax.ShapeDtypeStruct((pairs, rows, 2 * HEAD_DIM), F32)
        out_specs = whole()
    else:
        extra = [other]
        in_specs.append(whole())
        out_shape = [
            jax.ShapeDtypeStruct((rows, 2 * HEAD_DIM), F32 if j == 0 else BF16)
            for j in range(pairs)
        ]
        out_specs = [whole()] * pairs
    return pl.pallas_call(
        functools.partial(kv_kernel, count // KV_HEADS, pairs, odd),
        in_specs=in_specs,
        out_specs=out_specs,
        out_shape=out_shape,
        compiler_params=params(24),
        cost_estimate=cost(
            4 * pairs * rows * depth * HEAD_DIM, 4 * pairs * (depth + rows) * HEAD_DIM
        ),
        name="kv_partial_other_core" if odd else "kv_partial_own_core",
    )(pos, features, weight, *extra)


def project_kernel(places, pos_ref, *refs):
    blocks, (weight_ref, out_ref, held) = refs[:-3], refs[-3:]
    spans, _, span = held.shape
    for block, (p, first) in zip(blocks, places):
        rows, width = block.shape
        at = pl.multiple_of(lax.bitwise_xor(pos_ref[0], p) * rows, rows)
        for c in range(0, width, span):
            part = block[:, c : c + span].astype(held.dtype)
            held[(first + c) // span, pl.ds(at, rows), :] = part
    out_ref[...] = jnp.zeros_like(out_ref)

    @pl.loop(0, spans)
    def _(s):
        weight = weight_ref[0, pl.ds(pl.multiple_of(s * span, span), span), :]
        out_ref[...] += dot_nn(held[s].astype(BF16), weight)


def project(pos, blocks, weight, count):
    places = [(p, first) for p, first, _ in blocks]
    arrays = [array for _, _, array in blocks]
    rows = arrays[0].shape[0]
    depth, heads_width = weight.shape[1:]
    span = 1024
    held = BF16 if rows % 16 == 0 else F32
    return pl.pallas_call(
        functools.partial(project_kernel, places),
        in_specs=[whole(pltpu.SMEM)] + [whole()] * (len(arrays) + 1),
        out_specs=whole(),
        out_shape=jax.ShapeDtypeStruct((rows * count, heads_width), F32),
        scratch_shapes=[pltpu.VMEM((depth // span, rows * count, span), held)],
        compiler_params=params(24),
        cost_estimate=cost(
            2 * rows * count * depth * heads_width, 2 * depth * (rows * count + heads_width)
        ),
        name="query_projection",
    )(pos, *arrays, weight)


def attention_kernel(
    count_ref, start_ref, query_ref, grad_ref, q_gain_ref, k_gain_ref, own_ref, *refs
):
    parts, (attended_ref, block_ref) = refs[:-2], refs[-2:]
    heads = query_ref.shape[1] // HEAD_DIM
    slots = TILES * TILE_LEN
    scale = HEAD_DIM ** (-0.5)
    q_gain = q_gain_ref[...].astype(F32)
    k_gain = k_gain_ref[...].astype(F32)
    kv = own_ref[...]
    for part in parts:
        kv = kv + part[...].astype(F32)
    key_raw = kv[:, :HEAD_DIM]
    values = kv[:, HEAD_DIM:].astype(BF16)
    inverse = lax.rsqrt(jnp.mean(key_raw * key_raw, axis=-1, keepdims=True) + eps)
    key_hat = key_raw * inverse
    keys = (key_hat * k_gain).astype(BF16)
    for b in range(MB):
        img = slice(b * slots, (b + 1) * slots)
        txt = slice(b * TXT_TOK, (b + 1) * TXT_TOK)
        keys_b, values_b = keys[img], values[img]
        live = lax.broadcasted_iota(jnp.int32, (1, slots), 1) < count_ref[b] * TILE_LEN
        row_live = lax.broadcasted_iota(jnp.int32, (TXT_TOK, 1), 0) >= start_ref[b]
        queries, upstream = [], []
        for h in range(heads):
            cols = slice(h * HEAD_DIM, (h + 1) * HEAD_DIM)
            raw = query_ref[txt, cols]
            q_inverse = lax.rsqrt(jnp.mean(raw * raw, axis=-1, keepdims=True) + eps)
            queries.append((raw * q_inverse * q_gain).astype(BF16))
            upstream.append(
                jnp.where(row_live, grad_ref[0, txt, cols].astype(F32), 0.0).astype(BF16)
            )
        queries = jnp.concatenate(queries, axis=0)
        upstream = jnp.concatenate(upstream, axis=0)
        scores = dot_nt(queries, keys_b) * scale
        exponent = jnp.where(live, jnp.exp(scores), 0.0)
        probs = exponent * (1.0 / jnp.sum(exponent, axis=-1, keepdims=True))
        weights = probs.astype(BF16)
        head_out = dot_nn(weights, values_b)
        for h in range(heads):
            cols = slice(h * HEAD_DIM, (h + 1) * HEAD_DIM)
            one = head_out[h * TXT_TOK : (h + 1) * TXT_TOK]
            attended_ref[0, txt, cols] = jnp.where(row_live, one, 0.0).astype(BF16)
        d_weights = dot_nt(upstream, values_b)
        inner = jnp.sum(probs * d_weights, axis=-1, keepdims=True)
        d_scores = (probs * (d_weights - inner) * scale).astype(BF16)
        d_keys = dot_tn(d_scores, queries)
        d_values = dot_tn(weights, upstream)
        scaled = d_keys * k_gain
        hat_b = key_hat[img]
        d_raw = inverse[img] * (
            scaled - hat_b * jnp.mean(hat_b * scaled, axis=-1, keepdims=True)
        )
        block_ref[img, :HEAD_DIM] = d_raw.astype(BF16)
        block_ref[img, HEAD_DIM:] = d_values.astype(BF16)


def attention(tile_count, image_start, raw_q, grad_out, q_gain, k_gain, own, parts):
    image_rows = own.shape[0]
    return pl.pallas_call(
        attention_kernel,
        in_specs=[whole(pltpu.SMEM)] * 2 + [whole()] * (5 + len(parts)),
        out_specs=[whole()] * 2,
        out_shape=[
            jax.ShapeDtypeStruct(grad_out.shape, BF16),
            jax.ShapeDtypeStruct((image_rows, 2 * HEAD_DIM), BF16),
        ],
        compiler_params=params(24),
        cost_estimate=cost(10 * raw_q.size * TILES * TILE_LEN, 8 * raw_q.size),
        name="attention",
    )(tile_count, image_start, raw_q, grad_out, q_gain, k_gain, own, *parts)


def grad_kernel(count, sections, pos_ref, *refs):
    per_kv = count // KV_HEADS
    blocks, weight_ref = refs[:count], refs[count]
    out_refs = refs[count + 1 : count + 1 + sections]
    d_kv, total = refs[count + 1 + sections : count + 3 + sections]
    rows = out_refs[0].shape[0]

    @pl.when(pl.program_id(0) == 0)
    def _():
        if per_kv > 1:
            sums = refs[-1]
            sums[...] = jnp.zeros_like(sums)
        for p, block in enumerate(blocks):
            head = lax.div(lax.bitwise_xor(pos_ref[0], p), per_kv)
            for half in range(2):
                at = pl.multiple_of((half * KV_HEADS + head) * HEAD_DIM, HEAD_DIM)
                part = block[:, half * HEAD_DIM : (half + 1) * HEAD_DIM]
                if per_kv > 1:
                    sums[:, pl.ds(at, HEAD_DIM)] += part.astype(F32)
                else:
                    d_kv[:, pl.ds(at, HEAD_DIM)] = part
        if per_kv > 1:
            d_kv[...] = sums[...].astype(BF16)

    total[...] = dot_nt(d_kv[...], weight_ref[0])
    for k, out_ref in enumerate(out_refs):
        to = lax.rem(pos_ref[1] + k, sections)
        part = total[pl.ds(pl.multiple_of(to * rows, rows), rows), :]
        out_ref[...] = part.astype(out_ref.dtype)


def feature_pieces(pos, blocks, weight, sections):
    count = len(blocks)
    image_rows = blocks[0].shape[0]
    width, depth = weight.shape[1:]
    rows = image_rows // sections
    steps = max(1, width // 256)
    span = width // steps
    fixed = lambda i, pos_ref: (0, 0)
    scratch = [pltpu.VMEM((image_rows, depth), BF16), pltpu.VMEM((image_rows, span), F32)]
    if count > KV_HEADS:
        scratch.append(pltpu.VMEM((image_rows, depth), F32))
    return pl.pallas_call(
        functools.partial(grad_kernel, count, sections),
        grid_spec=pltpu.PrefetchScalarGridSpec(
            num_scalar_prefetch=1,
            grid=(steps,),
            in_specs=[pl.BlockSpec(blocks[0].shape, fixed)] * count
            + [pl.BlockSpec((1, span, depth), lambda i, pos_ref: (0, i, 0))],
            out_specs=[pl.BlockSpec((rows, span), lambda i, pos_ref: (0, i))] * sections,
            scratch_shapes=scratch,
        ),
        out_shape=[
            jax.ShapeDtypeStruct((rows, width), F32 if k == 0 else BF16)
            for k in range(sections)
        ],
        compiler_params=params(24),
        cost_estimate=cost(2 * image_rows * width * depth, 2 * width * depth),
        name="feature_grad",
    )(pos, *blocks, weight)


def shards(
    text, features, in_gain, w_query, q_gain, w_key_value, k_gain, tile_count, image_start, grad_out
):
    count = lax.axis_size("tensor")
    sections = lax.axis_size("section")
    pos = jnp.stack([lax.axis_index("tensor"), lax.axis_index("section")]).astype(jnp.int32)

    def swap(x, distance):
        return lax.ppermute(x, "tensor", [(i, i ^ distance) for i in range(count)])

    def gather(x):
        out = {0: x}
        out.update({j: swap(x, j) for j in range(2, count, 2)})
        out.update({p ^ 1: swap(block, 1) for p, block in out.items()})
        return [out[p] for p in range(count)]

    def gather_in_turn(x):
        bits = [1 << b for b in range(1, count.bit_length() - 1)]
        width = x.shape[1] // 2
        direct = {bit: swap(x, bit) for bit in bits}
        blocks = [(0, 0, x)] + [(bit, 0, block) for bit, block in direct.items()]
        for half, order in enumerate((bits, bits[::-1])):
            first = half * width
            held = {0: None}
            for bit in order:
                for p in list(held):
                    if p == 0:
                        held[bit] = direct[bit][:, first : first + width]
                    else:
                        held[p ^ bit] = swap(held[p], bit)
                        blocks.append((p ^ bit, first, held[p ^ bit]))
        return blocks + [(p ^ 1, first, swap(block, 1)) for p, first, block in blocks]

    blocks = gather_in_turn(norm_rows(text, in_gain))

    other = swap(kv_partial(pos, features, w_key_value, count), 1)
    own, *outgoing = kv_partial(pos, features, w_key_value, count, other)
    parts = [swap(x, 2 * (j + 1)) for j, x in enumerate(outgoing)]

    raw_q = project(pos, blocks, w_query, count)

    attended, block = attention(
        tile_count, image_start, raw_q, grad_out, q_gain, k_gain, own, parts
    )

    kept, *leaving = feature_pieces(pos, gather(block), w_key_value, sections)
    feature_grad = kept
    for k, x in enumerate(leaving):
        perm = [(i, (i + k + 1) % sections) for i in range(sections)]
        feature_grad = feature_grad + lax.ppermute(x, "section", perm).astype(F32)
    return (attended, feature_grad)


def solution(mesh):
    return jax.shard_map(
        shards,
        mesh=mesh,
        in_specs=(
            P("section", "tensor", None),
            P(None, "tensor"),
            P("section", None),
            P("section", None, "tensor"),
            P("section", None),
            P("section", "tensor", None),
            P("section", None),
            P(),
            P(),
            P("section", None, "tensor"),
        ),
        out_specs=(P("section", None, "tensor"), P("section", "tensor")),
        check_vma=False,
    )
```

```python
import functools

import jax
import jax.numpy as jnp
from jax import lax
from jax.experimental import pallas as pl
from jax.experimental.pallas import tpu as pltpu
from jax.sharding import PartitionSpec as P

KV_HEADS = 8
HEAD_DIM = 128
TILES = 4
TILE_LEN = 24
TXT_TOK = 128
MB = 2
SLOTS = TILES * TILE_LEN

eps = 1e-05

F32 = jnp.float32
BF16 = jnp.bfloat16
MIB = 1 << 20


def whole(memory=pltpu.VMEM):
    return pl.BlockSpec(memory_space=memory)


def dot_nn(a, b):
    return jnp.dot(a, b, preferred_element_type=F32)


def dot_nt(a, b):
    return lax.dot_general(a, b, (((1,), (1,)), ((), ())), preferred_element_type=F32)


def dot_tn(a, b):
    return lax.dot_general(a, b, (((0,), (0,)), ((), ())), preferred_element_type=F32)


def params(mib):
    return pltpu.CompilerParams(vmem_limit_bytes=mib * MIB)


def cost(flops, size):
    return pl.CostEstimate(flops=flops, bytes_accessed=size, transcendentals=0)


def head_columns(head):
    return [
        pl.ds(pl.multiple_of((half * KV_HEADS + head) * HEAD_DIM, HEAD_DIM), HEAD_DIM)
        for half in range(2)
    ]


def kv_kernel(per_kv, pairs, odd, pos_ref, feat_ref, weight_ref, *refs):
    features = feat_ref[...]
    for j in range(pairs):
        head = lax.div(lax.bitwise_xor(pos_ref[0], 2 * j + odd), per_kv)
        weight = jnp.concatenate([weight_ref[0, :, c] for c in head_columns(head)], axis=1)
        total = dot_nn(features, weight)
        out_ref = refs[j - pairs]
        if not odd:
            total = total + refs[j][...]
        out_ref[...] = total.astype(out_ref.dtype)


def kv_partial(pos, features, weight, count, other=None):
    rows, depth = features.shape
    pairs = count // 2
    odd = 1 if other is None else 0
    out_shape = [
        jax.ShapeDtypeStruct((rows, 2 * HEAD_DIM), F32 if odd or j == 0 else BF16)
        for j in range(pairs)
    ]
    operands = (pos, features, weight, *(other or ()))
    return pl.pallas_call(
        functools.partial(kv_kernel, count // KV_HEADS, pairs, odd),
        in_specs=[whole(pltpu.SMEM)] + [whole()] * (len(operands) - 1),
        out_specs=[whole()] * pairs,
        out_shape=out_shape,
        compiler_params=params(24),
        cost_estimate=cost(0, 0),
        name="kv_partial_other_core" if odd else "kv_partial_own_core",
    )(*operands)


def query_kernel(shape, gain_ref, weight_ref, q_gain_ref, *refs):
    refs, out_ref = refs[:-1], refs[-1]
    groups, at = [], 0
    for parts in shape:
        groups.append(refs[at : at + parts])
        at += parts
    depth, heads_width = weight_ref.shape[1:]
    span = 1024

    def columns(parts, c):
        for part in parts:
            if c < part.shape[1]:
                return part[:, c : c + span].astype(F32)
            c -= part.shape[1]

    inverses = []
    for parts in groups:
        total = 0.0
        for c in range(0, depth, span):
            x = columns(parts, c)
            total = total + jnp.sum(x * x, axis=-1, keepdims=True)
        inverses.append(lax.rsqrt(total / depth + eps))
    raw = 0.0
    for c in range(0, depth, span):
        gain = gain_ref[:, c : c + span].astype(F32)
        x = jnp.concatenate(
            [columns(parts, c) * inverse * gain for parts, inverse in zip(groups, inverses)],
            axis=0,
        )
        raw = raw + dot_nn(x.astype(BF16), weight_ref[0, c : c + span, :])
    q_gain = q_gain_ref[...].astype(F32)
    for c in range(0, heads_width, HEAD_DIM):
        head = raw[:, c : c + HEAD_DIM]
        inverse = lax.rsqrt(jnp.mean(head * head, axis=-1, keepdims=True) + eps)
        out_ref[:, c : c + HEAD_DIM] = (head * inverse * q_gain).astype(BF16)


def queries_of(groups, gain, weight, q_gain, name):
    arrays = [part for parts in groups for part in parts]
    rows = sum(parts[0].shape[0] for parts in groups)
    depth, heads_width = weight.shape[1:]
    return pl.pallas_call(
        functools.partial(query_kernel, [len(parts) for parts in groups]),
        in_specs=[whole()] * (3 + len(arrays)),
        out_specs=whole(),
        out_shape=jax.ShapeDtypeStruct((rows, heads_width), BF16),
        compiler_params=params(24),
        cost_estimate=cost(0, 0),
        name=name,
    )(gain, weight, q_gain, *arrays)


def attention_kernel(places, count, rows, last, sizes, pos_ref, count_ref, start_ref, *refs):
    queries_refs, refs = refs[:sizes], refs[sizes:]
    grad_ref, k_gain_ref, refs = refs[0], refs[1], refs[2:]
    narrow = rows % 16 != 0
    if narrow:
        refs, (grad_rows, att_rows) = refs[:-2], refs[-2:]
        grad_rows[...] = grad_ref[0].astype(F32)
    if last:
        att_in, d_keys_in, d_values_in, keys_ref, values_ref, hat_ref, inverse_ref = refs[:7]
        att_ref, block_ref, d_keys_ref, d_values_ref = refs[7:]
        if narrow:
            att_rows[...] = att_in[0].astype(F32)
        else:
            att_ref[...] = att_in[...]
        d_keys_ref[...] = d_keys_in[...]
        d_values_ref[...] = d_values_in[...]
    else:
        parts = refs[:-7]
        att_ref, d_keys_ref, d_values_ref, keys_ref, values_ref, hat_ref, inverse_ref = refs[-7:]
        kv = sum(part[...].astype(F32) for part in parts)
        key_raw = kv[:, :HEAD_DIM]
        inverse = lax.rsqrt(jnp.mean(key_raw * key_raw, axis=-1, keepdims=True) + eps)
        hat_ref[...] = key_raw * inverse
        inverse_ref[...] = jnp.broadcast_to(inverse, key_raw.shape)
        keys_ref[...] = (key_raw * inverse * k_gain_ref[...].astype(F32)).astype(BF16)
        values_ref[...] = kv[:, HEAD_DIM:].astype(BF16)
        d_keys_ref[...] = jnp.zeros_like(d_keys_ref)
        d_values_ref[...] = jnp.zeros_like(d_values_ref)
        if narrow:
            att_rows[...] = jnp.zeros_like(att_rows)

    scale = HEAD_DIM ** (-0.5)
    heads = grad_ref.shape[2] // HEAD_DIM
    per_sample = count // MB
    mine = lax.div(pos_ref[0], per_sample)
    for far in range(MB):
        chosen = [(p, ref, at) for p, ref, at in zip(*places_of(places, queries_refs, rows)) if p // per_sample == far]
        if not chosen:
            continue
        sample = lax.bitwise_xor(mine, far)
        img = pl.ds(pl.multiple_of(sample * SLOTS, SLOTS), SLOTS)
        keys, values = keys_ref[img, :], values_ref[img, :]
        live = lax.broadcasted_iota(jnp.int32, (1, SLOTS), 1) < count_ref[sample] * TILE_LEN
        queries, upstream, masks, spots = [], [], [], []
        for p, _, _ in chosen:
            at = pl.multiple_of(lax.bitwise_xor(pos_ref[0], p) * rows, rows)
            token = lax.broadcasted_iota(jnp.int32, (rows, 1), 0) + (at - sample * TXT_TOK)
            masks.append(token >= start_ref[sample])
            spots.append(pl.ds(at, rows))
        for h in range(heads):
            cols = slice(h * HEAD_DIM, (h + 1) * HEAD_DIM)
            for (p, ref, at), mask, spot in zip(chosen, masks, spots):
                queries.append(ref[at : at + rows, cols])
                grad = grad_rows[spot, cols] if narrow else grad_ref[0, spot, cols].astype(F32)
                upstream.append(jnp.where(mask, grad, 0.0).astype(BF16))
        queries = jnp.concatenate(queries, axis=0)
        upstream = jnp.concatenate(upstream, axis=0)
        scores = dot_nt(queries, keys) * scale
        exponent = jnp.where(live, jnp.exp(scores), 0.0)
        probs = exponent * (1.0 / jnp.sum(exponent, axis=-1, keepdims=True))
        weights = probs.astype(BF16)
        head_out = dot_nn(weights, values)
        at = 0
        for h in range(heads):
            cols = slice(h * HEAD_DIM, (h + 1) * HEAD_DIM)
            for mask, spot in zip(masks, spots):
                one = jnp.where(mask, head_out[at : at + rows], 0.0)
                if narrow:
                    att_rows[spot, cols] = one
                else:
                    att_ref[0, spot, cols] = one.astype(BF16)
                at += rows
        d_weights = dot_nt(upstream, values)
        inner = jnp.sum(probs * d_weights, axis=-1, keepdims=True)
        d_scores = (probs * (d_weights - inner) * scale).astype(BF16)
        d_keys_ref[img, :] += dot_tn(d_scores, queries)
        d_values_ref[img, :] += dot_tn(weights, upstream)
    if narrow:
        att_ref[0] = att_rows[...].astype(BF16)
    if last:
        hat = hat_ref[...]
        scaled = d_keys_ref[...] * k_gain_ref[...].astype(F32)
        d_raw = inverse_ref[...] * (
            scaled - hat * jnp.mean(hat * scaled, axis=-1, keepdims=True)
        )
        block_ref[:, :HEAD_DIM] = d_raw.astype(BF16)
        block_ref[:, HEAD_DIM:] = d_values_ref[...].astype(BF16)


def places_of(places, arrays, rows):
    found = [
        (p, array, i * rows) for group, array in zip(places, arrays) for i, p in enumerate(group)
    ]
    return zip(*found)


def attention(pos, tile_count, image_start, queries, places, count, grad_out, k_gain, state, last):
    rows = grad_out.shape[1] // count
    image_rows = MB * SLOTS
    vector = jax.ShapeDtypeStruct((image_rows, HEAD_DIM), F32)
    rounded = jax.ShapeDtypeStruct((image_rows, HEAD_DIM), BF16)
    attended = jax.ShapeDtypeStruct(grad_out.shape, BF16)
    scratch = []
    if last:
        out_shape = [attended, jax.ShapeDtypeStruct((image_rows, 2 * HEAD_DIM), BF16)]
        scratch += [pltpu.VMEM(vector.shape, F32)] * 2
    else:
        out_shape = [attended, vector, vector, rounded, rounded, vector, vector]
    if rows % 16 != 0:
        scratch += [pltpu.VMEM(grad_out.shape[1:], F32)] * 2
    operands = [*queries, grad_out, k_gain, *state]
    size = sum(array.size for array in queries)
    return pl.pallas_call(
        functools.partial(attention_kernel, places, count, rows, last, len(queries)),
        in_specs=[whole(pltpu.SMEM)] * 3 + [whole()] * len(operands),
        out_specs=[whole()] * len(out_shape),
        out_shape=out_shape,
        scratch_shapes=scratch,
        compiler_params=params(24),
        cost_estimate=cost(40 * size * SLOTS, 8 * size),
        name="attention_last" if last else "attention_first",
    )(pos, tile_count, image_start, *operands)


def grad_kernel(distances, per_kv, sections, first, last, pos_ref, *refs):
    blocks, weight_ref, refs = refs[: len(distances)], refs[len(distances)], refs[len(distances) + 1 :]
    if not first:
        before_ref, refs = refs[0], refs[1:]
    total = refs[-1]
    image_rows, width = total.shape
    heads = []
    for i in range(0, len(distances), per_kv):
        head = lax.div(lax.bitwise_xor(pos_ref[0], distances[i]), per_kv)
        if per_kv == 1:
            block = blocks[i][...]
        else:
            block = sum(b[...].astype(F32) for b in blocks[i : i + per_kv]).astype(BF16)
        heads.append((head_columns(head), block))
    span = 256
    for c in range(0, width, span):
        here = slice(c, c + span)
        part = 0.0 if first else before_ref[:, here]
        for columns, block in heads:
            weight = jnp.concatenate([weight_ref[0, here, k] for k in columns], axis=1)
            part = part + dot_nt(block, weight)
        total[:, here] = part
    if last:
        rows = image_rows // sections
        for k in range(sections):
            to = lax.rem(pos_ref[1] + k, sections)
            piece = total[pl.ds(pl.multiple_of(to * rows, rows), rows), :]
            refs[k][...] = piece.astype(refs[k].dtype)


def feature_gradient(pos, blocks, weight, per_kv, sections, before=None, last=True):
    distances = [p for p, _ in blocks]
    arrays = [block for _, block in blocks]
    image_rows = arrays[0].shape[0]
    width, depth = weight.shape[1:]
    rows = image_rows // sections
    if last:
        out_shape = [
            jax.ShapeDtypeStruct((rows, width), F32 if k == 0 else BF16) for k in range(sections)
        ]
        out_specs = [whole()] * sections
        scratch = [pltpu.VMEM((image_rows, width), F32)]
    else:
        out_shape = jax.ShapeDtypeStruct((image_rows, width), F32)
        out_specs = whole()
        scratch = []
    operands = [*arrays, weight] + ([] if before is None else [before])
    return pl.pallas_call(
        functools.partial(grad_kernel, distances, per_kv, sections, before is None, last),
        in_specs=[whole(pltpu.SMEM)] + [whole()] * len(operands),
        out_specs=out_specs,
        out_shape=out_shape,
        scratch_shapes=scratch,
        compiler_params=params(24),
        cost_estimate=cost(
            4 * HEAD_DIM * len(arrays) * image_rows * width, 4 * HEAD_DIM * width * len(arrays)
        ),
        name="feature_grad_last" if last else "feature_grad_first",
    )(pos, *operands)


def shards(
    text, features, in_gain, w_query, q_gain, w_key_value, k_gain, tile_count, image_start, grad_out
):
    count = lax.axis_size("tensor")
    sections = lax.axis_size("section")
    per_kv = count // KV_HEADS
    pos = jnp.stack([lax.axis_index("tensor"), lax.axis_index("section")]).astype(jnp.int32)

    def swap(x, distance):
        return lax.ppermute(x, "tensor", [(i, i ^ distance) for i in range(count)])

    own_text = text[0]
    bits = [1 << b for b in range(1, count.bit_length() - 1)]
    width = own_text.shape[1] // 2
    direct = {bit: swap(own_text, bit) for bit in bits}
    def both_cores(blocks):
        out = {}
        for p, parts in blocks.items():
            out[p] = parts
            out[p ^ 1] = [swap(part, 1) for part in parts]
        return list(out), list(out.values())

    def queries(both, name):
        return queries_of(both[1], in_gain, w_query, q_gain, name)

    near = both_cores({0: [own_text]})
    q_near = queries(near, "queries_own_chip")
    other = [swap(x, 1) for x in kv_partial(pos, features, w_key_value, count)]
    own, *outgoing = kv_partial(pos, features, w_key_value, count, other)
    direct, outgoing, q_near = lax.optimization_barrier((direct, outgoing, q_near))
    forwarded = {}
    for half, order in enumerate((bits, bits[::-1])):
        first = half * width
        held = {0: None}
        for bit in order:
            for p in list(held):
                if p == 0:
                    held[bit] = direct[bit][:, first : first + width]
                else:
                    held[p ^ bit] = swap(held[p], bit)
                    forwarded.setdefault(p ^ bit, []).append(held[p ^ bit])

    parts = [own] + [swap(x, 2 * (j + 1)) for j, x in enumerate(outgoing)]
    next_to = both_cores({p: [block] for p, block in direct.items()})
    q_next = queries(next_to, "queries_neighbours")

    attend = functools.partial(attention, pos, tile_count, image_start)
    state = attend(
        [q_near, q_next], [near[0], next_to[0]], count, grad_out, k_gain, parts, last=False
    )
    forwarded, state = lax.optimization_barrier((forwarded, state))
    far = both_cores(forwarded)
    q_far = queries(far, "queries_forwarded")
    attended, block = attend([q_far], [far[0]], count, grad_out, k_gain, state, last=True)

    same_core = {0: block}
    same_core.update({j: swap(block, j) for j in range(2, count, 2)})
    gathered = dict(same_core)
    gathered.update({p ^ 1: swap(x, 1) for p, x in same_core.items()})
    before = None
    if per_kv == 1:
        before = feature_gradient(
            pos, sorted(same_core.items()), w_key_value, per_kv, sections, last=False
        )
        gathered = {p: x for p, x in gathered.items() if p not in same_core}
    feature_grad, *leaving = feature_gradient(
        pos, sorted(gathered.items()), w_key_value, per_kv, sections, before
    )
    for k, x in enumerate(leaving):
        perm = [(i, (i + k + 1) % sections) for i in range(sections)]
        feature_grad = feature_grad + lax.ppermute(x, "section", perm).astype(F32)
    return (attended, feature_grad)


def solution(mesh):
    return jax.shard_map(
        shards,
        mesh=mesh,
        in_specs=(
            P("section", "tensor", None),
            P(None, "tensor"),
            P("section", None),
            P("section", None, "tensor"),
            P("section", None),
            P("section", "tensor", None),
            P("section", None),
            P(),
            P(),
            P("section", None, "tensor"),
        ),
        out_specs=(P("section", None, "tensor"), P("section", "tensor")),
        check_vma=False,
    )
```

```python
import functools

import jax
import jax.numpy as jnp
from jax import lax
from jax.experimental import pallas as pl
from jax.experimental.pallas import tpu as pltpu
from jax.sharding import PartitionSpec as P

KV_HEADS = 8
HEAD_DIM = 128
TILES = 4
TILE_LEN = 24
TXT_TOK = 128
MB = 2
SLOTS = TILES * TILE_LEN

eps = 1e-05

F32 = jnp.float32
BF16 = jnp.bfloat16
MIB = 1 << 20


def whole(memory=pltpu.VMEM):
    return pl.BlockSpec(memory_space=memory)


def dot_nn(a, b):
    return jnp.dot(a, b, preferred_element_type=F32)


def dot_nt(a, b):
    return lax.dot_general(a, b, (((1,), (1,)), ((), ())), preferred_element_type=F32)


def dot_tn(a, b):
    return lax.dot_general(a, b, (((0,), (0,)), ((), ())), preferred_element_type=F32)


def params(mib):
    return pltpu.CompilerParams(vmem_limit_bytes=mib * MIB)


def cost(flops, size):
    return pl.CostEstimate(flops=flops, bytes_accessed=size, transcendentals=0)


def here():
    return lax.axis_index("tensor")


def head_columns(head):
    return [
        pl.ds(pl.multiple_of((half * KV_HEADS + head) * HEAD_DIM, HEAD_DIM), HEAD_DIM)
        for half in range(2)
    ]


def kv_kernel(per_kv, pairs, odd, feat_ref, weight_ref, *refs):
    features = feat_ref[...]
    for j in range(pairs):
        head = lax.div(lax.bitwise_xor(here(), 2 * j + odd), per_kv)
        weight = jnp.concatenate([weight_ref[0, :, c] for c in head_columns(head)], axis=1)
        total = dot_nn(features, weight)
        out_ref = refs[j - pairs]
        if not odd:
            total = total + refs[j][...]
        out_ref[...] = total.astype(out_ref.dtype)


def kv_partial(features, weight, count, other=None):
    rows, depth = features.shape
    pairs = count // 2
    odd = 1 if other is None else 0
    out_shape = [
        jax.ShapeDtypeStruct((rows, 2 * HEAD_DIM), F32 if odd or j == 0 else BF16)
        for j in range(pairs)
    ]
    operands = (features, weight, *(other or ()))
    return pl.pallas_call(
        functools.partial(kv_kernel, count // KV_HEADS, pairs, odd),
        in_specs=[whole()] * len(operands),
        out_specs=[whole()] * pairs,
        out_shape=out_shape,
        compiler_params=params(24),
        cost_estimate=cost(0, 0),
        name="kv_partial_other_core" if odd else "kv_partial_own_core",
    )(*operands)


def query_kernel(shape, gain_ref, weight_ref, q_gain_ref, *refs):
    refs, out_ref = refs[:-1], refs[-1]
    groups, at = [], 0
    for parts in shape:
        groups.append(refs[at : at + parts])
        at += parts
    depth, heads_width = weight_ref.shape[1:]
    span = 1024

    def columns(parts, c):
        for part in parts:
            if c < part.shape[1]:
                return part[:, c : c + span].astype(F32)
            c -= part.shape[1]

    inverses = []
    for parts in groups:
        total = 0.0
        for c in range(0, depth, span):
            x = columns(parts, c)
            total = total + jnp.sum(x * x, axis=-1, keepdims=True)
        inverses.append(lax.rsqrt(total / depth + eps))
    raw = 0.0
    for c in range(0, depth, span):
        gain = gain_ref[:, c : c + span].astype(F32)
        x = jnp.concatenate(
            [columns(parts, c) * inverse * gain for parts, inverse in zip(groups, inverses)],
            axis=0,
        )
        raw = raw + dot_nn(x.astype(BF16), weight_ref[0, c : c + span, :])
    q_gain = q_gain_ref[...].astype(F32)
    for c in range(0, heads_width, HEAD_DIM):
        head = raw[:, c : c + HEAD_DIM]
        inverse = lax.rsqrt(jnp.mean(head * head, axis=-1, keepdims=True) + eps)
        out_ref[:, c : c + HEAD_DIM] = (head * inverse * q_gain).astype(BF16)


def queries_of(groups, gain, weight, q_gain, name):
    arrays = [part for parts in groups for part in parts]
    rows = sum(parts[0].shape[0] for parts in groups)
    depth, heads_width = weight.shape[1:]
    return pl.pallas_call(
        functools.partial(query_kernel, [len(parts) for parts in groups]),
        in_specs=[whole()] * (3 + len(arrays)),
        out_specs=whole(),
        out_shape=jax.ShapeDtypeStruct((rows, heads_width), BF16),
        compiler_params=params(24),
        cost_estimate=cost(0, 0),
        name=name,
    )(gain, weight, q_gain, *arrays)


def attention_kernel(places, count, rows, last, sizes, *refs):
    if not last:
        count_ref, start_ref, refs = refs[0], refs[1], refs[2:]
    queries_refs, refs = refs[:sizes], refs[sizes:]
    grad_ref, k_gain_ref, refs = refs[0], refs[1], refs[2:]
    narrow = rows % 16 != 0
    if narrow:
        refs, grad_rows = refs[:-1], refs[-1]
        grad_rows[...] = grad_ref[0].astype(F32)
    if last:
        d_keys_in, d_values_in, keys_ref, values_ref, hat_ref, inverse_ref, token_ref, slot_ref = refs[:8]
        att_ref, block_ref, d_keys_ref, d_values_ref = refs[8:]
        d_keys_ref[...] = d_keys_in[...]
        d_values_ref[...] = d_values_in[...]
    else:
        parts = refs[:-9]
        att_ref, d_keys_ref, d_values_ref, keys_ref, values_ref = refs[-9:-4]
        hat_ref, inverse_ref, token_ref, slot_ref = refs[-4:]
        kv = sum(part[...].astype(F32) for part in parts)
        key_raw = kv[:, :HEAD_DIM]
        inverse = lax.rsqrt(jnp.mean(key_raw * key_raw, axis=-1, keepdims=True) + eps)
        hat_ref[...] = key_raw * inverse
        inverse_ref[...] = jnp.broadcast_to(inverse, key_raw.shape)
        keys_ref[...] = (key_raw * inverse * k_gain_ref[...].astype(F32)).astype(BF16)
        values_ref[...] = kv[:, HEAD_DIM:].astype(BF16)
        d_keys_ref[...] = jnp.zeros_like(d_keys_ref)
        d_values_ref[...] = jnp.zeros_like(d_values_ref)
        for b in range(MB):
            token = lax.broadcasted_iota(jnp.int32, (TXT_TOK, HEAD_DIM), 0)
            token_ref[b * TXT_TOK : (b + 1) * TXT_TOK, :] = (token >= start_ref[b]).astype(F32)
            slot = lax.broadcasted_iota(jnp.int32, slot_ref.shape[1:], 1)
            slot_ref[b] = (slot < count_ref[b] * TILE_LEN).astype(F32)

    scale = HEAD_DIM ** (-0.5)
    heads = grad_ref.shape[2] // HEAD_DIM
    per_sample = count // MB
    mine = lax.div(here(), per_sample)
    blocks = [
        (p, ref, i * rows) for group, ref in zip(places, queries_refs) for i, p in enumerate(group)
    ]
    for far in range(MB):
        chosen = [block for block in blocks if block[0] // per_sample == far]
        if not chosen:
            continue
        sample = lax.bitwise_xor(mine, far)
        img = pl.ds(pl.multiple_of(sample * SLOTS, SLOTS), SLOTS)
        keys, values = keys_ref[img, :], values_ref[img, :]
        live = slot_ref[sample][:1, :] > 0
        spots = [
            pl.ds(pl.multiple_of(lax.bitwise_xor(here(), p) * rows, rows), rows)
            for p, _, _ in chosen
        ]
        masks = [token_ref[spot, :] for spot in spots]
        queries, upstream = [], []
        for h in range(heads):
            cols = slice(h * HEAD_DIM, (h + 1) * HEAD_DIM)
            for (p, ref, at), mask, spot in zip(chosen, masks, spots):
                queries.append(ref[at : at + rows, cols])
                grad = grad_rows[spot, cols] if narrow else grad_ref[0, spot, cols].astype(F32)
                upstream.append((grad * mask).astype(BF16))
        queries = jnp.concatenate(queries, axis=0)
        upstream = jnp.concatenate(upstream, axis=0)
        scores = dot_nt(queries, keys) * scale
        exponent = jnp.where(live, jnp.exp(scores), 0.0)
        probs = exponent * (1.0 / jnp.sum(exponent, axis=-1, keepdims=True))
        weights = probs.astype(BF16)
        head_out = dot_nn(weights, values)
        step = 0
        for h in range(heads):
            cols = slice(h * HEAD_DIM, (h + 1) * HEAD_DIM)
            for block, mask in zip(chosen, masks):
                at = blocks.index(block) * rows
                att_ref[at : at + rows, cols] = head_out[step : step + rows] * mask
                step += rows
        d_weights = dot_nt(upstream, values)
        inner = jnp.sum(probs * d_weights, axis=-1, keepdims=True)
        d_scores = (probs * (d_weights - inner) * scale).astype(BF16)
        d_keys_ref[img, :] += dot_tn(d_scores, queries)
        d_values_ref[img, :] += dot_tn(weights, upstream)
    if last:
        hat = hat_ref[...]
        scaled = d_keys_ref[...] * k_gain_ref[...].astype(F32)
        d_raw = inverse_ref[...] * (
            scaled - hat * jnp.mean(hat * scaled, axis=-1, keepdims=True)
        )
        block_ref[:, :HEAD_DIM] = d_raw.astype(BF16)
        block_ref[:, HEAD_DIM:] = d_values_ref[...].astype(BF16)


def attention(scalars, queries, places, count, grad_out, k_gain, state, last):
    rows, width = grad_out.shape[1] // count, grad_out.shape[2]
    image_rows = MB * SLOTS
    vector = jax.ShapeDtypeStruct((image_rows, HEAD_DIM), F32)
    rounded = jax.ShapeDtypeStruct((image_rows, HEAD_DIM), BF16)
    attended = jax.ShapeDtypeStruct((sum(map(len, places)) * rows, width), F32)
    scratch = []
    if last:
        out_shape = [attended, jax.ShapeDtypeStruct((image_rows, 2 * HEAD_DIM), BF16)]
        scratch += [pltpu.VMEM(vector.shape, F32)] * 2
    else:
        token = jax.ShapeDtypeStruct((grad_out.shape[1], HEAD_DIM), F32)
        slot = jax.ShapeDtypeStruct((MB, 8, SLOTS), F32)
        out_shape = [attended, vector, vector, rounded, rounded, vector, vector, token, slot]
    if rows % 16 != 0:
        scratch += [pltpu.VMEM(grad_out.shape[1:], F32)]
    operands = [*queries, grad_out, k_gain, *state]
    return pl.pallas_call(
        functools.partial(attention_kernel, places, count, rows, last, len(queries)),
        in_specs=[whole(pltpu.SMEM)] * len(scalars) + [whole()] * len(operands),
        out_specs=[whole()] * len(out_shape),
        out_shape=out_shape,
        scratch_shapes=scratch,
        compiler_params=params(24),
        cost_estimate=cost(0, 0),
        name="attention_last" if last else "attention_first",
    )(*scalars, *operands)


def assemble_kernel(places, rows, *refs):
    refs, out_ref, held = refs[:-2], refs[-2], refs[-1]
    for group, ref in zip(places, refs):
        for i, p in enumerate(group):
            at = pl.multiple_of(lax.bitwise_xor(here(), p) * rows, rows)
            held[pl.ds(at, rows), :] = ref[i * rows : (i + 1) * rows, :]
    out_ref[0] = held[...].astype(BF16)


def assemble(places, arrays, like):
    rows = arrays[0].shape[0] // len(places[0])
    return pl.pallas_call(
        functools.partial(assemble_kernel, places, rows),
        in_specs=[whole()] * len(arrays),
        out_specs=whole(),
        out_shape=jax.ShapeDtypeStruct(like.shape, BF16),
        scratch_shapes=[pltpu.VMEM(like.shape[1:], F32)],
        compiler_params=params(24),
        cost_estimate=cost(0, 0),
        name="attended_rows",
    )(*arrays)


def grad_kernel(distances, per_kv, sections, first, last, *refs):
    blocks, weight_ref, refs = refs[: len(distances)], refs[len(distances)], refs[len(distances) + 1 :]
    if not first:
        before_ref, refs = refs[0], refs[1:]
    total = refs[-1]
    image_rows, width = total.shape
    heads = []
    for i in range(0, len(distances), per_kv):
        head = lax.div(lax.bitwise_xor(here(), distances[i]), per_kv)
        if per_kv == 1:
            block = blocks[i][...]
        else:
            block = sum(b[...].astype(F32) for b in blocks[i : i + per_kv]).astype(BF16)
        heads.append((head_columns(head), block))
    span = 256
    for c in range(0, width, span):
        cols = slice(c, c + span)
        part = 0.0 if first else before_ref[:, cols]
        for columns, block in heads:
            weight = jnp.concatenate([weight_ref[0, cols, k] for k in columns], axis=1)
            part = part + dot_nt(block, weight)
        total[:, cols] = part
    if last:
        rows = image_rows // sections
        for k in range(sections):
            to = lax.rem(lax.axis_index("section") + k, sections)
            piece = total[pl.ds(pl.multiple_of(to * rows, rows), rows), :]
            refs[k][...] = piece.astype(refs[k].dtype)


def feature_gradient(blocks, weight, per_kv, sections, before=None, last=True):
    distances = [p for p, _ in blocks]
    arrays = [block for _, block in blocks]
    image_rows = arrays[0].shape[0]
    width, depth = weight.shape[1:]
    rows = image_rows // sections
    if last:
        out_shape = [
            jax.ShapeDtypeStruct((rows, width), F32 if k == 0 else BF16) for k in range(sections)
        ]
        out_specs = [whole()] * sections
        scratch = [pltpu.VMEM((image_rows, width), F32)]
    else:
        out_shape = jax.ShapeDtypeStruct((image_rows, width), F32)
        out_specs = whole()
        scratch = []
    operands = [*arrays, weight] + ([] if before is None else [before])
    return pl.pallas_call(
        functools.partial(grad_kernel, distances, per_kv, sections, before is None, last),
        in_specs=[whole()] * len(operands),
        out_specs=out_specs,
        out_shape=out_shape,
        scratch_shapes=scratch,
        compiler_params=params(24),
        cost_estimate=cost(0, 0),
        name="feature_grad_last" if last else "feature_grad_first",
    )(*operands)


def shards(
    text, features, in_gain, w_query, q_gain, w_key_value, k_gain, tile_count, image_start, grad_out
):
    count = lax.axis_size("tensor")
    sections = lax.axis_size("section")
    per_kv = count // KV_HEADS

    def swap(x, distance):
        return lax.ppermute(x, "tensor", [(i, i ^ distance) for i in range(count)])

    own_text = text[0]
    bits = [1 << b for b in range(1, count.bit_length() - 1)]
    width = own_text.shape[1] // 2
    direct = {bit: swap(own_text, bit) for bit in bits}
    def both_cores(blocks):
        out = {}
        for p, parts in blocks.items():
            out[p] = parts
            out[p ^ 1] = [swap(part, 1) for part in parts]
        return list(out), list(out.values())

    def queries(both, name):
        return queries_of(both[1], in_gain, w_query, q_gain, name)

    def fast_swap(arrays):
        return [swap(x, 1) for x in arrays]

    other_heads = kv_partial(features, w_key_value, count)
    own, *outgoing = kv_partial(features, w_key_value, count, fast_swap(other_heads))
    parts = [own] + [swap(x, 2 * (j + 1)) for j, x in enumerate(outgoing)]
    direct, parts = lax.optimization_barrier((direct, parts))
    near = both_cores({0: [own_text]})
    q_near = queries(near, "queries_own_chip")
    forwarded = {}
    for half, order in enumerate((bits, bits[::-1])):
        first = half * width
        held = {0: None}
        for bit in order:
            for p in list(held):
                if p == 0:
                    held[bit] = direct[bit][:, first : first + width]
                else:
                    held[p ^ bit] = swap(held[p], bit)
                    forwarded.setdefault(p ^ bit, []).append(held[p ^ bit])

    next_to = both_cores({p: [block] for p, block in direct.items()})
    q_next = queries(next_to, "queries_neighbours")

    early, *state = attention(
        [tile_count, image_start],
        [q_near, q_next],
        [near[0], next_to[0]],
        count,
        grad_out,
        k_gain,
        parts,
        last=False,
    )
    forwarded, state = lax.optimization_barrier((forwarded, state))
    far = both_cores(forwarded)
    q_far = queries(far, "queries_forwarded")
    late, block = attention([], [q_far], [far[0]], count, grad_out, k_gain, state, last=True)
    attended = assemble([near[0] + next_to[0], far[0]], [early, late], grad_out)

    gathered = {0: [block]}
    gathered.update({p: [swap(block, p)] for p in range(2, count, 2)})
    before = None
    if per_kv == 1:
        soon = {0: block, 1: swap(block, 1), **{bit: gathered[bit][0] for bit in bits}}
        before = feature_gradient(
            sorted(soon.items()), w_key_value, per_kv, sections, last=False
        )
        rest = {p: x for p, x in gathered.items() if p not in soon}
        rest, before = lax.optimization_barrier((rest, before))
        blocks = {p ^ 1: swap(gathered[p][0], 1) for p in bits}
        for p, (x,) in rest.items():
            blocks.update({p: x, p ^ 1: swap(x, 1)})
    else:
        blocks = {p: x for p, (x,) in gathered.items()}
        blocks.update({p ^ 1: swap(x, 1) for p, x in list(blocks.items())})
    pieces = feature_gradient(sorted(blocks.items()), w_key_value, per_kv, sections, before)
    feature_grad, leaving = pieces[0], pieces[1:]
    arrived = []
    for k in sorted(range(1, sections), key=lambda k: -min(k, sections - k)):
        perm = [(i, (i + k) % sections) for i in range(sections)]
        arrived.append(lax.ppermute(leaving[k - 1], "section", perm))
    for x in arrived:
        feature_grad = feature_grad + x.astype(F32)
    return (attended, feature_grad)


def solution(mesh):
    return jax.shard_map(
        shards,
        mesh=mesh,
        in_specs=(
            P("section", "tensor", None),
            P(None, "tensor"),
            P("section", None),
            P("section", None, "tensor"),
            P("section", None),
            P("section", "tensor", None),
            P("section", None),
            P(),
            P(),
            P("section", None, "tensor"),
        ),
        out_specs=(P("section", None, "tensor"), P("section", "tensor")),
        check_vma=False,
    )
```

```python
import functools

import jax
import jax.numpy as jnp
from jax import lax
from jax.experimental import pallas as pl
from jax.experimental.pallas import tpu as pltpu
from jax.sharding import PartitionSpec as P

KV_HEADS = 8
HEAD_DIM = 128
TILES = 4
TILE_LEN = 24
TXT_TOK = 128
MB = 2
SLOTS = TILES * TILE_LEN

eps = 1e-05

F32 = jnp.float32
BF16 = jnp.bfloat16
MIB = 1 << 20


def whole(memory=pltpu.VMEM):
    return pl.BlockSpec(memory_space=memory)


def dot_nn(a, b):
    return jnp.dot(a, b, preferred_element_type=F32)


def dot_nt(a, b):
    return lax.dot_general(a, b, (((1,), (1,)), ((), ())), preferred_element_type=F32)


def dot_tn(a, b):
    return lax.dot_general(a, b, (((0,), (0,)), ((), ())), preferred_element_type=F32)


def params(mib):
    return pltpu.CompilerParams(vmem_limit_bytes=mib * MIB)


def cost(flops, size):
    return pl.CostEstimate(flops=flops, bytes_accessed=size, transcendentals=0)


def here():
    return lax.axis_index("tensor")


def head_columns(head):
    return [
        pl.ds(pl.multiple_of((half * KV_HEADS + head) * HEAD_DIM, HEAD_DIM), HEAD_DIM)
        for half in range(2)
    ]


def kv_kernel(per_kv, distances, feat_ref, weight_ref, *refs):
    features = feat_ref[...]
    size = len(distances)
    for i, p in enumerate(distances):
        head = lax.div(lax.bitwise_xor(here(), p), per_kv)
        weight = jnp.concatenate([weight_ref[0, :, c] for c in head_columns(head)], axis=1)
        total = dot_nn(features, weight)
        if len(refs) > size:
            total = total + refs[i][...]
        out_ref = refs[i - size]
        out_ref[...] = total.astype(out_ref.dtype)


def kv_partial(features, weight, count, distances, other=()):
    operands = (features, weight, *other)
    shape = (features.shape[0], 2 * HEAD_DIM)
    goes_on = [bool(other) and 2 * i >= len(distances) for i in range(len(distances))]
    return pl.pallas_call(
        functools.partial(kv_kernel, count // KV_HEADS, distances),
        in_specs=[whole()] * len(operands),
        out_specs=[whole()] * len(distances),
        out_shape=[jax.ShapeDtypeStruct(shape, BF16 if on else F32) for on in goes_on],
        compiler_params=params(24),
        cost_estimate=cost(0, 0),
        name="kv_partial_own_core" if other else "kv_partial_other_core",
    )(*operands)


def kv_sum_kernel(*refs):
    size = len(refs) // 3
    for i in range(size):
        total = refs[i][...] + refs[size + i][...].astype(F32)
        refs[2 * size + i][...] = total.astype(refs[2 * size + i].dtype)


def kv_sum(kept, other):
    size = len(kept)
    return pl.pallas_call(
        kv_sum_kernel,
        in_specs=[whole()] * (2 * size),
        out_specs=[whole()] * size,
        out_shape=[
            jax.ShapeDtypeStruct(x.shape, BF16 if 2 * i >= size else F32)
            for i, x in enumerate(kept)
        ],
        compiler_params=params(24),
        cost_estimate=cost(0, 0),
        name="kv_sum",
    )(*kept, *other)


def query_kernel(shape, gain_ref, weight_ref, q_gain_ref, *refs):
    refs, out_ref = refs[:-1], refs[-1]
    groups, at = [], 0
    for parts in shape:
        groups.append(refs[at : at + parts])
        at += parts
    depth, heads_width = weight_ref.shape[1:]
    span = 1024

    def columns(parts, c):
        for part in parts:
            if c < part.shape[1]:
                return part[:, c : c + span].astype(F32)
            c -= part.shape[1]

    inverses = []
    for parts in groups:
        total = 0.0
        for c in range(0, depth, span):
            x = columns(parts, c)
            total = total + jnp.sum(x * x, axis=-1, keepdims=True)
        inverses.append(lax.rsqrt(total / depth + eps))
    raw = 0.0
    for c in range(0, depth, span):
        gain = gain_ref[:, c : c + span].astype(F32)
        x = jnp.concatenate(
            [columns(parts, c) * inverse * gain for parts, inverse in zip(groups, inverses)],
            axis=0,
        )
        raw = raw + dot_nn(x.astype(BF16), weight_ref[0, c : c + span, :])
    q_gain = q_gain_ref[...].astype(F32)
    for c in range(0, heads_width, HEAD_DIM):
        head = raw[:, c : c + HEAD_DIM]
        inverse = lax.rsqrt(jnp.mean(head * head, axis=-1, keepdims=True) + eps)
        out_ref[:, c : c + HEAD_DIM] = (head * inverse * q_gain).astype(BF16)


def queries_of(groups, gain, weight, q_gain, name):
    arrays = [part for parts in groups for part in parts]
    rows = sum(parts[0].shape[0] for parts in groups)
    depth, heads_width = weight.shape[1:]
    return pl.pallas_call(
        functools.partial(query_kernel, [len(parts) for parts in groups]),
        in_specs=[whole()] * (3 + len(arrays)),
        out_specs=whole(),
        out_shape=jax.ShapeDtypeStruct((rows, heads_width), BF16),
        compiler_params=params(24),
        cost_estimate=cost(0, 0),
        name=name,
    )(gain, weight, q_gain, *arrays)


def attention_kernel(places, count, rows, last, sizes, *refs):
    if not last:
        count_ref, start_ref, refs = refs[0], refs[1], refs[2:]
    queries_refs, refs = refs[:sizes], refs[sizes:]
    grad_ref, k_gain_ref, refs = refs[0], refs[1], refs[2:]
    narrow = rows % 16 != 0
    if narrow:
        refs, grad_rows = refs[:-1], refs[-1]
        grad_rows[...] = grad_ref[0].astype(F32)
    if last:
        d_keys_in, d_values_in, keys_ref, values_ref, hat_ref, inverse_ref, token_ref, slot_ref = refs[:8]
        att_ref, block_ref, d_keys_ref, d_values_ref = refs[8:]
        d_keys_ref[...] = d_keys_in[...]
        d_values_ref[...] = d_values_in[...]
    else:
        parts = refs[:-9]
        att_ref, d_keys_ref, d_values_ref, keys_ref, values_ref = refs[-9:-4]
        hat_ref, inverse_ref, token_ref, slot_ref = refs[-4:]
        kv = sum(part[...].astype(F32) for part in parts)
        key_raw = kv[:, :HEAD_DIM]
        inverse = lax.rsqrt(jnp.mean(key_raw * key_raw, axis=-1, keepdims=True) + eps)
        hat_ref[...] = key_raw * inverse
        inverse_ref[...] = jnp.broadcast_to(inverse, key_raw.shape)
        keys_ref[...] = (key_raw * inverse * k_gain_ref[...].astype(F32)).astype(BF16)
        values_ref[...] = kv[:, HEAD_DIM:].astype(BF16)
        d_keys_ref[...] = jnp.zeros_like(d_keys_ref)
        d_values_ref[...] = jnp.zeros_like(d_values_ref)
        for b in range(MB):
            token = lax.broadcasted_iota(jnp.int32, (TXT_TOK, HEAD_DIM), 0)
            token_ref[b * TXT_TOK : (b + 1) * TXT_TOK, :] = (token >= start_ref[b]).astype(F32)
            slot = lax.broadcasted_iota(jnp.int32, slot_ref.shape[1:], 1)
            slot_ref[b] = (slot < count_ref[b] * TILE_LEN).astype(F32)

    scale = HEAD_DIM ** (-0.5)
    heads = grad_ref.shape[2] // HEAD_DIM
    per_sample = count // MB
    mine = lax.div(here(), per_sample)
    blocks = [
        (p, ref, i * rows) for group, ref in zip(places, queries_refs) for i, p in enumerate(group)
    ]
    for far in range(MB):
        chosen = [block for block in blocks if block[0] // per_sample == far]
        if not chosen:
            continue
        sample = lax.bitwise_xor(mine, far)
        img = pl.ds(pl.multiple_of(sample * SLOTS, SLOTS), SLOTS)
        keys, values = keys_ref[img, :], values_ref[img, :]
        live = slot_ref[sample][:1, :] > 0
        spots = [
            pl.ds(pl.multiple_of(lax.bitwise_xor(here(), p) * rows, rows), rows)
            for p, _, _ in chosen
        ]
        masks = [token_ref[spot, :] for spot in spots]
        queries, upstream = [], []
        for h in range(heads):
            cols = slice(h * HEAD_DIM, (h + 1) * HEAD_DIM)
            for (p, ref, at), mask, spot in zip(chosen, masks, spots):
                queries.append(ref[at : at + rows, cols])
                grad = grad_rows[spot, cols] if narrow else grad_ref[0, spot, cols].astype(F32)
                upstream.append((grad * mask).astype(BF16))
        queries = jnp.concatenate(queries, axis=0)
        upstream = jnp.concatenate(upstream, axis=0)
        scores = dot_nt(queries, keys) * scale
        exponent = jnp.where(live, jnp.exp(scores), 0.0)
        probs = exponent * (1.0 / jnp.sum(exponent, axis=-1, keepdims=True))
        weights = probs.astype(BF16)
        head_out = dot_nn(weights, values)
        step = 0
        for h in range(heads):
            cols = slice(h * HEAD_DIM, (h + 1) * HEAD_DIM)
            for block, mask in zip(chosen, masks):
                at = blocks.index(block) * rows
                att_ref[at : at + rows, cols] = head_out[step : step + rows] * mask
                step += rows
        d_weights = dot_nt(upstream, values)
        inner = jnp.sum(probs * d_weights, axis=-1, keepdims=True)
        d_scores = (probs * (d_weights - inner) * scale).astype(BF16)
        d_keys_ref[img, :] += dot_tn(d_scores, queries)
        d_values_ref[img, :] += dot_tn(weights, upstream)
    if last:
        hat = hat_ref[...]
        scaled = d_keys_ref[...] * k_gain_ref[...].astype(F32)
        d_raw = inverse_ref[...] * (
            scaled - hat * jnp.mean(hat * scaled, axis=-1, keepdims=True)
        )
        block_ref[:, :HEAD_DIM] = d_raw.astype(BF16)
        block_ref[:, HEAD_DIM:] = d_values_ref[...].astype(BF16)


def attention(scalars, queries, places, count, grad_out, k_gain, state, last):
    rows, width = grad_out.shape[1] // count, grad_out.shape[2]
    image_rows = MB * SLOTS
    vector = jax.ShapeDtypeStruct((image_rows, HEAD_DIM), F32)
    rounded = jax.ShapeDtypeStruct((image_rows, HEAD_DIM), BF16)
    attended = jax.ShapeDtypeStruct((sum(map(len, places)) * rows, width), F32)
    scratch = []
    if last:
        out_shape = [attended, jax.ShapeDtypeStruct((image_rows, 2 * HEAD_DIM), BF16)]
        scratch += [pltpu.VMEM(vector.shape, F32)] * 2
    else:
        token = jax.ShapeDtypeStruct((grad_out.shape[1], HEAD_DIM), F32)
        slot = jax.ShapeDtypeStruct((MB, 8, SLOTS), F32)
        out_shape = [attended, vector, vector, rounded, rounded, vector, vector, token, slot]
    if rows % 16 != 0:
        scratch += [pltpu.VMEM(grad_out.shape[1:], F32)]
    operands = [*queries, grad_out, k_gain, *state]
    return pl.pallas_call(
        functools.partial(attention_kernel, places, count, rows, last, len(queries)),
        in_specs=[whole(pltpu.SMEM)] * len(scalars) + [whole()] * len(operands),
        out_specs=[whole()] * len(out_shape),
        out_shape=out_shape,
        scratch_shapes=scratch,
        compiler_params=params(24),
        cost_estimate=cost(0, 0),
        name="attention_last" if last else "attention_first",
    )(*scalars, *operands)


def assemble_kernel(places, rows, *refs):
    refs, out_ref, held = refs[:-2], refs[-2], refs[-1]
    for group, ref in zip(places, refs):
        for i, p in enumerate(group):
            at = pl.multiple_of(lax.bitwise_xor(here(), p) * rows, rows)
            held[pl.ds(at, rows), :] = ref[i * rows : (i + 1) * rows, :]
    out_ref[0] = held[...].astype(BF16)


def assemble(places, arrays, like):
    rows = arrays[0].shape[0] // len(places[0])
    return pl.pallas_call(
        functools.partial(assemble_kernel, places, rows),
        in_specs=[whole()] * len(arrays),
        out_specs=whole(),
        out_shape=jax.ShapeDtypeStruct(like.shape, BF16),
        scratch_shapes=[pltpu.VMEM(like.shape[1:], F32)],
        compiler_params=params(24),
        cost_estimate=cost(0, 0),
        name="attended_rows",
    )(*arrays)


def grad_kernel(distances, per_kv, sections, first, last, *refs):
    blocks = []
    for _, cuts in distances:
        blocks.append(jnp.concatenate([ref[...] for ref in refs[:cuts]], axis=0))
        refs = refs[cuts:]
    weight_ref, refs = refs[0], refs[1:]
    if not first:
        before_ref, refs = refs[0], refs[1:]
    total = refs[-1]
    image_rows, width = total.shape
    heads = []
    for i in range(0, len(distances), per_kv):
        head = lax.div(lax.bitwise_xor(here(), distances[i][0]), per_kv)
        if per_kv == 1:
            block = blocks[i]
        else:
            block = sum(b.astype(F32) for b in blocks[i : i + per_kv]).astype(BF16)
        heads.append((head_columns(head), block))
    span = 256
    for c in range(0, width, span):
        cols = slice(c, c + span)
        part = 0.0 if first else before_ref[:, cols]
        for columns, block in heads:
            weight = jnp.concatenate([weight_ref[0, cols, k] for k in columns], axis=1)
            part = part + dot_nt(block, weight)
        total[:, cols] = part
    if last:
        rows = image_rows // sections
        for k in range(sections):
            to = lax.rem(lax.axis_index("section") + k, sections)
            piece = total[pl.ds(pl.multiple_of(to * rows, rows), rows), :]
            refs[k][...] = piece.astype(refs[k].dtype)


def feature_gradient(blocks, weight, per_kv, sections, before=None, last=True):
    distances = [(p, len(parts)) for p, parts in blocks]
    arrays = [part for _, parts in blocks for part in parts]
    image_rows = sum(part.shape[0] for part in blocks[0][1])
    width, depth = weight.shape[1:]
    rows = image_rows // sections
    if last:
        out_shape = [
            jax.ShapeDtypeStruct((rows, width), F32 if k == 0 else BF16) for k in range(sections)
        ]
        out_specs = [whole()] * sections
        scratch = [pltpu.VMEM((image_rows, width), F32)]
    else:
        out_shape = jax.ShapeDtypeStruct((image_rows, width), F32)
        out_specs = whole()
        scratch = []
    operands = [*arrays, weight] + ([] if before is None else [before])
    return pl.pallas_call(
        functools.partial(grad_kernel, distances, per_kv, sections, before is None, last),
        in_specs=[whole()] * len(operands),
        out_specs=out_specs,
        out_shape=out_shape,
        scratch_shapes=scratch,
        compiler_params=params(24),
        cost_estimate=cost(0, 0),
        name="feature_grad_last" if last else "feature_grad_first",
    )(*operands)


def shards(
    text, features, in_gain, w_query, q_gain, w_key_value, k_gain, tile_count, image_start, grad_out
):
    count = lax.axis_size("tensor")
    sections = lax.axis_size("section")
    per_kv = count // KV_HEADS

    def swap(x, distance):
        return lax.ppermute(x, "tensor", [(i, i ^ distance) for i in range(count)])

    own_text = text[0]
    bits = [1 << b for b in range(1, count.bit_length() - 1)]
    cut = own_text.shape[1] * 3 // 8
    direct = {bit: swap(own_text, bit) for bit in bits}

    distances = [0]
    for bit in bits[::-1]:
        distances = distances + [p + bit for p in distances]
    others = kv_partial(features, w_key_value, count, [p + 1 for p in distances])
    others = [swap(x, 1) for x in others]
    sums = kv_partial(features, w_key_value, count, distances, others)
    arrived = [swap(x, bits[0]) for x in sums[len(sums) // 2 :]]

    def with_swapped(blocks):
        return {p: ([x], [swap(x, 1)]) for p, x in blocks.items()}

    def queries(blocks, name):
        out = {}
        for p, (own_parts, swapped) in blocks.items():
            out[p] = own_parts
            out[p ^ 1] = swapped
        return list(out), queries_of(list(out.values()), in_gain, w_query, q_gain, name)

    def send_on(order, columns):
        held, out = {0: None}, {}
        for bit in order:
            for p in list(held):
                if p == 0:
                    held[bit] = direct[bit][:, columns]
                else:
                    held[p ^ bit] = out[p ^ bit] = swap(held[p], bit)
        return out

    own_text, direct, arrived = lax.optimization_barrier((own_text, direct, arrived))
    for bit in bits[1:]:
        sums = kv_sum(sums[: len(arrived)], arrived)
        arrived = [swap(x, bit) for x in sums[len(sums) // 2 :]]
    parts = [sums[0], arrived[0]]
    firsts = send_on(bits, slice(0, cut))
    rests = send_on(bits[::-1], slice(cut, None))
    near, q_near = queries(with_swapped({0: own_text, **direct}), "queries_near")

    firsts, rests, parts, q_near = lax.optimization_barrier((firsts, rests, parts, q_near))
    swapped = {p: [swap(x, 1), swap(rests[p], 1)] for p, x in firsts.items()}
    early, *state = attention(
        [tile_count, image_start],
        [q_near],
        [near],
        count,
        grad_out,
        k_gain,
        parts,
        last=False,
    )
    firsts, rests, state = lax.optimization_barrier((firsts, rests, state))
    far, q_far = queries(
        {p: ([x, rests[p]], swapped[p]) for p, x in firsts.items()}, "queries_forwarded"
    )
    late, block = attention([], [q_far], [far], count, grad_out, k_gain, state, last=True)
    attended = assemble([near, far], [early, late], grad_out)

    blocks = {0: block}
    blocks.update({p: swap(block, p) for p in range(2, count, 2)})
    before = None
    if per_kv == 1:
        soon = {p: [blocks[p]] for p in [0] + bits}
        soon[1] = [swap(block, 1)]
        soon.update(
            {p ^ 1: [swap(x, 1) for x in jnp.split(blocks[p], 2, axis=0)] for p in bits}
        )
        before = feature_gradient(sorted(soon.items()), w_key_value, per_kv, sections, last=False)
        blocks = {p: x for p, x in blocks.items() if p not in soon}
        blocks, before = lax.optimization_barrier((blocks, before))
    blocks.update({p ^ 1: swap(x, 1) for p, x in list(blocks.items())})
    blocks = {p: [x] for p, x in blocks.items()}
    pieces = feature_gradient(sorted(blocks.items()), w_key_value, per_kv, sections, before)
    feature_grad, leaving = pieces[0], pieces[1:]
    arrived = []
    for k in range(1, sections):
        perm = [(i, (i + k) % sections) for i in range(sections)]
        arrived.append(lax.ppermute(leaving[k - 1], "section", perm))
    for x in arrived:
        feature_grad = feature_grad + x.astype(F32)
    return (attended, feature_grad)


def solution(mesh):
    return jax.shard_map(
        shards,
        mesh=mesh,
        in_specs=(
            P("section", "tensor", None),
            P(None, "tensor"),
            P("section", None),
            P("section", None, "tensor"),
            P("section", None),
            P("section", "tensor", None),
            P("section", None),
            P(),
            P(),
            P("section", None, "tensor"),
        ),
        out_specs=(P("section", None, "tensor"), P("section", "tensor")),
        check_vma=False,
    )
```

```python
import functools

import jax
import jax.numpy as jnp
from jax import lax
from jax.experimental import pallas as pl
from jax.experimental.pallas import tpu as pltpu
from jax.sharding import PartitionSpec as P

KV_HEADS = 8
HEAD_DIM = 128
TILES = 4
TILE_LEN = 24
TXT_TOK = 128
MB = 2
SLOTS = TILES * TILE_LEN

eps = 1e-05

F32 = jnp.float32
BF16 = jnp.bfloat16
MIB = 1 << 20


def whole(memory=pltpu.VMEM):
    return pl.BlockSpec(memory_space=memory)


def dot_nn(a, b):
    return jnp.dot(a, b, preferred_element_type=F32)


def dot_nt(a, b):
    return lax.dot_general(a, b, (((1,), (1,)), ((), ())), preferred_element_type=F32)


def dot_tn(a, b):
    return lax.dot_general(a, b, (((0,), (0,)), ((), ())), preferred_element_type=F32)


def params(mib):
    return pltpu.CompilerParams(vmem_limit_bytes=mib * MIB)


def cost(flops, size):
    return pl.CostEstimate(flops=flops, bytes_accessed=size, transcendentals=0)


def here():
    return lax.axis_index("tensor")


def head_columns(head):
    return [
        pl.ds(pl.multiple_of((half * KV_HEADS + head) * HEAD_DIM, HEAD_DIM), HEAD_DIM)
        for half in range(2)
    ]


def kv_kernel(per_kv, pairs, odd, feat_ref, weight_ref, *refs):
    features = feat_ref[...]
    for j in range(pairs):
        head = lax.div(lax.bitwise_xor(here(), 2 * j + odd), per_kv)
        weight = jnp.concatenate([weight_ref[0, :, c] for c in head_columns(head)], axis=1)
        total = dot_nn(features, weight)
        out_ref = refs[j - pairs]
        if not odd:
            total = total + refs[j][...]
        out_ref[...] = total.astype(out_ref.dtype)


def kv_partial(features, weight, count, other=None):
    rows, depth = features.shape
    pairs = count // 2
    odd = 1 if other is None else 0
    out_shape = [
        jax.ShapeDtypeStruct((rows, 2 * HEAD_DIM), F32 if odd or j == 0 else BF16)
        for j in range(pairs)
    ]
    operands = (features, weight, *(other or ()))
    return pl.pallas_call(
        functools.partial(kv_kernel, count // KV_HEADS, pairs, odd),
        in_specs=[whole()] * len(operands),
        out_specs=[whole()] * pairs,
        out_shape=out_shape,
        compiler_params=params(24),
        cost_estimate=cost(0, 0),
        name="kv_partial_other_core" if odd else "kv_partial_own_core",
    )(*operands)


def query_kernel(shape, gain_ref, weight_ref, q_gain_ref, *refs):
    refs, out_ref = refs[:-1], refs[-1]
    groups, at = [], 0
    for parts in shape:
        groups.append(refs[at : at + parts])
        at += parts
    depth, heads_width = weight_ref.shape[1:]
    span = 1024

    def columns(parts, c):
        for part in parts:
            if c < part.shape[1]:
                return part[:, c : c + span].astype(F32)
            c -= part.shape[1]

    inverses = []
    for parts in groups:
        total = 0.0
        for c in range(0, depth, span):
            x = columns(parts, c)
            total = total + jnp.sum(x * x, axis=-1, keepdims=True)
        inverses.append(lax.rsqrt(total / depth + eps))
    raw = 0.0
    for c in range(0, depth, span):
        gain = gain_ref[:, c : c + span].astype(F32)
        x = jnp.concatenate(
            [columns(parts, c) * inverse * gain for parts, inverse in zip(groups, inverses)],
            axis=0,
        )
        raw = raw + dot_nn(x.astype(BF16), weight_ref[0, c : c + span, :])
    q_gain = q_gain_ref[...].astype(F32)
    for c in range(0, heads_width, HEAD_DIM):
        head = raw[:, c : c + HEAD_DIM]
        inverse = lax.rsqrt(jnp.mean(head * head, axis=-1, keepdims=True) + eps)
        out_ref[:, c : c + HEAD_DIM] = (head * inverse * q_gain).astype(BF16)


def queries_of(groups, gain, weight, q_gain, name):
    arrays = [part for parts in groups for part in parts]
    rows = sum(parts[0].shape[0] for parts in groups)
    depth, heads_width = weight.shape[1:]
    return pl.pallas_call(
        functools.partial(query_kernel, [len(parts) for parts in groups]),
        in_specs=[whole()] * (3 + len(arrays)),
        out_specs=whole(),
        out_shape=jax.ShapeDtypeStruct((rows, heads_width), BF16),
        compiler_params=params(24),
        cost_estimate=cost(0, 0),
        name=name,
    )(gain, weight, q_gain, *arrays)


def attention_kernel(places, count, rows, last, sizes, *refs):
    if not last:
        count_ref, start_ref, refs = refs[0], refs[1], refs[2:]
    queries_refs, refs = refs[:sizes], refs[sizes:]
    grad_ref, k_gain_ref, refs = refs[0], refs[1], refs[2:]
    narrow = rows % 16 != 0
    if narrow:
        refs, grad_rows = refs[:-1], refs[-1]
        grad_rows[...] = grad_ref[0].astype(F32)
    if last:
        d_keys_in, d_values_in, keys_ref, values_ref, hat_ref, inverse_ref, token_ref, slot_ref = refs[:8]
        att_ref, block_ref, d_keys_ref, d_values_ref = refs[8:]
        d_keys_ref[...] = d_keys_in[...]
        d_values_ref[...] = d_values_in[...]
    else:
        parts = refs[:-9]
        att_ref, d_keys_ref, d_values_ref, keys_ref, values_ref = refs[-9:-4]
        hat_ref, inverse_ref, token_ref, slot_ref = refs[-4:]
        kv = sum(part[...].astype(F32) for part in parts)
        key_raw = kv[:, :HEAD_DIM]
        inverse = lax.rsqrt(jnp.mean(key_raw * key_raw, axis=-1, keepdims=True) + eps)
        hat_ref[...] = key_raw * inverse
        inverse_ref[...] = jnp.broadcast_to(inverse, key_raw.shape)
        keys_ref[...] = (key_raw * inverse * k_gain_ref[...].astype(F32)).astype(BF16)
        values_ref[...] = kv[:, HEAD_DIM:].astype(BF16)
        d_keys_ref[...] = jnp.zeros_like(d_keys_ref)
        d_values_ref[...] = jnp.zeros_like(d_values_ref)
        for b in range(MB):
            token = lax.broadcasted_iota(jnp.int32, (TXT_TOK, HEAD_DIM), 0)
            token_ref[b * TXT_TOK : (b + 1) * TXT_TOK, :] = (token >= start_ref[b]).astype(F32)
            slot = lax.broadcasted_iota(jnp.int32, slot_ref.shape[1:], 1)
            slot_ref[b] = (slot < count_ref[b] * TILE_LEN).astype(F32)

    scale = HEAD_DIM ** (-0.5)
    heads = grad_ref.shape[2] // HEAD_DIM
    per_sample = count // MB
    mine = lax.div(here(), per_sample)
    blocks = [
        (p, ref, i * rows) for group, ref in zip(places, queries_refs) for i, p in enumerate(group)
    ]
    for far in range(MB):
        chosen = [block for block in blocks if block[0] // per_sample == far]
        if not chosen:
            continue
        sample = lax.bitwise_xor(mine, far)
        img = pl.ds(pl.multiple_of(sample * SLOTS, SLOTS), SLOTS)
        keys, values = keys_ref[img, :], values_ref[img, :]
        live = slot_ref[sample][:1, :] > 0
        spots = [
            pl.ds(pl.multiple_of(lax.bitwise_xor(here(), p) * rows, rows), rows)
            for p, _, _ in chosen
        ]
        masks = [token_ref[spot, :] for spot in spots]
        queries, upstream = [], []
        for h in range(heads):
            cols = slice(h * HEAD_DIM, (h + 1) * HEAD_DIM)
            for (p, ref, at), mask, spot in zip(chosen, masks, spots):
                queries.append(ref[at : at + rows, cols])
                grad = grad_rows[spot, cols] if narrow else grad_ref[0, spot, cols].astype(F32)
                upstream.append((grad * mask).astype(BF16))
        queries = jnp.concatenate(queries, axis=0)
        upstream = jnp.concatenate(upstream, axis=0)
        scores = dot_nt(queries, keys) * scale
        exponent = jnp.where(live, jnp.exp(scores), 0.0)
        probs = exponent * (1.0 / jnp.sum(exponent, axis=-1, keepdims=True))
        weights = probs.astype(BF16)
        head_out = dot_nn(weights, values)
        step = 0
        for h in range(heads):
            cols = slice(h * HEAD_DIM, (h + 1) * HEAD_DIM)
            for block, mask in zip(chosen, masks):
                at = blocks.index(block) * rows
                att_ref[at : at + rows, cols] = head_out[step : step + rows] * mask
                step += rows
        d_weights = dot_nt(upstream, values)
        inner = jnp.sum(probs * d_weights, axis=-1, keepdims=True)
        d_scores = (probs * (d_weights - inner) * scale).astype(BF16)
        d_keys_ref[img, :] += dot_tn(d_scores, queries)
        d_values_ref[img, :] += dot_tn(weights, upstream)
    if last:
        hat = hat_ref[...]
        scaled = d_keys_ref[...] * k_gain_ref[...].astype(F32)
        d_raw = inverse_ref[...] * (
            scaled - hat * jnp.mean(hat * scaled, axis=-1, keepdims=True)
        )
        block_ref[:, :HEAD_DIM] = d_raw.astype(BF16)
        block_ref[:, HEAD_DIM:] = d_values_ref[...].astype(BF16)


def attention(scalars, queries, places, count, grad_out, k_gain, state, last):
    rows, width = grad_out.shape[1] // count, grad_out.shape[2]
    image_rows = MB * SLOTS
    vector = jax.ShapeDtypeStruct((image_rows, HEAD_DIM), F32)
    rounded = jax.ShapeDtypeStruct((image_rows, HEAD_DIM), BF16)
    attended = jax.ShapeDtypeStruct((sum(map(len, places)) * rows, width), F32)
    scratch = []
    if last:
        out_shape = [attended, jax.ShapeDtypeStruct((image_rows, 2 * HEAD_DIM), BF16)]
        scratch += [pltpu.VMEM(vector.shape, F32)] * 2
    else:
        token = jax.ShapeDtypeStruct((grad_out.shape[1], HEAD_DIM), F32)
        slot = jax.ShapeDtypeStruct((MB, 8, SLOTS), F32)
        out_shape = [attended, vector, vector, rounded, rounded, vector, vector, token, slot]
    if rows % 16 != 0:
        scratch += [pltpu.VMEM(grad_out.shape[1:], F32)]
    operands = [*queries, grad_out, k_gain, *state]
    return pl.pallas_call(
        functools.partial(attention_kernel, places, count, rows, last, len(queries)),
        in_specs=[whole(pltpu.SMEM)] * len(scalars) + [whole()] * len(operands),
        out_specs=[whole()] * len(out_shape),
        out_shape=out_shape,
        scratch_shapes=scratch,
        compiler_params=params(24),
        cost_estimate=cost(0, 0),
        name="attention_last" if last else "attention_first",
    )(*scalars, *operands)


def assemble_kernel(places, rows, *refs):
    refs, out_ref, held = refs[:-2], refs[-2], refs[-1]
    for group, ref in zip(places, refs):
        for i, p in enumerate(group):
            at = pl.multiple_of(lax.bitwise_xor(here(), p) * rows, rows)
            held[pl.ds(at, rows), :] = ref[i * rows : (i + 1) * rows, :]
    out_ref[0] = held[...].astype(BF16)


def assemble(places, arrays, like):
    rows = arrays[0].shape[0] // len(places[0])
    return pl.pallas_call(
        functools.partial(assemble_kernel, places, rows),
        in_specs=[whole()] * len(arrays),
        out_specs=whole(),
        out_shape=jax.ShapeDtypeStruct(like.shape, BF16),
        scratch_shapes=[pltpu.VMEM(like.shape[1:], F32)],
        compiler_params=params(24),
        cost_estimate=cost(0, 0),
        name="attended_rows",
    )(*arrays)


def grad_kernel(distances, per_kv, sections, first, last, *refs):
    blocks, weight_ref, refs = refs[: len(distances)], refs[len(distances)], refs[len(distances) + 1 :]
    if not first:
        before_ref, refs = refs[0], refs[1:]
    total = refs[-1]
    image_rows, width = total.shape
    heads = []
    for i in range(0, len(distances), per_kv):
        head = lax.div(lax.bitwise_xor(here(), distances[i]), per_kv)
        if per_kv == 1:
            block = blocks[i][...]
        else:
            block = sum(b[...].astype(F32) for b in blocks[i : i + per_kv]).astype(BF16)
        heads.append((head_columns(head), block))
    span = 256
    for c in range(0, width, span):
        cols = slice(c, c + span)
        part = 0.0 if first else before_ref[:, cols]
        for columns, block in heads:
            weight = jnp.concatenate([weight_ref[0, cols, k] for k in columns], axis=1)
            part = part + dot_nt(block, weight)
        total[:, cols] = part
    if last:
        rows = image_rows // sections
        for k in range(sections):
            to = lax.rem(lax.axis_index("section") + k, sections)
            piece = total[pl.ds(pl.multiple_of(to * rows, rows), rows), :]
            refs[k][...] = piece.astype(refs[k].dtype)


def feature_gradient(blocks, weight, per_kv, sections, before=None, last=True):
    distances = [p for p, _ in blocks]
    arrays = [block for _, block in blocks]
    image_rows = arrays[0].shape[0]
    width, depth = weight.shape[1:]
    rows = image_rows // sections
    if last:
        out_shape = [
            jax.ShapeDtypeStruct((rows, width), F32 if k == 0 else BF16) for k in range(sections)
        ]
        out_specs = [whole()] * sections
        scratch = [pltpu.VMEM((image_rows, width), F32)]
    else:
        out_shape = jax.ShapeDtypeStruct((image_rows, width), F32)
        out_specs = whole()
        scratch = []
    operands = [*arrays, weight] + ([] if before is None else [before])
    return pl.pallas_call(
        functools.partial(grad_kernel, distances, per_kv, sections, before is None, last),
        in_specs=[whole()] * len(operands),
        out_specs=out_specs,
        out_shape=out_shape,
        scratch_shapes=scratch,
        compiler_params=params(24),
        cost_estimate=cost(0, 0),
        name="feature_grad_last" if last else "feature_grad_first",
    )(*operands)


def shards(
    text, features, in_gain, w_query, q_gain, w_key_value, k_gain, tile_count, image_start, grad_out
):
    count = lax.axis_size("tensor")
    sections = lax.axis_size("section")
    per_kv = count // KV_HEADS

    def swap(x, distance):
        return lax.ppermute(x, "tensor", [(i, i ^ distance) for i in range(count)])

    own_text = text[0]
    bits = [1 << b for b in range(1, count.bit_length() - 1)]
    width = own_text.shape[1] // 2
    direct = {bit: swap(own_text, bit) for bit in bits}
    def both_cores(blocks):
        out = {}
        for p, parts in blocks.items():
            out[p] = parts
            out[p ^ 1] = [swap(part, 1) for part in parts]
        return list(out), list(out.values())

    def queries(both, name):
        return queries_of(both[1], in_gain, w_query, q_gain, name)

    def fast_swap(arrays):
        return [swap(x, 1) for x in arrays]

    other_heads = kv_partial(features, w_key_value, count)
    own, *outgoing = kv_partial(features, w_key_value, count, fast_swap(other_heads))
    parts = [own] + [swap(x, 2 * (j + 1)) for j, x in enumerate(outgoing)]
    direct, parts = lax.optimization_barrier((direct, parts))
    near = both_cores({0: [own_text]})
    q_near = queries(near, "queries_own_chip")
    forwarded = {}
    for half, order in enumerate((bits, bits[::-1])):
        first = half * width
        held = {0: None}
        for bit in order:
            for p in list(held):
                if p == 0:
                    held[bit] = direct[bit][:, first : first + width]
                else:
                    held[p ^ bit] = swap(held[p], bit)
                    forwarded.setdefault(p ^ bit, []).append(held[p ^ bit])

    next_to = both_cores({p: [block] for p, block in direct.items()})
    q_next = queries(next_to, "queries_neighbours")

    early, *state = attention(
        [tile_count, image_start],
        [q_near, q_next],
        [near[0], next_to[0]],
        count,
        grad_out,
        k_gain,
        parts,
        last=False,
    )
    forwarded, state = lax.optimization_barrier((forwarded, state))
    far = both_cores(forwarded)
    q_far = queries(far, "queries_forwarded")
    late, block = attention([], [q_far], [far[0]], count, grad_out, k_gain, state, last=True)
    attended = assemble([near[0] + next_to[0], far[0]], [early, late], grad_out)

    blocks = {0: block}
    blocks.update({p: swap(block, p) for p in range(count - 2, 0, -2)})
    blocks.update({p ^ 1: swap(x, 1) for p, x in blocks.items()})
    before = None
    if per_kv == 1:
        soon = {p: blocks.pop(p) for p in (0, 1)}
        before = feature_gradient(sorted(soon.items()), w_key_value, per_kv, sections, last=False)
    pieces = feature_gradient(sorted(blocks.items(), reverse=True), w_key_value, per_kv, sections, before)
    feature_grad, leaving = pieces[0], pieces[1:]
    arrived = []
    for k in range(1, sections):
        perm = [(i, (i + k) % sections) for i in range(sections)]
        arrived.append(lax.ppermute(leaving[k - 1], "section", perm))
    for x in arrived:
        feature_grad = feature_grad + x.astype(F32)
    return (attended, feature_grad)


def solution(mesh):
    return jax.shard_map(
        shards,
        mesh=mesh,
        in_specs=(
            P("section", "tensor", None),
            P(None, "tensor"),
            P("section", None),
            P("section", None, "tensor"),
            P("section", None),
            P("section", "tensor", None),
            P("section", None),
            P(),
            P(),
            P("section", None, "tensor"),
        ),
        out_specs=(P("section", None, "tensor"), P("section", "tensor")),
        check_vma=False,
    )
```

```python
import functools

import jax
import jax.numpy as jnp
from jax import lax
from jax.experimental import pallas as pl
from jax.experimental.pallas import tpu as pltpu
from jax.sharding import PartitionSpec as P

KV_HEADS = 8
HEAD_DIM = 128
TILES = 4
TILE_LEN = 24
TXT_TOK = 128
MB = 2
SLOTS = TILES * TILE_LEN

eps = 1e-05

F32 = jnp.float32
BF16 = jnp.bfloat16
MIB = 1 << 20


def whole(memory=pltpu.VMEM):
    return pl.BlockSpec(memory_space=memory)


def dot_nn(a, b):
    return jnp.dot(a, b, preferred_element_type=F32)


def dot_nt(a, b):
    return lax.dot_general(a, b, (((1,), (1,)), ((), ())), preferred_element_type=F32)


def dot_tn(a, b):
    return lax.dot_general(a, b, (((0,), (0,)), ((), ())), preferred_element_type=F32)


def params(mib):
    return pltpu.CompilerParams(vmem_limit_bytes=mib * MIB)


def cost(flops, size):
    return pl.CostEstimate(flops=flops, bytes_accessed=size, transcendentals=0)


def here():
    return lax.axis_index("tensor")


def head_columns(head):
    return [
        pl.ds(pl.multiple_of((half * KV_HEADS + head) * HEAD_DIM, HEAD_DIM), HEAD_DIM)
        for half in range(2)
    ]


def kv_kernel(per_kv, pairs, odd, feat_ref, weight_ref, *refs):
    features = feat_ref[...]
    for j in range(pairs):
        head = lax.div(lax.bitwise_xor(here(), 2 * j + odd), per_kv)
        weight = jnp.concatenate([weight_ref[0, :, c] for c in head_columns(head)], axis=1)
        total = dot_nn(features, weight)
        out_ref = refs[j - pairs]
        if not odd:
            total = total + refs[j][...]
        out_ref[...] = total.astype(out_ref.dtype)


def kv_partial(features, weight, count, other=None):
    rows, depth = features.shape
    pairs = count // 2
    odd = 1 if other is None else 0
    out_shape = [
        jax.ShapeDtypeStruct((rows, 2 * HEAD_DIM), F32 if odd or j == 0 else BF16)
        for j in range(pairs)
    ]
    operands = (features, weight, *(other or ()))
    return pl.pallas_call(
        functools.partial(kv_kernel, count // KV_HEADS, pairs, odd),
        in_specs=[whole()] * len(operands),
        out_specs=[whole()] * pairs,
        out_shape=out_shape,
        compiler_params=params(24),
        cost_estimate=cost(0, 0),
        name="kv_partial_other_core" if odd else "kv_partial_own_core",
    )(*operands)


def query_kernel(shape, start, *refs):
    gain_ref, weight_ref, q_gain_ref, refs = refs[0], refs[1], refs[2], refs[3:]
    groups = []
    for parts in shape:
        groups.append(refs[:parts])
        refs = refs[parts:]
    depth, heads_width = weight_ref.shape[1:]
    width = sum(part.shape[1] for part in groups[0])
    last = start + width == depth
    span = 1024

    def columns(parts, c):
        for part in parts:
            if c < part.shape[1]:
                return part[:, c : c + span].astype(F32)
            c -= part.shape[1]

    if start:
        raw, squares, refs = refs[0][...], refs[1][:, :1], refs[2:]
    else:
        raw, squares = 0.0, 0.0
    for c in range(0, width, span):
        x = jnp.concatenate([columns(parts, c) for parts in groups], axis=0)
        squares = squares + jnp.sum(x * x, axis=-1, keepdims=True)
        cols = slice(start + c, start + c + span)
        scaled = (x * gain_ref[:, cols].astype(F32)).astype(BF16)
        raw = raw + dot_nn(scaled, weight_ref[0, cols, :])
    if not last:
        refs[0][...] = raw
        refs[1][...] = jnp.broadcast_to(squares, refs[1].shape)
        return
    out_ref = refs[0]
    inverse = lax.rsqrt(squares / depth + eps)
    q_gain = q_gain_ref[...].astype(F32)
    for c in range(0, heads_width, HEAD_DIM):
        head = raw[:, c : c + HEAD_DIM] * inverse
        q_inverse = lax.rsqrt(jnp.mean(head * head, axis=-1, keepdims=True) + eps)
        out_ref[:, c : c + HEAD_DIM] = (head * q_inverse * q_gain).astype(BF16)


def queries_of(groups, gain, weight, q_gain, name, start=0, before=()):
    arrays = [part for parts in groups for part in parts]
    rows = sum(parts[0].shape[0] for parts in groups)
    depth, heads_width = weight.shape[1:]
    last = start + sum(part.shape[1] for part in groups[0]) == depth
    if last:
        out_shape = [jax.ShapeDtypeStruct((rows, heads_width), BF16)]
    else:
        out_shape = [jax.ShapeDtypeStruct((rows, w), F32) for w in (heads_width, HEAD_DIM)]
    out = pl.pallas_call(
        functools.partial(query_kernel, [len(parts) for parts in groups], start),
        in_specs=[whole()] * (3 + len(arrays) + len(before)),
        out_specs=[whole()] * len(out_shape),
        out_shape=out_shape,
        compiler_params=params(24),
        cost_estimate=cost(0, 0),
        name=name,
    )(gain, weight, q_gain, *arrays, *before)
    return out[0] if last else out


def attention_kernel(places, count, rows, last, sizes, *refs):
    if not last:
        count_ref, start_ref, refs = refs[0], refs[1], refs[2:]
    queries_refs, refs = refs[:sizes], refs[sizes:]
    grad_ref, k_gain_ref, refs = refs[0], refs[1], refs[2:]
    narrow = rows % 16 != 0
    if narrow:
        refs, grad_rows = refs[:-1], refs[-1]
        grad_rows[...] = grad_ref[0].astype(F32)
    if last:
        d_keys_in, d_values_in, keys_ref, values_ref, hat_ref, inverse_ref, token_ref, slot_ref = refs[:8]
        att_ref, block_ref, d_keys_ref, d_values_ref = refs[8:]
        d_keys_ref[...] = d_keys_in[...]
        d_values_ref[...] = d_values_in[...]
    else:
        parts = refs[:-9]
        att_ref, d_keys_ref, d_values_ref, keys_ref, values_ref = refs[-9:-4]
        hat_ref, inverse_ref, token_ref, slot_ref = refs[-4:]
        kv = sum(part[...].astype(F32) for part in parts)
        key_raw = kv[:, :HEAD_DIM]
        inverse = lax.rsqrt(jnp.mean(key_raw * key_raw, axis=-1, keepdims=True) + eps)
        hat_ref[...] = key_raw * inverse
        inverse_ref[...] = jnp.broadcast_to(inverse, key_raw.shape)
        keys_ref[...] = (key_raw * inverse * k_gain_ref[...].astype(F32)).astype(BF16)
        values_ref[...] = kv[:, HEAD_DIM:].astype(BF16)
        d_keys_ref[...] = jnp.zeros_like(d_keys_ref)
        d_values_ref[...] = jnp.zeros_like(d_values_ref)
        for b in range(MB):
            token = lax.broadcasted_iota(jnp.int32, (TXT_TOK, HEAD_DIM), 0)
            token_ref[b * TXT_TOK : (b + 1) * TXT_TOK, :] = (token >= start_ref[b]).astype(F32)
            slot = lax.broadcasted_iota(jnp.int32, slot_ref.shape[1:], 1)
            slot_ref[b] = (slot < count_ref[b] * TILE_LEN).astype(F32)

    scale = HEAD_DIM ** (-0.5)
    heads = grad_ref.shape[2] // HEAD_DIM
    per_sample = count // MB
    mine = lax.div(here(), per_sample)
    blocks = [
        (p, ref, i * rows) for group, ref in zip(places, queries_refs) for i, p in enumerate(group)
    ]
    for far in range(MB):
        chosen = [block for block in blocks if block[0] // per_sample == far]
        if not chosen:
            continue
        sample = lax.bitwise_xor(mine, far)
        img = pl.ds(pl.multiple_of(sample * SLOTS, SLOTS), SLOTS)
        keys, values = keys_ref[img, :], values_ref[img, :]
        live = slot_ref[sample][:1, :] > 0
        spots = [
            pl.ds(pl.multiple_of(lax.bitwise_xor(here(), p) * rows, rows), rows)
            for p, _, _ in chosen
        ]
        masks = [token_ref[spot, :] for spot in spots]
        queries, upstream = [], []
        for h in range(heads):
            cols = slice(h * HEAD_DIM, (h + 1) * HEAD_DIM)
            for (p, ref, at), mask, spot in zip(chosen, masks, spots):
                queries.append(ref[at : at + rows, cols])
                grad = grad_rows[spot, cols] if narrow else grad_ref[0, spot, cols].astype(F32)
                upstream.append((grad * mask).astype(BF16))
        queries = jnp.concatenate(queries, axis=0)
        upstream = jnp.concatenate(upstream, axis=0)
        scores = dot_nt(queries, keys) * scale
        exponent = jnp.where(live, jnp.exp(scores), 0.0)
        probs = exponent * (1.0 / jnp.sum(exponent, axis=-1, keepdims=True))
        weights = probs.astype(BF16)
        head_out = dot_nn(weights, values)
        step = 0
        for h in range(heads):
            cols = slice(h * HEAD_DIM, (h + 1) * HEAD_DIM)
            for block, mask in zip(chosen, masks):
                at = blocks.index(block) * rows
                att_ref[at : at + rows, cols] = head_out[step : step + rows] * mask
                step += rows
        d_weights = dot_nt(upstream, values)
        inner = jnp.sum(probs * d_weights, axis=-1, keepdims=True)
        d_scores = (probs * (d_weights - inner) * scale).astype(BF16)
        d_keys_ref[img, :] += dot_tn(d_scores, queries)
        d_values_ref[img, :] += dot_tn(weights, upstream)
    if last:
        hat = hat_ref[...]
        scaled = d_keys_ref[...] * k_gain_ref[...].astype(F32)
        d_raw = inverse_ref[...] * (
            scaled - hat * jnp.mean(hat * scaled, axis=-1, keepdims=True)
        )
        block_ref[:, :HEAD_DIM] = d_raw.astype(BF16)
        block_ref[:, HEAD_DIM:] = d_values_ref[...].astype(BF16)


def attention(scalars, queries, places, count, grad_out, k_gain, state, last):
    rows, width = grad_out.shape[1] // count, grad_out.shape[2]
    image_rows = MB * SLOTS
    vector = jax.ShapeDtypeStruct((image_rows, HEAD_DIM), F32)
    rounded = jax.ShapeDtypeStruct((image_rows, HEAD_DIM), BF16)
    attended = jax.ShapeDtypeStruct((sum(map(len, places)) * rows, width), F32)
    scratch = []
    if last:
        out_shape = [attended, jax.ShapeDtypeStruct((image_rows, 2 * HEAD_DIM), BF16)]
        scratch += [pltpu.VMEM(vector.shape, F32)] * 2
    else:
        token = jax.ShapeDtypeStruct((grad_out.shape[1], HEAD_DIM), F32)
        slot = jax.ShapeDtypeStruct((MB, 8, SLOTS), F32)
        out_shape = [attended, vector, vector, rounded, rounded, vector, vector, token, slot]
    if rows % 16 != 0:
        scratch += [pltpu.VMEM(grad_out.shape[1:], F32)]
    operands = [*queries, grad_out, k_gain, *state]
    return pl.pallas_call(
        functools.partial(attention_kernel, places, count, rows, last, len(queries)),
        in_specs=[whole(pltpu.SMEM)] * len(scalars) + [whole()] * len(operands),
        out_specs=[whole()] * len(out_shape),
        out_shape=out_shape,
        scratch_shapes=scratch,
        compiler_params=params(24),
        cost_estimate=cost(0, 0),
        name="attention_last" if last else "attention_first",
    )(*scalars, *operands)


def assemble_kernel(places, rows, *refs):
    refs, out_ref, held = refs[:-2], refs[-2], refs[-1]
    for group, ref in zip(places, refs):
        for i, p in enumerate(group):
            at = pl.multiple_of(lax.bitwise_xor(here(), p) * rows, rows)
            held[pl.ds(at, rows), :] = ref[i * rows : (i + 1) * rows, :]
    out_ref[0] = held[...].astype(BF16)


def assemble(places, arrays, like):
    rows = arrays[0].shape[0] // len(places[0])
    return pl.pallas_call(
        functools.partial(assemble_kernel, places, rows),
        in_specs=[whole()] * len(arrays),
        out_specs=whole(),
        out_shape=jax.ShapeDtypeStruct(like.shape, BF16),
        scratch_shapes=[pltpu.VMEM(like.shape[1:], F32)],
        compiler_params=params(24),
        cost_estimate=cost(0, 0),
        name="attended_rows",
    )(*arrays)


def grad_kernel(distances, per_kv, sections, first, last, *refs):
    blocks, weight_ref, refs = refs[: len(distances)], refs[len(distances)], refs[len(distances) + 1 :]
    if not first:
        before_ref, refs = refs[0], refs[1:]
    total = refs[-1]
    image_rows, width = total.shape
    heads = []
    for i in range(0, len(distances), per_kv):
        head = lax.div(lax.bitwise_xor(here(), distances[i]), per_kv)
        if per_kv == 1:
            block = blocks[i][...]
        else:
            block = sum(b[...].astype(F32) for b in blocks[i : i + per_kv]).astype(BF16)
        heads.append((head_columns(head), block))
    span = 256
    for c in range(0, width, span):
        cols = slice(c, c + span)
        part = 0.0 if first else before_ref[:, cols]
        for columns, block in heads:
            weight = jnp.concatenate([weight_ref[0, cols, k] for k in columns], axis=1)
            part = part + dot_nt(block, weight)
        total[:, cols] = part
    if last:
        rows = image_rows // sections
        for k in range(sections):
            to = lax.rem(lax.axis_index("section") + k, sections)
            piece = total[pl.ds(pl.multiple_of(to * rows, rows), rows), :]
            refs[k][...] = piece.astype(refs[k].dtype)


def feature_gradient(blocks, weight, per_kv, sections, before=None, last=True):
    distances = [p for p, _ in blocks]
    arrays = [block for _, block in blocks]
    image_rows = arrays[0].shape[0]
    width, depth = weight.shape[1:]
    rows = image_rows // sections
    if last:
        out_shape = [
            jax.ShapeDtypeStruct((rows, width), F32 if k == 0 else BF16) for k in range(sections)
        ]
        out_specs = [whole()] * sections
        scratch = [pltpu.VMEM((image_rows, width), F32)]
    else:
        out_shape = jax.ShapeDtypeStruct((image_rows, width), F32)
        out_specs = whole()
        scratch = []
    operands = [*arrays, weight] + ([] if before is None else [before])
    return pl.pallas_call(
        functools.partial(grad_kernel, distances, per_kv, sections, before is None, last),
        in_specs=[whole()] * len(operands),
        out_specs=out_specs,
        out_shape=out_shape,
        scratch_shapes=scratch,
        compiler_params=params(24),
        cost_estimate=cost(0, 0),
        name="feature_grad_last" if last else "feature_grad_first",
    )(*operands)


def shards(
    text, features, in_gain, w_query, q_gain, w_key_value, k_gain, tile_count, image_start, grad_out
):
    count = lax.axis_size("tensor")
    sections = lax.axis_size("section")
    per_kv = count // KV_HEADS

    def swap(x, distance):
        return lax.ppermute(x, "tensor", [(i, i ^ distance) for i in range(count)])

    own_text = text[0]
    bits = [1 << b for b in range(1, count.bit_length() - 1)]
    width = own_text.shape[1] // 2
    direct = {bit: swap(own_text, bit) for bit in bits}
    def queries(blocks, name, **more):
        return queries_of(list(blocks.values()), in_gain, w_query, q_gain, name, **more)

    def both_cores(blocks):
        out = {}
        for p, x in blocks.items():
            out[p] = [x]
            out[p ^ 1] = [swap(x, 1)]
        return out

    def fast_swap(arrays):
        return [swap(x, 1) for x in arrays]

    other_heads = kv_partial(features, w_key_value, count)
    own, *outgoing = kv_partial(features, w_key_value, count, fast_swap(other_heads))
    parts = [own] + [swap(x, 2 * (j + 1)) for j, x in enumerate(outgoing)]
    direct, parts = lax.optimization_barrier((direct, parts))
    near = both_cores({0: own_text})
    q_near = queries(near, "queries_own_chip")
    forwarded = []
    for half, order in enumerate((bits, bits[::-1])):
        first = half * width
        held, passed = {0: None}, {}
        for bit in order:
            for p in list(held):
                if p == 0:
                    held[bit] = direct[bit][:, first : first + width]
                else:
                    held[p ^ bit] = passed[p ^ bit] = swap(held[p], bit)
        forwarded.append(dict(sorted(passed.items())))

    next_to = both_cores(direct)
    q_next = queries(next_to, "queries_neighbours")

    early, *state = attention(
        [tile_count, image_start],
        [q_near, q_next],
        [list(near), list(next_to)],
        count,
        grad_out,
        k_gain,
        parts,
        last=False,
    )
    first_half, state = lax.optimization_barrier((forwarded[0], state))
    far = both_cores(first_half)
    second_half, far = lax.optimization_barrier((forwarded[1], far))
    sums = queries(far, "queries_forwarded_first")
    far = both_cores(second_half)
    q_far = queries(far, "queries_forwarded_last", start=width, before=sums)
    late, block = attention([], [q_far], [list(far)], count, grad_out, k_gain, state, last=True)
    attended = assemble([list(near) + list(next_to), list(far)], [early, late], grad_out)

    blocks = {0: block}
    blocks.update({p: swap(block, p) for p in range(count - 2, 0, -2)})
    blocks.update({p ^ 1: swap(x, 1) for p, x in blocks.items()})
    before = None
    if per_kv == 1:
        soon = {p: blocks.pop(p) for p in [1, *range(0, count, 2)]}
        before = feature_gradient(sorted(soon.items()), w_key_value, per_kv, sections, last=False)
    pieces = feature_gradient(sorted(blocks.items(), reverse=True), w_key_value, per_kv, sections, before)
    feature_grad, leaving = pieces[0], pieces[1:]
    arrived = []
    for k in range(1, sections):
        perm = [(i, (i + k) % sections) for i in range(sections)]
        arrived.append(lax.ppermute(leaving[k - 1], "section", perm))
    for x in arrived:
        feature_grad = feature_grad + x.astype(F32)
    return (attended, feature_grad)


def solution(mesh):
    return jax.shard_map(
        shards,
        mesh=mesh,
        in_specs=(
            P("section", "tensor", None),
            P(None, "tensor"),
            P("section", None),
            P("section", None, "tensor"),
            P("section", None),
            P("section", "tensor", None),
            P("section", None),
            P(),
            P(),
            P("section", None, "tensor"),
        ),
        out_specs=(P("section", None, "tensor"), P("section", "tensor")),
        check_vma=False,
    )
```

```python
import functools

import jax
import jax.numpy as jnp
from jax import lax
from jax.experimental import pallas as pl
from jax.experimental.pallas import tpu as pltpu
from jax.sharding import PartitionSpec as P

KV_HEADS = 8
HEAD_DIM = 128
TILES = 4
TILE_LEN = 24
TXT_TOK = 128
MB = 2
SLOTS = TILES * TILE_LEN

eps = 1e-05

F32 = jnp.float32
BF16 = jnp.bfloat16
MIB = 1 << 20


def whole(memory=pltpu.VMEM):
    return pl.BlockSpec(memory_space=memory)


def dot_nn(a, b):
    return jnp.dot(a, b, preferred_element_type=F32)


def dot_nt(a, b):
    return lax.dot_general(a, b, (((1,), (1,)), ((), ())), preferred_element_type=F32)


def dot_tn(a, b):
    return lax.dot_general(a, b, (((0,), (0,)), ((), ())), preferred_element_type=F32)


def params(mib):
    return pltpu.CompilerParams(vmem_limit_bytes=mib * MIB)


def cost(flops, size):
    return pl.CostEstimate(flops=flops, bytes_accessed=size, transcendentals=0)


def here():
    return lax.axis_index("tensor")


def head_columns(head):
    return [
        pl.ds(pl.multiple_of((half * KV_HEADS + head) * HEAD_DIM, HEAD_DIM), HEAD_DIM)
        for half in range(2)
    ]


def orders(bits):
    return bits, bits[::-1]


def kv_other_kernel(per_kv, distances, feat_ref, weight_ref, *out_refs):
    for p, out_ref in zip(distances, out_refs):
        head = lax.div(lax.bitwise_xor(here(), p ^ 1), per_kv)
        weight = jnp.concatenate([weight_ref[0, :, c] for c in head_columns(head)], axis=1)
        out_ref[...] = dot_nn(feat_ref[...], weight)


def kv_own_kernel(per_kv, distances, bits, feat_ref, weight_ref, *refs):
    others, out_refs = refs[: len(distances)], refs[len(distances) :]
    rows = feat_ref.shape[0] // 2
    for p, other_ref in zip(distances, others):
        head = lax.div(lax.bitwise_xor(here(), p), per_kv)
        weight = jnp.concatenate([weight_ref[0, :, c] for c in head_columns(head)], axis=1)
        total = dot_nn(feat_ref[...], weight) + other_ref[...]
        for half, order in enumerate(orders(bits)):
            ref = out_refs[2 * half + (p & order[0] > 0)]
            at = [q for q in distances if not q & order[0]].index(p & ~order[0])
            ref[at] = total[half * rows : (half + 1) * rows].astype(ref.dtype)


def kv_sum_kernel(step, distances, bits, *refs):
    ins, outs = refs[:4], refs[4:]
    for half, order in enumerate(orders(bits)):
        left = [p for p in distances if not any(p & bit for bit in order[:step])]
        for at, p in enumerate(left):
            total = ins[2 * half][at] + ins[2 * half + 1][at].astype(F32)
            ref = outs[2 * half + (p & order[step] > 0)]
            to = [q for q in left if not q & order[step]].index(p & ~order[step])
            ref[to] = total.astype(ref.dtype)


def kv_call(kernel, operands, out_shape, name):
    return pl.pallas_call(
        kernel,
        in_specs=[whole()] * len(operands),
        out_specs=[whole()] * len(out_shape),
        out_shape=out_shape,
        compiler_params=params(24),
        cost_estimate=cost(0, 0),
        name=name,
    )(*operands)


def kv_sums(features, weight, count, bits, swap, between):
    per_kv = count // KV_HEADS
    distances = list(range(0, count, 2))
    rows = features.shape[0]
    pieces = [jax.ShapeDtypeStruct((rows, 2 * HEAD_DIM), F32)] * len(distances)
    others = kv_call(
        functools.partial(kv_other_kernel, per_kv, distances),
        [features, weight],
        pieces,
        "kv_partial_other_core",
    )
    operands = [features, weight, *[swap(x, 1) for x in others]]
    kernel = functools.partial(kv_own_kernel, per_kv, distances, bits)
    name = "kv_partial_own_core"
    for step in range(len(bits)):
        shape = (len(distances) >> (step + 1), rows // 2, 2 * HEAD_DIM)
        out_shape = [jax.ShapeDtypeStruct(shape, dtype) for dtype in (F32, BF16)] * 2
        sums = kv_call(kernel, operands, out_shape, name)
        operands = []
        for half, order in enumerate(orders(bits)):
            operands += [sums[2 * half], swap(sums[2 * half + 1], order[step])]
        if step == 0:
            operands[1], operands[3] = between([operands[1], operands[3]])
        kernel = functools.partial(kv_sum_kernel, step + 1, distances, bits)
        name = "kv_sum"
    return operands


def query_kernel(shape, start, *refs):
    gain_ref, weight_ref, q_gain_ref, refs = refs[0], refs[1], refs[2], refs[3:]
    groups = []
    for parts in shape:
        groups.append(refs[:parts])
        refs = refs[parts:]
    depth, heads_width = weight_ref.shape[1:]
    width = sum(part.shape[1] for part in groups[0])
    last = start + width == depth
    span = 512 if width % 1024 else 1024

    def columns(parts, c):
        for part in parts:
            if c < part.shape[1]:
                return part[:, c : c + span].astype(F32)
            c -= part.shape[1]

    if start:
        raw, squares, refs = refs[0][...], refs[1][:, :1], refs[2:]
    else:
        raw, squares = 0.0, 0.0
    for c in range(0, width, span):
        x = jnp.concatenate([columns(parts, c) for parts in groups], axis=0)
        squares = squares + jnp.sum(x * x, axis=-1, keepdims=True)
        cols = slice(start + c, start + c + span)
        scaled = (x * gain_ref[:, cols].astype(F32)).astype(BF16)
        raw = raw + dot_nn(scaled, weight_ref[0, cols, :])
    if not last:
        refs[0][...] = raw
        refs[1][...] = jnp.broadcast_to(squares, refs[1].shape)
        return
    out_ref = refs[0]
    inverse = lax.rsqrt(squares / depth + eps)
    q_gain = q_gain_ref[...].astype(F32)
    for c in range(0, heads_width, HEAD_DIM):
        head = raw[:, c : c + HEAD_DIM] * inverse
        q_inverse = lax.rsqrt(jnp.mean(head * head, axis=-1, keepdims=True) + eps)
        out_ref[:, c : c + HEAD_DIM] = (head * q_inverse * q_gain).astype(BF16)


def queries_of(groups, gain, weight, q_gain, name, start=0, before=()):
    arrays = [part for parts in groups for part in parts]
    rows = sum(parts[0].shape[0] for parts in groups)
    depth, heads_width = weight.shape[1:]
    last = start + sum(part.shape[1] for part in groups[0]) == depth
    if last:
        out_shape = [jax.ShapeDtypeStruct((rows, heads_width), BF16)]
    else:
        out_shape = [jax.ShapeDtypeStruct((rows, w), F32) for w in (heads_width, HEAD_DIM)]
    out = pl.pallas_call(
        functools.partial(query_kernel, [len(parts) for parts in groups], start),
        in_specs=[whole()] * (3 + len(arrays) + len(before)),
        out_specs=[whole()] * len(out_shape),
        out_shape=out_shape,
        compiler_params=params(24),
        cost_estimate=cost(0, 0),
        name=name,
    )(gain, weight, q_gain, *arrays, *before)
    return out[0] if last else out


def attention_kernel(places, count, rows, last, sizes, *refs):
    if not last:
        count_ref, start_ref, refs = refs[0], refs[1], refs[2:]
    queries_refs, refs = refs[:sizes], refs[sizes:]
    grad_ref, k_gain_ref, refs = refs[0], refs[1], refs[2:]
    narrow = rows % 16 != 0
    if narrow:
        refs, grad_rows = refs[:-1], refs[-1]
        grad_rows[...] = grad_ref[0].astype(F32)
    if last:
        d_keys_in, d_values_in, keys_ref, values_ref, hat_ref, inverse_ref, token_ref, slot_ref = refs[:8]
        att_ref, block_ref, d_keys_ref, d_values_ref = refs[8:]
        d_keys_ref[...] = d_keys_in[...]
        d_values_ref[...] = d_values_in[...]
    else:
        parts = refs[:-9]
        att_ref, d_keys_ref, d_values_ref, keys_ref, values_ref = refs[-9:-4]
        hat_ref, inverse_ref, token_ref, slot_ref = refs[-4:]
        sums = [kept[0] + came[0].astype(F32) for kept, came in zip(parts[::2], parts[1::2])]
        kv = jnp.concatenate(sums, axis=0)
        key_raw = kv[:, :HEAD_DIM]
        inverse = lax.rsqrt(jnp.mean(key_raw * key_raw, axis=-1, keepdims=True) + eps)
        hat_ref[...] = key_raw * inverse
        inverse_ref[...] = jnp.broadcast_to(inverse, key_raw.shape)
        keys_ref[...] = (key_raw * inverse * k_gain_ref[...].astype(F32)).astype(BF16)
        values_ref[...] = kv[:, HEAD_DIM:].astype(BF16)
        d_keys_ref[...] = jnp.zeros_like(d_keys_ref)
        d_values_ref[...] = jnp.zeros_like(d_values_ref)
        for b in range(MB):
            token = lax.broadcasted_iota(jnp.int32, (TXT_TOK, HEAD_DIM), 0)
            token_ref[b * TXT_TOK : (b + 1) * TXT_TOK, :] = (token >= start_ref[b]).astype(F32)
            slot = lax.broadcasted_iota(jnp.int32, slot_ref.shape[1:], 1)
            slot_ref[b] = (slot < count_ref[b] * TILE_LEN).astype(F32)

    scale = HEAD_DIM ** (-0.5)
    heads = grad_ref.shape[2] // HEAD_DIM
    per_sample = count // MB
    mine = lax.div(here(), per_sample)
    blocks = [
        (p, ref, i * rows) for group, ref in zip(places, queries_refs) for i, p in enumerate(group)
    ]
    for far in range(MB):
        chosen = [block for block in blocks if block[0] // per_sample == far]
        if not chosen:
            continue
        sample = lax.bitwise_xor(mine, far)
        img = pl.ds(pl.multiple_of(sample * SLOTS, SLOTS), SLOTS)
        keys, values = keys_ref[img, :], values_ref[img, :]
        live = slot_ref[sample][:1, :] > 0
        spots = [
            pl.ds(pl.multiple_of(lax.bitwise_xor(here(), p) * rows, rows), rows)
            for p, _, _ in chosen
        ]
        masks = [token_ref[spot, :] for spot in spots]
        queries, upstream = [], []
        for h in range(heads):
            cols = slice(h * HEAD_DIM, (h + 1) * HEAD_DIM)
            for (p, ref, at), mask, spot in zip(chosen, masks, spots):
                queries.append(ref[at : at + rows, cols])
                grad = grad_rows[spot, cols] if narrow else grad_ref[0, spot, cols].astype(F32)
                upstream.append((grad * mask).astype(BF16))
        queries = jnp.concatenate(queries, axis=0)
        upstream = jnp.concatenate(upstream, axis=0)
        scores = dot_nt(queries, keys) * scale
        exponent = jnp.where(live, jnp.exp(scores), 0.0)
        probs = exponent * (1.0 / jnp.sum(exponent, axis=-1, keepdims=True))
        weights = probs.astype(BF16)
        head_out = dot_nn(weights, values)
        step = 0
        for h in range(heads):
            cols = slice(h * HEAD_DIM, (h + 1) * HEAD_DIM)
            for block, mask in zip(chosen, masks):
                at = blocks.index(block) * rows
                att_ref[at : at + rows, cols] = head_out[step : step + rows] * mask
                step += rows
        d_weights = dot_nt(upstream, values)
        inner = jnp.sum(probs * d_weights, axis=-1, keepdims=True)
        d_scores = (probs * (d_weights - inner) * scale).astype(BF16)
        d_keys_ref[img, :] += dot_tn(d_scores, queries)
        d_values_ref[img, :] += dot_tn(weights, upstream)
    if last:
        hat = hat_ref[...]
        scaled = d_keys_ref[...] * k_gain_ref[...].astype(F32)
        d_raw = inverse_ref[...] * (
            scaled - hat * jnp.mean(hat * scaled, axis=-1, keepdims=True)
        )
        block_ref[:, :HEAD_DIM] = d_raw.astype(BF16)
        block_ref[:, HEAD_DIM:] = d_values_ref[...].astype(BF16)


def attention(scalars, queries, places, count, grad_out, k_gain, state, last):
    rows, width = grad_out.shape[1] // count, grad_out.shape[2]
    image_rows = MB * SLOTS
    vector = jax.ShapeDtypeStruct((image_rows, HEAD_DIM), F32)
    rounded = jax.ShapeDtypeStruct((image_rows, HEAD_DIM), BF16)
    attended = jax.ShapeDtypeStruct((sum(map(len, places)) * rows, width), F32)
    scratch = []
    if last:
        out_shape = [attended, jax.ShapeDtypeStruct((image_rows, 2 * HEAD_DIM), BF16)]
        scratch += [pltpu.VMEM(vector.shape, F32)] * 2
    else:
        token = jax.ShapeDtypeStruct((grad_out.shape[1], HEAD_DIM), F32)
        slot = jax.ShapeDtypeStruct((MB, 8, SLOTS), F32)
        out_shape = [attended, vector, vector, rounded, rounded, vector, vector, token, slot]
    if rows % 16 != 0:
        scratch += [pltpu.VMEM(grad_out.shape[1:], F32)]
    operands = [*queries, grad_out, k_gain, *state]
    return pl.pallas_call(
        functools.partial(attention_kernel, places, count, rows, last, len(queries)),
        in_specs=[whole(pltpu.SMEM)] * len(scalars) + [whole()] * len(operands),
        out_specs=[whole()] * len(out_shape),
        out_shape=out_shape,
        scratch_shapes=scratch,
        compiler_params=params(24),
        cost_estimate=cost(0, 0),
        name="attention_last" if last else "attention_first",
    )(*scalars, *operands)


def assemble_kernel(places, rows, *refs):
    refs, out_ref, held = refs[:-2], refs[-2], refs[-1]
    for group, ref in zip(places, refs):
        for i, p in enumerate(group):
            at = pl.multiple_of(lax.bitwise_xor(here(), p) * rows, rows)
            held[pl.ds(at, rows), :] = ref[i * rows : (i + 1) * rows, :]
    out_ref[0] = held[...].astype(BF16)


def assemble(places, arrays, like):
    rows = arrays[0].shape[0] // len(places[0])
    return pl.pallas_call(
        functools.partial(assemble_kernel, places, rows),
        in_specs=[whole()] * len(arrays),
        out_specs=whole(),
        out_shape=jax.ShapeDtypeStruct(like.shape, BF16),
        scratch_shapes=[pltpu.VMEM(like.shape[1:], F32)],
        compiler_params=params(24),
        cost_estimate=cost(0, 0),
        name="attended_rows",
    )(*arrays)


def grad_kernel(distances, per_kv, sections, first, last, *refs):
    blocks, weight_ref, refs = refs[: len(distances)], refs[len(distances)], refs[len(distances) + 1 :]
    if not first:
        before_ref, refs = refs[0], refs[1:]
    total = refs[-1]
    image_rows, width = total.shape
    heads = []
    for i in range(0, len(distances), per_kv):
        head = lax.div(lax.bitwise_xor(here(), distances[i]), per_kv)
        if per_kv == 1:
            block = blocks[i][...]
        else:
            block = sum(b[...].astype(F32) for b in blocks[i : i + per_kv]).astype(BF16)
        heads.append((head_columns(head), block))
    span = 256
    for c in range(0, width, span):
        cols = slice(c, c + span)
        part = 0.0 if first else before_ref[:, cols]
        for columns, block in heads:
            weight = jnp.concatenate([weight_ref[0, cols, k] for k in columns], axis=1)
            part = part + dot_nt(block, weight)
        total[:, cols] = part
    if last:
        rows = image_rows // sections
        for k in range(sections):
            to = lax.rem(lax.axis_index("section") + k, sections)
            piece = total[pl.ds(pl.multiple_of(to * rows, rows), rows), :]
            refs[k][...] = piece.astype(refs[k].dtype)


def feature_gradient(blocks, weight, per_kv, sections, before=None, last=True):
    distances = [p for p, _ in blocks]
    arrays = [block for _, block in blocks]
    image_rows = arrays[0].shape[0]
    width, depth = weight.shape[1:]
    rows = image_rows // sections
    if last:
        out_shape = [
            jax.ShapeDtypeStruct((rows, width), F32 if k == 0 else BF16) for k in range(sections)
        ]
        out_specs = [whole()] * sections
        scratch = [pltpu.VMEM((image_rows, width), F32)]
    else:
        out_shape = jax.ShapeDtypeStruct((image_rows, width), F32)
        out_specs = whole()
        scratch = []
    operands = [*arrays, weight] + ([] if before is None else [before])
    return pl.pallas_call(
        functools.partial(grad_kernel, distances, per_kv, sections, before is None, last),
        in_specs=[whole()] * len(operands),
        out_specs=out_specs,
        out_shape=out_shape,
        scratch_shapes=scratch,
        compiler_params=params(24),
        cost_estimate=cost(0, 0),
        name="feature_grad_last" if last else "feature_grad_first",
    )(*operands)


def shards(
    text, features, in_gain, w_query, q_gain, w_key_value, k_gain, tile_count, image_start, grad_out
):
    count = lax.axis_size("tensor")
    sections = lax.axis_size("section")
    per_kv = count // KV_HEADS

    def swap(x, distance):
        return lax.ppermute(x, "tensor", [(i, i ^ distance) for i in range(count)])

    own_text = text[0]
    bits = [1 << b for b in range(1, count.bit_length() - 1)]
    cut = own_text.shape[1] * 7 // 16
    direct = {bit: swap(own_text, bit) for bit in bits}
    def queries(blocks, name, **more):
        return queries_of(list(blocks.values()), in_gain, w_query, q_gain, name, **more)

    def both_cores(blocks):
        out = {}
        for p, x in blocks.items():
            out[p] = [x]
            out[p ^ 1] = [swap(x, 1)]
        return out

    own_chip = both_cores({0: own_text})

    def first_arrivals(arrived):
        nonlocal direct, own_chip
        direct, own_chip, arrived = lax.optimization_barrier((direct, own_chip, arrived))
        return arrived

    parts = kv_sums(features, w_key_value, count, bits, swap, first_arrivals)
    forwarded = []
    for order, columns in ((bits, slice(0, cut)), (bits[::-1], slice(cut, None))):
        held, passed = {0: None}, {}
        for bit in order:
            for p in list(held):
                if p == 0:
                    held[bit] = direct[bit][:, columns]
                else:
                    held[p ^ bit] = passed[p ^ bit] = swap(held[p], bit)
        forwarded.append(dict(sorted(passed.items())))

    near = {**own_chip, **both_cores(direct)}
    q_near = queries(near, "queries_near")

    early, *state = attention(
        [tile_count, image_start],
        [q_near],
        [list(near)],
        count,
        grad_out,
        k_gain,
        parts,
        last=False,
    )
    first_half, state = lax.optimization_barrier((forwarded[0], state))
    far = both_cores(first_half)
    second_half, far = lax.optimization_barrier((forwarded[1], far))
    sums = queries(far, "queries_forwarded_first")
    far = both_cores(second_half)
    q_far = queries(far, "queries_forwarded_last", start=cut, before=sums)
    late, block = attention([], [q_far], [list(far)], count, grad_out, k_gain, state, last=True)
    attended = assemble([list(near), list(far)], [early, late], grad_out)

    blocks = {0: block}
    blocks.update({p: swap(block, p) for p in range(count - 2, 0, -2)})
    blocks.update({p ^ 1: swap(x, 1) for p, x in blocks.items()})
    before = None
    if per_kv == 1:
        soon = {p: blocks.pop(p) for p in [1, *range(0, count, 2)]}
        before = feature_gradient(sorted(soon.items()), w_key_value, per_kv, sections, last=False)
    pieces = feature_gradient(sorted(blocks.items(), reverse=True), w_key_value, per_kv, sections, before)
    feature_grad, leaving = pieces[0], pieces[1:]
    arrived = []
    for k in range(1, sections):
        perm = [(i, (i + k) % sections) for i in range(sections)]
        arrived.append(lax.ppermute(leaving[k - 1], "section", perm))
    for x in arrived:
        feature_grad = feature_grad + x.astype(F32)
    return (attended, feature_grad)


def solution(mesh):
    return jax.shard_map(
        shards,
        mesh=mesh,
        in_specs=(
            P("section", "tensor", None),
            P(None, "tensor"),
            P("section", None),
            P("section", None, "tensor"),
            P("section", None),
            P("section", "tensor", None),
            P("section", None),
            P(),
            P(),
            P("section", None, "tensor"),
        ),
        out_specs=(P("section", None, "tensor"), P("section", "tensor")),
        check_vma=False,
    )
```

```python
import functools

import jax
import jax.numpy as jnp
from jax import lax
from jax.experimental import pallas as pl
from jax.experimental.pallas import tpu as pltpu
from jax.sharding import PartitionSpec as P

KV_HEADS = 8
HEAD_DIM = 128
TILES = 4
TILE_LEN = 24
TXT_TOK = 128
MB = 2
SLOTS = TILES * TILE_LEN

eps = 1e-05

F32 = jnp.float32
BF16 = jnp.bfloat16
MIB = 1 << 20


def whole(memory=pltpu.VMEM):
    return pl.BlockSpec(memory_space=memory)


def dot_nn(a, b):
    return jnp.dot(a, b, preferred_element_type=F32)


def dot_nt(a, b):
    return lax.dot_general(a, b, (((1,), (1,)), ((), ())), preferred_element_type=F32)


def dot_tn(a, b):
    return lax.dot_general(a, b, (((0,), (0,)), ((), ())), preferred_element_type=F32)


def params(mib):
    return pltpu.CompilerParams(vmem_limit_bytes=mib * MIB)


def cost(flops, size):
    return pl.CostEstimate(flops=flops, bytes_accessed=size, transcendentals=0)


def here():
    return lax.axis_index("tensor")


def head_columns(head):
    return [
        pl.ds(pl.multiple_of((half * KV_HEADS + head) * HEAD_DIM, HEAD_DIM), HEAD_DIM)
        for half in range(2)
    ]


def kv_kernel(per_kv, pairs, odd, feat_ref, weight_ref, *refs):
    features = feat_ref[...]
    for j in range(pairs):
        head = lax.div(lax.bitwise_xor(here(), 2 * j + odd), per_kv)
        weight = jnp.concatenate([weight_ref[0, :, c] for c in head_columns(head)], axis=1)
        total = dot_nn(features, weight)
        out_ref = refs[j - pairs]
        if not odd:
            total = total + refs[j][...]
        out_ref[...] = total.astype(out_ref.dtype)


def kv_partial(features, weight, count, other=None):
    rows, depth = features.shape
    pairs = count // 2
    odd = 1 if other is None else 0
    out_shape = [
        jax.ShapeDtypeStruct((rows, 2 * HEAD_DIM), F32 if odd or j == 0 else BF16)
        for j in range(pairs)
    ]
    operands = (features, weight, *(other or ()))
    return pl.pallas_call(
        functools.partial(kv_kernel, count // KV_HEADS, pairs, odd),
        in_specs=[whole()] * len(operands),
        out_specs=[whole()] * pairs,
        out_shape=out_shape,
        compiler_params=params(24),
        cost_estimate=cost(0, 0),
        name="kv_partial_other_core" if odd else "kv_partial_own_core",
    )(*operands)


def query_kernel(shape, start, *refs):
    gain_ref, weight_ref, q_gain_ref, refs = refs[0], refs[1], refs[2], refs[3:]
    groups = []
    for parts in shape:
        groups.append(refs[:parts])
        refs = refs[parts:]
    depth, heads_width = weight_ref.shape[1:]
    width = sum(part.shape[1] for part in groups[0])
    last = start + width == depth
    span = 1024

    def columns(parts, c):
        for part in parts:
            if c < part.shape[1]:
                return part[:, c : c + span].astype(F32)
            c -= part.shape[1]

    if start:
        raw, squares, refs = refs[0][...], refs[1][:, :1], refs[2:]
    else:
        raw, squares = 0.0, 0.0
    for c in range(0, width, span):
        x = jnp.concatenate([columns(parts, c) for parts in groups], axis=0)
        squares = squares + jnp.sum(x * x, axis=-1, keepdims=True)
        cols = slice(start + c, start + c + span)
        scaled = (x * gain_ref[:, cols].astype(F32)).astype(BF16)
        raw = raw + dot_nn(scaled, weight_ref[0, cols, :])
    if not last:
        refs[0][...] = raw
        refs[1][...] = jnp.broadcast_to(squares, refs[1].shape)
        return
    out_ref = refs[0]
    inverse = lax.rsqrt(squares / depth + eps)
    q_gain = q_gain_ref[...].astype(F32)
    for c in range(0, heads_width, HEAD_DIM):
        head = raw[:, c : c + HEAD_DIM] * inverse
        q_inverse = lax.rsqrt(jnp.mean(head * head, axis=-1, keepdims=True) + eps)
        out_ref[:, c : c + HEAD_DIM] = (head * q_inverse * q_gain).astype(BF16)


def queries_of(groups, gain, weight, q_gain, name, start=0, before=()):
    arrays = [part for parts in groups for part in parts]
    rows = sum(parts[0].shape[0] for parts in groups)
    depth, heads_width = weight.shape[1:]
    last = start + sum(part.shape[1] for part in groups[0]) == depth
    if last:
        out_shape = [jax.ShapeDtypeStruct((rows, heads_width), BF16)]
    else:
        out_shape = [jax.ShapeDtypeStruct((rows, w), F32) for w in (heads_width, HEAD_DIM)]
    out = pl.pallas_call(
        functools.partial(query_kernel, [len(parts) for parts in groups], start),
        in_specs=[whole()] * (3 + len(arrays) + len(before)),
        out_specs=[whole()] * len(out_shape),
        out_shape=out_shape,
        compiler_params=params(24),
        cost_estimate=cost(0, 0),
        name=name,
    )(gain, weight, q_gain, *arrays, *before)
    return out[0] if last else out


def attention_kernel(places, count, rows, last, sizes, *refs):
    if not last:
        count_ref, start_ref, refs = refs[0], refs[1], refs[2:]
    queries_refs, refs = refs[:sizes], refs[sizes:]
    grad_ref, k_gain_ref, refs = refs[0], refs[1], refs[2:]
    narrow = rows % 16 != 0
    if narrow:
        refs, grad_rows = refs[:-1], refs[-1]
        grad_rows[...] = grad_ref[0].astype(F32)
    if last:
        d_keys_in, d_values_in, keys_ref, values_ref, hat_ref, inverse_ref, token_ref, slot_ref = refs[:8]
        att_ref, block_ref, d_keys_ref, d_values_ref = refs[8:]
        d_keys_ref[...] = d_keys_in[...]
        d_values_ref[...] = d_values_in[...]
    else:
        parts = refs[:-9]
        att_ref, d_keys_ref, d_values_ref, keys_ref, values_ref = refs[-9:-4]
        hat_ref, inverse_ref, token_ref, slot_ref = refs[-4:]
        kv = sum(part[...].astype(F32) for part in parts)
        key_raw = kv[:, :HEAD_DIM]
        inverse = lax.rsqrt(jnp.mean(key_raw * key_raw, axis=-1, keepdims=True) + eps)
        hat_ref[...] = key_raw * inverse
        inverse_ref[...] = jnp.broadcast_to(inverse, key_raw.shape)
        keys_ref[...] = (key_raw * inverse * k_gain_ref[...].astype(F32)).astype(BF16)
        values_ref[...] = kv[:, HEAD_DIM:].astype(BF16)
        d_keys_ref[...] = jnp.zeros_like(d_keys_ref)
        d_values_ref[...] = jnp.zeros_like(d_values_ref)
        for b in range(MB):
            token = lax.broadcasted_iota(jnp.int32, (TXT_TOK, HEAD_DIM), 0)
            token_ref[b * TXT_TOK : (b + 1) * TXT_TOK, :] = (token >= start_ref[b]).astype(F32)
            slot = lax.broadcasted_iota(jnp.int32, slot_ref.shape[1:], 1)
            slot_ref[b] = (slot < count_ref[b] * TILE_LEN).astype(F32)

    scale = HEAD_DIM ** (-0.5)
    heads = grad_ref.shape[2] // HEAD_DIM
    per_sample = count // MB
    mine = lax.div(here(), per_sample)
    blocks = [
        (p, ref, i * rows) for group, ref in zip(places, queries_refs) for i, p in enumerate(group)
    ]
    for far in range(MB):
        chosen = [block for block in blocks if block[0] // per_sample == far]
        if not chosen:
            continue
        sample = lax.bitwise_xor(mine, far)
        img = pl.ds(pl.multiple_of(sample * SLOTS, SLOTS), SLOTS)
        keys, values = keys_ref[img, :], values_ref[img, :]
        live = slot_ref[sample][:1, :] > 0
        spots = [
            pl.ds(pl.multiple_of(lax.bitwise_xor(here(), p) * rows, rows), rows)
            for p, _, _ in chosen
        ]
        masks = [token_ref[spot, :] for spot in spots]
        queries, upstream = [], []
        for h in range(heads):
            cols = slice(h * HEAD_DIM, (h + 1) * HEAD_DIM)
            for (p, ref, at), mask, spot in zip(chosen, masks, spots):
                queries.append(ref[at : at + rows, cols])
                grad = grad_rows[spot, cols] if narrow else grad_ref[0, spot, cols].astype(F32)
                upstream.append((grad * mask).astype(BF16))
        queries = jnp.concatenate(queries, axis=0)
        upstream = jnp.concatenate(upstream, axis=0)
        scores = dot_nt(queries, keys) * scale
        exponent = jnp.where(live, jnp.exp(scores), 0.0)
        probs = exponent * (1.0 / jnp.sum(exponent, axis=-1, keepdims=True))
        weights = probs.astype(BF16)
        head_out = dot_nn(weights, values)
        step = 0
        for h in range(heads):
            cols = slice(h * HEAD_DIM, (h + 1) * HEAD_DIM)
            for block, mask in zip(chosen, masks):
                at = blocks.index(block) * rows
                att_ref[at : at + rows, cols] = head_out[step : step + rows] * mask
                step += rows
        d_weights = dot_nt(upstream, values)
        inner = jnp.sum(probs * d_weights, axis=-1, keepdims=True)
        d_scores = (probs * (d_weights - inner) * scale).astype(BF16)
        d_keys_ref[img, :] += dot_tn(d_scores, queries)
        d_values_ref[img, :] += dot_tn(weights, upstream)
    if last:
        hat = hat_ref[...]
        scaled = d_keys_ref[...] * k_gain_ref[...].astype(F32)
        d_raw = inverse_ref[...] * (
            scaled - hat * jnp.mean(hat * scaled, axis=-1, keepdims=True)
        )
        block_ref[:, :HEAD_DIM] = d_raw.astype(BF16)
        block_ref[:, HEAD_DIM:] = d_values_ref[...].astype(BF16)


def attention(scalars, queries, places, count, grad_out, k_gain, state, last):
    rows, width = grad_out.shape[1] // count, grad_out.shape[2]
    image_rows = MB * SLOTS
    vector = jax.ShapeDtypeStruct((image_rows, HEAD_DIM), F32)
    rounded = jax.ShapeDtypeStruct((image_rows, HEAD_DIM), BF16)
    attended = jax.ShapeDtypeStruct((sum(map(len, places)) * rows, width), F32)
    scratch = []
    if last:
        out_shape = [attended, jax.ShapeDtypeStruct((image_rows, 2 * HEAD_DIM), BF16)]
        scratch += [pltpu.VMEM(vector.shape, F32)] * 2
    else:
        token = jax.ShapeDtypeStruct((grad_out.shape[1], HEAD_DIM), F32)
        slot = jax.ShapeDtypeStruct((MB, 8, SLOTS), F32)
        out_shape = [attended, vector, vector, rounded, rounded, vector, vector, token, slot]
    if rows % 16 != 0:
        scratch += [pltpu.VMEM(grad_out.shape[1:], F32)]
    operands = [*queries, grad_out, k_gain, *state]
    return pl.pallas_call(
        functools.partial(attention_kernel, places, count, rows, last, len(queries)),
        in_specs=[whole(pltpu.SMEM)] * len(scalars) + [whole()] * len(operands),
        out_specs=[whole()] * len(out_shape),
        out_shape=out_shape,
        scratch_shapes=scratch,
        compiler_params=params(24),
        cost_estimate=cost(0, 0),
        name="attention_last" if last else "attention_first",
    )(*scalars, *operands)


def assemble_kernel(places, rows, *refs):
    refs, out_ref, held = refs[:-2], refs[-2], refs[-1]
    for group, ref in zip(places, refs):
        for i, p in enumerate(group):
            at = pl.multiple_of(lax.bitwise_xor(here(), p) * rows, rows)
            held[pl.ds(at, rows), :] = ref[i * rows : (i + 1) * rows, :]
    out_ref[0] = held[...].astype(BF16)


def assemble(places, arrays, like):
    rows = arrays[0].shape[0] // len(places[0])
    return pl.pallas_call(
        functools.partial(assemble_kernel, places, rows),
        in_specs=[whole()] * len(arrays),
        out_specs=whole(),
        out_shape=jax.ShapeDtypeStruct(like.shape, BF16),
        scratch_shapes=[pltpu.VMEM(like.shape[1:], F32)],
        compiler_params=params(24),
        cost_estimate=cost(0, 0),
        name="attended_rows",
    )(*arrays)


def grad_kernel(distances, per_kv, sections, first, last, *refs):
    blocks = []
    for _, pieces in distances:
        blocks.append(jnp.concatenate([ref[...] for ref in refs[:pieces]], axis=0))
        refs = refs[pieces:]
    weight_ref, refs = refs[0], refs[1:]
    if not first:
        before_ref, refs = refs[0], refs[1:]
    total = refs[-1]
    image_rows, width = total.shape
    heads = []
    for i in range(0, len(distances), per_kv):
        head = lax.div(lax.bitwise_xor(here(), distances[i][0]), per_kv)
        if per_kv == 1:
            block = blocks[i]
        else:
            block = sum(b.astype(F32) for b in blocks[i : i + per_kv]).astype(BF16)
        heads.append((head_columns(head), block))
    span = 256
    for c in range(0, width, span):
        cols = slice(c, c + span)
        part = 0.0 if first else before_ref[:, cols]
        for columns, block in heads:
            weight = jnp.concatenate([weight_ref[0, cols, k] for k in columns], axis=1)
            part = part + dot_nt(block, weight)
        total[:, cols] = part
    if last:
        rows = image_rows // sections
        for k in range(sections):
            to = lax.rem(lax.axis_index("section") + k, sections)
            piece = total[pl.ds(pl.multiple_of(to * rows, rows), rows), :]
            refs[k][...] = piece.astype(refs[k].dtype)


def feature_gradient(blocks, weight, per_kv, sections, before=None, last=True):
    distances = [(p, len(parts)) for p, parts in blocks]
    arrays = [part for _, parts in blocks for part in parts]
    image_rows = sum(part.shape[0] for part in blocks[0][1])
    width, depth = weight.shape[1:]
    rows = image_rows // sections
    if last:
        out_shape = [
            jax.ShapeDtypeStruct((rows, width), F32 if k == 0 else BF16) for k in range(sections)
        ]
        out_specs = [whole()] * sections
        scratch = [pltpu.VMEM((image_rows, width), F32)]
    else:
        out_shape = jax.ShapeDtypeStruct((image_rows, width), F32)
        out_specs = whole()
        scratch = []
    operands = [*arrays, weight] + ([] if before is None else [before])
    return pl.pallas_call(
        functools.partial(grad_kernel, distances, per_kv, sections, before is None, last),
        in_specs=[whole()] * len(operands),
        out_specs=out_specs,
        out_shape=out_shape,
        scratch_shapes=scratch,
        compiler_params=params(24),
        cost_estimate=cost(0, 0),
        name="feature_grad_last" if last else "feature_grad_first",
    )(*operands)


def shards(
    text, features, in_gain, w_query, q_gain, w_key_value, k_gain, tile_count, image_start, grad_out
):
    count = lax.axis_size("tensor")
    sections = lax.axis_size("section")
    per_kv = count // KV_HEADS

    def swap(x, distance):
        return lax.ppermute(x, "tensor", [(i, i ^ distance) for i in range(count)])

    own_text = text[0]
    bits = [1 << b for b in range(1, count.bit_length() - 1)]
    width = own_text.shape[1] // 2
    direct = {bit: swap(own_text, bit) for bit in bits}
    def queries(blocks, name, **more):
        return queries_of(list(blocks.values()), in_gain, w_query, q_gain, name, **more)

    def both_cores(blocks):
        out = {}
        for p, x in blocks.items():
            out[p] = [x]
            out[p ^ 1] = [swap(x, 1)]
        return out

    def fast_swap(arrays):
        return [swap(x, 1) for x in arrays]

    other_heads = kv_partial(features, w_key_value, count)
    own, *outgoing = kv_partial(features, w_key_value, count, fast_swap(other_heads))
    parts = [own] + [swap(x, 2 * (j + 1)) for j, x in enumerate(outgoing)]
    direct, parts = lax.optimization_barrier((direct, parts))
    near = both_cores({0: own_text})
    q_near = queries(near, "queries_own_chip")
    forwarded = []
    for half, order in enumerate((bits, bits[::-1])):
        first = half * width
        held, passed = {0: None}, {}
        for bit in order:
            for p in list(held):
                if p == 0:
                    held[bit] = direct[bit][:, first : first + width]
                else:
                    held[p ^ bit] = passed[p ^ bit] = swap(held[p], bit)
        forwarded.append(dict(sorted(passed.items())))

    next_to = both_cores(direct)
    q_next = queries(next_to, "queries_neighbours")

    early, *state = attention(
        [tile_count, image_start],
        [q_near, q_next],
        [list(near), list(next_to)],
        count,
        grad_out,
        k_gain,
        parts,
        last=False,
    )
    first_half, state = lax.optimization_barrier((forwarded[0], state))
    far = both_cores(first_half)
    second_half, far = lax.optimization_barrier((forwarded[1], far))
    sums = queries(far, "queries_forwarded_first")
    far = both_cores(second_half)
    q_far = queries(far, "queries_forwarded_last", start=width, before=sums)
    late, block = attention([], [q_far], [list(far)], count, grad_out, k_gain, state, last=True)
    attended = assemble([list(near) + list(next_to), list(far)], [early, late], grad_out)

    came = {bit: swap(block, bit) for bit in bits}
    on_the_way = []
    for half, order in enumerate((bits, bits[::-1])):
        held, passed = {0: None}, {}
        for bit in order:
            for p in list(held):
                if p == 0:
                    held[bit] = jnp.split(came[bit], 2, axis=0)[half]
                else:
                    held[p ^ bit] = passed[p ^ bit] = swap(held[p], bit)
        on_the_way.append(passed)
    soon = {0: [block], **{p: [x] for p, x in came.items()}}
    soon.update({p ^ 1: [swap(x, 1) for x in parts] for p, parts in soon.items()})
    blocks = {p: [passed[p] for passed in on_the_way] for p in sorted(on_the_way[0])}
    blocks.update({p ^ 1: [swap(x, 1) for x in parts] for p, parts in blocks.items()})
    before = None
    if per_kv == 1:
        before = feature_gradient(sorted(soon.items()), w_key_value, per_kv, sections, last=False)
    else:
        blocks.update(soon)
    pieces = feature_gradient(sorted(blocks.items()), w_key_value, per_kv, sections, before)
    feature_grad, leaving = pieces[0], pieces[1:]
    arrived = []
    for k in range(1, sections):
        perm = [(i, (i + k) % sections) for i in range(sections)]
        arrived.append(lax.ppermute(leaving[k - 1], "section", perm))
    for x in arrived:
        feature_grad = feature_grad + x.astype(F32)
    return (attended, feature_grad)


def solution(mesh):
    return jax.shard_map(
        shards,
        mesh=mesh,
        in_specs=(
            P("section", "tensor", None),
            P(None, "tensor"),
            P("section", None),
            P("section", None, "tensor"),
            P("section", None),
            P("section", "tensor", None),
            P("section", None),
            P(),
            P(),
            P("section", None, "tensor"),
        ),
        out_specs=(P("section", None, "tensor"), P("section", "tensor")),
        check_vma=False,
    )
```

```python
import functools

import jax
import jax.numpy as jnp
from jax import lax
from jax.experimental import pallas as pl
from jax.experimental.pallas import tpu as pltpu
from jax.sharding import PartitionSpec as P

KV_HEADS = 8
HEAD_DIM = 128
TILES = 4
TILE_LEN = 24
TXT_TOK = 128
MB = 2
SLOTS = TILES * TILE_LEN

eps = 1e-05

F32 = jnp.float32
BF16 = jnp.bfloat16
MIB = 1 << 20


def whole(memory=pltpu.VMEM):
    return pl.BlockSpec(memory_space=memory)


def dot_nn(a, b):
    return jnp.dot(a, b, preferred_element_type=F32)


def dot_nt(a, b):
    return lax.dot_general(a, b, (((1,), (1,)), ((), ())), preferred_element_type=F32)


def dot_tn(a, b):
    return lax.dot_general(a, b, (((0,), (0,)), ((), ())), preferred_element_type=F32)


def params(mib):
    return pltpu.CompilerParams(vmem_limit_bytes=mib * MIB)


def cost(flops, size):
    return pl.CostEstimate(flops=flops, bytes_accessed=size, transcendentals=0)


def here():
    return lax.axis_index("tensor")


def of_core(pair):
    even, odd = pair
    return even if even == odd else even + lax.rem(here(), 2) * (odd - even)


def partner_at(pair):
    return lax.bitwise_xor(here(), of_core(pair))


def other_core(pair):
    return (1 ^ pair[1], 1 ^ pair[0])


def head_columns(head):
    return [
        pl.ds(pl.multiple_of((half * KV_HEADS + head) * HEAD_DIM, HEAD_DIM), HEAD_DIM)
        for half in range(2)
    ]


def kv_kernel(per_kv, pairs, feat_ref, weight_ref, *refs):
    features = feat_ref[...]
    for j, pair in enumerate(pairs):
        head = lax.div(partner_at(pair), per_kv)
        weight = jnp.concatenate([weight_ref[0, :, c] for c in head_columns(head)], axis=1)
        total = dot_nn(features, weight)
        out_ref = refs[j - len(pairs)]
        if len(refs) > len(pairs):
            total = total + refs[j][...]
        out_ref[...] = total.astype(out_ref.dtype)


def kv_partial(features, weight, per_kv, pairs, other=()):
    rows = features.shape[0]
    operands = (features, weight, *other)
    out_shape = [
        jax.ShapeDtypeStruct((rows, 2 * HEAD_DIM), BF16 if other and j > 0 else F32)
        for j in range(len(pairs))
    ]
    return pl.pallas_call(
        functools.partial(kv_kernel, per_kv, pairs),
        in_specs=[whole()] * len(operands),
        out_specs=[whole()] * len(pairs),
        out_shape=out_shape,
        compiler_params=params(24),
        cost_estimate=cost(0, 0),
        name="kv_partial_own_core" if other else "kv_partial_other_core",
    )(*operands)


def query_kernel(shape, slots, start, *refs):
    gain_ref, weight_ref, q_gain_ref, refs = refs[0], refs[1], refs[2], refs[3:]
    groups = []
    for parts in shape:
        groups.append(refs[:parts])
        refs = refs[parts:]
    depth, heads_width = weight_ref.shape[1:]
    width = sum(part.shape[1] for part in groups[0])
    last = start + width == depth
    span = 1024

    def columns(parts, c):
        for part in parts:
            if c < part.shape[1]:
                return part[:, c : c + span].astype(F32)
            c -= part.shape[1]

    if start:
        raw, squares, refs = refs[0][...], refs[1][:, :1], refs[2:]
    else:
        raw, squares = 0.0, 0.0
    for c in range(0, width, span):
        x = jnp.concatenate([columns(parts, c) for parts in groups], axis=0)
        squares = squares + jnp.sum(x * x, axis=-1, keepdims=True)
        cols = slice(start + c, start + c + span)
        scaled = (x * gain_ref[:, cols].astype(F32)).astype(BF16)
        raw = raw + dot_nn(scaled, weight_ref[0, cols, :])
    if not last:
        refs[0][...] = raw
        refs[1][...] = jnp.broadcast_to(squares, refs[1].shape)
        return
    out_ref = refs[-1]
    rows = groups[0][0].shape[0]
    inverse = lax.rsqrt(squares / depth + eps)
    q_gain = q_gain_ref[...].astype(F32)
    for c in range(0, heads_width, HEAD_DIM):
        head = raw[:, c : c + HEAD_DIM] * inverse
        q_inverse = lax.rsqrt(jnp.mean(head * head, axis=-1, keepdims=True) + eps)
        head = head * q_inverse * q_gain
        for i, pair in enumerate(slots):
            at = of_core(pair) * rows
            if pair[0] != pair[1]:
                at = pl.multiple_of(at, rows)
            part = head[i * rows : (i + 1) * rows]
            out_ref[pl.ds(at, rows), c : c + HEAD_DIM] = part.astype(out_ref.dtype)
    if len(refs) > 1:
        refs[0][...] = out_ref[...].astype(BF16)


def queries_of(groups, slots, gain, weight, q_gain, name, start=0, before=()):
    arrays = [part for parts in groups for part in parts]
    rows = sum(parts[0].shape[0] for parts in groups)
    depth, heads_width = weight.shape[1:]
    last = start + sum(part.shape[1] for part in groups[0]) == depth
    scratch = []
    if last:
        out_shape = [jax.ShapeDtypeStruct((rows, heads_width), BF16)]
        if arrays[0].shape[0] % 16 != 0:
            scratch.append(pltpu.VMEM((rows, heads_width), F32))
    else:
        out_shape = [jax.ShapeDtypeStruct((rows, w), F32) for w in (heads_width, HEAD_DIM)]
    out = pl.pallas_call(
        functools.partial(query_kernel, [len(parts) for parts in groups], slots, start),
        in_specs=[whole()] * (3 + len(arrays) + len(before)),
        out_specs=[whole()] * len(out_shape),
        out_shape=out_shape,
        scratch_shapes=scratch,
        compiler_params=params(24),
        cost_estimate=cost(0, 0),
        name=name,
    )(gain, weight, q_gain, *arrays, *before)
    return out[0] if last else out


def attention_kernel(places, count, rows, last, sizes, *refs):
    if not last:
        count_ref, start_ref, refs = refs[0], refs[1], refs[2:]
    queries_refs, refs = refs[:sizes], refs[sizes:]
    grad_ref, k_gain_ref, refs = refs[0], refs[1], refs[2:]
    narrow = rows % 16 != 0
    if narrow:
        refs, grad_rows = refs[:-1], refs[-1]
        grad_rows[...] = grad_ref[0].astype(F32)
    if last:
        d_keys_in, d_values_in, keys_ref, values_ref, hat_ref, inverse_ref, token_ref, slot_ref = refs[:8]
        att_ref, block_ref, d_keys_ref, d_values_ref = refs[8:]
        d_keys_ref[...] = d_keys_in[...]
        d_values_ref[...] = d_values_in[...]
    else:
        parts = refs[:-9]
        att_ref, d_keys_ref, d_values_ref, keys_ref, values_ref = refs[-9:-4]
        hat_ref, inverse_ref, token_ref, slot_ref = refs[-4:]
        kv = sum(part[...].astype(F32) for part in parts)
        key_raw = kv[:, :HEAD_DIM]
        inverse = lax.rsqrt(jnp.mean(key_raw * key_raw, axis=-1, keepdims=True) + eps)
        hat_ref[...] = key_raw * inverse
        inverse_ref[...] = jnp.broadcast_to(inverse, key_raw.shape)
        keys_ref[...] = (key_raw * inverse * k_gain_ref[...].astype(F32)).astype(BF16)
        values_ref[...] = kv[:, HEAD_DIM:].astype(BF16)
        d_keys_ref[...] = jnp.zeros_like(d_keys_ref)
        d_values_ref[...] = jnp.zeros_like(d_values_ref)
        for b in range(MB):
            token = lax.broadcasted_iota(jnp.int32, (TXT_TOK, HEAD_DIM), 0)
            token_ref[b * TXT_TOK : (b + 1) * TXT_TOK, :] = (token >= start_ref[b]).astype(F32)
            slot = lax.broadcasted_iota(jnp.int32, slot_ref.shape[1:], 1)
            slot_ref[b] = (slot < count_ref[b] * TILE_LEN).astype(F32)

    scale = HEAD_DIM ** (-0.5)
    heads = grad_ref.shape[2] // HEAD_DIM
    per_sample = count // MB
    mine = lax.div(here(), per_sample)
    blocks = [
        (p, ref, i * rows) for group, ref in zip(places, queries_refs) for i, p in enumerate(group)
    ]
    for far in range(MB):
        chosen = [block for block in blocks if block[0] // per_sample == far]
        if not chosen:
            continue
        sample = lax.bitwise_xor(mine, far)
        img = pl.ds(pl.multiple_of(sample * SLOTS, SLOTS), SLOTS)
        keys, values = keys_ref[img, :], values_ref[img, :]
        live = slot_ref[sample][:1, :] > 0
        spots = [
            pl.ds(pl.multiple_of(lax.bitwise_xor(here(), p) * rows, rows), rows)
            for p, _, _ in chosen
        ]
        masks = [token_ref[spot, :] for spot in spots]
        queries, upstream = [], []
        for h in range(heads):
            cols = slice(h * HEAD_DIM, (h + 1) * HEAD_DIM)
            for (p, ref, at), mask, spot in zip(chosen, masks, spots):
                queries.append(ref[at : at + rows, cols])
                grad = grad_rows[spot, cols] if narrow else grad_ref[0, spot, cols].astype(F32)
                upstream.append((grad * mask).astype(BF16))
        queries = jnp.concatenate(queries, axis=0)
        upstream = jnp.concatenate(upstream, axis=0)
        scores = dot_nt(queries, keys) * scale
        exponent = jnp.where(live, jnp.exp(scores), 0.0)
        probs = exponent * (1.0 / jnp.sum(exponent, axis=-1, keepdims=True))
        weights = probs.astype(BF16)
        head_out = dot_nn(weights, values)
        step = 0
        for h in range(heads):
            cols = slice(h * HEAD_DIM, (h + 1) * HEAD_DIM)
            for block, mask in zip(chosen, masks):
                at = blocks.index(block) * rows
                att_ref[at : at + rows, cols] = head_out[step : step + rows] * mask
                step += rows
        d_weights = dot_nt(upstream, values)
        inner = jnp.sum(probs * d_weights, axis=-1, keepdims=True)
        d_scores = (probs * (d_weights - inner) * scale).astype(BF16)
        d_keys_ref[img, :] += dot_tn(d_scores, queries)
        d_values_ref[img, :] += dot_tn(weights, upstream)
    if last:
        hat = hat_ref[...]
        scaled = d_keys_ref[...] * k_gain_ref[...].astype(F32)
        d_raw = inverse_ref[...] * (
            scaled - hat * jnp.mean(hat * scaled, axis=-1, keepdims=True)
        )
        block_ref[:, :HEAD_DIM] = d_raw.astype(BF16)
        block_ref[:, HEAD_DIM:] = d_values_ref[...].astype(BF16)


def attention(scalars, queries, places, count, grad_out, k_gain, state, last):
    rows, width = grad_out.shape[1] // count, grad_out.shape[2]
    image_rows = MB * SLOTS
    vector = jax.ShapeDtypeStruct((image_rows, HEAD_DIM), F32)
    rounded = jax.ShapeDtypeStruct((image_rows, HEAD_DIM), BF16)
    attended = jax.ShapeDtypeStruct((sum(map(len, places)) * rows, width), F32)
    scratch = []
    if last:
        out_shape = [attended, jax.ShapeDtypeStruct((image_rows, 2 * HEAD_DIM), BF16)]
        scratch += [pltpu.VMEM(vector.shape, F32)] * 2
    else:
        token = jax.ShapeDtypeStruct((grad_out.shape[1], HEAD_DIM), F32)
        slot = jax.ShapeDtypeStruct((MB, 8, SLOTS), F32)
        out_shape = [attended, vector, vector, rounded, rounded, vector, vector, token, slot]
    if rows % 16 != 0:
        scratch += [pltpu.VMEM(grad_out.shape[1:], F32)]
    operands = [*queries, grad_out, k_gain, *state]
    return pl.pallas_call(
        functools.partial(attention_kernel, places, count, rows, last, len(queries)),
        in_specs=[whole(pltpu.SMEM)] * len(scalars) + [whole()] * len(operands),
        out_specs=[whole()] * len(out_shape),
        out_shape=out_shape,
        scratch_shapes=scratch,
        compiler_params=params(24),
        cost_estimate=cost(0, 0),
        name="attention_last" if last else "attention_first",
    )(*scalars, *operands)


def assemble_kernel(places, rows, *refs):
    refs, out_ref, held = refs[:-2], refs[-2], refs[-1]
    for group, ref in zip(places, refs):
        for i, p in enumerate(group):
            at = pl.multiple_of(lax.bitwise_xor(here(), p) * rows, rows)
            held[pl.ds(at, rows), :] = ref[i * rows : (i + 1) * rows, :]
    out_ref[0] = held[...].astype(BF16)


def assemble(places, arrays, like):
    rows = arrays[0].shape[0] // len(places[0])
    return pl.pallas_call(
        functools.partial(assemble_kernel, places, rows),
        in_specs=[whole()] * len(arrays),
        out_specs=whole(),
        out_shape=jax.ShapeDtypeStruct(like.shape, BF16),
        scratch_shapes=[pltpu.VMEM(like.shape[1:], F32)],
        compiler_params=params(24),
        cost_estimate=cost(0, 0),
        name="attended_rows",
    )(*arrays)


def grad_kernel(pairs, per_kv, sections, first, last, *refs):
    blocks, weight_ref, refs = refs[: len(pairs)], refs[len(pairs)], refs[len(pairs) + 1 :]
    if not first:
        before_ref, refs = refs[0], refs[1:]
    if per_kv > 1:
        refs, sums = refs[:-1], refs[-1]
        sums[...] = jnp.zeros_like(sums)
    total = refs[-1]
    image_rows, width = total.shape
    heads = []
    for block, pair in zip(blocks, pairs):
        columns = head_columns(lax.div(partner_at(pair), per_kv))
        if per_kv == 1:
            heads.append((columns, block[...]))
        else:
            for half, k in enumerate(columns):
                part = block[:, half * HEAD_DIM : (half + 1) * HEAD_DIM]
                sums[:, k] += part.astype(F32)
    if per_kv > 1:
        heads = [((slice(None),), sums[...].astype(BF16))]
    span = 256
    for c in range(0, width, span):
        cols = slice(c, c + span)
        part = 0.0 if first else before_ref[:, cols]
        for columns, block in heads:
            weight = jnp.concatenate([weight_ref[0, cols, k] for k in columns], axis=1)
            part = part + dot_nt(block, weight)
        total[:, cols] = part
    if last:
        rows = image_rows // sections
        for k in range(sections):
            to = lax.rem(lax.axis_index("section") + k, sections)
            piece = total[pl.ds(pl.multiple_of(to * rows, rows), rows), :]
            refs[k][...] = piece.astype(refs[k].dtype)


def feature_gradient(blocks, weight, per_kv, sections, before=None, last=True):
    pairs, arrays = list(blocks), list(blocks.values())
    image_rows = arrays[0].shape[0]
    width, depth = weight.shape[1:]
    rows = image_rows // sections
    if last:
        out_shape = [
            jax.ShapeDtypeStruct((rows, width), F32 if k == 0 else BF16) for k in range(sections)
        ]
        out_specs = [whole()] * sections
        scratch = [pltpu.VMEM((image_rows, width), F32)]
    else:
        out_shape = jax.ShapeDtypeStruct((image_rows, width), F32)
        out_specs = whole()
        scratch = []
    if per_kv > 1:
        scratch.append(pltpu.VMEM((image_rows, depth), F32))
    operands = [*arrays, weight] + ([] if before is None else [before])
    return pl.pallas_call(
        functools.partial(grad_kernel, pairs, per_kv, sections, before is None, last),
        in_specs=[whole()] * len(operands),
        out_specs=out_specs,
        out_shape=out_shape,
        scratch_shapes=scratch,
        compiler_params=params(24),
        cost_estimate=cost(0, 0),
        name="feature_grad_last" if last else "feature_grad_first",
    )(*operands)


def shards(
    text, features, in_gain, w_query, q_gain, w_key_value, k_gain, tile_count, image_start, grad_out
):
    count = lax.axis_size("tensor")
    sections = lax.axis_size("section")
    per_kv = count // KV_HEADS

    def exchange(x, pair):
        return lax.ppermute(x, "tensor", [(i, i ^ pair[i % 2]) for i in range(count)])

    def swap(x):
        return exchange(x, (1, 1))

    bits = [1 << b for b in range(1, count.bit_length() - 1)]
    steps = len(bits)

    def distance(mask):
        taken = [s for s in range(steps) if mask >> s & 1]
        return sum(bits[s] for s in taken), sum(bits[steps - 1 - s] for s in taken)

    masks = range(1, 1 << steps)

    own_text = text[0]
    width = own_text.shape[1] // 2
    direct = {1 << s: exchange(own_text, distance(1 << s)) for s in range(steps)}

    def both_cores(blocks):
        out = {}
        for pair, x in blocks.items():
            out[pair] = [x]
            out[other_core(pair)] = [swap(x)]
        return out

    def places_of(blocks):
        return sorted(even for even, _ in blocks)

    def queries(blocks, name, **more):
        order = places_of(blocks)
        slots = [(order.index(even), order.index(odd)) for even, odd in blocks]
        groups = list(blocks.values())
        return queries_of(groups, slots, in_gain, w_query, q_gain, name, **more)

    kv_pairs = [distance(mask) for mask in range(1 << steps)]
    other_heads = kv_partial(features, w_key_value, per_kv, [other_core(pair) for pair in kv_pairs])
    other_heads = [swap(x) for x in other_heads]
    own, *outgoing = kv_partial(features, w_key_value, per_kv, kv_pairs, other_heads)
    parts = [own] + [exchange(x, pair) for x, pair in zip(outgoing, kv_pairs[1:])]
    direct, parts = lax.optimization_barrier((direct, parts))
    near = both_cores({(0, 0): own_text})
    q_near = queries(near, "queries_own_chip")
    forwarded = []
    for first in (0, width):
        held = {mask: x[:, first : first + width] for mask, x in direct.items()}
        passed = {}
        for s in range(1, steps):
            for mask in range(1, 1 << s):
                more = mask | 1 << s
                held[more] = passed[distance(more)] = exchange(held[mask], distance(1 << s))
        forwarded.append(passed)

    next_to = both_cores({distance(mask): x for mask, x in direct.items()})
    q_next = queries(next_to, "queries_neighbours")

    early, *state = attention(
        [tile_count, image_start],
        [q_near, q_next],
        [places_of(near), places_of(next_to)],
        count,
        grad_out,
        k_gain,
        parts,
        last=False,
    )
    first_half, state = lax.optimization_barrier((forwarded[0], state))
    far = both_cores(first_half)
    second_half, far = lax.optimization_barrier((forwarded[1], far))
    sums = queries(far, "queries_forwarded_first")
    far = both_cores(second_half)
    q_far = queries(far, "queries_forwarded_last", start=width, before=sums)
    far = places_of(far)
    late, block = attention([], [q_far], [far], count, grad_out, k_gain, state, last=True)
    attended = assemble([places_of(near) + places_of(next_to), far], [early, late], grad_out)

    same_core = {(0, 0): block}
    same_core.update({distance(m): exchange(block, distance(m)) for m in reversed(masks)})
    swapped = {other_core(pair): swap(x) for pair, x in same_core.items()}
    before = None
    blocks = {**same_core, **swapped}
    if per_kv == 1:
        soon = {pair: blocks.pop(pair) for pair in [*same_core, (1, 1)]}
        before = feature_gradient(soon, w_key_value, per_kv, sections, last=False)
    pieces = feature_gradient(blocks, w_key_value, per_kv, sections, before)
    feature_grad, leaving = pieces[0], pieces[1:]
    arrived = []
    for k in range(1, sections):
        perm = [(i, (i + k) % sections) for i in range(sections)]
        arrived.append(lax.ppermute(leaving[k - 1], "section", perm))
    for x in arrived:
        feature_grad = feature_grad + x.astype(F32)
    return (attended, feature_grad)


def solution(mesh):
    return jax.shard_map(
        shards,
        mesh=mesh,
        in_specs=(
            P("section", "tensor", None),
            P(None, "tensor"),
            P("section", None),
            P("section", None, "tensor"),
            P("section", None),
            P("section", "tensor", None),
            P("section", None),
            P(),
            P(),
            P("section", None, "tensor"),
        ),
        out_specs=(P("section", None, "tensor"), P("section", "tensor")),
        check_vma=False,
    )
```

```python
import functools

import jax
import jax.numpy as jnp
from jax import lax
from jax.experimental import pallas as pl
from jax.experimental.pallas import tpu as pltpu
from jax.sharding import PartitionSpec as P

KV_HEADS = 8
HEAD_DIM = 128
TILES = 4
TILE_LEN = 24
TXT_TOK = 128
MB = 2
SLOTS = TILES * TILE_LEN

eps = 1e-05

F32 = jnp.float32
BF16 = jnp.bfloat16
MIB = 1 << 20


def whole(memory=pltpu.VMEM):
    return pl.BlockSpec(memory_space=memory)


def dot_nn(a, b):
    return jnp.dot(a, b, preferred_element_type=F32)


def dot_nt(a, b):
    return lax.dot_general(a, b, (((1,), (1,)), ((), ())), preferred_element_type=F32)


def dot_tn(a, b):
    return lax.dot_general(a, b, (((0,), (0,)), ((), ())), preferred_element_type=F32)


def params(mib):
    return pltpu.CompilerParams(vmem_limit_bytes=mib * MIB)


def cost(flops, size):
    return pl.CostEstimate(flops=flops, bytes_accessed=size, transcendentals=0)


def here():
    return lax.axis_index("tensor")


def of_core(pair):
    even, odd = pair
    return even if even == odd else even + lax.rem(here(), 2) * (odd - even)


def partner_at(pair):
    return lax.bitwise_xor(here(), of_core(pair))


def other_core(pair):
    return (1 ^ pair[1], 1 ^ pair[0])


def head_columns(head):
    return [
        pl.ds(pl.multiple_of((half * KV_HEADS + head) * HEAD_DIM, HEAD_DIM), HEAD_DIM)
        for half in range(2)
    ]


def kv_kernel(per_kv, pairs, feat_ref, weight_ref, *refs):
    features = feat_ref[...]
    for j, pair in enumerate(pairs):
        head = lax.div(partner_at(pair), per_kv)
        weight = jnp.concatenate([weight_ref[0, :, c] for c in head_columns(head)], axis=1)
        total = dot_nn(features, weight)
        out_ref = refs[j - len(pairs)]
        if len(refs) > len(pairs):
            total = total + refs[j][...]
        out_ref[...] = total.astype(out_ref.dtype)


def kv_partial(features, weight, per_kv, pairs, other=()):
    rows = features.shape[0]
    operands = (features, weight, *other)
    out_shape = [
        jax.ShapeDtypeStruct((rows, 2 * HEAD_DIM), BF16 if other and j % 2 else F32)
        for j in range(len(pairs))
    ]
    return pl.pallas_call(
        functools.partial(kv_kernel, per_kv, pairs),
        in_specs=[whole()] * len(operands),
        out_specs=[whole()] * len(pairs),
        out_shape=out_shape,
        compiler_params=params(24),
        cost_estimate=cost(0, 0),
        name="kv_partial_own_core" if other else "kv_partial_other_core",
    )(*operands)


def kv_sum_kernel(*refs):
    size = len(refs) // 3
    for kept_ref, came_ref, out_ref in zip(refs, refs[size:], refs[2 * size :]):
        total = kept_ref[...] + came_ref[...].astype(F32)
        out_ref[...] = total.astype(out_ref.dtype)


def kv_sum(kept, came):
    return pl.pallas_call(
        kv_sum_kernel,
        in_specs=[whole()] * (2 * len(kept)),
        out_specs=[whole()] * len(kept),
        out_shape=[
            jax.ShapeDtypeStruct(x.shape, BF16 if i % 2 else F32) for i, x in enumerate(kept)
        ],
        compiler_params=params(24),
        cost_estimate=cost(0, 0),
        name="kv_sum",
    )(*kept, *came)


def query_kernel(shape, slots, start, *refs):
    gain_ref, weight_ref, q_gain_ref, refs = refs[0], refs[1], refs[2], refs[3:]
    groups = []
    for parts in shape:
        groups.append(refs[:parts])
        refs = refs[parts:]
    depth, heads_width = weight_ref.shape[1:]
    width = sum(part.shape[1] for part in groups[0])
    last = start + width == depth
    span = 1024

    def columns(parts, c):
        for part in parts:
            if c < part.shape[1]:
                return part[:, c : c + span].astype(F32)
            c -= part.shape[1]

    if start:
        raw, squares, refs = refs[0][...], refs[1][:, :1], refs[2:]
    else:
        raw, squares = 0.0, 0.0
    for c in range(0, width, span):
        x = jnp.concatenate([columns(parts, c) for parts in groups], axis=0)
        squares = squares + jnp.sum(x * x, axis=-1, keepdims=True)
        cols = slice(start + c, start + c + span)
        scaled = (x * gain_ref[:, cols].astype(F32)).astype(BF16)
        raw = raw + dot_nn(scaled, weight_ref[0, cols, :])
    if not last:
        refs[0][...] = raw
        refs[1][...] = jnp.broadcast_to(squares, refs[1].shape)
        return
    out_ref = refs[-1]
    rows = groups[0][0].shape[0]
    inverse = lax.rsqrt(squares / depth + eps)
    q_gain = q_gain_ref[...].astype(F32)
    for c in range(0, heads_width, HEAD_DIM):
        head = raw[:, c : c + HEAD_DIM] * inverse
        q_inverse = lax.rsqrt(jnp.mean(head * head, axis=-1, keepdims=True) + eps)
        head = head * q_inverse * q_gain
        for i, pair in enumerate(slots):
            at = of_core(pair) * rows
            if pair[0] != pair[1]:
                at = pl.multiple_of(at, rows)
            part = head[i * rows : (i + 1) * rows]
            out_ref[pl.ds(at, rows), c : c + HEAD_DIM] = part.astype(out_ref.dtype)
    if len(refs) > 1:
        refs[0][...] = out_ref[...].astype(BF16)


def queries_of(groups, slots, gain, weight, q_gain, name, start=0, before=()):
    arrays = [part for parts in groups for part in parts]
    rows = sum(parts[0].shape[0] for parts in groups)
    depth, heads_width = weight.shape[1:]
    last = start + sum(part.shape[1] for part in groups[0]) == depth
    scratch = []
    if last:
        out_shape = [jax.ShapeDtypeStruct((rows, heads_width), BF16)]
        if arrays[0].shape[0] % 16 != 0:
            scratch.append(pltpu.VMEM((rows, heads_width), F32))
    else:
        out_shape = [jax.ShapeDtypeStruct((rows, w), F32) for w in (heads_width, HEAD_DIM)]
    out = pl.pallas_call(
        functools.partial(query_kernel, [len(parts) for parts in groups], slots, start),
        in_specs=[whole()] * (3 + len(arrays) + len(before)),
        out_specs=[whole()] * len(out_shape),
        out_shape=out_shape,
        scratch_shapes=scratch,
        compiler_params=params(24),
        cost_estimate=cost(0, 0),
        name=name,
    )(gain, weight, q_gain, *arrays, *before)
    return out[0] if last else out


def attention_kernel(places, count, rows, last, sizes, *refs):
    if not last:
        count_ref, start_ref, refs = refs[0], refs[1], refs[2:]
    queries_refs, refs = refs[:sizes], refs[sizes:]
    grad_ref, k_gain_ref, refs = refs[0], refs[1], refs[2:]
    narrow = rows % 16 != 0
    if narrow:
        refs, grad_rows = refs[:-1], refs[-1]
        grad_rows[...] = grad_ref[0].astype(F32)
    if last:
        d_keys_in, d_values_in, keys_ref, values_ref, hat_ref, inverse_ref, token_ref, slot_ref = refs[:8]
        att_ref, block_ref, d_keys_ref, d_values_ref = refs[8:]
        d_keys_ref[...] = d_keys_in[...]
        d_values_ref[...] = d_values_in[...]
    else:
        parts = refs[:-9]
        att_ref, d_keys_ref, d_values_ref, keys_ref, values_ref = refs[-9:-4]
        hat_ref, inverse_ref, token_ref, slot_ref = refs[-4:]
        kv = sum(part[...].astype(F32) for part in parts)
        key_raw = kv[:, :HEAD_DIM]
        inverse = lax.rsqrt(jnp.mean(key_raw * key_raw, axis=-1, keepdims=True) + eps)
        hat_ref[...] = key_raw * inverse
        inverse_ref[...] = jnp.broadcast_to(inverse, key_raw.shape)
        keys_ref[...] = (key_raw * inverse * k_gain_ref[...].astype(F32)).astype(BF16)
        values_ref[...] = kv[:, HEAD_DIM:].astype(BF16)
        d_keys_ref[...] = jnp.zeros_like(d_keys_ref)
        d_values_ref[...] = jnp.zeros_like(d_values_ref)
        for b in range(MB):
            token = lax.broadcasted_iota(jnp.int32, (TXT_TOK, HEAD_DIM), 0)
            token_ref[b * TXT_TOK : (b + 1) * TXT_TOK, :] = (token >= start_ref[b]).astype(F32)
            slot = lax.broadcasted_iota(jnp.int32, slot_ref.shape[1:], 1)
            slot_ref[b] = (slot < count_ref[b] * TILE_LEN).astype(F32)

    scale = HEAD_DIM ** (-0.5)
    heads = grad_ref.shape[2] // HEAD_DIM
    per_sample = count // MB
    mine = lax.div(here(), per_sample)
    blocks = [
        (p, ref, i * rows) for group, ref in zip(places, queries_refs) for i, p in enumerate(group)
    ]
    for far in range(MB):
        chosen = [block for block in blocks if block[0] // per_sample == far]
        if not chosen:
            continue
        sample = lax.bitwise_xor(mine, far)
        img = pl.ds(pl.multiple_of(sample * SLOTS, SLOTS), SLOTS)
        keys, values = keys_ref[img, :], values_ref[img, :]
        live = slot_ref[sample][:1, :] > 0
        spots = [
            pl.ds(pl.multiple_of(lax.bitwise_xor(here(), p) * rows, rows), rows)
            for p, _, _ in chosen
        ]
        masks = [token_ref[spot, :] for spot in spots]
        queries, upstream = [], []
        for h in range(heads):
            cols = slice(h * HEAD_DIM, (h + 1) * HEAD_DIM)
            for (p, ref, at), mask, spot in zip(chosen, masks, spots):
                queries.append(ref[at : at + rows, cols])
                grad = grad_rows[spot, cols] if narrow else grad_ref[0, spot, cols].astype(F32)
                upstream.append((grad * mask).astype(BF16))
        queries = jnp.concatenate(queries, axis=0)
        upstream = jnp.concatenate(upstream, axis=0)
        scores = dot_nt(queries, keys) * scale
        exponent = jnp.where(live, jnp.exp(scores), 0.0)
        probs = exponent * (1.0 / jnp.sum(exponent, axis=-1, keepdims=True))
        weights = probs.astype(BF16)
        head_out = dot_nn(weights, values)
        step = 0
        for h in range(heads):
            cols = slice(h * HEAD_DIM, (h + 1) * HEAD_DIM)
            for block, mask in zip(chosen, masks):
                at = blocks.index(block) * rows
                att_ref[at : at + rows, cols] = head_out[step : step + rows] * mask
                step += rows
        d_weights = dot_nt(upstream, values)
        inner = jnp.sum(probs * d_weights, axis=-1, keepdims=True)
        d_scores = (probs * (d_weights - inner) * scale).astype(BF16)
        d_keys_ref[img, :] += dot_tn(d_scores, queries)
        d_values_ref[img, :] += dot_tn(weights, upstream)
    if last:
        hat = hat_ref[...]
        scaled = d_keys_ref[...] * k_gain_ref[...].astype(F32)
        d_raw = inverse_ref[...] * (
            scaled - hat * jnp.mean(hat * scaled, axis=-1, keepdims=True)
        )
        block_ref[:, :HEAD_DIM] = d_raw.astype(BF16)
        block_ref[:, HEAD_DIM:] = d_values_ref[...].astype(BF16)


def attention(scalars, queries, places, count, grad_out, k_gain, state, last):
    rows, width = grad_out.shape[1] // count, grad_out.shape[2]
    image_rows = MB * SLOTS
    vector = jax.ShapeDtypeStruct((image_rows, HEAD_DIM), F32)
    rounded = jax.ShapeDtypeStruct((image_rows, HEAD_DIM), BF16)
    attended = jax.ShapeDtypeStruct((sum(map(len, places)) * rows, width), F32)
    scratch = []
    if last:
        out_shape = [attended, jax.ShapeDtypeStruct((image_rows, 2 * HEAD_DIM), BF16)]
        scratch += [pltpu.VMEM(vector.shape, F32)] * 2
    else:
        token = jax.ShapeDtypeStruct((grad_out.shape[1], HEAD_DIM), F32)
        slot = jax.ShapeDtypeStruct((MB, 8, SLOTS), F32)
        out_shape = [attended, vector, vector, rounded, rounded, vector, vector, token, slot]
    if rows % 16 != 0:
        scratch += [pltpu.VMEM(grad_out.shape[1:], F32)]
    operands = [*queries, grad_out, k_gain, *state]
    return pl.pallas_call(
        functools.partial(attention_kernel, places, count, rows, last, len(queries)),
        in_specs=[whole(pltpu.SMEM)] * len(scalars) + [whole()] * len(operands),
        out_specs=[whole()] * len(out_shape),
        out_shape=out_shape,
        scratch_shapes=scratch,
        compiler_params=params(24),
        cost_estimate=cost(0, 0),
        name="attention_last" if last else "attention_first",
    )(*scalars, *operands)


def assemble_kernel(places, rows, *refs):
    refs, out_ref, held = refs[:-2], refs[-2], refs[-1]
    for group, ref in zip(places, refs):
        for i, p in enumerate(group):
            at = pl.multiple_of(lax.bitwise_xor(here(), p) * rows, rows)
            held[pl.ds(at, rows), :] = ref[i * rows : (i + 1) * rows, :]
    out_ref[0] = held[...].astype(BF16)


def assemble(places, arrays, like):
    rows = arrays[0].shape[0] // len(places[0])
    return pl.pallas_call(
        functools.partial(assemble_kernel, places, rows),
        in_specs=[whole()] * len(arrays),
        out_specs=whole(),
        out_shape=jax.ShapeDtypeStruct(like.shape, BF16),
        scratch_shapes=[pltpu.VMEM(like.shape[1:], F32)],
        compiler_params=params(24),
        cost_estimate=cost(0, 0),
        name="attended_rows",
    )(*arrays)


def grad_kernel(pairs, per_kv, sections, first, last, *refs):
    blocks, weight_ref, refs = refs[: len(pairs)], refs[len(pairs)], refs[len(pairs) + 1 :]
    if not first:
        before_ref, refs = refs[0], refs[1:]
    if per_kv > 1:
        refs, sums = refs[:-1], refs[-1]
        sums[...] = jnp.zeros_like(sums)
    total = refs[-1]
    image_rows, width = total.shape
    heads = []
    for block, pair in zip(blocks, pairs):
        columns = head_columns(lax.div(partner_at(pair), per_kv))
        if per_kv == 1:
            heads.append((columns, block[...]))
        else:
            for half, k in enumerate(columns):
                part = block[:, half * HEAD_DIM : (half + 1) * HEAD_DIM]
                sums[:, k] += part.astype(F32)
    if per_kv > 1:
        heads = [((slice(None),), sums[...].astype(BF16))]
    span = 256
    for c in range(0, width, span):
        cols = slice(c, c + span)
        part = 0.0 if first else before_ref[:, cols]
        for columns, block in heads:
            weight = jnp.concatenate([weight_ref[0, cols, k] for k in columns], axis=1)
            part = part + dot_nt(block, weight)
        total[:, cols] = part
    if last:
        rows = image_rows // sections
        for k in range(sections):
            to = lax.rem(lax.axis_index("section") + k, sections)
            piece = total[pl.ds(pl.multiple_of(to * rows, rows), rows), :]
            refs[k][...] = piece.astype(refs[k].dtype)


def feature_gradient(blocks, weight, per_kv, sections, before=None, last=True):
    pairs, arrays = list(blocks), list(blocks.values())
    image_rows = arrays[0].shape[0]
    width, depth = weight.shape[1:]
    rows = image_rows // sections
    if last:
        out_shape = [
            jax.ShapeDtypeStruct((rows, width), F32 if k == 0 else BF16) for k in range(sections)
        ]
        out_specs = [whole()] * sections
        scratch = [pltpu.VMEM((image_rows, width), F32)]
    else:
        out_shape = jax.ShapeDtypeStruct((image_rows, width), F32)
        out_specs = whole()
        scratch = []
    if per_kv > 1:
        scratch.append(pltpu.VMEM((image_rows, depth), F32))
    operands = [*arrays, weight] + ([] if before is None else [before])
    return pl.pallas_call(
        functools.partial(grad_kernel, pairs, per_kv, sections, before is None, last),
        in_specs=[whole()] * len(operands),
        out_specs=out_specs,
        out_shape=out_shape,
        scratch_shapes=scratch,
        compiler_params=params(24),
        cost_estimate=cost(0, 0),
        name="feature_grad_last" if last else "feature_grad_first",
    )(*operands)


def shards(
    text, features, in_gain, w_query, q_gain, w_key_value, k_gain, tile_count, image_start, grad_out
):
    count = lax.axis_size("tensor")
    sections = lax.axis_size("section")
    per_kv = count // KV_HEADS

    def exchange(x, pair):
        return lax.ppermute(x, "tensor", [(i, i ^ pair[i % 2]) for i in range(count)])

    def swap(x):
        return exchange(x, (1, 1))

    bits = [1 << b for b in range(1, count.bit_length() - 1)]
    steps = len(bits)

    def distance(mask):
        taken = [s for s in range(steps) if mask >> s & 1]
        return sum(bits[s] for s in taken), sum(bits[steps - 1 - s] for s in taken)

    masks = range(1, 1 << steps)

    own_text = text[0]
    width = own_text.shape[1] // 2
    direct = {1 << s: exchange(own_text, distance(1 << s)) for s in range(steps)}

    def both_cores(blocks):
        out = {}
        for pair, x in blocks.items():
            out[pair] = [x]
            out[other_core(pair)] = [swap(x)]
        return out

    def places_of(blocks):
        return sorted(even for even, _ in blocks)

    def queries(blocks, name, **more):
        order = places_of(blocks)
        slots = [(order.index(even), order.index(odd)) for even, odd in blocks]
        groups = list(blocks.values())
        return queries_of(groups, slots, in_gain, w_query, q_gain, name, **more)

    kv_pairs = [distance(mask) for mask in range(1 << steps)]
    other_heads = kv_partial(features, w_key_value, per_kv, [other_core(pair) for pair in kv_pairs])
    other_heads = [swap(x) for x in other_heads]
    sums = kv_partial(features, w_key_value, per_kv, kv_pairs, other_heads)
    for step in range(steps):
        kept, came = sums[::2], [exchange(x, distance(1 << step)) for x in sums[1::2]]
        if step == 0:
            direct, came = lax.optimization_barrier((direct, came))
        if step < steps - 1:
            sums = kv_sum(kept, came)
    parts = [kept[0], came[0]]
    near = both_cores({(0, 0): own_text})
    q_near = queries(near, "queries_own_chip")
    forwarded = []
    for first in (0, width):
        held = {mask: x[:, first : first + width] for mask, x in direct.items()}
        passed = {}
        for s in range(1, steps):
            for mask in range(1, 1 << s):
                more = mask | 1 << s
                held[more] = passed[distance(more)] = exchange(held[mask], distance(1 << s))
        forwarded.append(passed)

    next_to = both_cores({distance(mask): x for mask, x in direct.items()})
    q_next = queries(next_to, "queries_neighbours")

    early, *state = attention(
        [tile_count, image_start],
        [q_near, q_next],
        [places_of(near), places_of(next_to)],
        count,
        grad_out,
        k_gain,
        parts,
        last=False,
    )
    first_half, state = lax.optimization_barrier((forwarded[0], state))
    far = both_cores(first_half)
    second_half, far = lax.optimization_barrier((forwarded[1], far))
    sums = queries(far, "queries_forwarded_first")
    pieces = {pair: jnp.split(x, 2, axis=1) for pair, x in second_half.items()}
    far, rest = [both_cores({pair: x[i] for pair, x in pieces.items()}) for i in range(2)]
    sums = queries(far, "queries_forwarded_second", start=width, before=sums)
    q_far = queries(rest, "queries_forwarded_last", start=3 * width // 2, before=sums)
    far = places_of(far)
    late, block = attention([], [q_far], [far], count, grad_out, k_gain, state, last=True)
    attended = assemble([places_of(near) + places_of(next_to), far], [early, late], grad_out)

    same_core = {(0, 0): block}
    same_core.update({distance(m): exchange(block, distance(m)) for m in reversed(masks)})
    swapped = {other_core(pair): swap(x) for pair, x in same_core.items()}
    before = None
    blocks = {**same_core, **swapped}
    if per_kv == 1:
        soon = {pair: blocks.pop(pair) for pair in [*same_core, (1, 1)]}
        before = feature_gradient(soon, w_key_value, per_kv, sections, last=False)
    pieces = feature_gradient(blocks, w_key_value, per_kv, sections, before)
    feature_grad, leaving = pieces[0], pieces[1:]
    arrived = []
    for k in range(1, sections):
        perm = [(i, (i + k) % sections) for i in range(sections)]
        arrived.append(lax.ppermute(leaving[k - 1], "section", perm))
    for x in arrived:
        feature_grad = feature_grad + x.astype(F32)
    return (attended, feature_grad)


def solution(mesh):
    return jax.shard_map(
        shards,
        mesh=mesh,
        in_specs=(
            P("section", "tensor", None),
            P(None, "tensor"),
            P("section", None),
            P("section", None, "tensor"),
            P("section", None),
            P("section", "tensor", None),
            P("section", None),
            P(),
            P(),
            P("section", None, "tensor"),
        ),
        out_specs=(P("section", None, "tensor"), P("section", "tensor")),
        check_vma=False,
    )
```

```python
import functools

import jax
import jax.numpy as jnp
from jax import lax
from jax.experimental import pallas as pl
from jax.experimental.pallas import tpu as pltpu
from jax.sharding import PartitionSpec as P

KV_HEADS = 8
HEAD_DIM = 128
TILES = 4
TILE_LEN = 24
TXT_TOK = 128
MB = 2
SLOTS = TILES * TILE_LEN

eps = 1e-05

F32 = jnp.float32
BF16 = jnp.bfloat16
MIB = 1 << 20


def whole(memory=pltpu.VMEM):
    return pl.BlockSpec(memory_space=memory)


def dot_nn(a, b):
    return jnp.dot(a, b, preferred_element_type=F32)


def dot_nt(a, b):
    return lax.dot_general(a, b, (((1,), (1,)), ((), ())), preferred_element_type=F32)


def dot_tn(a, b):
    return lax.dot_general(a, b, (((0,), (0,)), ((), ())), preferred_element_type=F32)


def params(mib):
    return pltpu.CompilerParams(vmem_limit_bytes=mib * MIB)


def cost(flops, size):
    return pl.CostEstimate(flops=flops, bytes_accessed=size, transcendentals=0)


def here():
    return lax.axis_index("tensor")


def of_core(pair):
    even, odd = pair
    return even if even == odd else even + lax.rem(here(), 2) * (odd - even)


def partner_at(pair):
    return lax.bitwise_xor(here(), of_core(pair))


def other_core(pair):
    return (1 ^ pair[1], 1 ^ pair[0])


def head_columns(head):
    return [
        pl.ds(pl.multiple_of((half * KV_HEADS + head) * HEAD_DIM, HEAD_DIM), HEAD_DIM)
        for half in range(2)
    ]


def kv_kernel(per_kv, pairs, feat_ref, weight_ref, *refs):
    features = feat_ref[...]
    for j, pair in enumerate(pairs):
        head = lax.div(partner_at(pair), per_kv)
        weight = jnp.concatenate([weight_ref[0, :, c] for c in head_columns(head)], axis=1)
        total = dot_nn(features, weight)
        out_ref = refs[j - len(pairs)]
        if len(refs) > len(pairs):
            total = total + refs[j][...]
        out_ref[...] = total.astype(out_ref.dtype)


def kv_partial(features, weight, per_kv, pairs, other=()):
    rows = features.shape[0]
    operands = (features, weight, *other)
    out_shape = [
        jax.ShapeDtypeStruct((rows, 2 * HEAD_DIM), BF16 if other and j % 2 else F32)
        for j in range(len(pairs))
    ]
    return pl.pallas_call(
        functools.partial(kv_kernel, per_kv, pairs),
        in_specs=[whole()] * len(operands),
        out_specs=[whole()] * len(pairs),
        out_shape=out_shape,
        compiler_params=params(24),
        cost_estimate=cost(0, 0),
        name="kv_partial_own_core" if other else "kv_partial_other_core",
    )(*operands)


def kv_sum_kernel(*refs):
    size = len(refs) // 3
    for kept_ref, came_ref, out_ref in zip(refs, refs[size:], refs[2 * size :]):
        total = kept_ref[...] + came_ref[...].astype(F32)
        out_ref[...] = total.astype(out_ref.dtype)


def kv_sum(kept, came):
    return pl.pallas_call(
        kv_sum_kernel,
        in_specs=[whole()] * (2 * len(kept)),
        out_specs=[whole()] * len(kept),
        out_shape=[
            jax.ShapeDtypeStruct(x.shape, BF16 if i % 2 else F32) for i, x in enumerate(kept)
        ],
        compiler_params=params(24),
        cost_estimate=cost(0, 0),
        name="kv_sum",
    )(*kept, *came)


def query_kernel(shape, slots, start, *refs):
    gain_ref, weight_ref, q_gain_ref, refs = refs[0], refs[1], refs[2], refs[3:]
    groups = []
    for parts in shape:
        groups.append(refs[:parts])
        refs = refs[parts:]
    depth, heads_width = weight_ref.shape[1:]
    width = sum(part.shape[1] for part in groups[0])
    last = start + width == depth
    span = 1024

    def columns(parts, c):
        for part in parts:
            if c < part.shape[1]:
                return part[:, c : c + span].astype(F32)
            c -= part.shape[1]

    if start:
        raw, squares, refs = refs[0][...], refs[1][:, :1], refs[2:]
    else:
        raw, squares = 0.0, 0.0
    for c in range(0, width, span):
        x = jnp.concatenate([columns(parts, c) for parts in groups], axis=0)
        squares = squares + jnp.sum(x * x, axis=-1, keepdims=True)
        cols = slice(start + c, start + c + span)
        scaled = (x * gain_ref[:, cols].astype(F32)).astype(BF16)
        raw = raw + dot_nn(scaled, weight_ref[0, cols, :])
    if not last:
        refs[0][...] = raw
        refs[1][...] = jnp.broadcast_to(squares, refs[1].shape)
        return
    out_ref = refs[-1]
    rows = groups[0][0].shape[0]
    inverse = lax.rsqrt(squares / depth + eps)
    q_gain = q_gain_ref[...].astype(F32)
    for c in range(0, heads_width, HEAD_DIM):
        head = raw[:, c : c + HEAD_DIM] * inverse
        q_inverse = lax.rsqrt(jnp.mean(head * head, axis=-1, keepdims=True) + eps)
        head = head * q_inverse * q_gain
        for i, pair in enumerate(slots):
            at = of_core(pair) * rows
            if pair[0] != pair[1]:
                at = pl.multiple_of(at, rows)
            part = head[i * rows : (i + 1) * rows]
            out_ref[pl.ds(at, rows), c : c + HEAD_DIM] = part.astype(out_ref.dtype)
    if len(refs) > 1:
        refs[0][...] = out_ref[...].astype(BF16)


def queries_of(groups, slots, gain, weight, q_gain, name, start=0, before=()):
    arrays = [part for parts in groups for part in parts]
    rows = sum(parts[0].shape[0] for parts in groups)
    depth, heads_width = weight.shape[1:]
    last = start + sum(part.shape[1] for part in groups[0]) == depth
    scratch = []
    if last:
        out_shape = [jax.ShapeDtypeStruct((rows, heads_width), BF16)]
        if arrays[0].shape[0] % 16 != 0:
            scratch.append(pltpu.VMEM((rows, heads_width), F32))
    else:
        out_shape = [jax.ShapeDtypeStruct((rows, w), F32) for w in (heads_width, HEAD_DIM)]
    out = pl.pallas_call(
        functools.partial(query_kernel, [len(parts) for parts in groups], slots, start),
        in_specs=[whole()] * (3 + len(arrays) + len(before)),
        out_specs=[whole()] * len(out_shape),
        out_shape=out_shape,
        scratch_shapes=scratch,
        compiler_params=params(24),
        cost_estimate=cost(0, 0),
        name=name,
    )(gain, weight, q_gain, *arrays, *before)
    return out[0] if last else out


def mask_kernel(count_ref, start_ref, token_ref, slot_ref):
    for b in range(MB):
        token = lax.broadcasted_iota(jnp.int32, (TXT_TOK, HEAD_DIM), 0)
        token_ref[b * TXT_TOK : (b + 1) * TXT_TOK, :] = (token >= start_ref[b]).astype(F32)
        slot = lax.broadcasted_iota(jnp.int32, slot_ref.shape[1:], 1)
        slot_ref[b] = (slot < count_ref[b] * TILE_LEN).astype(F32)


def live_masks(tile_count, image_start):
    return pl.pallas_call(
        mask_kernel,
        in_specs=[whole(pltpu.SMEM)] * 2,
        out_specs=[whole()] * 2,
        out_shape=[
            jax.ShapeDtypeStruct((MB * TXT_TOK, HEAD_DIM), F32),
            jax.ShapeDtypeStruct((MB, 8, SLOTS), F32),
        ],
        cost_estimate=cost(0, 0),
        name="live_masks",
    )(tile_count, image_start)


def attention_kernel(places, count, rows, last, sizes, *refs):
    token_ref, slot_ref, refs = refs[0], refs[1], refs[2:]
    queries_refs, refs = refs[:sizes], refs[sizes:]
    grad_ref, k_gain_ref, refs = refs[0], refs[1], refs[2:]
    narrow = rows % 16 != 0
    if narrow:
        refs, grad_rows = refs[:-1], refs[-1]
        grad_rows[...] = grad_ref[0].astype(F32)
    if last:
        d_keys_in, d_values_in, keys_ref, values_ref, hat_ref, inverse_ref = refs[:6]
        att_ref, block_ref, d_keys_ref, d_values_ref = refs[6:]
        d_keys_ref[...] = d_keys_in[...]
        d_values_ref[...] = d_values_in[...]
    else:
        parts = refs[:-7]
        att_ref, d_keys_ref, d_values_ref, keys_ref, values_ref, hat_ref, inverse_ref = refs[-7:]
        kv = sum(part[...].astype(F32) for part in parts)
        key_raw = kv[:, :HEAD_DIM]
        inverse = lax.rsqrt(jnp.mean(key_raw * key_raw, axis=-1, keepdims=True) + eps)
        hat_ref[...] = key_raw * inverse
        inverse_ref[...] = jnp.broadcast_to(inverse, key_raw.shape)
        keys_ref[...] = (key_raw * inverse * k_gain_ref[...].astype(F32)).astype(BF16)
        values_ref[...] = kv[:, HEAD_DIM:].astype(BF16)
        d_keys_ref[...] = jnp.zeros_like(d_keys_ref)
        d_values_ref[...] = jnp.zeros_like(d_values_ref)

    scale = HEAD_DIM ** (-0.5)
    heads = grad_ref.shape[2] // HEAD_DIM
    per_sample = count // MB
    mine = lax.div(here(), per_sample)
    blocks = [
        (p, ref, i * rows) for group, ref in zip(places, queries_refs) for i, p in enumerate(group)
    ]
    for far in range(MB):
        chosen = [block for block in blocks if block[0] // per_sample == far]
        if not chosen:
            continue
        sample = lax.bitwise_xor(mine, far)
        img = pl.ds(pl.multiple_of(sample * SLOTS, SLOTS), SLOTS)
        keys, values = keys_ref[img, :], values_ref[img, :]
        live = slot_ref[sample][:1, :] > 0
        spots = [
            pl.ds(pl.multiple_of(lax.bitwise_xor(here(), p) * rows, rows), rows)
            for p, _, _ in chosen
        ]
        masks = [token_ref[spot, :] for spot in spots]
        queries, upstream = [], []
        for h in range(heads):
            cols = slice(h * HEAD_DIM, (h + 1) * HEAD_DIM)
            for (p, ref, at), mask, spot in zip(chosen, masks, spots):
                queries.append(ref[at : at + rows, cols])
                grad = grad_rows[spot, cols] if narrow else grad_ref[0, spot, cols].astype(F32)
                upstream.append((grad * mask).astype(BF16))
        queries = jnp.concatenate(queries, axis=0)
        upstream = jnp.concatenate(upstream, axis=0)
        scores = dot_nt(queries, keys) * scale
        exponent = jnp.where(live, jnp.exp(scores), 0.0)
        probs = exponent * (1.0 / jnp.sum(exponent, axis=-1, keepdims=True))
        weights = probs.astype(BF16)
        head_out = dot_nn(weights, values)
        step = 0
        for h in range(heads):
            cols = slice(h * HEAD_DIM, (h + 1) * HEAD_DIM)
            for block, mask in zip(chosen, masks):
                at = blocks.index(block) * rows
                att_ref[at : at + rows, cols] = head_out[step : step + rows] * mask
                step += rows
        d_weights = dot_nt(upstream, values)
        inner = jnp.sum(probs * d_weights, axis=-1, keepdims=True)
        d_scores = (probs * (d_weights - inner) * scale).astype(BF16)
        d_keys_ref[img, :] += dot_tn(d_scores, queries)
        d_values_ref[img, :] += dot_tn(weights, upstream)
    if last:
        hat = hat_ref[...]
        scaled = d_keys_ref[...] * k_gain_ref[...].astype(F32)
        d_raw = inverse_ref[...] * (
            scaled - hat * jnp.mean(hat * scaled, axis=-1, keepdims=True)
        )
        block_ref[:, :HEAD_DIM] = d_raw.astype(BF16)
        block_ref[:, HEAD_DIM:] = d_values_ref[...].astype(BF16)


def attention(masks, queries, places, count, grad_out, k_gain, state, last):
    rows, width = grad_out.shape[1] // count, grad_out.shape[2]
    image_rows = MB * SLOTS
    vector = jax.ShapeDtypeStruct((image_rows, HEAD_DIM), F32)
    rounded = jax.ShapeDtypeStruct((image_rows, HEAD_DIM), BF16)
    attended = jax.ShapeDtypeStruct((sum(map(len, places)) * rows, width), F32)
    scratch = []
    if last:
        out_shape = [attended, jax.ShapeDtypeStruct((image_rows, 2 * HEAD_DIM), BF16)]
        scratch += [pltpu.VMEM(vector.shape, F32)] * 2
    else:
        out_shape = [attended, vector, vector, rounded, rounded, vector, vector]
    if rows % 16 != 0:
        scratch += [pltpu.VMEM(grad_out.shape[1:], F32)]
    operands = [*queries, grad_out, k_gain, *state]
    return pl.pallas_call(
        functools.partial(attention_kernel, places, count, rows, last, len(queries)),
        in_specs=[whole()] * (2 + len(operands)),
        out_specs=[whole()] * len(out_shape),
        out_shape=out_shape,
        scratch_shapes=scratch,
        compiler_params=params(24),
        cost_estimate=cost(0, 0),
        name="attention_last" if last else "attention_first",
    )(*masks, *operands)


def assemble_kernel(places, rows, *refs):
    refs, out_ref, held = refs[:-2], refs[-2], refs[-1]
    for group, ref in zip(places, refs):
        for i, p in enumerate(group):
            at = pl.multiple_of(lax.bitwise_xor(here(), p) * rows, rows)
            held[pl.ds(at, rows), :] = ref[i * rows : (i + 1) * rows, :]
    out_ref[0] = held[...].astype(BF16)


def assemble(places, arrays, like):
    rows = arrays[0].shape[0] // len(places[0])
    return pl.pallas_call(
        functools.partial(assemble_kernel, places, rows),
        in_specs=[whole()] * len(arrays),
        out_specs=whole(),
        out_shape=jax.ShapeDtypeStruct(like.shape, BF16),
        scratch_shapes=[pltpu.VMEM(like.shape[1:], F32)],
        compiler_params=params(24),
        cost_estimate=cost(0, 0),
        name="attended_rows",
    )(*arrays)


def grad_kernel(pairs, per_kv, sections, first, last, *refs):
    blocks, weight_ref, refs = refs[: len(pairs)], refs[len(pairs)], refs[len(pairs) + 1 :]
    if not first:
        before_ref, refs = refs[0], refs[1:]
    if per_kv > 1:
        refs, sums = refs[:-1], refs[-1]
        sums[...] = jnp.zeros_like(sums)
    total = refs[-1]
    image_rows, width = total.shape
    heads = []
    for block, pair in zip(blocks, pairs):
        columns = head_columns(lax.div(partner_at(pair), per_kv))
        if per_kv == 1:
            heads.append((columns, block[...]))
        else:
            for half, k in enumerate(columns):
                part = block[:, half * HEAD_DIM : (half + 1) * HEAD_DIM]
                sums[:, k] += part.astype(F32)
    if per_kv > 1:
        heads = [((slice(None),), sums[...].astype(BF16))]
    span = 256
    for c in range(0, width, span):
        cols = slice(c, c + span)
        part = 0.0 if first else before_ref[:, cols]
        for columns, block in heads:
            weight = jnp.concatenate([weight_ref[0, cols, k] for k in columns], axis=1)
            part = part + dot_nt(block, weight)
        total[:, cols] = part
    if last:
        rows = image_rows // sections
        for k in range(sections):
            to = lax.rem(lax.axis_index("section") + k, sections)
            piece = total[pl.ds(pl.multiple_of(to * rows, rows), rows), :]
            refs[k][...] = piece.astype(refs[k].dtype)


def feature_gradient(blocks, weight, per_kv, sections, before=None, last=True):
    pairs, arrays = list(blocks), list(blocks.values())
    image_rows = arrays[0].shape[0]
    width, depth = weight.shape[1:]
    rows = image_rows // sections
    if last:
        out_shape = [
            jax.ShapeDtypeStruct((rows, width), F32 if k == 0 else BF16) for k in range(sections)
        ]
        out_specs = [whole()] * sections
        scratch = [pltpu.VMEM((image_rows, width), F32)]
    else:
        out_shape = jax.ShapeDtypeStruct((image_rows, width), F32)
        out_specs = whole()
        scratch = []
    if per_kv > 1:
        scratch.append(pltpu.VMEM((image_rows, depth), F32))
    operands = [*arrays, weight] + ([] if before is None else [before])
    return pl.pallas_call(
        functools.partial(grad_kernel, pairs, per_kv, sections, before is None, last),
        in_specs=[whole()] * len(operands),
        out_specs=out_specs,
        out_shape=out_shape,
        scratch_shapes=scratch,
        compiler_params=params(24),
        cost_estimate=cost(0, 0),
        name="feature_grad_last" if last else "feature_grad_first",
    )(*operands)


def shards(
    text, features, in_gain, w_query, q_gain, w_key_value, k_gain, tile_count, image_start, grad_out
):
    count = lax.axis_size("tensor")
    sections = lax.axis_size("section")
    per_kv = count // KV_HEADS

    def exchange(x, pair):
        return lax.ppermute(x, "tensor", [(i, i ^ pair[i % 2]) for i in range(count)])

    def swap(x):
        return exchange(x, (1, 1))

    bits = [1 << b for b in range(1, count.bit_length() - 1)]
    steps = len(bits)

    def distance(mask):
        taken = [s for s in range(steps) if mask >> s & 1]
        return sum(bits[s] for s in taken), sum(bits[steps - 1 - s] for s in taken)

    own_text = text[0]
    width = own_text.shape[1] // 2
    direct = {1 << s: exchange(own_text, distance(1 << s)) for s in range(steps)}

    def both_cores(blocks):
        out = {}
        for pair, x in blocks.items():
            out[pair] = [x]
            out[other_core(pair)] = [swap(x)]
        return out

    def places_of(blocks):
        return sorted(even for even, _ in blocks)

    def queries(blocks, name, **more):
        order = places_of(blocks)
        slots = [(order.index(even), order.index(odd)) for even, odd in blocks]
        groups = list(blocks.values())
        return queries_of(groups, slots, in_gain, w_query, q_gain, name, **more)

    kv_pairs = [distance(mask) for mask in range(1 << steps)]
    other_heads = kv_partial(features, w_key_value, per_kv, [other_core(pair) for pair in kv_pairs])
    other_heads = [swap(x) for x in other_heads]
    sums = kv_partial(features, w_key_value, per_kv, kv_pairs, other_heads)
    for step in range(steps):
        kept, came = sums[::2], [exchange(x, distance(1 << step)) for x in sums[1::2]]
        if step == 0:
            masks = live_masks(tile_count, image_start)
            direct, came, masks = lax.optimization_barrier((direct, came, masks))
        if step < steps - 1:
            sums = kv_sum(kept, came)
    parts = [kept[0], came[0]]
    near = both_cores({(0, 0): own_text})
    q_near = queries(near, "queries_own_chip")
    forwarded = []
    for first in (0, width):
        held = {mask: x[:, first : first + width] for mask, x in direct.items()}
        passed = {}
        for s in range(1, steps):
            for mask in range(1, 1 << s):
                more = mask | 1 << s
                held[more] = passed[distance(more)] = exchange(held[mask], distance(1 << s))
        forwarded.append(passed)

    next_to = both_cores({distance(mask): x for mask, x in direct.items()})
    q_next = queries(next_to, "queries_neighbours")

    early, *state = attention(
        masks,
        [q_near, q_next],
        [places_of(near), places_of(next_to)],
        count,
        grad_out,
        k_gain,
        parts,
        last=False,
    )
    first_half, state = lax.optimization_barrier((forwarded[0], state))
    far = both_cores(first_half)
    second_half, far = lax.optimization_barrier((forwarded[1], far))
    sums = queries(far, "queries_forwarded_first")
    pieces = {pair: jnp.split(x, 2, axis=1) for pair, x in second_half.items()}
    far, rest = [both_cores({pair: x[i] for pair, x in pieces.items()}) for i in range(2)]
    sums = queries(far, "queries_forwarded_second", start=width, before=sums)
    q_far = queries(rest, "queries_forwarded_last", start=3 * width // 2, before=sums)
    far = places_of(far)
    late, block = attention(masks, [q_far], [far], count, grad_out, k_gain, state, last=True)
    attended = assemble([places_of(near) + places_of(next_to), far], [early, late], grad_out)

    held = {0: block}
    held.update({1 << step: exchange(block, distance(1 << step)) for step in range(steps)})
    single = list(held)
    for step in range(1, steps):
        for mask in range(1, 1 << step):
            held[mask | 1 << step] = exchange(held[mask], distance(1 << step))
    soon = {distance(mask): held[mask] for mask in single}
    blocks = {distance(mask): x for mask, x in held.items() if mask not in single}
    soon.update({other_core(pair): swap(x) for pair, x in soon.items()})
    before = None
    if per_kv == 1:
        before = feature_gradient(soon, w_key_value, per_kv, sections, last=False)
    blocks.update({other_core(pair): swap(x) for pair, x in blocks.items()})
    if per_kv > 1:
        blocks.update(soon)
    pieces = feature_gradient(blocks, w_key_value, per_kv, sections, before)
    feature_grad, leaving = pieces[0], pieces[1:]
    arrived = []
    for k in range(1, sections):
        perm = [(i, (i + k) % sections) for i in range(sections)]
        arrived.append(lax.ppermute(leaving[k - 1], "section", perm))
    for x in arrived:
        feature_grad = feature_grad + x.astype(F32)
    return (attended, feature_grad)


def solution(mesh):
    return jax.shard_map(
        shards,
        mesh=mesh,
        in_specs=(
            P("section", "tensor", None),
            P(None, "tensor"),
            P("section", None),
            P("section", None, "tensor"),
            P("section", None),
            P("section", "tensor", None),
            P("section", None),
            P(),
            P(),
            P("section", None, "tensor"),
        ),
        out_specs=(P("section", None, "tensor"), P("section", "tensor")),
        check_vma=False,
    )
```

```python
import functools

import jax
import jax.numpy as jnp
from jax import lax
from jax.experimental import pallas as pl
from jax.experimental.pallas import tpu as pltpu
from jax.sharding import PartitionSpec as P

KV_HEADS = 8
HEAD_DIM = 128
TILES = 4
TILE_LEN = 24
TXT_TOK = 128
MB = 2
SLOTS = TILES * TILE_LEN

eps = 1e-05

F32 = jnp.float32
BF16 = jnp.bfloat16
MIB = 1 << 20


def whole(memory=pltpu.VMEM):
    return pl.BlockSpec(memory_space=memory)


def dot_nn(a, b):
    return jnp.dot(a, b, preferred_element_type=F32)


def dot_nt(a, b):
    return lax.dot_general(a, b, (((1,), (1,)), ((), ())), preferred_element_type=F32)


def dot_tn(a, b):
    return lax.dot_general(a, b, (((0,), (0,)), ((), ())), preferred_element_type=F32)


def params(mib):
    return pltpu.CompilerParams(vmem_limit_bytes=mib * MIB)


def cost(flops, size):
    return pl.CostEstimate(flops=flops, bytes_accessed=size, transcendentals=0)


def here():
    return lax.axis_index("tensor")


def of_core(pair):
    even, odd = pair
    return even if even == odd else even + lax.rem(here(), 2) * (odd - even)


def partner_at(pair):
    return lax.bitwise_xor(here(), of_core(pair))


def other_core(pair):
    return (1 ^ pair[1], 1 ^ pair[0])


def head_columns(head):
    return [
        pl.ds(pl.multiple_of((half * KV_HEADS + head) * HEAD_DIM, HEAD_DIM), HEAD_DIM)
        for half in range(2)
    ]


def kv_kernel(per_kv, pairs, feat_ref, weight_ref, *refs):
    features = feat_ref[...]
    for j, pair in enumerate(pairs):
        head = lax.div(partner_at(pair), per_kv)
        weight = jnp.concatenate([weight_ref[0, :, c] for c in head_columns(head)], axis=1)
        total = dot_nn(features, weight)
        out_ref = refs[j - len(pairs)]
        if len(refs) > len(pairs):
            total = total + refs[j][...]
        out_ref[...] = total.astype(out_ref.dtype)


def kv_partial(features, weight, per_kv, pairs, other=()):
    operands = (features, weight, *other)
    shape = (features.shape[0], 2 * HEAD_DIM)
    return pl.pallas_call(
        functools.partial(kv_kernel, per_kv, pairs),
        in_specs=[whole()] * len(operands),
        out_specs=[whole()] * len(pairs),
        out_shape=[
            jax.ShapeDtypeStruct(shape, BF16 if other and j % 2 else F32)
            for j in range(len(pairs))
        ],
        compiler_params=params(24),
        cost_estimate=cost(0, 0),
        name="kv_partial_own_core" if other else "kv_partial_other_core",
    )(*operands)


def kv_sum_kernel(*refs):
    size = len(refs) // 3
    for kept_ref, came_ref, out_ref in zip(refs, refs[size:], refs[2 * size :]):
        total = kept_ref[...] + came_ref[...].astype(F32)
        out_ref[...] = total.astype(out_ref.dtype)


def kv_sum(kept, came):
    return pl.pallas_call(
        kv_sum_kernel,
        in_specs=[whole()] * (2 * len(kept)),
        out_specs=[whole()] * len(kept),
        out_shape=[
            jax.ShapeDtypeStruct(x.shape, BF16 if i % 2 else F32) for i, x in enumerate(kept)
        ],
        compiler_params=params(24),
        cost_estimate=cost(0, 0),
        name="kv_sum",
    )(*kept, *came)


def live_masks(count_ref, start_ref, token_ref, slot_ref):
    for b in range(MB):
        token = lax.broadcasted_iota(jnp.int32, (TXT_TOK, HEAD_DIM), 0)
        token_ref[b * TXT_TOK : (b + 1) * TXT_TOK, :] = (token >= start_ref[b]).astype(F32)
        slot = lax.broadcasted_iota(jnp.int32, slot_ref.shape[1:], 1)
        slot_ref[b] = (slot < count_ref[b] * TILE_LEN).astype(F32)


def query_kernel(shape, slots, start, scalars, scratch, *refs):
    if scalars:
        end = len(refs) - scratch
        live_masks(refs[0], refs[1], refs[end - 2], refs[end - 1])
        refs = refs[2 : end - 2] + refs[end:]
    gain_ref, weight_ref, q_gain_ref, refs = refs[0], refs[1], refs[2], refs[3:]
    groups = []
    for parts in shape:
        groups.append(refs[:parts])
        refs = refs[parts:]
    depth, heads_width = weight_ref.shape[1:]
    width = sum(part.shape[1] for part in groups[0])
    last = start + width == depth
    span = 1024

    def columns(parts, c):
        for part in parts:
            if c < part.shape[1]:
                return part[:, c : c + span].astype(F32)
            c -= part.shape[1]

    if start:
        raw, squares, refs = refs[0][...], refs[1][:, :1], refs[2:]
    else:
        raw, squares = 0.0, 0.0
    for c in range(0, width, span):
        x = jnp.concatenate([columns(parts, c) for parts in groups], axis=0)
        squares = squares + jnp.sum(x * x, axis=-1, keepdims=True)
        cols = slice(start + c, start + c + span)
        scaled = (x * gain_ref[:, cols].astype(F32)).astype(BF16)
        raw = raw + dot_nn(scaled, weight_ref[0, cols, :])
    if not last:
        refs[0][...] = raw
        refs[1][...] = jnp.broadcast_to(squares, refs[1].shape)
        return
    out_ref = refs[-1]
    rows = groups[0][0].shape[0]
    inverse = lax.rsqrt(squares / depth + eps)
    q_gain = q_gain_ref[...].astype(F32)
    for c in range(0, heads_width, HEAD_DIM):
        head = raw[:, c : c + HEAD_DIM] * inverse
        q_inverse = lax.rsqrt(jnp.mean(head * head, axis=-1, keepdims=True) + eps)
        head = head * q_inverse * q_gain
        for i, pair in enumerate(slots):
            at = of_core(pair) * rows
            if pair[0] != pair[1]:
                at = pl.multiple_of(at, rows)
            part = head[i * rows : (i + 1) * rows]
            out_ref[pl.ds(at, rows), c : c + HEAD_DIM] = part.astype(out_ref.dtype)
    if len(refs) > 1:
        refs[0][...] = out_ref[...].astype(BF16)


def queries_of(groups, slots, gain, weight, q_gain, name, start=0, before=(), scalars=()):
    arrays = [part for parts in groups for part in parts]
    rows = sum(parts[0].shape[0] for parts in groups)
    depth, heads_width = weight.shape[1:]
    last = start + sum(part.shape[1] for part in groups[0]) == depth
    scratch = []
    if last:
        out_shape = [jax.ShapeDtypeStruct((rows, heads_width), BF16)]
        if arrays[0].shape[0] % 16 != 0:
            scratch.append(pltpu.VMEM((rows, heads_width), F32))
        if scalars:
            out_shape.append(jax.ShapeDtypeStruct((MB * TXT_TOK, HEAD_DIM), F32))
            out_shape.append(jax.ShapeDtypeStruct((MB, 8, SLOTS), F32))
    else:
        out_shape = [jax.ShapeDtypeStruct((rows, w), F32) for w in (heads_width, HEAD_DIM)]
    out = pl.pallas_call(
        functools.partial(
            query_kernel,
            [len(parts) for parts in groups],
            slots,
            start,
            len(scalars),
            len(scratch),
        ),
        in_specs=[whole(pltpu.SMEM)] * len(scalars)
        + [whole()] * (3 + len(arrays) + len(before)),
        out_specs=[whole()] * len(out_shape),
        out_shape=out_shape,
        scratch_shapes=scratch,
        compiler_params=params(24),
        cost_estimate=cost(0, 0),
        name=name,
    )(*scalars, gain, weight, q_gain, *arrays, *before)
    return out[0] if last and not scalars else out


def attention_kernel(places, count, rows, last, sizes, *refs):
    token_ref, slot_ref, refs = refs[0], refs[1], refs[2:]
    queries_refs, refs = refs[:sizes], refs[sizes:]
    grad_ref, k_gain_ref, refs = refs[0], refs[1], refs[2:]
    narrow = rows % 16 != 0
    if narrow:
        refs, grad_rows = refs[:-1], refs[-1]
        grad_rows[...] = grad_ref[0].astype(F32)
    if last:
        d_keys_in, d_values_in, keys_ref, values_ref, hat_ref, inverse_ref = refs[:6]
        att_ref, block_ref, d_keys_ref, d_values_ref = refs[6:]
        d_keys_ref[...] = d_keys_in[...]
        d_values_ref[...] = d_values_in[...]
    else:
        parts = refs[:-7]
        att_ref, d_keys_ref, d_values_ref, keys_ref, values_ref, hat_ref, inverse_ref = refs[-7:]
        kv = sum(part[...].astype(F32) for part in parts)
        key_raw = kv[:, :HEAD_DIM]
        inverse = lax.rsqrt(jnp.mean(key_raw * key_raw, axis=-1, keepdims=True) + eps)
        hat_ref[...] = key_raw * inverse
        inverse_ref[...] = jnp.broadcast_to(inverse, key_raw.shape)
        keys_ref[...] = (key_raw * inverse * k_gain_ref[...].astype(F32)).astype(BF16)
        values_ref[...] = kv[:, HEAD_DIM:].astype(BF16)
        d_keys_ref[...] = jnp.zeros_like(d_keys_ref)
        d_values_ref[...] = jnp.zeros_like(d_values_ref)

    scale = HEAD_DIM ** (-0.5)
    heads = grad_ref.shape[2] // HEAD_DIM
    per_sample = count // MB
    mine = lax.div(here(), per_sample)
    blocks = [
        (p, ref, i * rows) for group, ref in zip(places, queries_refs) for i, p in enumerate(group)
    ]
    for far in range(MB):
        chosen = [block for block in blocks if block[0] // per_sample == far]
        if not chosen:
            continue
        sample = lax.bitwise_xor(mine, far)
        img = pl.ds(pl.multiple_of(sample * SLOTS, SLOTS), SLOTS)
        keys, values = keys_ref[img, :], values_ref[img, :]
        live = slot_ref[sample][:1, :] > 0
        spots = [
            pl.ds(pl.multiple_of(lax.bitwise_xor(here(), p) * rows, rows), rows)
            for p, _, _ in chosen
        ]
        masks = [token_ref[spot, :] for spot in spots]
        queries, upstream = [], []
        for h in range(heads):
            cols = slice(h * HEAD_DIM, (h + 1) * HEAD_DIM)
            for (p, ref, at), mask, spot in zip(chosen, masks, spots):
                queries.append(ref[at : at + rows, cols])
                grad = grad_rows[spot, cols] if narrow else grad_ref[0, spot, cols].astype(F32)
                upstream.append((grad * mask).astype(BF16))
        queries = jnp.concatenate(queries, axis=0)
        upstream = jnp.concatenate(upstream, axis=0)
        scores = dot_nt(queries, keys) * scale
        exponent = jnp.where(live, jnp.exp(scores), 0.0)
        probs = exponent * (1.0 / jnp.sum(exponent, axis=-1, keepdims=True))
        weights = probs.astype(BF16)
        head_out = dot_nn(weights, values)
        step = 0
        for h in range(heads):
            cols = slice(h * HEAD_DIM, (h + 1) * HEAD_DIM)
            for block, mask in zip(chosen, masks):
                at = blocks.index(block) * rows
                att_ref[at : at + rows, cols] = head_out[step : step + rows] * mask
                step += rows
        d_weights = dot_nt(upstream, values)
        inner = jnp.sum(probs * d_weights, axis=-1, keepdims=True)
        d_scores = (probs * (d_weights - inner) * scale).astype(BF16)
        d_keys_ref[img, :] += dot_tn(d_scores, queries)
        d_values_ref[img, :] += dot_tn(weights, upstream)
    if last:
        hat = hat_ref[...]
        scaled = d_keys_ref[...] * k_gain_ref[...].astype(F32)
        d_raw = inverse_ref[...] * (
            scaled - hat * jnp.mean(hat * scaled, axis=-1, keepdims=True)
        )
        block_ref[:, :HEAD_DIM] = d_raw.astype(BF16)
        block_ref[:, HEAD_DIM:] = d_values_ref[...].astype(BF16)


def attention(live, queries, places, count, grad_out, k_gain, state, last):
    rows, width = grad_out.shape[1] // count, grad_out.shape[2]
    image_rows = MB * SLOTS
    vector = jax.ShapeDtypeStruct((image_rows, HEAD_DIM), F32)
    rounded = jax.ShapeDtypeStruct((image_rows, HEAD_DIM), BF16)
    attended = jax.ShapeDtypeStruct((sum(map(len, places)) * rows, width), F32)
    scratch = []
    if last:
        out_shape = [attended, jax.ShapeDtypeStruct((image_rows, 2 * HEAD_DIM), BF16)]
        scratch += [pltpu.VMEM(vector.shape, F32)] * 2
    else:
        out_shape = [attended, vector, vector, rounded, rounded, vector, vector]
    if rows % 16 != 0:
        scratch += [pltpu.VMEM(grad_out.shape[1:], F32)]
    operands = [*queries, grad_out, k_gain, *state]
    return pl.pallas_call(
        functools.partial(attention_kernel, places, count, rows, last, len(queries)),
        in_specs=[whole()] * (2 + len(operands)),
        out_specs=[whole()] * len(out_shape),
        out_shape=out_shape,
        scratch_shapes=scratch,
        compiler_params=params(24),
        cost_estimate=cost(0, 0),
        name="attention_last" if last else "attention_first",
    )(*live, *operands)


def assemble_kernel(places, rows, *refs):
    refs, out_ref, held = refs[:-2], refs[-2], refs[-1]
    for group, ref in zip(places, refs):
        for i, p in enumerate(group):
            at = pl.multiple_of(lax.bitwise_xor(here(), p) * rows, rows)
            held[pl.ds(at, rows), :] = ref[i * rows : (i + 1) * rows, :]
    out_ref[0] = held[...].astype(BF16)


def assemble(places, arrays, like):
    rows = arrays[0].shape[0] // len(places[0])
    return pl.pallas_call(
        functools.partial(assemble_kernel, places, rows),
        in_specs=[whole()] * len(arrays),
        out_specs=whole(),
        out_shape=jax.ShapeDtypeStruct(like.shape, BF16),
        scratch_shapes=[pltpu.VMEM(like.shape[1:], F32)],
        compiler_params=params(24),
        cost_estimate=cost(0, 0),
        name="attended_rows",
    )(*arrays)


def grad_kernel(pairs, per_kv, sections, first, last, *refs):
    blocks, weight_ref, refs = refs[: len(pairs)], refs[len(pairs)], refs[len(pairs) + 1 :]
    if not first:
        before_ref, refs = refs[0], refs[1:]
    if per_kv > 1:
        refs, sums = refs[:-1], refs[-1]
        sums[...] = jnp.zeros_like(sums)
    total = refs[-1]
    image_rows, width = total.shape
    heads = []
    for block, pair in zip(blocks, pairs):
        columns = head_columns(lax.div(partner_at(pair), per_kv))
        if per_kv == 1:
            heads.append((columns, block[...]))
        else:
            for half, k in enumerate(columns):
                part = block[:, half * HEAD_DIM : (half + 1) * HEAD_DIM]
                sums[:, k] += part.astype(F32)
    if per_kv > 1:
        heads = [((slice(None),), sums[...].astype(BF16))]
    span = 256
    for c in range(0, width, span):
        cols = slice(c, c + span)
        part = 0.0 if first else before_ref[:, cols]
        for columns, block in heads:
            weight = jnp.concatenate([weight_ref[0, cols, k] for k in columns], axis=1)
            part = part + dot_nt(block, weight)
        total[:, cols] = part
    if last:
        rows = image_rows // sections
        for k in range(sections):
            to = lax.rem(lax.axis_index("section") + k, sections)
            piece = total[pl.ds(pl.multiple_of(to * rows, rows), rows), :]
            refs[k][...] = piece.astype(refs[k].dtype)


def feature_gradient(blocks, weight, per_kv, sections, before=None, last=True):
    pairs, arrays = list(blocks), list(blocks.values())
    image_rows = arrays[0].shape[0]
    width, depth = weight.shape[1:]
    rows = image_rows // sections
    if last:
        out_shape = [
            jax.ShapeDtypeStruct((rows, width), F32 if k == 0 else BF16) for k in range(sections)
        ]
        out_specs = [whole()] * sections
        scratch = [pltpu.VMEM((image_rows, width), F32)]
    else:
        out_shape = jax.ShapeDtypeStruct((image_rows, width), F32)
        out_specs = whole()
        scratch = []
    if per_kv > 1:
        scratch.append(pltpu.VMEM((image_rows, depth), F32))
    operands = [*arrays, weight] + ([] if before is None else [before])
    return pl.pallas_call(
        functools.partial(grad_kernel, pairs, per_kv, sections, before is None, last),
        in_specs=[whole()] * len(operands),
        out_specs=out_specs,
        out_shape=out_shape,
        scratch_shapes=scratch,
        compiler_params=params(24),
        cost_estimate=cost(0, 0),
        name="feature_grad_last" if last else "feature_grad_first",
    )(*operands)


def shards(
    text, features, in_gain, w_query, q_gain, w_key_value, k_gain, tile_count, image_start, grad_out
):
    count = lax.axis_size("tensor")
    sections = lax.axis_size("section")
    per_kv = count // KV_HEADS

    def exchange(x, pair):
        return lax.ppermute(x, "tensor", [(i, i ^ pair[i % 2]) for i in range(count)])

    def swap(x):
        return exchange(x, (1, 1))

    bits = [1 << b for b in range(1, count.bit_length() - 1)]
    steps = len(bits)

    def distance(mask):
        taken = [s for s in range(steps) if mask >> s & 1]
        return sum(bits[s] for s in taken), sum(bits[steps - 1 - s] for s in taken)

    masks = range(1, 1 << steps)

    own_text = text[0]
    width = own_text.shape[1] // 2
    direct = {1 << s: exchange(own_text, distance(1 << s)) for s in range(steps)}

    def both_cores(blocks):
        out = {}
        for pair, x in blocks.items():
            out[pair] = [x]
            out[other_core(pair)] = [swap(x)]
        return out

    def places_of(blocks):
        return sorted(even for even, _ in blocks)

    def queries(blocks, name, **more):
        order = places_of(blocks)
        slots = [(order.index(even), order.index(odd)) for even, odd in blocks]
        groups = list(blocks.values())
        return queries_of(groups, slots, in_gain, w_query, q_gain, name, **more)

    kv_pairs = [distance(mask) for mask in range(1 << steps)]
    other_heads = kv_partial(features, w_key_value, per_kv, [other_core(pair) for pair in kv_pairs])
    other_heads = [swap(x) for x in other_heads]
    sums = kv_partial(features, w_key_value, per_kv, kv_pairs, other_heads)
    for step in range(steps):
        kept, came = sums[::2], [exchange(x, distance(1 << step)) for x in sums[1::2]]
        if step == 0:
            direct, came = lax.optimization_barrier((direct, came))
        if step < steps - 1:
            sums = kv_sum(kept, came)
    parts = [kept[0], came[0]]
    near = both_cores({(0, 0): own_text})
    scalars = (tile_count, image_start)
    q_near, *live = queries(near, "queries_own_chip", scalars=scalars)
    forwarded = []
    for first in (0, width):
        held = {mask: x[:, first : first + width] for mask, x in direct.items()}
        passed = {}
        for s in range(1, steps):
            for mask in range(1, 1 << s):
                more = mask | 1 << s
                held[more] = passed[distance(more)] = exchange(held[mask], distance(1 << s))
        forwarded.append(passed)

    next_to = both_cores({distance(mask): x for mask, x in direct.items()})
    q_next = queries(next_to, "queries_neighbours")

    early, *state = attention(
        live,
        [q_near, q_next],
        [places_of(near), places_of(next_to)],
        count,
        grad_out,
        k_gain,
        parts,
        last=False,
    )
    first_half, state = lax.optimization_barrier((forwarded[0], state))
    far = both_cores(first_half)
    second_half, far = lax.optimization_barrier((forwarded[1], far))
    sums = queries(far, "queries_forwarded_first")
    pieces = {pair: jnp.split(x, 2, axis=1) for pair, x in second_half.items()}
    far, rest = [both_cores({pair: x[i] for pair, x in pieces.items()}) for i in range(2)]
    sums = queries(far, "queries_forwarded_second", start=width, before=sums)
    q_far = queries(rest, "queries_forwarded_last", start=3 * width // 2, before=sums)
    far = places_of(far)
    late, block = attention(live, [q_far], [far], count, grad_out, k_gain, state, last=True)
    attended = assemble([places_of(near) + places_of(next_to), far], [early, late], grad_out)

    same_core = {(0, 0): block}
    same_core.update({distance(m): exchange(block, distance(m)) for m in reversed(masks)})
    swapped = {other_core(pair): swap(x) for pair, x in same_core.items()}
    before = None
    blocks = {**same_core, **swapped}
    if per_kv == 1:
        soon = {pair: blocks.pop(pair) for pair in [*same_core, (1, 1)]}
        before = feature_gradient(soon, w_key_value, per_kv, sections, last=False)
    pieces = feature_gradient(blocks, w_key_value, per_kv, sections, before)
    feature_grad, leaving = pieces[0], pieces[1:]
    arrived = []
    for k in range(1, sections):
        perm = [(i, (i + k) % sections) for i in range(sections)]
        arrived.append(lax.ppermute(leaving[k - 1], "section", perm))
    for x in arrived:
        feature_grad = feature_grad + x.astype(F32)
    return (attended, feature_grad)


def solution(mesh):
    return jax.shard_map(
        shards,
        mesh=mesh,
        in_specs=(
            P("section", "tensor", None),
            P(None, "tensor"),
            P("section", None),
            P("section", None, "tensor"),
            P("section", None),
            P("section", "tensor", None),
            P("section", None),
            P(),
            P(),
            P("section", None, "tensor"),
        ),
        out_specs=(P("section", None, "tensor"), P("section", "tensor")),
        check_vma=False,
    )
```

```python
import functools

import jax
import jax.numpy as jnp
from jax import lax
from jax.experimental import pallas as pl
from jax.experimental.pallas import tpu as pltpu
from jax.sharding import PartitionSpec as P

KV_HEADS = 8
HEAD_DIM = 128
TILES = 4
TILE_LEN = 24
TXT_TOK = 128
MB = 2
SLOTS = TILES * TILE_LEN

eps = 1e-05

F32 = jnp.float32
BF16 = jnp.bfloat16
MIB = 1 << 20


def whole(memory=pltpu.VMEM):
    return pl.BlockSpec(memory_space=memory)


def dot_nn(a, b):
    return jnp.dot(a, b, preferred_element_type=F32)


def dot_nt(a, b):
    return lax.dot_general(a, b, (((1,), (1,)), ((), ())), preferred_element_type=F32)


def dot_tn(a, b):
    return lax.dot_general(a, b, (((0,), (0,)), ((), ())), preferred_element_type=F32)


def params(mib):
    return pltpu.CompilerParams(vmem_limit_bytes=mib * MIB)


def cost(flops, size):
    return pl.CostEstimate(flops=flops, bytes_accessed=size, transcendentals=0)


def here():
    return lax.axis_index("tensor")


def of_core(pair):
    even, odd = pair
    return even if even == odd else even + lax.rem(here(), 2) * (odd - even)


def partner_at(pair):
    return lax.bitwise_xor(here(), of_core(pair))


def other_core(pair):
    return (1 ^ pair[1], 1 ^ pair[0])


def head_columns(head):
    return [
        pl.ds(pl.multiple_of((half * KV_HEADS + head) * HEAD_DIM, HEAD_DIM), HEAD_DIM)
        for half in range(2)
    ]


def kv_kernel(per_kv, pairs, feat_ref, weight_ref, *refs):
    features = feat_ref[...]
    for j, pair in enumerate(pairs):
        head = lax.div(partner_at(pair), per_kv)
        weight = jnp.concatenate([weight_ref[0, :, c] for c in head_columns(head)], axis=1)
        total = dot_nn(features, weight)
        out_ref = refs[j - len(pairs)]
        if len(refs) > len(pairs):
            total = total + refs[j][...]
        out_ref[...] = total.astype(out_ref.dtype)


def kv_partial(features, weight, per_kv, pairs, other=()):
    operands = (features, weight, *other)
    shape = (features.shape[0], 2 * HEAD_DIM)
    return pl.pallas_call(
        functools.partial(kv_kernel, per_kv, pairs),
        in_specs=[whole()] * len(operands),
        out_specs=[whole()] * len(pairs),
        out_shape=[
            jax.ShapeDtypeStruct(shape, BF16 if other and j % 2 else F32)
            for j in range(len(pairs))
        ],
        compiler_params=params(24),
        cost_estimate=cost(0, 0),
        name="kv_partial_own_core" if other else "kv_partial_other_core",
    )(*operands)


def kv_sum_kernel(*refs):
    size = len(refs) // 3
    for kept_ref, came_ref, out_ref in zip(refs, refs[size:], refs[2 * size :]):
        total = kept_ref[...] + came_ref[...].astype(F32)
        out_ref[...] = total.astype(out_ref.dtype)


def kv_sum(kept, came):
    return pl.pallas_call(
        kv_sum_kernel,
        in_specs=[whole()] * (2 * len(kept)),
        out_specs=[whole()] * len(kept),
        out_shape=[
            jax.ShapeDtypeStruct(x.shape, BF16 if i % 2 else F32) for i, x in enumerate(kept)
        ],
        compiler_params=params(24),
        cost_estimate=cost(0, 0),
        name="kv_sum",
    )(*kept, *came)


def live_masks(count_ref, start_ref, token_ref, slot_ref):
    for b in range(MB):
        token = lax.broadcasted_iota(jnp.int32, (TXT_TOK, HEAD_DIM), 0)
        token_ref[b * TXT_TOK : (b + 1) * TXT_TOK, :] = (token >= start_ref[b]).astype(F32)
        slot = lax.broadcasted_iota(jnp.int32, slot_ref.shape[1:], 1)
        slot_ref[b] = (slot < count_ref[b] * TILE_LEN).astype(F32)


def query_kernel(shape, slots, start, scalars, scratch, *refs):
    if scalars:
        end = len(refs) - scratch
        live_masks(refs[0], refs[1], refs[end - 2], refs[end - 1])
        refs = refs[2 : end - 2] + refs[end:]
    gain_ref, weight_ref, q_gain_ref, refs = refs[0], refs[1], refs[2], refs[3:]
    groups = []
    for parts in shape:
        groups.append(refs[:parts])
        refs = refs[parts:]
    depth, heads_width = weight_ref.shape[1:]
    width = sum(part.shape[1] for part in groups[0])
    last = start + width == depth
    span = 1024

    def columns(parts, c):
        for part in parts:
            if c < part.shape[1]:
                return part[:, c : c + span].astype(F32)
            c -= part.shape[1]

    if start:
        raw, squares, refs = refs[0][...], refs[1][:, :1], refs[2:]
    else:
        raw, squares = 0.0, 0.0
    for c in range(0, width, span):
        x = jnp.concatenate([columns(parts, c) for parts in groups], axis=0)
        squares = squares + jnp.sum(x * x, axis=-1, keepdims=True)
        cols = slice(start + c, start + c + span)
        scaled = (x * gain_ref[:, cols].astype(F32)).astype(BF16)
        raw = raw + dot_nn(scaled, weight_ref[0, cols, :])
    if not last:
        refs[0][...] = raw
        refs[1][...] = jnp.broadcast_to(squares, refs[1].shape)
        return
    out_ref = refs[-1]
    rows = groups[0][0].shape[0]
    inverse = lax.rsqrt(squares / depth + eps)
    q_gain = q_gain_ref[...].astype(F32)
    for c in range(0, heads_width, HEAD_DIM):
        head = raw[:, c : c + HEAD_DIM] * inverse
        q_inverse = lax.rsqrt(jnp.mean(head * head, axis=-1, keepdims=True) + eps)
        head = head * q_inverse * q_gain
        for i, pair in enumerate(slots):
            at = of_core(pair) * rows
            if pair[0] != pair[1]:
                at = pl.multiple_of(at, rows)
            part = head[i * rows : (i + 1) * rows]
            out_ref[pl.ds(at, rows), c : c + HEAD_DIM] = part.astype(out_ref.dtype)
    if len(refs) > 1:
        refs[0][...] = out_ref[...].astype(BF16)


def queries_of(groups, slots, gain, weight, q_gain, name, start=0, before=(), scalars=()):
    arrays = [part for parts in groups for part in parts]
    rows = sum(parts[0].shape[0] for parts in groups)
    depth, heads_width = weight.shape[1:]
    last = start + sum(part.shape[1] for part in groups[0]) == depth
    scratch = []
    if last:
        out_shape = [jax.ShapeDtypeStruct((rows, heads_width), BF16)]
        if arrays[0].shape[0] % 16 != 0:
            scratch.append(pltpu.VMEM((rows, heads_width), F32))
        if scalars:
            out_shape.append(jax.ShapeDtypeStruct((MB * TXT_TOK, HEAD_DIM), F32))
            out_shape.append(jax.ShapeDtypeStruct((MB, 8, SLOTS), F32))
    else:
        out_shape = [jax.ShapeDtypeStruct((rows, w), F32) for w in (heads_width, HEAD_DIM)]
    out = pl.pallas_call(
        functools.partial(
            query_kernel,
            [len(parts) for parts in groups],
            slots,
            start,
            len(scalars),
            len(scratch),
        ),
        in_specs=[whole(pltpu.SMEM)] * len(scalars)
        + [whole()] * (3 + len(arrays) + len(before)),
        out_specs=[whole()] * len(out_shape),
        out_shape=out_shape,
        scratch_shapes=scratch,
        compiler_params=params(24),
        cost_estimate=cost(0, 0),
        name=name,
    )(*scalars, gain, weight, q_gain, *arrays, *before)
    return out[0] if last and not scalars else out


def attention_kernel(places, count, rows, last, sizes, *refs):
    token_ref, slot_ref, refs = refs[0], refs[1], refs[2:]
    queries_refs, refs = refs[:sizes], refs[sizes:]
    grad_ref, k_gain_ref, refs = refs[0], refs[1], refs[2:]
    narrow = rows % 16 != 0
    if narrow:
        refs, grad_rows = refs[:-1], refs[-1]
        grad_rows[...] = grad_ref[0].astype(F32)
    if last:
        d_keys_in, d_values_in, keys_ref, values_ref, hat_ref, inverse_ref = refs[:6]
        att_ref, block_ref, d_keys_ref, d_values_ref = refs[6:]
        d_keys_ref[...] = d_keys_in[...]
        d_values_ref[...] = d_values_in[...]
    else:
        parts = refs[:-7]
        att_ref, d_keys_ref, d_values_ref, keys_ref, values_ref, hat_ref, inverse_ref = refs[-7:]
        kv = sum(part[...].astype(F32) for part in parts)
        key_raw = kv[:, :HEAD_DIM]
        inverse = lax.rsqrt(jnp.mean(key_raw * key_raw, axis=-1, keepdims=True) + eps)
        hat_ref[...] = key_raw * inverse
        inverse_ref[...] = jnp.broadcast_to(inverse, key_raw.shape)
        keys_ref[...] = (key_raw * inverse * k_gain_ref[...].astype(F32)).astype(BF16)
        values_ref[...] = kv[:, HEAD_DIM:].astype(BF16)
        d_keys_ref[...] = jnp.zeros_like(d_keys_ref)
        d_values_ref[...] = jnp.zeros_like(d_values_ref)

    scale = HEAD_DIM ** (-0.5)
    heads = grad_ref.shape[2] // HEAD_DIM
    per_sample = count // MB
    mine = lax.div(here(), per_sample)
    blocks = [
        (p, ref, i * rows) for group, ref in zip(places, queries_refs) for i, p in enumerate(group)
    ]
    for far in range(MB):
        chosen = [block for block in blocks if block[0] // per_sample == far]
        if not chosen:
            continue
        sample = lax.bitwise_xor(mine, far)
        img = pl.ds(pl.multiple_of(sample * SLOTS, SLOTS), SLOTS)
        keys, values = keys_ref[img, :], values_ref[img, :]
        live = slot_ref[sample][:1, :] > 0
        spots = [
            pl.ds(pl.multiple_of(lax.bitwise_xor(here(), p) * rows, rows), rows)
            for p, _, _ in chosen
        ]
        masks = [token_ref[spot, :] for spot in spots]
        queries, upstream = [], []
        for h in range(heads):
            cols = slice(h * HEAD_DIM, (h + 1) * HEAD_DIM)
            for (p, ref, at), mask, spot in zip(chosen, masks, spots):
                queries.append(ref[at : at + rows, cols])
                grad = grad_rows[spot, cols] if narrow else grad_ref[0, spot, cols].astype(F32)
                upstream.append((grad * mask).astype(BF16))
        queries = jnp.concatenate(queries, axis=0)
        upstream = jnp.concatenate(upstream, axis=0)
        scores = dot_nt(queries, keys) * scale
        exponent = jnp.where(live, jnp.exp(scores), 0.0)
        probs = exponent * (1.0 / jnp.sum(exponent, axis=-1, keepdims=True))
        weights = probs.astype(BF16)
        head_out = dot_nn(weights, values)
        step = 0
        for h in range(heads):
            cols = slice(h * HEAD_DIM, (h + 1) * HEAD_DIM)
            for block, mask in zip(chosen, masks):
                at = blocks.index(block) * rows
                att_ref[at : at + rows, cols] = head_out[step : step + rows] * mask
                step += rows
        d_weights = dot_nt(upstream, values)
        inner = jnp.sum(probs * d_weights, axis=-1, keepdims=True)
        d_scores = (probs * (d_weights - inner) * scale).astype(BF16)
        d_keys_ref[img, :] += dot_tn(d_scores, queries)
        d_values_ref[img, :] += dot_tn(weights, upstream)
    if last:
        hat = hat_ref[...]
        scaled = d_keys_ref[...] * k_gain_ref[...].astype(F32)
        d_raw = inverse_ref[...] * (
            scaled - hat * jnp.mean(hat * scaled, axis=-1, keepdims=True)
        )
        block_ref[:, :HEAD_DIM] = d_raw.astype(BF16)
        block_ref[:, HEAD_DIM:] = d_values_ref[...].astype(BF16)


def attention(live, queries, places, count, grad_out, k_gain, state, last):
    rows, width = grad_out.shape[1] // count, grad_out.shape[2]
    image_rows = MB * SLOTS
    vector = jax.ShapeDtypeStruct((image_rows, HEAD_DIM), F32)
    rounded = jax.ShapeDtypeStruct((image_rows, HEAD_DIM), BF16)
    attended = jax.ShapeDtypeStruct((sum(map(len, places)) * rows, width), F32)
    scratch = []
    if last:
        out_shape = [attended, jax.ShapeDtypeStruct((image_rows, 2 * HEAD_DIM), BF16)]
        scratch += [pltpu.VMEM(vector.shape, F32)] * 2
    else:
        out_shape = [attended, vector, vector, rounded, rounded, vector, vector]
    if rows % 16 != 0:
        scratch += [pltpu.VMEM(grad_out.shape[1:], F32)]
    operands = [*queries, grad_out, k_gain, *state]
    return pl.pallas_call(
        functools.partial(attention_kernel, places, count, rows, last, len(queries)),
        in_specs=[whole()] * (2 + len(operands)),
        out_specs=[whole()] * len(out_shape),
        out_shape=out_shape,
        scratch_shapes=scratch,
        compiler_params=params(24),
        cost_estimate=cost(0, 0),
        name="attention_last" if last else "attention_first",
    )(*live, *operands)


def assemble_kernel(places, rows, *refs):
    refs, out_ref, held = refs[:-2], refs[-2], refs[-1]
    for group, ref in zip(places, refs):
        for i, p in enumerate(group):
            at = pl.multiple_of(lax.bitwise_xor(here(), p) * rows, rows)
            held[pl.ds(at, rows), :] = ref[i * rows : (i + 1) * rows, :]
    out_ref[0] = held[...].astype(BF16)


def assemble(places, arrays, like):
    rows = arrays[0].shape[0] // len(places[0])
    return pl.pallas_call(
        functools.partial(assemble_kernel, places, rows),
        in_specs=[whole()] * len(arrays),
        out_specs=whole(),
        out_shape=jax.ShapeDtypeStruct(like.shape, BF16),
        scratch_shapes=[pltpu.VMEM(like.shape[1:], F32)],
        compiler_params=params(24),
        cost_estimate=cost(0, 0),
        name="attended_rows",
    )(*arrays)


def grad_kernel(pairs, per_kv, sections, first, last, *refs):
    blocks, weight_ref, refs = refs[: len(pairs)], refs[len(pairs)], refs[len(pairs) + 1 :]
    if not first:
        before_ref, refs = refs[0], refs[1:]
    if per_kv > 1:
        refs, sums = refs[:-1], refs[-1]
        sums[...] = jnp.zeros_like(sums)
    total = refs[-1]
    image_rows, width = total.shape
    heads = []
    for block, pair in zip(blocks, pairs):
        columns = head_columns(lax.div(partner_at(pair), per_kv))
        if per_kv == 1:
            heads.append((columns, block[...]))
        else:
            for half, k in enumerate(columns):
                part = block[:, half * HEAD_DIM : (half + 1) * HEAD_DIM]
                sums[:, k] += part.astype(F32)
    if per_kv > 1:
        heads = [((slice(None),), sums[...].astype(BF16))]
    span = 256
    for c in range(0, width, span):
        cols = slice(c, c + span)
        part = 0.0 if first else before_ref[:, cols]
        for columns, block in heads:
            weight = jnp.concatenate([weight_ref[0, cols, k] for k in columns], axis=1)
            part = part + dot_nt(block, weight)
        total[:, cols] = part
    if last:
        rows = image_rows // sections
        for k in range(sections):
            to = lax.rem(lax.axis_index("section") + k, sections)
            piece = total[pl.ds(pl.multiple_of(to * rows, rows), rows), :]
            refs[k][...] = piece.astype(refs[k].dtype)


def feature_gradient(blocks, weight, per_kv, sections, before=None, last=True):
    pairs, arrays = list(blocks), list(blocks.values())
    image_rows = arrays[0].shape[0]
    width, depth = weight.shape[1:]
    rows = image_rows // sections
    if last:
        out_shape = [
            jax.ShapeDtypeStruct((rows, width), F32 if k == 0 else BF16) for k in range(sections)
        ]
        out_specs = [whole()] * sections
        scratch = [pltpu.VMEM((image_rows, width), F32)]
    else:
        out_shape = jax.ShapeDtypeStruct((image_rows, width), F32)
        out_specs = whole()
        scratch = []
    if per_kv > 1:
        scratch.append(pltpu.VMEM((image_rows, depth), F32))
    operands = [*arrays, weight] + ([] if before is None else [before])
    return pl.pallas_call(
        functools.partial(grad_kernel, pairs, per_kv, sections, before is None, last),
        in_specs=[whole()] * len(operands),
        out_specs=out_specs,
        out_shape=out_shape,
        scratch_shapes=scratch,
        compiler_params=params(24),
        cost_estimate=cost(0, 0),
        name="feature_grad_last" if last else "feature_grad_first",
    )(*operands)


def shards(
    text, features, in_gain, w_query, q_gain, w_key_value, k_gain, tile_count, image_start, grad_out
):
    count = lax.axis_size("tensor")
    sections = lax.axis_size("section")
    per_kv = count // KV_HEADS

    def exchange(x, pair):
        return lax.ppermute(x, "tensor", [(i, i ^ pair[i % 2]) for i in range(count)])

    def swap(x):
        return exchange(x, (1, 1))

    bits = [1 << b for b in range(1, count.bit_length() - 1)]
    steps = len(bits)

    def distance(mask):
        taken = [s for s in range(steps) if mask >> s & 1]
        return sum(bits[s] for s in taken), sum(bits[steps - 1 - s] for s in taken)

    masks = range(1, 1 << steps)

    own_text = text[0]
    width = own_text.shape[1] // 2
    direct = {1 << s: exchange(own_text, distance(1 << s)) for s in range(steps)}

    def both_cores(blocks):
        out = {}
        for pair, x in blocks.items():
            out[pair] = [x]
            out[other_core(pair)] = [swap(x)]
        return out

    def places_of(blocks):
        return sorted(even for even, _ in blocks)

    def queries(blocks, name, **more):
        order = places_of(blocks)
        slots = [(order.index(even), order.index(odd)) for even, odd in blocks]
        groups = list(blocks.values())
        return queries_of(groups, slots, in_gain, w_query, q_gain, name, **more)

    kv_pairs = [distance(mask) for mask in range(1 << steps)]
    other_heads = kv_partial(features, w_key_value, per_kv, [other_core(pair) for pair in kv_pairs])
    other_heads = [swap(x) for x in other_heads]
    sums = kv_partial(features, w_key_value, per_kv, kv_pairs, other_heads)
    for step in range(steps):
        kept, came = sums[::2], [exchange(x, distance(1 << step)) for x in sums[1::2]]
        if step == 0:
            direct, came = lax.optimization_barrier((direct, came))
        if step < steps - 1:
            sums = kv_sum(kept, came)
    parts = [kept[0], came[0]]
    near = both_cores({(0, 0): own_text})
    scalars = (tile_count, image_start)
    q_near, *live = queries(near, "queries_own_chip", scalars=scalars)
    forwarded = []
    for first in (0, width):
        held = {mask: x[:, first : first + width] for mask, x in direct.items()}
        passed = {}
        for s in range(1, steps):
            for mask in range(1, 1 << s):
                more = mask | 1 << s
                held[more] = passed[distance(more)] = exchange(held[mask], distance(1 << s))
        forwarded.append(passed)

    next_to = both_cores({distance(mask): x for mask, x in direct.items()})
    q_next = queries(next_to, "queries_neighbours")

    early, *state = attention(
        live,
        [q_near, q_next],
        [places_of(near), places_of(next_to)],
        count,
        grad_out,
        k_gain,
        parts,
        last=False,
    )
    first_half, state = lax.optimization_barrier((forwarded[0], state))
    far = both_cores(first_half)
    second_half, far = lax.optimization_barrier((forwarded[1], far))
    sums = queries(far, "queries_forwarded_first")
    pieces = {pair: jnp.split(x, 2, axis=1) for pair, x in second_half.items()}
    far, rest = [both_cores({pair: x[i] for pair, x in pieces.items()}) for i in range(2)]
    sums = queries(far, "queries_forwarded_second", start=width, before=sums)
    q_far = queries(rest, "queries_forwarded_last", start=3 * width // 2, before=sums)
    far = places_of(far)
    late, block = attention(live, [q_far], [far], count, grad_out, k_gain, state, last=True)
    attended = assemble([places_of(near) + places_of(next_to), far], [early, late], grad_out)

    same_core = {(0, 0): block}
    same_core.update({distance(m): exchange(block, distance(m)) for m in masks})
    swapped = {other_core(pair): swap(x) for pair, x in same_core.items()}
    before = None
    blocks = {**same_core, **swapped}
    if per_kv == 1:
        first = [*same_core, *list(swapped)[:2]]
        soon = {pair: blocks.pop(pair) for pair in first}
        before = feature_gradient(soon, w_key_value, per_kv, sections, last=False)
    pieces = feature_gradient(blocks, w_key_value, per_kv, sections, before)
    feature_grad, leaving = pieces[0], pieces[1:]
    arrived = []
    for k in range(1, sections):
        perm = [(i, (i + k) % sections) for i in range(sections)]
        arrived.append(lax.ppermute(leaving[k - 1], "section", perm))
    for x in arrived:
        feature_grad = feature_grad + x.astype(F32)
    return (attended, feature_grad)


def solution(mesh):
    return jax.shard_map(
        shards,
        mesh=mesh,
        in_specs=(
            P("section", "tensor", None),
            P(None, "tensor"),
            P("section", None),
            P("section", None, "tensor"),
            P("section", None),
            P("section", "tensor", None),
            P("section", None),
            P(),
            P(),
            P("section", None, "tensor"),
        ),
        out_specs=(P("section", None, "tensor"), P("section", "tensor")),
        check_vma=False,
    )
```

```python
import functools

import jax
import jax.numpy as jnp
from jax import lax
from jax.experimental import pallas as pl
from jax.experimental.pallas import tpu as pltpu
from jax.sharding import PartitionSpec as P

KV_HEADS = 8
HEAD_DIM = 128
TILES = 4
TILE_LEN = 24
TXT_TOK = 128
MB = 2
SLOTS = TILES * TILE_LEN

eps = 1e-05

F32 = jnp.float32
BF16 = jnp.bfloat16
MIB = 1 << 20


def whole(memory=pltpu.VMEM):
    return pl.BlockSpec(memory_space=memory)


def dot_nn(a, b):
    return jnp.dot(a, b, preferred_element_type=F32)


def dot_nt(a, b):
    return lax.dot_general(a, b, (((1,), (1,)), ((), ())), preferred_element_type=F32)


def dot_tn(a, b):
    return lax.dot_general(a, b, (((0,), (0,)), ((), ())), preferred_element_type=F32)


def params(mib):
    return pltpu.CompilerParams(vmem_limit_bytes=mib * MIB)


def cost(flops, size):
    return pl.CostEstimate(flops=flops, bytes_accessed=size, transcendentals=0)


def here():
    return lax.axis_index("tensor")


def of_core(pair):
    even, odd = pair
    return even if even == odd else even + lax.rem(here(), 2) * (odd - even)


def partner_at(pair):
    return lax.bitwise_xor(here(), of_core(pair))


def other_core(pair):
    return (1 ^ pair[1], 1 ^ pair[0])


def head_columns(head):
    return [
        pl.ds(pl.multiple_of((half * KV_HEADS + head) * HEAD_DIM, HEAD_DIM), HEAD_DIM)
        for half in range(2)
    ]


def kv_kernel(per_kv, pairs, feat_ref, weight_ref, *refs):
    features = feat_ref[...]
    for j, pair in enumerate(pairs):
        head = lax.div(partner_at(pair), per_kv)
        weight = jnp.concatenate([weight_ref[0, :, c] for c in head_columns(head)], axis=1)
        total = dot_nn(features, weight)
        out_ref = refs[j - len(pairs)]
        if len(refs) > len(pairs):
            total = total + refs[j][...]
        out_ref[...] = total.astype(out_ref.dtype)


def kv_partial(features, weight, per_kv, pairs, other=()):
    operands = (features, weight, *other)
    shape = (features.shape[0], 2 * HEAD_DIM)
    return pl.pallas_call(
        functools.partial(kv_kernel, per_kv, pairs),
        in_specs=[whole()] * len(operands),
        out_specs=[whole()] * len(pairs),
        out_shape=[
            jax.ShapeDtypeStruct(shape, BF16 if other and j % 2 else F32)
            for j in range(len(pairs))
        ],
        compiler_params=params(24),
        cost_estimate=cost(0, 0),
        name="kv_partial_own_core" if other else "kv_partial_other_core",
    )(*operands)


def kv_sum_kernel(*refs):
    size = len(refs) // 3
    for kept_ref, came_ref, out_ref in zip(refs, refs[size:], refs[2 * size :]):
        total = kept_ref[...] + came_ref[...].astype(F32)
        out_ref[...] = total.astype(out_ref.dtype)


def kv_sum(kept, came):
    return pl.pallas_call(
        kv_sum_kernel,
        in_specs=[whole()] * (2 * len(kept)),
        out_specs=[whole()] * len(kept),
        out_shape=[
            jax.ShapeDtypeStruct(x.shape, BF16 if i % 2 else F32) for i, x in enumerate(kept)
        ],
        compiler_params=params(24),
        cost_estimate=cost(0, 0),
        name="kv_sum",
    )(*kept, *came)


def live_masks(count_ref, start_ref, token_ref, slot_ref):
    for b in range(MB):
        token = lax.broadcasted_iota(jnp.int32, (TXT_TOK, HEAD_DIM), 0)
        token_ref[b * TXT_TOK : (b + 1) * TXT_TOK, :] = (token >= start_ref[b]).astype(F32)
        slot = lax.broadcasted_iota(jnp.int32, slot_ref.shape[1:], 1)
        slot_ref[b] = (slot < count_ref[b] * TILE_LEN).astype(F32)


def query_kernel(shape, slots, start, scalars, scratch, *refs):
    if scalars:
        end = len(refs) - scratch
        live_masks(refs[0], refs[1], refs[end - 2], refs[end - 1])
        refs = refs[2 : end - 2] + refs[end:]
    gain_ref, weight_ref, q_gain_ref, refs = refs[0], refs[1], refs[2], refs[3:]
    groups = []
    for parts in shape:
        groups.append(refs[:parts])
        refs = refs[parts:]
    depth, heads_width = weight_ref.shape[1:]
    width = sum(part.shape[1] for part in groups[0])
    last = start + width == depth
    span = 1024

    def columns(parts, c):
        for part in parts:
            if c < part.shape[1]:
                return part[:, c : c + span].astype(F32)
            c -= part.shape[1]

    if start:
        raw, squares, refs = refs[0][...], refs[1][:, :1], refs[2:]
    else:
        raw, squares = 0.0, 0.0
    for c in range(0, width, span):
        x = jnp.concatenate([columns(parts, c) for parts in groups], axis=0)
        squares = squares + jnp.sum(x * x, axis=-1, keepdims=True)
        cols = slice(start + c, start + c + span)
        scaled = (x * gain_ref[:, cols].astype(F32)).astype(BF16)
        raw = raw + dot_nn(scaled, weight_ref[0, cols, :])
    if not last:
        refs[0][...] = raw
        refs[1][...] = jnp.broadcast_to(squares, refs[1].shape)
        return
    out_ref = refs[-1]
    rows = groups[0][0].shape[0]
    inverse = lax.rsqrt(squares / depth + eps)
    q_gain = q_gain_ref[...].astype(F32)
    for c in range(0, heads_width, HEAD_DIM):
        head = raw[:, c : c + HEAD_DIM] * inverse
        q_inverse = lax.rsqrt(jnp.mean(head * head, axis=-1, keepdims=True) + eps)
        head = head * q_inverse * q_gain
        for i, pair in enumerate(slots):
            at = of_core(pair) * rows
            if pair[0] != pair[1]:
                at = pl.multiple_of(at, rows)
            part = head[i * rows : (i + 1) * rows]
            out_ref[pl.ds(at, rows), c : c + HEAD_DIM] = part.astype(out_ref.dtype)
    if len(refs) > 1:
        refs[0][...] = out_ref[...].astype(BF16)


def queries_of(groups, slots, gain, weight, q_gain, name, start=0, before=(), scalars=()):
    arrays = [part for parts in groups for part in parts]
    rows = sum(parts[0].shape[0] for parts in groups)
    depth, heads_width = weight.shape[1:]
    last = start + sum(part.shape[1] for part in groups[0]) == depth
    scratch = []
    if last:
        out_shape = [jax.ShapeDtypeStruct((rows, heads_width), BF16)]
        if arrays[0].shape[0] % 16 != 0:
            scratch.append(pltpu.VMEM((rows, heads_width), F32))
        if scalars:
            out_shape.append(jax.ShapeDtypeStruct((MB * TXT_TOK, HEAD_DIM), F32))
            out_shape.append(jax.ShapeDtypeStruct((MB, 8, SLOTS), F32))
    else:
        out_shape = [jax.ShapeDtypeStruct((rows, w), F32) for w in (heads_width, HEAD_DIM)]
    out = pl.pallas_call(
        functools.partial(
            query_kernel,
            [len(parts) for parts in groups],
            slots,
            start,
            len(scalars),
            len(scratch),
        ),
        in_specs=[whole(pltpu.SMEM)] * len(scalars)
        + [whole()] * (3 + len(arrays) + len(before)),
        out_specs=[whole()] * len(out_shape),
        out_shape=out_shape,
        scratch_shapes=scratch,
        compiler_params=params(24),
        cost_estimate=cost(0, 0),
        name=name,
    )(*scalars, gain, weight, q_gain, *arrays, *before)
    return out[0] if last and not scalars else out


def attention_kernel(places, count, rows, last, sizes, *refs):
    token_ref, slot_ref, refs = refs[0], refs[1], refs[2:]
    queries_refs, refs = refs[:sizes], refs[sizes:]
    grad_ref, k_gain_ref, refs = refs[0], refs[1], refs[2:]
    narrow = rows % 16 != 0
    if narrow:
        refs, grad_rows = refs[:-1], refs[-1]
        grad_rows[...] = grad_ref[0].astype(F32)
    if last:
        d_keys_in, d_values_in, keys_ref, values_ref, hat_ref, inverse_ref = refs[:6]
        att_ref, block_ref, d_keys_ref, d_values_ref = refs[6:]
        d_keys_ref[...] = d_keys_in[...]
        d_values_ref[...] = d_values_in[...]
    else:
        parts = refs[:-7]
        att_ref, d_keys_ref, d_values_ref, keys_ref, values_ref, hat_ref, inverse_ref = refs[-7:]
        kv = sum(part[...].astype(F32) for part in parts)
        key_raw = kv[:, :HEAD_DIM]
        inverse = lax.rsqrt(jnp.mean(key_raw * key_raw, axis=-1, keepdims=True) + eps)
        hat_ref[...] = key_raw * inverse
        inverse_ref[...] = jnp.broadcast_to(inverse, key_raw.shape)
        keys_ref[...] = (key_raw * inverse * k_gain_ref[...].astype(F32)).astype(BF16)
        values_ref[...] = kv[:, HEAD_DIM:].astype(BF16)
        d_keys_ref[...] = jnp.zeros_like(d_keys_ref)
        d_values_ref[...] = jnp.zeros_like(d_values_ref)

    scale = HEAD_DIM ** (-0.5)
    heads = grad_ref.shape[2] // HEAD_DIM
    per_sample = count // MB
    mine = lax.div(here(), per_sample)
    blocks = [
        (p, ref, i * rows) for group, ref in zip(places, queries_refs) for i, p in enumerate(group)
    ]
    for far in range(MB):
        chosen = [block for block in blocks if block[0] // per_sample == far]
        if not chosen:
            continue
        sample = lax.bitwise_xor(mine, far)
        img = pl.ds(pl.multiple_of(sample * SLOTS, SLOTS), SLOTS)
        keys, values = keys_ref[img, :], values_ref[img, :]
        live = slot_ref[sample][:1, :] > 0
        spots = [
            pl.ds(pl.multiple_of(lax.bitwise_xor(here(), p) * rows, rows), rows)
            for p, _, _ in chosen
        ]
        masks = [token_ref[spot, :] for spot in spots]
        queries, upstream = [], []
        for h in range(heads):
            cols = slice(h * HEAD_DIM, (h + 1) * HEAD_DIM)
            for (p, ref, at), mask, spot in zip(chosen, masks, spots):
                queries.append(ref[at : at + rows, cols])
                grad = grad_rows[spot, cols] if narrow else grad_ref[0, spot, cols].astype(F32)
                upstream.append((grad * mask).astype(BF16))
        queries = jnp.concatenate(queries, axis=0)
        upstream = jnp.concatenate(upstream, axis=0)
        scores = dot_nt(queries, keys) * scale
        exponent = jnp.where(live, jnp.exp(scores), 0.0)
        probs = exponent * (1.0 / jnp.sum(exponent, axis=-1, keepdims=True))
        weights = probs.astype(BF16)
        head_out = dot_nn(weights, values)
        step = 0
        for h in range(heads):
            cols = slice(h * HEAD_DIM, (h + 1) * HEAD_DIM)
            for block, mask in zip(chosen, masks):
                at = blocks.index(block) * rows
                att_ref[at : at + rows, cols] = head_out[step : step + rows] * mask
                step += rows
        d_weights = dot_nt(upstream, values)
        inner = jnp.sum(probs * d_weights, axis=-1, keepdims=True)
        d_scores = (probs * (d_weights - inner) * scale).astype(BF16)
        d_keys_ref[img, :] += dot_tn(d_scores, queries)
        d_values_ref[img, :] += dot_tn(weights, upstream)
    if last:
        hat = hat_ref[...]
        scaled = d_keys_ref[...] * k_gain_ref[...].astype(F32)
        d_raw = inverse_ref[...] * (
            scaled - hat * jnp.mean(hat * scaled, axis=-1, keepdims=True)
        )
        block_ref[:, :HEAD_DIM] = d_raw.astype(BF16)
        block_ref[:, HEAD_DIM:] = d_values_ref[...].astype(BF16)


def attention(live, queries, places, count, grad_out, k_gain, state, last):
    rows, width = grad_out.shape[1] // count, grad_out.shape[2]
    image_rows = MB * SLOTS
    vector = jax.ShapeDtypeStruct((image_rows, HEAD_DIM), F32)
    rounded = jax.ShapeDtypeStruct((image_rows, HEAD_DIM), BF16)
    attended = jax.ShapeDtypeStruct((sum(map(len, places)) * rows, width), F32)
    scratch = []
    if last:
        out_shape = [attended, jax.ShapeDtypeStruct((image_rows, 2 * HEAD_DIM), BF16)]
        scratch += [pltpu.VMEM(vector.shape, F32)] * 2
    else:
        out_shape = [attended, vector, vector, rounded, rounded, vector, vector]
    if rows % 16 != 0:
        scratch += [pltpu.VMEM(grad_out.shape[1:], F32)]
    operands = [*queries, grad_out, k_gain, *state]
    return pl.pallas_call(
        functools.partial(attention_kernel, places, count, rows, last, len(queries)),
        in_specs=[whole()] * (2 + len(operands)),
        out_specs=[whole()] * len(out_shape),
        out_shape=out_shape,
        scratch_shapes=scratch,
        compiler_params=params(24),
        cost_estimate=cost(0, 0),
        name="attention_last" if last else "attention_first",
    )(*live, *operands)


def assemble_kernel(places, rows, *refs):
    refs, out_ref, held = refs[:-2], refs[-2], refs[-1]
    for group, ref in zip(places, refs):
        for i, p in enumerate(group):
            at = pl.multiple_of(lax.bitwise_xor(here(), p) * rows, rows)
            held[pl.ds(at, rows), :] = ref[i * rows : (i + 1) * rows, :]
    out_ref[0] = held[...].astype(BF16)


def assemble(places, arrays, like):
    rows = arrays[0].shape[0] // len(places[0])
    return pl.pallas_call(
        functools.partial(assemble_kernel, places, rows),
        in_specs=[whole()] * len(arrays),
        out_specs=whole(),
        out_shape=jax.ShapeDtypeStruct(like.shape, BF16),
        scratch_shapes=[pltpu.VMEM(like.shape[1:], F32)],
        compiler_params=params(24),
        cost_estimate=cost(0, 0),
        name="attended_rows",
    )(*arrays)


def section_at(i, k, sections):
    if sections & (sections - 1) == 0:
        return i ^ k
    return (i + k) % sections if isinstance(i, int) else lax.rem(i + k, sections)


def grad_kernel(pairs, per_kv, sections, first, last, *refs):
    blocks, weight_ref, refs = refs[: len(pairs)], refs[len(pairs)], refs[len(pairs) + 1 :]
    if not first:
        before_ref, refs = refs[0], refs[1:]
    if per_kv > 1:
        refs, sums = refs[:-1], refs[-1]
        sums[...] = jnp.zeros_like(sums)
    total = refs[-1]
    image_rows, width = total.shape
    heads = []
    for block, pair in zip(blocks, pairs):
        columns = head_columns(lax.div(partner_at(pair), per_kv))
        if per_kv == 1:
            heads.append((columns, block[...]))
        else:
            for half, k in enumerate(columns):
                part = block[:, half * HEAD_DIM : (half + 1) * HEAD_DIM]
                sums[:, k] += part.astype(F32)
    if per_kv > 1:
        heads = [((slice(None),), sums[...].astype(BF16))]
    span = 256
    for c in range(0, width, span):
        cols = slice(c, c + span)
        part = 0.0 if first else before_ref[:, cols]
        for columns, block in heads:
            weight = jnp.concatenate([weight_ref[0, cols, k] for k in columns], axis=1)
            part = part + dot_nt(block, weight)
        total[:, cols] = part
    if last:
        rows = image_rows // sections
        for k in range(sections):
            to = section_at(lax.axis_index("section"), k, sections)
            piece = total[pl.ds(pl.multiple_of(to * rows, rows), rows), :]
            refs[k][...] = piece.astype(refs[k].dtype)


def feature_gradient(blocks, weight, per_kv, sections, before=None, last=True):
    pairs, arrays = list(blocks), list(blocks.values())
    image_rows = arrays[0].shape[0]
    width, depth = weight.shape[1:]
    rows = image_rows // sections
    if last:
        out_shape = [
            jax.ShapeDtypeStruct((rows, width), F32 if k == 0 else BF16) for k in range(sections)
        ]
        out_specs = [whole()] * sections
        scratch = [pltpu.VMEM((image_rows, width), F32)]
    else:
        out_shape = jax.ShapeDtypeStruct((image_rows, width), F32)
        out_specs = whole()
        scratch = []
    if per_kv > 1:
        scratch.append(pltpu.VMEM((image_rows, depth), F32))
    operands = [*arrays, weight] + ([] if before is None else [before])
    return pl.pallas_call(
        functools.partial(grad_kernel, pairs, per_kv, sections, before is None, last),
        in_specs=[whole()] * len(operands),
        out_specs=out_specs,
        out_shape=out_shape,
        scratch_shapes=scratch,
        compiler_params=params(24),
        cost_estimate=cost(0, 0),
        name="feature_grad_last" if last else "feature_grad_first",
    )(*operands)


def shards(
    text, features, in_gain, w_query, q_gain, w_key_value, k_gain, tile_count, image_start, grad_out
):
    count = lax.axis_size("tensor")
    sections = lax.axis_size("section")
    per_kv = count // KV_HEADS

    def exchange(x, pair):
        return lax.ppermute(x, "tensor", [(i, i ^ pair[i % 2]) for i in range(count)])

    def swap(x):
        return exchange(x, (1, 1))

    bits = [1 << b for b in range(1, count.bit_length() - 1)]
    steps = len(bits)

    def distance(mask):
        taken = [s for s in range(steps) if mask >> s & 1]
        return sum(bits[s] for s in taken), sum(bits[steps - 1 - s] for s in taken)

    masks = range(1, 1 << steps)

    own_text = text[0]
    width = own_text.shape[1] // 2
    direct = {1 << s: exchange(own_text, distance(1 << s)) for s in range(steps)}

    def both_cores(blocks):
        out = {}
        for pair, x in blocks.items():
            out[pair] = [x]
            out[other_core(pair)] = [swap(x)]
        return out

    def places_of(blocks):
        return sorted(even for even, _ in blocks)

    def queries(blocks, name, **more):
        order = places_of(blocks)
        slots = [(order.index(even), order.index(odd)) for even, odd in blocks]
        groups = list(blocks.values())
        return queries_of(groups, slots, in_gain, w_query, q_gain, name, **more)

    kv_pairs = [distance(mask) for mask in range(1 << steps)]
    other_heads = kv_partial(features, w_key_value, per_kv, [other_core(pair) for pair in kv_pairs])
    other_heads = [swap(x) for x in other_heads]
    sums = kv_partial(features, w_key_value, per_kv, kv_pairs, other_heads)
    for step in range(steps):
        kept, came = sums[::2], [exchange(x, distance(1 << step)) for x in sums[1::2]]
        if step == 0:
            direct, came = lax.optimization_barrier((direct, came))
        if step < steps - 1:
            sums = kv_sum(kept, came)
    parts = [kept[0], came[0]]
    near = both_cores({(0, 0): own_text})
    scalars = (tile_count, image_start)
    q_near, *live = queries(near, "queries_own_chip", scalars=scalars)
    forwarded = []
    for first in (0, width):
        held = {mask: x[:, first : first + width] for mask, x in direct.items()}
        passed = {}
        for s in range(1, steps):
            for mask in range(1, 1 << s):
                more = mask | 1 << s
                held[more] = passed[distance(more)] = exchange(held[mask], distance(1 << s))
        forwarded.append(passed)

    next_to = both_cores({distance(mask): x for mask, x in direct.items()})
    q_next = queries(next_to, "queries_neighbours")

    early, *state = attention(
        live,
        [q_near, q_next],
        [places_of(near), places_of(next_to)],
        count,
        grad_out,
        k_gain,
        parts,
        last=False,
    )
    first_half, state = lax.optimization_barrier((forwarded[0], state))
    far = both_cores(first_half)
    second_half, far = lax.optimization_barrier((forwarded[1], far))
    sums = queries(far, "queries_forwarded_first")
    pieces = {pair: jnp.split(x, 2, axis=1) for pair, x in second_half.items()}
    far, rest = [both_cores({pair: x[i] for pair, x in pieces.items()}) for i in range(2)]
    sums = queries(far, "queries_forwarded_second", start=width, before=sums)
    q_far = queries(rest, "queries_forwarded_last", start=3 * width // 2, before=sums)
    far = places_of(far)
    late, block = attention(live, [q_far], [far], count, grad_out, k_gain, state, last=True)
    attended = assemble([places_of(near) + places_of(next_to), far], [early, late], grad_out)

    same_core = {(0, 0): block}
    same_core.update({distance(m): exchange(block, distance(m)) for m in reversed(masks)})
    swapped = {other_core(pair): swap(x) for pair, x in same_core.items()}
    before = None
    blocks = {**same_core, **swapped}
    if per_kv == 1:
        soon = {pair: blocks.pop(pair) for pair in [*same_core, (1, 1)]}
        before = feature_gradient(soon, w_key_value, per_kv, sections, last=False)
    pieces = feature_gradient(blocks, w_key_value, per_kv, sections, before)
    feature_grad, leaving = pieces[0], pieces[1:]
    arrived = []
    for k in range(sections - 1, 0, -1):
        perm = [(i, section_at(i, k, sections)) for i in range(sections)]
        arrived.append(lax.ppermute(leaving[k - 1], "section", perm))
    for x in arrived:
        feature_grad = feature_grad + x.astype(F32)
    return (attended, feature_grad)


def solution(mesh):
    return jax.shard_map(
        shards,
        mesh=mesh,
        in_specs=(
            P("section", "tensor", None),
            P(None, "tensor"),
            P("section", None),
            P("section", None, "tensor"),
            P("section", None),
            P("section", "tensor", None),
            P("section", None),
            P(),
            P(),
            P("section", None, "tensor"),
        ),
        out_specs=(P("section", None, "tensor"), P("section", "tensor")),
        check_vma=False,
    )
```

```python
import functools

import jax
import jax.numpy as jnp
from jax import lax
from jax.experimental import pallas as pl
from jax.experimental.pallas import tpu as pltpu
from jax.sharding import PartitionSpec as P

KV_HEADS = 8
HEAD_DIM = 128
TILES = 4
TILE_LEN = 24
TXT_TOK = 128
MB = 2
SLOTS = TILES * TILE_LEN

eps = 1e-05

F32 = jnp.float32
BF16 = jnp.bfloat16
MIB = 1 << 20


def whole(memory=pltpu.VMEM):
    return pl.BlockSpec(memory_space=memory)


def dot_nn(a, b):
    return jnp.dot(a, b, preferred_element_type=F32)


def dot_nt(a, b):
    return lax.dot_general(a, b, (((1,), (1,)), ((), ())), preferred_element_type=F32)


def dot_tn(a, b):
    return lax.dot_general(a, b, (((0,), (0,)), ((), ())), preferred_element_type=F32)


def params(mib):
    return pltpu.CompilerParams(vmem_limit_bytes=mib * MIB)


def cost(flops, size):
    return pl.CostEstimate(flops=flops, bytes_accessed=size, transcendentals=0)


def here():
    return lax.axis_index("tensor")


def of_core(pair):
    even, odd = pair
    return even if even == odd else even + lax.rem(here(), 2) * (odd - even)


def partner_at(pair):
    return lax.bitwise_xor(here(), of_core(pair))


def other_core(pair):
    return (1 ^ pair[1], 1 ^ pair[0])


def head_columns(head):
    return [
        pl.ds(pl.multiple_of((half * KV_HEADS + head) * HEAD_DIM, HEAD_DIM), HEAD_DIM)
        for half in range(2)
    ]


def kv_kernel(per_kv, pairs, feat_ref, weight_ref, *refs):
    features = feat_ref[...]
    for j, pair in enumerate(pairs):
        head = lax.div(partner_at(pair), per_kv)
        weight = jnp.concatenate([weight_ref[0, :, c] for c in head_columns(head)], axis=1)
        total = dot_nn(features, weight)
        out_ref = refs[j - len(pairs)]
        if len(refs) > len(pairs):
            total = total + refs[j][...]
        out_ref[...] = total.astype(out_ref.dtype)


def kv_partial(features, weight, per_kv, pairs, other=()):
    operands = (features, weight, *other)
    shape = (features.shape[0], 2 * HEAD_DIM)
    return pl.pallas_call(
        functools.partial(kv_kernel, per_kv, pairs),
        in_specs=[whole()] * len(operands),
        out_specs=[whole()] * len(pairs),
        out_shape=[
            jax.ShapeDtypeStruct(shape, BF16 if other and j % 2 else F32)
            for j in range(len(pairs))
        ],
        compiler_params=params(24),
        cost_estimate=cost(0, 0),
        name="kv_partial_own_core" if other else "kv_partial_other_core",
    )(*operands)


def kv_sum_kernel(*refs):
    size = len(refs) // 3
    for kept_ref, came_ref, out_ref in zip(refs, refs[size:], refs[2 * size :]):
        total = kept_ref[...] + came_ref[...].astype(F32)
        out_ref[...] = total.astype(out_ref.dtype)


def kv_sum(kept, came):
    return pl.pallas_call(
        kv_sum_kernel,
        in_specs=[whole()] * (2 * len(kept)),
        out_specs=[whole()] * len(kept),
        out_shape=[
            jax.ShapeDtypeStruct(x.shape, BF16 if i % 2 else F32) for i, x in enumerate(kept)
        ],
        compiler_params=params(24),
        cost_estimate=cost(0, 0),
        name="kv_sum",
    )(*kept, *came)


def live_masks(count_ref, start_ref, token_ref, slot_ref):
    for b in range(MB):
        token = lax.broadcasted_iota(jnp.int32, (TXT_TOK, HEAD_DIM), 0)
        token_ref[b * TXT_TOK : (b + 1) * TXT_TOK, :] = (token >= start_ref[b]).astype(F32)
        slot = lax.broadcasted_iota(jnp.int32, slot_ref.shape[1:], 1)
        slot_ref[b] = (slot < count_ref[b] * TILE_LEN).astype(F32)


def query_kernel(shape, slots, start, scalars, scratch, *refs):
    if scalars:
        end = len(refs) - scratch
        live_masks(refs[0], refs[1], refs[end - 2], refs[end - 1])
        refs = refs[2 : end - 2] + refs[end:]
    gain_ref, weight_ref, q_gain_ref, refs = refs[0], refs[1], refs[2], refs[3:]
    groups = []
    for parts in shape:
        groups.append(refs[:parts])
        refs = refs[parts:]
    depth, heads_width = weight_ref.shape[1:]
    width = sum(part.shape[1] for part in groups[0])
    last = start + width == depth
    span = 1024 if width % 1024 == 0 else 512

    def columns(parts, c):
        for part in parts:
            if c < part.shape[1]:
                return part[:, c : c + span].astype(F32)
            c -= part.shape[1]

    if start:
        raw, squares, refs = refs[0][...], refs[1][:, :1], refs[2:]
    else:
        raw, squares = 0.0, 0.0
    for c in range(0, width, span):
        x = jnp.concatenate([columns(parts, c) for parts in groups], axis=0)
        squares = squares + jnp.sum(x * x, axis=-1, keepdims=True)
        cols = slice(start + c, start + c + span)
        scaled = (x * gain_ref[:, cols].astype(F32)).astype(BF16)
        raw = raw + dot_nn(scaled, weight_ref[0, cols, :])
    if not last:
        refs[0][...] = raw
        refs[1][...] = jnp.broadcast_to(squares, refs[1].shape)
        return
    out_ref = refs[-1]
    rows = groups[0][0].shape[0]
    inverse = lax.rsqrt(squares / depth + eps)
    q_gain = q_gain_ref[...].astype(F32)
    for c in range(0, heads_width, HEAD_DIM):
        head = raw[:, c : c + HEAD_DIM] * inverse
        q_inverse = lax.rsqrt(jnp.mean(head * head, axis=-1, keepdims=True) + eps)
        head = head * q_inverse * q_gain
        for i, pair in enumerate(slots):
            at = of_core(pair) * rows
            if pair[0] != pair[1]:
                at = pl.multiple_of(at, rows)
            part = head[i * rows : (i + 1) * rows]
            out_ref[pl.ds(at, rows), c : c + HEAD_DIM] = part.astype(out_ref.dtype)
    if len(refs) > 1:
        refs[0][...] = out_ref[...].astype(BF16)


def queries_of(groups, slots, gain, weight, q_gain, name, start=0, before=(), scalars=()):
    arrays = [part for parts in groups for part in parts]
    rows = sum(parts[0].shape[0] for parts in groups)
    depth, heads_width = weight.shape[1:]
    last = start + sum(part.shape[1] for part in groups[0]) == depth
    scratch = []
    if last:
        out_shape = [jax.ShapeDtypeStruct((rows, heads_width), BF16)]
        if arrays[0].shape[0] % 16 != 0:
            scratch.append(pltpu.VMEM((rows, heads_width), F32))
        if scalars:
            out_shape.append(jax.ShapeDtypeStruct((MB * TXT_TOK, HEAD_DIM), F32))
            out_shape.append(jax.ShapeDtypeStruct((MB, 8, SLOTS), F32))
    else:
        out_shape = [jax.ShapeDtypeStruct((rows, w), F32) for w in (heads_width, HEAD_DIM)]
    out = pl.pallas_call(
        functools.partial(
            query_kernel,
            [len(parts) for parts in groups],
            slots,
            start,
            len(scalars),
            len(scratch),
        ),
        in_specs=[whole(pltpu.SMEM)] * len(scalars)
        + [whole()] * (3 + len(arrays) + len(before)),
        out_specs=[whole()] * len(out_shape),
        out_shape=out_shape,
        scratch_shapes=scratch,
        compiler_params=params(24),
        cost_estimate=cost(0, 0),
        name=name,
    )(*scalars, gain, weight, q_gain, *arrays, *before)
    return out[0] if last and not scalars else out


def attention_kernel(places, count, rows, last, sizes, *refs):
    token_ref, slot_ref, refs = refs[0], refs[1], refs[2:]
    queries_refs, refs = refs[:sizes], refs[sizes:]
    grad_ref, k_gain_ref, refs = refs[0], refs[1], refs[2:]
    narrow = rows % 16 != 0
    if narrow:
        refs, grad_rows = refs[:-1], refs[-1]
        grad_rows[...] = grad_ref[0].astype(F32)
    if last:
        d_keys_in, d_values_in, keys_ref, values_ref, hat_ref, inverse_ref = refs[:6]
        att_ref, block_ref, d_keys_ref, d_values_ref = refs[6:]
        d_keys_ref[...] = d_keys_in[...]
        d_values_ref[...] = d_values_in[...]
    else:
        parts = refs[:-7]
        att_ref, d_keys_ref, d_values_ref, keys_ref, values_ref, hat_ref, inverse_ref = refs[-7:]
        kv = sum(part[...].astype(F32) for part in parts)
        key_raw = kv[:, :HEAD_DIM]
        inverse = lax.rsqrt(jnp.mean(key_raw * key_raw, axis=-1, keepdims=True) + eps)
        hat_ref[...] = key_raw * inverse
        inverse_ref[...] = jnp.broadcast_to(inverse, key_raw.shape)
        keys_ref[...] = (key_raw * inverse * k_gain_ref[...].astype(F32)).astype(BF16)
        values_ref[...] = kv[:, HEAD_DIM:].astype(BF16)
        d_keys_ref[...] = jnp.zeros_like(d_keys_ref)
        d_values_ref[...] = jnp.zeros_like(d_values_ref)

    scale = HEAD_DIM ** (-0.5)
    heads = grad_ref.shape[2] // HEAD_DIM
    per_sample = count // MB
    mine = lax.div(here(), per_sample)
    blocks = [
        (p, ref, i * rows) for group, ref in zip(places, queries_refs) for i, p in enumerate(group)
    ]
    for far in range(MB):
        chosen = [block for block in blocks if block[0] // per_sample == far]
        if not chosen:
            continue
        sample = lax.bitwise_xor(mine, far)
        img = pl.ds(pl.multiple_of(sample * SLOTS, SLOTS), SLOTS)
        keys, values = keys_ref[img, :], values_ref[img, :]
        live = slot_ref[sample][:1, :] > 0
        spots = [
            pl.ds(pl.multiple_of(lax.bitwise_xor(here(), p) * rows, rows), rows)
            for p, _, _ in chosen
        ]
        masks = [token_ref[spot, :] for spot in spots]
        queries, upstream = [], []
        for h in range(heads):
            cols = slice(h * HEAD_DIM, (h + 1) * HEAD_DIM)
            for (p, ref, at), mask, spot in zip(chosen, masks, spots):
                queries.append(ref[at : at + rows, cols])
                grad = grad_rows[spot, cols] if narrow else grad_ref[0, spot, cols].astype(F32)
                upstream.append((grad * mask).astype(BF16))
        queries = jnp.concatenate(queries, axis=0)
        upstream = jnp.concatenate(upstream, axis=0)
        scores = dot_nt(queries, keys) * scale
        exponent = jnp.where(live, jnp.exp(scores), 0.0)
        probs = exponent * (1.0 / jnp.sum(exponent, axis=-1, keepdims=True))
        weights = probs.astype(BF16)
        head_out = dot_nn(weights, values)
        step = 0
        for h in range(heads):
            cols = slice(h * HEAD_DIM, (h + 1) * HEAD_DIM)
            for block, mask in zip(chosen, masks):
                at = blocks.index(block) * rows
                att_ref[at : at + rows, cols] = head_out[step : step + rows] * mask
                step += rows
        d_weights = dot_nt(upstream, values)
        inner = jnp.sum(probs * d_weights, axis=-1, keepdims=True)
        d_scores = (probs * (d_weights - inner) * scale).astype(BF16)
        d_keys_ref[img, :] += dot_tn(d_scores, queries)
        d_values_ref[img, :] += dot_tn(weights, upstream)
    if last:
        hat = hat_ref[...]
        scaled = d_keys_ref[...] * k_gain_ref[...].astype(F32)
        d_raw = inverse_ref[...] * (
            scaled - hat * jnp.mean(hat * scaled, axis=-1, keepdims=True)
        )
        block_ref[:, :HEAD_DIM] = d_raw.astype(BF16)
        block_ref[:, HEAD_DIM:] = d_values_ref[...].astype(BF16)


def attention(live, queries, places, count, grad_out, k_gain, state, last):
    rows, width = grad_out.shape[1] // count, grad_out.shape[2]
    image_rows = MB * SLOTS
    vector = jax.ShapeDtypeStruct((image_rows, HEAD_DIM), F32)
    rounded = jax.ShapeDtypeStruct((image_rows, HEAD_DIM), BF16)
    attended = jax.ShapeDtypeStruct((sum(map(len, places)) * rows, width), F32)
    scratch = []
    if last:
        out_shape = [attended, jax.ShapeDtypeStruct((image_rows, 2 * HEAD_DIM), BF16)]
        scratch += [pltpu.VMEM(vector.shape, F32)] * 2
    else:
        out_shape = [attended, vector, vector, rounded, rounded, vector, vector]
    if rows % 16 != 0:
        scratch += [pltpu.VMEM(grad_out.shape[1:], F32)]
    operands = [*queries, grad_out, k_gain, *state]
    return pl.pallas_call(
        functools.partial(attention_kernel, places, count, rows, last, len(queries)),
        in_specs=[whole()] * (2 + len(operands)),
        out_specs=[whole()] * len(out_shape),
        out_shape=out_shape,
        scratch_shapes=scratch,
        compiler_params=params(24),
        cost_estimate=cost(0, 0),
        name="attention_last" if last else "attention_first",
    )(*live, *operands)


def assemble_kernel(places, rows, *refs):
    refs, out_ref, held = refs[:-2], refs[-2], refs[-1]
    for group, ref in zip(places, refs):
        for i, p in enumerate(group):
            at = pl.multiple_of(lax.bitwise_xor(here(), p) * rows, rows)
            held[pl.ds(at, rows), :] = ref[i * rows : (i + 1) * rows, :]
    out_ref[0] = held[...].astype(BF16)


def assemble(places, arrays, like):
    rows = arrays[0].shape[0] // len(places[0])
    return pl.pallas_call(
        functools.partial(assemble_kernel, places, rows),
        in_specs=[whole()] * len(arrays),
        out_specs=whole(),
        out_shape=jax.ShapeDtypeStruct(like.shape, BF16),
        scratch_shapes=[pltpu.VMEM(like.shape[1:], F32)],
        compiler_params=params(24),
        cost_estimate=cost(0, 0),
        name="attended_rows",
    )(*arrays)


def grad_kernel(pairs, per_kv, sections, first, last, *refs):
    blocks, weight_ref, refs = refs[: len(pairs)], refs[len(pairs)], refs[len(pairs) + 1 :]
    if not first:
        before_ref, refs = refs[0], refs[1:]
    if per_kv > 1:
        refs, sums = refs[:-1], refs[-1]
        sums[...] = jnp.zeros_like(sums)
    total = refs[-1]
    image_rows, width = total.shape
    heads = []
    for block, pair in zip(blocks, pairs):
        columns = head_columns(lax.div(partner_at(pair), per_kv))
        if per_kv == 1:
            heads.append((columns, block[...]))
        else:
            for half, k in enumerate(columns):
                part = block[:, half * HEAD_DIM : (half + 1) * HEAD_DIM]
                sums[:, k] += part.astype(F32)
    if per_kv > 1:
        heads = [((slice(None),), sums[...].astype(BF16))]
    span = 256
    for c in range(0, width, span):
        cols = slice(c, c + span)
        part = 0.0 if first else before_ref[:, cols]
        for columns, block in heads:
            weight = jnp.concatenate([weight_ref[0, cols, k] for k in columns], axis=1)
            part = part + dot_nt(block, weight)
        total[:, cols] = part
    if last:
        rows = image_rows // sections
        for k in range(sections):
            to = lax.rem(lax.axis_index("section") + k, sections)
            piece = total[pl.ds(pl.multiple_of(to * rows, rows), rows), :]
            refs[k][...] = piece.astype(refs[k].dtype)


def feature_gradient(blocks, weight, per_kv, sections, before=None, last=True):
    pairs, arrays = list(blocks), list(blocks.values())
    image_rows = arrays[0].shape[0]
    width, depth = weight.shape[1:]
    rows = image_rows // sections
    if last:
        out_shape = [
            jax.ShapeDtypeStruct((rows, width), F32 if k == 0 else BF16) for k in range(sections)
        ]
        out_specs = [whole()] * sections
        scratch = [pltpu.VMEM((image_rows, width), F32)]
    else:
        out_shape = jax.ShapeDtypeStruct((image_rows, width), F32)
        out_specs = whole()
        scratch = []
    if per_kv > 1:
        scratch.append(pltpu.VMEM((image_rows, depth), F32))
    operands = [*arrays, weight] + ([] if before is None else [before])
    return pl.pallas_call(
        functools.partial(grad_kernel, pairs, per_kv, sections, before is None, last),
        in_specs=[whole()] * len(operands),
        out_specs=out_specs,
        out_shape=out_shape,
        scratch_shapes=scratch,
        compiler_params=params(24),
        cost_estimate=cost(0, 0),
        name="feature_grad_last" if last else "feature_grad_first",
    )(*operands)


def shards(
    text, features, in_gain, w_query, q_gain, w_key_value, k_gain, tile_count, image_start, grad_out
):
    count = lax.axis_size("tensor")
    sections = lax.axis_size("section")
    per_kv = count // KV_HEADS

    def exchange(x, pair):
        return lax.ppermute(x, "tensor", [(i, i ^ pair[i % 2]) for i in range(count)])

    def swap(x):
        return exchange(x, (1, 1))

    bits = [1 << b for b in range(1, count.bit_length() - 1)]
    steps = len(bits)

    def distance(mask):
        taken = [s for s in range(steps) if mask >> s & 1]
        return sum(bits[s] for s in taken), sum(bits[steps - 1 - s] for s in taken)

    masks = range(1, 1 << steps)

    own_text = text[0]
    depth = own_text.shape[1]
    cuts = (0, depth * 7 // 16, depth * 3 // 4, depth)
    direct = {1 << s: exchange(own_text, distance(1 << s)) for s in range(steps)}

    def both_cores(blocks):
        out = {}
        for pair, x in blocks.items():
            out[pair] = [x]
            out[other_core(pair)] = [swap(x)]
        return out

    def places_of(blocks):
        return sorted(even for even, _ in blocks)

    def queries(blocks, name, **more):
        order = places_of(blocks)
        slots = [(order.index(even), order.index(odd)) for even, odd in blocks]
        groups = list(blocks.values())
        return queries_of(groups, slots, in_gain, w_query, q_gain, name, **more)

    kv_pairs = [distance(mask) for mask in range(1 << steps)]
    other_heads = kv_partial(features, w_key_value, per_kv, [other_core(pair) for pair in kv_pairs])
    other_heads = [swap(x) for x in other_heads]
    sums = kv_partial(features, w_key_value, per_kv, kv_pairs, other_heads)
    for step in range(steps):
        kept, came = sums[::2], [exchange(x, distance(1 << step)) for x in sums[1::2]]
        if step == 0:
            direct, came = lax.optimization_barrier((direct, came))
        if step < steps - 1:
            sums = kv_sum(kept, came)
    parts = [kept[0], came[0]]
    near = both_cores({(0, 0): own_text})
    scalars = (tile_count, image_start)
    q_near, *live = queries(near, "queries_own_chip", scalars=scalars)
    forwarded = []
    for first, last in ((0, cuts[1]), (cuts[1], depth)):
        held = {mask: x[:, first:last] for mask, x in direct.items()}
        passed = {}
        for s in range(1, steps):
            for mask in range(1, 1 << s):
                more = mask | 1 << s
                held[more] = passed[distance(more)] = exchange(held[mask], distance(1 << s))
        forwarded.append(passed)

    next_to = both_cores({distance(mask): x for mask, x in direct.items()})
    q_next = queries(next_to, "queries_neighbours")

    first_half, parts, q_near, q_next = lax.optimization_barrier(
        (forwarded[0], parts, q_near, q_next)
    )
    far = both_cores(first_half)
    sums = queries(far, "queries_forwarded_first")
    early, *state = attention(
        live,
        [q_near, q_next],
        [places_of(near), places_of(next_to)],
        count,
        grad_out,
        k_gain,
        parts,
        last=False,
    )
    second_half, sums, state = lax.optimization_barrier((forwarded[1], sums, state))
    split = cuts[2] - cuts[1]
    pieces = {pair: (x[:, :split], x[:, split:]) for pair, x in second_half.items()}
    far, rest = [both_cores({pair: x[i] for pair, x in pieces.items()}) for i in range(2)]
    sums = queries(far, "queries_forwarded_second", start=cuts[1], before=sums)
    q_far = queries(rest, "queries_forwarded_last", start=cuts[2], before=sums)
    far = places_of(far)
    late, block = attention(live, [q_far], [far], count, grad_out, k_gain, state, last=True)
    attended = assemble([places_of(near) + places_of(next_to), far], [early, late], grad_out)

    same_core = {(0, 0): block}
    same_core.update({distance(m): exchange(block, distance(m)) for m in reversed(masks)})
    swapped = {other_core(pair): swap(x) for pair, x in same_core.items()}
    before = None
    blocks = {**same_core, **swapped}
    if per_kv == 1:
        soon = {pair: blocks.pop(pair) for pair in [*same_core, (1, 1)]}
        before = feature_gradient(soon, w_key_value, per_kv, sections, last=False)
    pieces = feature_gradient(blocks, w_key_value, per_kv, sections, before)
    feature_grad, leaving = pieces[0], pieces[1:]
    arrived = []
    for k in range(1, sections):
        perm = [(i, (i + k) % sections) for i in range(sections)]
        arrived.append(lax.ppermute(leaving[k - 1], "section", perm))
    for x in arrived:
        feature_grad = feature_grad + x.astype(F32)
    return (attended, feature_grad)


def solution(mesh):
    return jax.shard_map(
        shards,
        mesh=mesh,
        in_specs=(
            P("section", "tensor", None),
            P(None, "tensor"),
            P("section", None),
            P("section", None, "tensor"),
            P("section", None),
            P("section", "tensor", None),
            P("section", None),
            P(),
            P(),
            P("section", None, "tensor"),
        ),
        out_specs=(P("section", None, "tensor"), P("section", "tensor")),
        check_vma=False,
    )
```

```python
import functools

import jax
import jax.numpy as jnp
from jax import lax
from jax.experimental import pallas as pl
from jax.experimental.pallas import tpu as pltpu
from jax.sharding import PartitionSpec as P

KV_HEADS = 8
HEAD_DIM = 128
TILES = 4
TILE_LEN = 24
TXT_TOK = 128
MB = 2
SLOTS = TILES * TILE_LEN

eps = 1e-05

F32 = jnp.float32
BF16 = jnp.bfloat16
MIB = 1 << 20


def whole(memory=pltpu.VMEM):
    return pl.BlockSpec(memory_space=memory)


def dot_nn(a, b):
    return jnp.dot(a, b, preferred_element_type=F32)


def dot_nt(a, b):
    return lax.dot_general(a, b, (((1,), (1,)), ((), ())), preferred_element_type=F32)


def dot_tn(a, b):
    return lax.dot_general(a, b, (((0,), (0,)), ((), ())), preferred_element_type=F32)


def params(mib):
    return pltpu.CompilerParams(vmem_limit_bytes=mib * MIB)


def cost(flops, size):
    return pl.CostEstimate(flops=flops, bytes_accessed=size, transcendentals=0)


def here():
    return lax.axis_index("tensor")


def of_core(pair):
    even, odd = pair
    return even if even == odd else even + lax.rem(here(), 2) * (odd - even)


def partner_at(pair):
    return lax.bitwise_xor(here(), of_core(pair))


def other_core(pair):
    return (1 ^ pair[1], 1 ^ pair[0])


def head_columns(head):
    return [
        pl.ds(pl.multiple_of((half * KV_HEADS + head) * HEAD_DIM, HEAD_DIM), HEAD_DIM)
        for half in range(2)
    ]


def kv_kernel(per_kv, pairs, feat_ref, weight_ref, *refs):
    features = feat_ref[...]
    for j, pair in enumerate(pairs):
        head = lax.div(partner_at(pair), per_kv)
        weight = jnp.concatenate([weight_ref[0, :, c] for c in head_columns(head)], axis=1)
        total = dot_nn(features, weight)
        out_ref = refs[j - len(pairs)]
        if len(refs) > len(pairs):
            total = total + refs[j][...]
        out_ref[...] = total.astype(out_ref.dtype)


def kv_partial(features, weight, per_kv, pairs, other=()):
    operands = (features, weight, *other)
    shape = (features.shape[0], 2 * HEAD_DIM)
    return pl.pallas_call(
        functools.partial(kv_kernel, per_kv, pairs),
        in_specs=[whole()] * len(operands),
        out_specs=[whole()] * len(pairs),
        out_shape=[
            jax.ShapeDtypeStruct(shape, BF16 if other and j % 2 else F32)
            for j in range(len(pairs))
        ],
        compiler_params=params(24),
        cost_estimate=cost(0, 0),
        name="kv_partial_own_core" if other else "kv_partial_other_core",
    )(*operands)


def kv_sum_kernel(*refs):
    size = len(refs) // 3
    for kept_ref, came_ref, out_ref in zip(refs, refs[size:], refs[2 * size :]):
        total = kept_ref[...] + came_ref[...].astype(F32)
        out_ref[...] = total.astype(out_ref.dtype)


def kv_sum(kept, came):
    return pl.pallas_call(
        kv_sum_kernel,
        in_specs=[whole()] * (2 * len(kept)),
        out_specs=[whole()] * len(kept),
        out_shape=[
            jax.ShapeDtypeStruct(x.shape, BF16 if i % 2 else F32) for i, x in enumerate(kept)
        ],
        compiler_params=params(24),
        cost_estimate=cost(0, 0),
        name="kv_sum",
    )(*kept, *came)


def live_masks(count_ref, start_ref, token_ref, slot_ref):
    for b in range(MB):
        token = lax.broadcasted_iota(jnp.int32, (TXT_TOK, HEAD_DIM), 0)
        token_ref[b * TXT_TOK : (b + 1) * TXT_TOK, :] = (token >= start_ref[b]).astype(F32)
        slot = lax.broadcasted_iota(jnp.int32, slot_ref.shape[1:], 1)
        slot_ref[b] = (slot < count_ref[b] * TILE_LEN).astype(F32)


def query_kernel(shape, slots, start, scalars, scratch, *refs):
    if scalars:
        end = len(refs) - scratch
        live_masks(refs[0], refs[1], refs[end - 2], refs[end - 1])
        refs = refs[2 : end - 2] + refs[end:]
    gain_ref, weight_ref, q_gain_ref, refs = refs[0], refs[1], refs[2], refs[3:]
    groups = []
    for parts in shape:
        groups.append(refs[:parts])
        refs = refs[parts:]
    depth, heads_width = weight_ref.shape[1:]
    width = sum(part.shape[1] for part in groups[0])
    last = start + width == depth
    span = 1024 if width % 1024 == 0 else 512

    def columns(parts, c):
        for part in parts:
            if c < part.shape[1]:
                return part[:, c : c + span].astype(F32)
            c -= part.shape[1]

    if start:
        raw, squares, refs = refs[0][...], refs[1][:, :1], refs[2:]
    else:
        raw, squares = 0.0, 0.0
    for c in range(0, width, span):
        x = jnp.concatenate([columns(parts, c) for parts in groups], axis=0)
        squares = squares + jnp.sum(x * x, axis=-1, keepdims=True)
        cols = slice(start + c, start + c + span)
        scaled = (x * gain_ref[:, cols].astype(F32)).astype(BF16)
        raw = raw + dot_nn(scaled, weight_ref[0, cols, :])
    if not last:
        refs[0][...] = raw
        refs[1][...] = jnp.broadcast_to(squares, refs[1].shape)
        return
    out_ref = refs[-1]
    rows = groups[0][0].shape[0]
    inverse = lax.rsqrt(squares / depth + eps)
    q_gain = q_gain_ref[...].astype(F32)
    for c in range(0, heads_width, HEAD_DIM):
        head = raw[:, c : c + HEAD_DIM] * inverse
        q_inverse = lax.rsqrt(jnp.mean(head * head, axis=-1, keepdims=True) + eps)
        head = head * q_inverse * q_gain
        for i, pair in enumerate(slots):
            at = of_core(pair) * rows
            if pair[0] != pair[1]:
                at = pl.multiple_of(at, rows)
            part = head[i * rows : (i + 1) * rows]
            out_ref[pl.ds(at, rows), c : c + HEAD_DIM] = part.astype(out_ref.dtype)
    if len(refs) > 1:
        refs[0][...] = out_ref[...].astype(BF16)


def queries_of(groups, slots, gain, weight, q_gain, name, start=0, before=(), scalars=()):
    arrays = [part for parts in groups for part in parts]
    rows = sum(parts[0].shape[0] for parts in groups)
    depth, heads_width = weight.shape[1:]
    last = start + sum(part.shape[1] for part in groups[0]) == depth
    scratch = []
    if last:
        out_shape = [jax.ShapeDtypeStruct((rows, heads_width), BF16)]
        if arrays[0].shape[0] % 16 != 0:
            scratch.append(pltpu.VMEM((rows, heads_width), F32))
        if scalars:
            out_shape.append(jax.ShapeDtypeStruct((MB * TXT_TOK, HEAD_DIM), F32))
            out_shape.append(jax.ShapeDtypeStruct((MB, 8, SLOTS), F32))
    else:
        out_shape = [jax.ShapeDtypeStruct((rows, w), F32) for w in (heads_width, HEAD_DIM)]
    out = pl.pallas_call(
        functools.partial(
            query_kernel,
            [len(parts) for parts in groups],
            slots,
            start,
            len(scalars),
            len(scratch),
        ),
        in_specs=[whole(pltpu.SMEM)] * len(scalars)
        + [whole()] * (3 + len(arrays) + len(before)),
        out_specs=[whole()] * len(out_shape),
        out_shape=out_shape,
        scratch_shapes=scratch,
        compiler_params=params(24),
        cost_estimate=cost(0, 0),
        name=name,
    )(*scalars, gain, weight, q_gain, *arrays, *before)
    return out[0] if last and not scalars else out


def attention_kernel(places, count, rows, last, sizes, *refs):
    token_ref, slot_ref, refs = refs[0], refs[1], refs[2:]
    queries_refs, refs = refs[:sizes], refs[sizes:]
    grad_ref, k_gain_ref, refs = refs[0], refs[1], refs[2:]
    narrow = rows % 16 != 0
    if narrow:
        refs, grad_rows = refs[:-1], refs[-1]
        grad_rows[...] = grad_ref[0].astype(F32)
    if last:
        d_keys_in, d_values_in, keys_ref, values_ref, hat_ref, inverse_ref = refs[:6]
        att_ref, block_ref, d_keys_ref, d_values_ref = refs[6:]
        d_keys_ref[...] = d_keys_in[...]
        d_values_ref[...] = d_values_in[...]
    else:
        parts = refs[:-7]
        att_ref, d_keys_ref, d_values_ref, keys_ref, values_ref, hat_ref, inverse_ref = refs[-7:]
        kv = sum(part[...].astype(F32) for part in parts)
        key_raw = kv[:, :HEAD_DIM]
        inverse = lax.rsqrt(jnp.mean(key_raw * key_raw, axis=-1, keepdims=True) + eps)
        hat_ref[...] = key_raw * inverse
        inverse_ref[...] = jnp.broadcast_to(inverse, key_raw.shape)
        keys_ref[...] = (key_raw * inverse * k_gain_ref[...].astype(F32)).astype(BF16)
        values_ref[...] = kv[:, HEAD_DIM:].astype(BF16)
        d_keys_ref[...] = jnp.zeros_like(d_keys_ref)
        d_values_ref[...] = jnp.zeros_like(d_values_ref)

    scale = HEAD_DIM ** (-0.5)
    heads = grad_ref.shape[2] // HEAD_DIM
    per_sample = count // MB
    mine = lax.div(here(), per_sample)
    blocks = [
        (p, ref, i * rows) for group, ref in zip(places, queries_refs) for i, p in enumerate(group)
    ]
    for far in range(MB):
        chosen = [block for block in blocks if block[0] // per_sample == far]
        if not chosen:
            continue
        sample = lax.bitwise_xor(mine, far)
        img = pl.ds(pl.multiple_of(sample * SLOTS, SLOTS), SLOTS)
        keys, values = keys_ref[img, :], values_ref[img, :]
        live = slot_ref[sample][:1, :] > 0
        spots = [
            pl.ds(pl.multiple_of(lax.bitwise_xor(here(), p) * rows, rows), rows)
            for p, _, _ in chosen
        ]
        masks = [token_ref[spot, :] for spot in spots]
        queries, upstream = [], []
        for h in range(heads):
            cols = slice(h * HEAD_DIM, (h + 1) * HEAD_DIM)
            for (p, ref, at), mask, spot in zip(chosen, masks, spots):
                queries.append(ref[at : at + rows, cols])
                grad = grad_rows[spot, cols] if narrow else grad_ref[0, spot, cols].astype(F32)
                upstream.append((grad * mask).astype(BF16))
        queries = jnp.concatenate(queries, axis=0)
        upstream = jnp.concatenate(upstream, axis=0)
        scores = dot_nt(queries, keys) * scale
        exponent = jnp.where(live, jnp.exp(scores), 0.0)
        probs = exponent * (1.0 / jnp.sum(exponent, axis=-1, keepdims=True))
        weights = probs.astype(BF16)
        head_out = dot_nn(weights, values)
        step = 0
        for h in range(heads):
            cols = slice(h * HEAD_DIM, (h + 1) * HEAD_DIM)
            for block, mask in zip(chosen, masks):
                at = blocks.index(block) * rows
                att_ref[at : at + rows, cols] = head_out[step : step + rows] * mask
                step += rows
        d_weights = dot_nt(upstream, values)
        inner = jnp.sum(probs * d_weights, axis=-1, keepdims=True)
        d_scores = (probs * (d_weights - inner) * scale).astype(BF16)
        d_keys_ref[img, :] += dot_tn(d_scores, queries)
        d_values_ref[img, :] += dot_tn(weights, upstream)
    if last:
        hat = hat_ref[...]
        scaled = d_keys_ref[...] * k_gain_ref[...].astype(F32)
        d_raw = inverse_ref[...] * (
            scaled - hat * jnp.mean(hat * scaled, axis=-1, keepdims=True)
        )
        block_ref[:, :HEAD_DIM] = d_raw.astype(BF16)
        block_ref[:, HEAD_DIM:] = d_values_ref[...].astype(BF16)


def attention(live, queries, places, count, grad_out, k_gain, state, last):
    rows, width = grad_out.shape[1] // count, grad_out.shape[2]
    image_rows = MB * SLOTS
    vector = jax.ShapeDtypeStruct((image_rows, HEAD_DIM), F32)
    rounded = jax.ShapeDtypeStruct((image_rows, HEAD_DIM), BF16)
    attended = jax.ShapeDtypeStruct((sum(map(len, places)) * rows, width), F32)
    scratch = []
    if last:
        out_shape = [attended, jax.ShapeDtypeStruct((image_rows, 2 * HEAD_DIM), BF16)]
        scratch += [pltpu.VMEM(vector.shape, F32)] * 2
    else:
        out_shape = [attended, vector, vector, rounded, rounded, vector, vector]
    if rows % 16 != 0:
        scratch += [pltpu.VMEM(grad_out.shape[1:], F32)]
    operands = [*queries, grad_out, k_gain, *state]
    return pl.pallas_call(
        functools.partial(attention_kernel, places, count, rows, last, len(queries)),
        in_specs=[whole()] * (2 + len(operands)),
        out_specs=[whole()] * len(out_shape),
        out_shape=out_shape,
        scratch_shapes=scratch,
        compiler_params=params(24),
        cost_estimate=cost(0, 0),
        name="attention_last" if last else "attention_first",
    )(*live, *operands)


def assemble_kernel(places, rows, *refs):
    refs, out_ref, held = refs[:-2], refs[-2], refs[-1]
    for group, ref in zip(places, refs):
        for i, p in enumerate(group):
            at = pl.multiple_of(lax.bitwise_xor(here(), p) * rows, rows)
            held[pl.ds(at, rows), :] = ref[i * rows : (i + 1) * rows, :]
    out_ref[0] = held[...].astype(BF16)


def assemble(places, arrays, like):
    rows = arrays[0].shape[0] // len(places[0])
    return pl.pallas_call(
        functools.partial(assemble_kernel, places, rows),
        in_specs=[whole()] * len(arrays),
        out_specs=whole(),
        out_shape=jax.ShapeDtypeStruct(like.shape, BF16),
        scratch_shapes=[pltpu.VMEM(like.shape[1:], F32)],
        compiler_params=params(24),
        cost_estimate=cost(0, 0),
        name="attended_rows",
    )(*arrays)


def grad_kernel(pairs, per_kv, sections, first, last, *refs):
    blocks, weight_ref, refs = refs[: len(pairs)], refs[len(pairs)], refs[len(pairs) + 1 :]
    if not first:
        before_ref, refs = refs[0], refs[1:]
    if per_kv > 1:
        refs, sums = refs[:-1], refs[-1]
        sums[...] = jnp.zeros_like(sums)
    total = refs[-1]
    image_rows, width = total.shape
    heads = []
    for block, pair in zip(blocks, pairs):
        columns = head_columns(lax.div(partner_at(pair), per_kv))
        if per_kv == 1:
            heads.append((columns, block[...]))
        else:
            for half, k in enumerate(columns):
                part = block[:, half * HEAD_DIM : (half + 1) * HEAD_DIM]
                sums[:, k] += part.astype(F32)
    if per_kv > 1:
        heads = [((slice(None),), sums[...].astype(BF16))]
    span = 256
    for c in range(0, width, span):
        cols = slice(c, c + span)
        part = 0.0 if first else before_ref[:, cols]
        for columns, block in heads:
            weight = jnp.concatenate([weight_ref[0, cols, k] for k in columns], axis=1)
            part = part + dot_nt(block, weight)
        total[:, cols] = part
    if last:
        rows = image_rows // sections
        for k in range(sections):
            to = lax.rem(lax.axis_index("section") + k, sections)
            piece = total[pl.ds(pl.multiple_of(to * rows, rows), rows), :]
            refs[k][...] = piece.astype(refs[k].dtype)


def feature_gradient(blocks, weight, per_kv, sections, before=None, last=True):
    pairs, arrays = list(blocks), list(blocks.values())
    image_rows = arrays[0].shape[0]
    width, depth = weight.shape[1:]
    rows = image_rows // sections
    if last:
        out_shape = [
            jax.ShapeDtypeStruct((rows, width), F32 if k == 0 else BF16) for k in range(sections)
        ]
        out_specs = [whole()] * sections
        scratch = [pltpu.VMEM((image_rows, width), F32)]
    else:
        out_shape = jax.ShapeDtypeStruct((image_rows, width), F32)
        out_specs = whole()
        scratch = []
    if per_kv > 1:
        scratch.append(pltpu.VMEM((image_rows, depth), F32))
    operands = [*arrays, weight] + ([] if before is None else [before])
    return pl.pallas_call(
        functools.partial(grad_kernel, pairs, per_kv, sections, before is None, last),
        in_specs=[whole()] * len(operands),
        out_specs=out_specs,
        out_shape=out_shape,
        scratch_shapes=scratch,
        compiler_params=params(24),
        cost_estimate=cost(0, 0),
        name="feature_grad_last" if last else "feature_grad_first",
    )(*operands)


def shards(
    text, features, in_gain, w_query, q_gain, w_key_value, k_gain, tile_count, image_start, grad_out
):
    count = lax.axis_size("tensor")
    sections = lax.axis_size("section")
    per_kv = count // KV_HEADS

    def exchange(x, pair):
        return lax.ppermute(x, "tensor", [(i, i ^ pair[i % 2]) for i in range(count)])

    def swap(x):
        return exchange(x, (1, 1))

    bits = [1 << b for b in range(1, count.bit_length() - 1)]
    steps = len(bits)

    def distance(mask):
        taken = [s for s in range(steps) if mask >> s & 1]
        return sum(bits[s] for s in taken), sum(bits[steps - 1 - s] for s in taken)

    masks = range(1, 1 << steps)

    own_text = text[0]
    depth = own_text.shape[1]
    cuts = (0, depth * 7 // 16, depth * 3 // 4, depth)
    direct = {1 << s: exchange(own_text, distance(1 << s)) for s in range(steps)}

    def both_cores(blocks):
        out = {}
        for pair, x in blocks.items():
            out[pair] = [x]
            out[other_core(pair)] = [swap(x)]
        return out

    def places_of(blocks):
        return sorted(even for even, _ in blocks)

    def queries(blocks, name, **more):
        order = places_of(blocks)
        slots = [(order.index(even), order.index(odd)) for even, odd in blocks]
        groups = list(blocks.values())
        return queries_of(groups, slots, in_gain, w_query, q_gain, name, **more)

    kv_pairs = [distance(mask) for mask in range(1 << steps)]
    other_heads = kv_partial(features, w_key_value, per_kv, [other_core(pair) for pair in kv_pairs])
    other_heads = [swap(x) for x in other_heads]
    sums = kv_partial(features, w_key_value, per_kv, kv_pairs, other_heads)
    for step in range(steps):
        kept, came = sums[::2], [exchange(x, distance(1 << step)) for x in sums[1::2]]
        if step == 0:
            direct, came = lax.optimization_barrier((direct, came))
        if step < steps - 1:
            sums = kv_sum(kept, came)
    parts = [kept[0], came[0]]
    near = both_cores({(0, 0): own_text})
    scalars = (tile_count, image_start)
    q_near, *live = queries(near, "queries_own_chip", scalars=scalars)
    forwarded = []
    for order, columns in (
        (range(steps), slice(0, cuts[1])),
        (range(steps)[::-1], slice(cuts[1], depth)),
    ):
        held = {mask: x[:, columns] for mask, x in direct.items()}
        known, passed = [], {}
        for step in order:
            for mask in known:
                more = mask | 1 << step
                held[more] = passed[distance(more)] = exchange(held[mask], distance(1 << step))
            known += [mask | 1 << step for mask in known] + [1 << step]
        forwarded.append(dict(sorted(passed.items())))

    next_to = both_cores({distance(mask): x for mask, x in direct.items()})
    q_next = queries(next_to, "queries_neighbours")

    first_half, parts, q_near, q_next = lax.optimization_barrier(
        (forwarded[0], parts, q_near, q_next)
    )
    far = both_cores(first_half)
    sums = queries(far, "queries_forwarded_first")
    early, *state = attention(
        live,
        [q_near, q_next],
        [places_of(near), places_of(next_to)],
        count,
        grad_out,
        k_gain,
        parts,
        last=False,
    )
    second_half, sums, state = lax.optimization_barrier((forwarded[1], sums, state))
    split = cuts[2] - cuts[1]
    pieces = {pair: (x[:, :split], x[:, split:]) for pair, x in second_half.items()}
    far, rest = [both_cores({pair: x[i] for pair, x in pieces.items()}) for i in range(2)]
    sums = queries(far, "queries_forwarded_second", start=cuts[1], before=sums)
    q_far = queries(rest, "queries_forwarded_last", start=cuts[2], before=sums)
    far = places_of(far)
    late, block = attention(live, [q_far], [far], count, grad_out, k_gain, state, last=True)
    attended = assemble([places_of(near) + places_of(next_to), far], [early, late], grad_out)

    same_core = {(0, 0): block}
    same_core.update({distance(m): exchange(block, distance(m)) for m in reversed(masks)})
    swapped = {other_core(pair): swap(x) for pair, x in same_core.items()}
    before = None
    blocks = {**same_core, **swapped}
    if per_kv == 1:
        soon = {pair: blocks.pop(pair) for pair in [*same_core, (1, 1)]}
        before = feature_gradient(soon, w_key_value, per_kv, sections, last=False)
    pieces = feature_gradient(blocks, w_key_value, per_kv, sections, before)
    feature_grad, leaving = pieces[0], pieces[1:]
    arrived = []
    for k in range(1, sections):
        perm = [(i, (i + k) % sections) for i in range(sections)]
        arrived.append(lax.ppermute(leaving[k - 1], "section", perm))
    for x in arrived:
        feature_grad = feature_grad + x.astype(F32)
    return (attended, feature_grad)


def solution(mesh):
    return jax.shard_map(
        shards,
        mesh=mesh,
        in_specs=(
            P("section", "tensor", None),
            P(None, "tensor"),
            P("section", None),
            P("section", None, "tensor"),
            P("section", None),
            P("section", "tensor", None),
            P("section", None),
            P(),
            P(),
            P("section", None, "tensor"),
        ),
        out_specs=(P("section", None, "tensor"), P("section", "tensor")),
        check_vma=False,
    )
```

```python
import functools

import jax
import jax.numpy as jnp
from jax import lax
from jax.experimental import pallas as pl
from jax.experimental.pallas import tpu as pltpu
from jax.sharding import PartitionSpec as P

KV_HEADS = 8
HEAD_DIM = 128
TILES = 4
TILE_LEN = 24
TXT_TOK = 128
MB = 2
SLOTS = TILES * TILE_LEN

eps = 1e-05

F32 = jnp.float32
BF16 = jnp.bfloat16
MIB = 1 << 20


def whole(memory=pltpu.VMEM):
    return pl.BlockSpec(memory_space=memory)


def dot_nn(a, b):
    return jnp.dot(a, b, preferred_element_type=F32)


def dot_nt(a, b):
    return lax.dot_general(a, b, (((1,), (1,)), ((), ())), preferred_element_type=F32)


def dot_tn(a, b):
    return lax.dot_general(a, b, (((0,), (0,)), ((), ())), preferred_element_type=F32)


def params(mib):
    return pltpu.CompilerParams(vmem_limit_bytes=mib * MIB)


def cost(flops, size):
    return pl.CostEstimate(flops=flops, bytes_accessed=size, transcendentals=0)


def here():
    return lax.axis_index("tensor")


def of_core(pair):
    even, odd = pair
    return even if even == odd else even + lax.rem(here(), 2) * (odd - even)


def partner_at(pair):
    return lax.bitwise_xor(here(), of_core(pair))


def other_core(pair):
    return (1 ^ pair[1], 1 ^ pair[0])


def head_columns(head):
    return [
        pl.ds(pl.multiple_of((half * KV_HEADS + head) * HEAD_DIM, HEAD_DIM), HEAD_DIM)
        for half in range(2)
    ]


def kv_kernel(per_kv, pairs, feat_ref, weight_ref, *refs):
    features = feat_ref[...]
    for j, pair in enumerate(pairs):
        head = lax.div(partner_at(pair), per_kv)
        weight = jnp.concatenate([weight_ref[0, :, c] for c in head_columns(head)], axis=1)
        total = dot_nn(features, weight)
        out_ref = refs[j - len(pairs)]
        if len(refs) > len(pairs):
            total = total + refs[j][...]
        out_ref[...] = total.astype(out_ref.dtype)


def kv_partial(features, weight, per_kv, pairs, other=()):
    operands = (features, weight, *other)
    shape = (features.shape[0], 2 * HEAD_DIM)
    return pl.pallas_call(
        functools.partial(kv_kernel, per_kv, pairs),
        in_specs=[whole()] * len(operands),
        out_specs=[whole()] * len(pairs),
        out_shape=[
            jax.ShapeDtypeStruct(shape, BF16 if other and j % 2 else F32)
            for j in range(len(pairs))
        ],
        compiler_params=params(24),
        cost_estimate=cost(0, 0),
        name="kv_partial_own_core" if other else "kv_partial_other_core",
    )(*operands)


def kv_sum_kernel(*refs):
    size = len(refs) // 3
    for kept_ref, came_ref, out_ref in zip(refs, refs[size:], refs[2 * size :]):
        total = kept_ref[...] + came_ref[...].astype(F32)
        out_ref[...] = total.astype(out_ref.dtype)


def kv_sum(kept, came):
    return pl.pallas_call(
        kv_sum_kernel,
        in_specs=[whole()] * (2 * len(kept)),
        out_specs=[whole()] * len(kept),
        out_shape=[
            jax.ShapeDtypeStruct(x.shape, BF16 if i % 2 else F32) for i, x in enumerate(kept)
        ],
        compiler_params=params(24),
        cost_estimate=cost(0, 0),
        name="kv_sum",
    )(*kept, *came)


def live_masks(count_ref, start_ref, token_ref, slot_ref):
    for b in range(MB):
        token = lax.broadcasted_iota(jnp.int32, (TXT_TOK, HEAD_DIM), 0)
        token_ref[b * TXT_TOK : (b + 1) * TXT_TOK, :] = (token >= start_ref[b]).astype(F32)
        slot = lax.broadcasted_iota(jnp.int32, slot_ref.shape[1:], 1)
        slot_ref[b] = (slot < count_ref[b] * TILE_LEN).astype(F32)


def query_kernel(shape, slots, start, scalars, scratch, *refs):
    if scalars:
        end = len(refs) - scratch
        live_masks(refs[0], refs[1], refs[end - 2], refs[end - 1])
        refs = refs[2 : end - 2] + refs[end:]
    gain_ref, weight_ref, q_gain_ref, refs = refs[0], refs[1], refs[2], refs[3:]
    groups = []
    for parts in shape:
        groups.append(refs[:parts])
        refs = refs[parts:]
    depth, heads_width = weight_ref.shape[1:]
    width = sum(part.shape[1] for part in groups[0])
    last = start + width == depth
    span = 1024 if width % 1024 == 0 else 512

    def columns(parts, c):
        for part in parts:
            if c < part.shape[1]:
                return part[:, c : c + span].astype(F32)
            c -= part.shape[1]

    if start:
        raw, squares, refs = refs[0][...], refs[1][:, :1], refs[2:]
    else:
        raw, squares = 0.0, 0.0
    def rows_at(c):
        return jnp.concatenate([columns(parts, c) for parts in groups], axis=0)

    ahead = 1.0
    if not start and last:
        for c in range(0, width, span):
            squares = squares + jnp.sum(rows_at(c) ** 2, axis=-1, keepdims=True)
        ahead = lax.rsqrt(squares / depth + eps)
    for c in range(0, width, span):
        x = rows_at(c)
        if start or not last:
            squares = squares + jnp.sum(x * x, axis=-1, keepdims=True)
        cols = slice(start + c, start + c + span)
        scaled = (x * ahead * gain_ref[:, cols].astype(F32)).astype(BF16)
        raw = raw + dot_nn(scaled, weight_ref[0, cols, :])
    if not last:
        refs[0][...] = raw
        refs[1][...] = jnp.broadcast_to(squares, refs[1].shape)
        return
    out_ref = refs[-1]
    rows = groups[0][0].shape[0]
    inverse = lax.rsqrt(squares / depth + eps) if start else 1.0
    q_gain = q_gain_ref[...].astype(F32)
    for c in range(0, heads_width, HEAD_DIM):
        head = raw[:, c : c + HEAD_DIM] * inverse
        q_inverse = lax.rsqrt(jnp.mean(head * head, axis=-1, keepdims=True) + eps)
        head = head * q_inverse * q_gain
        for i, pair in enumerate(slots):
            at = of_core(pair) * rows
            if pair[0] != pair[1]:
                at = pl.multiple_of(at, rows)
            part = head[i * rows : (i + 1) * rows]
            out_ref[pl.ds(at, rows), c : c + HEAD_DIM] = part.astype(out_ref.dtype)
    if len(refs) > 1:
        refs[0][...] = out_ref[...].astype(BF16)


def queries_of(groups, slots, gain, weight, q_gain, name, start=0, before=(), scalars=()):
    arrays = [part for parts in groups for part in parts]
    rows = sum(parts[0].shape[0] for parts in groups)
    depth, heads_width = weight.shape[1:]
    last = start + sum(part.shape[1] for part in groups[0]) == depth
    scratch = []
    if last:
        out_shape = [jax.ShapeDtypeStruct((rows, heads_width), BF16)]
        if arrays[0].shape[0] % 16 != 0:
            scratch.append(pltpu.VMEM((rows, heads_width), F32))
        if scalars:
            out_shape.append(jax.ShapeDtypeStruct((MB * TXT_TOK, HEAD_DIM), F32))
            out_shape.append(jax.ShapeDtypeStruct((MB, 8, SLOTS), F32))
    else:
        out_shape = [jax.ShapeDtypeStruct((rows, w), F32) for w in (heads_width, HEAD_DIM)]
    out = pl.pallas_call(
        functools.partial(
            query_kernel,
            [len(parts) for parts in groups],
            slots,
            start,
            len(scalars),
            len(scratch),
        ),
        in_specs=[whole(pltpu.SMEM)] * len(scalars)
        + [whole()] * (3 + len(arrays) + len(before)),
        out_specs=[whole()] * len(out_shape),
        out_shape=out_shape,
        scratch_shapes=scratch,
        compiler_params=params(24),
        cost_estimate=cost(0, 0),
        name=name,
    )(*scalars, gain, weight, q_gain, *arrays, *before)
    return out[0] if last and not scalars else out


def attention_kernel(places, count, rows, last, sizes, *refs):
    token_ref, slot_ref, refs = refs[0], refs[1], refs[2:]
    queries_refs, refs = refs[:sizes], refs[sizes:]
    grad_ref, k_gain_ref, refs = refs[0], refs[1], refs[2:]
    narrow = rows % 16 != 0
    if narrow:
        refs, grad_rows = refs[:-1], refs[-1]
        grad_rows[...] = grad_ref[0].astype(F32)
    if last:
        d_keys_in, d_values_in, keys_ref, values_ref, hat_ref, inverse_ref = refs[:6]
        att_ref, block_ref, d_keys_ref, d_values_ref = refs[6:]
        d_keys_ref[...] = d_keys_in[...]
        d_values_ref[...] = d_values_in[...]
    else:
        parts = refs[:-7]
        att_ref, d_keys_ref, d_values_ref, keys_ref, values_ref, hat_ref, inverse_ref = refs[-7:]
        kv = sum(part[...].astype(F32) for part in parts)
        key_raw = kv[:, :HEAD_DIM]
        inverse = lax.rsqrt(jnp.mean(key_raw * key_raw, axis=-1, keepdims=True) + eps)
        hat_ref[...] = key_raw * inverse
        inverse_ref[...] = jnp.broadcast_to(inverse, key_raw.shape)
        keys_ref[...] = (key_raw * inverse * k_gain_ref[...].astype(F32)).astype(BF16)
        values_ref[...] = kv[:, HEAD_DIM:].astype(BF16)
        d_keys_ref[...] = jnp.zeros_like(d_keys_ref)
        d_values_ref[...] = jnp.zeros_like(d_values_ref)

    scale = HEAD_DIM ** (-0.5)
    heads = grad_ref.shape[2] // HEAD_DIM
    per_sample = count // MB
    mine = lax.div(here(), per_sample)
    blocks = [
        (p, ref, i * rows) for group, ref in zip(places, queries_refs) for i, p in enumerate(group)
    ]
    for far in range(MB):
        chosen = [block for block in blocks if block[0] // per_sample == far]
        if not chosen:
            continue
        sample = lax.bitwise_xor(mine, far)
        img = pl.ds(pl.multiple_of(sample * SLOTS, SLOTS), SLOTS)
        keys, values = keys_ref[img, :], values_ref[img, :]
        live = slot_ref[sample][:1, :] > 0
        spots = [
            pl.ds(pl.multiple_of(lax.bitwise_xor(here(), p) * rows, rows), rows)
            for p, _, _ in chosen
        ]
        masks = [token_ref[spot, :] for spot in spots]
        queries, upstream = [], []
        for h in range(heads):
            cols = slice(h * HEAD_DIM, (h + 1) * HEAD_DIM)
            for (p, ref, at), mask, spot in zip(chosen, masks, spots):
                queries.append(ref[at : at + rows, cols])
                grad = grad_rows[spot, cols] if narrow else grad_ref[0, spot, cols].astype(F32)
                upstream.append((grad * mask).astype(BF16))
        queries = jnp.concatenate(queries, axis=0)
        upstream = jnp.concatenate(upstream, axis=0)
        scores = dot_nt(queries, keys) * scale
        exponent = jnp.where(live, jnp.exp(scores), 0.0)
        probs = exponent * (1.0 / jnp.sum(exponent, axis=-1, keepdims=True))
        weights = probs.astype(BF16)
        head_out = dot_nn(weights, values)
        step = 0
        for h in range(heads):
            cols = slice(h * HEAD_DIM, (h + 1) * HEAD_DIM)
            for block, mask in zip(chosen, masks):
                at = blocks.index(block) * rows
                att_ref[at : at + rows, cols] = head_out[step : step + rows] * mask
                step += rows
        d_weights = dot_nt(upstream, values)
        inner = jnp.sum(probs * d_weights, axis=-1, keepdims=True)
        d_scores = (probs * (d_weights - inner) * scale).astype(BF16)
        d_keys_ref[img, :] += dot_tn(d_scores, queries)
        d_values_ref[img, :] += dot_tn(weights, upstream)
    if last:
        hat = hat_ref[...]
        scaled = d_keys_ref[...] * k_gain_ref[...].astype(F32)
        d_raw = inverse_ref[...] * (
            scaled - hat * jnp.mean(hat * scaled, axis=-1, keepdims=True)
        )
        block_ref[:, :HEAD_DIM] = d_raw.astype(BF16)
        block_ref[:, HEAD_DIM:] = d_values_ref[...].astype(BF16)


def attention(live, queries, places, count, grad_out, k_gain, state, last):
    rows, width = grad_out.shape[1] // count, grad_out.shape[2]
    image_rows = MB * SLOTS
    vector = jax.ShapeDtypeStruct((image_rows, HEAD_DIM), F32)
    rounded = jax.ShapeDtypeStruct((image_rows, HEAD_DIM), BF16)
    attended = jax.ShapeDtypeStruct((sum(map(len, places)) * rows, width), F32)
    scratch = []
    if last:
        out_shape = [attended, jax.ShapeDtypeStruct((image_rows, 2 * HEAD_DIM), BF16)]
        scratch += [pltpu.VMEM(vector.shape, F32)] * 2
    else:
        out_shape = [attended, vector, vector, rounded, rounded, vector, vector]
    if rows % 16 != 0:
        scratch += [pltpu.VMEM(grad_out.shape[1:], F32)]
    operands = [*queries, grad_out, k_gain, *state]
    return pl.pallas_call(
        functools.partial(attention_kernel, places, count, rows, last, len(queries)),
        in_specs=[whole()] * (2 + len(operands)),
        out_specs=[whole()] * len(out_shape),
        out_shape=out_shape,
        scratch_shapes=scratch,
        compiler_params=params(24),
        cost_estimate=cost(0, 0),
        name="attention_last" if last else "attention_first",
    )(*live, *operands)


def assemble_kernel(places, rows, *refs):
    refs, out_ref, held = refs[:-2], refs[-2], refs[-1]
    for group, ref in zip(places, refs):
        for i, p in enumerate(group):
            at = pl.multiple_of(lax.bitwise_xor(here(), p) * rows, rows)
            held[pl.ds(at, rows), :] = ref[i * rows : (i + 1) * rows, :]
    out_ref[0] = held[...].astype(BF16)


def assemble(places, arrays, like):
    rows = arrays[0].shape[0] // len(places[0])
    return pl.pallas_call(
        functools.partial(assemble_kernel, places, rows),
        in_specs=[whole()] * len(arrays),
        out_specs=whole(),
        out_shape=jax.ShapeDtypeStruct(like.shape, BF16),
        scratch_shapes=[pltpu.VMEM(like.shape[1:], F32)],
        compiler_params=params(24),
        cost_estimate=cost(0, 0),
        name="attended_rows",
    )(*arrays)


def grad_kernel(pairs, per_kv, sections, first, last, *refs):
    blocks, weight_ref, refs = refs[: len(pairs)], refs[len(pairs)], refs[len(pairs) + 1 :]
    if not first:
        before_ref, refs = refs[0], refs[1:]
    if per_kv > 1:
        refs, sums = refs[:-1], refs[-1]
        sums[...] = jnp.zeros_like(sums)
    total = refs[-1]
    image_rows, width = total.shape
    heads = []
    for block, pair in zip(blocks, pairs):
        columns = head_columns(lax.div(partner_at(pair), per_kv))
        if per_kv == 1:
            heads.append((columns, block[...]))
        else:
            for half, k in enumerate(columns):
                part = block[:, half * HEAD_DIM : (half + 1) * HEAD_DIM]
                sums[:, k] += part.astype(F32)
    if per_kv > 1:
        heads = [((slice(None),), sums[...].astype(BF16))]
    span = 256
    for c in range(0, width, span):
        cols = slice(c, c + span)
        part = 0.0 if first else before_ref[:, cols]
        for columns, block in heads:
            weight = jnp.concatenate([weight_ref[0, cols, k] for k in columns], axis=1)
            part = part + dot_nt(block, weight)
        total[:, cols] = part
    if last:
        rows = image_rows // sections
        for k in range(sections):
            to = lax.rem(lax.axis_index("section") + k, sections)
            piece = total[pl.ds(pl.multiple_of(to * rows, rows), rows), :]
            refs[k][...] = piece.astype(refs[k].dtype)


def feature_gradient(blocks, weight, per_kv, sections, before=None, last=True):
    pairs, arrays = list(blocks), list(blocks.values())
    image_rows = arrays[0].shape[0]
    width, depth = weight.shape[1:]
    rows = image_rows // sections
    if last:
        out_shape = [
            jax.ShapeDtypeStruct((rows, width), F32 if k == 0 else BF16) for k in range(sections)
        ]
        out_specs = [whole()] * sections
        scratch = [pltpu.VMEM((image_rows, width), F32)]
    else:
        out_shape = jax.ShapeDtypeStruct((image_rows, width), F32)
        out_specs = whole()
        scratch = []
    if per_kv > 1:
        scratch.append(pltpu.VMEM((image_rows, depth), F32))
    operands = [*arrays, weight] + ([] if before is None else [before])
    return pl.pallas_call(
        functools.partial(grad_kernel, pairs, per_kv, sections, before is None, last),
        in_specs=[whole()] * len(operands),
        out_specs=out_specs,
        out_shape=out_shape,
        scratch_shapes=scratch,
        compiler_params=params(24),
        cost_estimate=cost(0, 0),
        name="feature_grad_last" if last else "feature_grad_first",
    )(*operands)


def shards(
    text, features, in_gain, w_query, q_gain, w_key_value, k_gain, tile_count, image_start, grad_out
):
    count = lax.axis_size("tensor")
    sections = lax.axis_size("section")
    per_kv = count // KV_HEADS

    def exchange(x, pair):
        return lax.ppermute(x, "tensor", [(i, i ^ pair[i % 2]) for i in range(count)])

    def swap(x):
        return exchange(x, (1, 1))

    bits = [1 << b for b in range(1, count.bit_length() - 1)]
    steps = len(bits)

    def distance(mask):
        taken = [s for s in range(steps) if mask >> s & 1]
        return sum(bits[s] for s in taken), sum(bits[steps - 1 - s] for s in taken)

    masks = range(1, 1 << steps)

    own_text = text[0]
    depth = own_text.shape[1]
    cuts = (0, depth * 7 // 16, depth * 3 // 4, depth)
    direct = {1 << s: exchange(own_text, distance(1 << s)) for s in range(steps)}

    def both_cores(blocks):
        out = {}
        for pair, x in blocks.items():
            out[pair] = [x]
            out[other_core(pair)] = [swap(x)]
        return out

    def places_of(blocks):
        return sorted(even for even, _ in blocks)

    def queries(blocks, name, **more):
        order = places_of(blocks)
        slots = [(order.index(even), order.index(odd)) for even, odd in blocks]
        groups = list(blocks.values())
        return queries_of(groups, slots, in_gain, w_query, q_gain, name, **more)

    kv_pairs = [distance(mask) for mask in range(1 << steps)]
    other_heads = kv_partial(features, w_key_value, per_kv, [other_core(pair) for pair in kv_pairs])
    other_heads = [swap(x) for x in other_heads]
    sums = kv_partial(features, w_key_value, per_kv, kv_pairs, other_heads)
    for step in range(steps):
        kept, came = sums[::2], [exchange(x, distance(1 << step)) for x in sums[1::2]]
        if step == 0:
            direct, came = lax.optimization_barrier((direct, came))
        if step < steps - 1:
            sums = kv_sum(kept, came)
    parts = [kept[0], came[0]]
    near = both_cores({(0, 0): own_text})
    scalars = (tile_count, image_start)
    q_near, *live = queries(near, "queries_own_chip", scalars=scalars)
    forwarded = []
    for first, last in ((0, cuts[1]), (cuts[1], depth)):
        held = {mask: x[:, first:last] for mask, x in direct.items()}
        passed = {}
        for s in range(1, steps):
            for mask in range(1, 1 << s):
                more = mask | 1 << s
                held[more] = passed[distance(more)] = exchange(held[mask], distance(1 << s))
        forwarded.append(passed)

    next_to = both_cores({distance(mask): x for mask, x in direct.items()})
    q_next = queries(next_to, "queries_neighbours")

    first_half, parts, q_near, q_next = lax.optimization_barrier(
        (forwarded[0], parts, q_near, q_next)
    )
    far = both_cores(first_half)
    sums = queries(far, "queries_forwarded_first")
    early, *state = attention(
        live,
        [q_near, q_next],
        [places_of(near), places_of(next_to)],
        count,
        grad_out,
        k_gain,
        parts,
        last=False,
    )
    second_half, sums, state = lax.optimization_barrier((forwarded[1], sums, state))
    split = cuts[2] - cuts[1]
    pieces = {pair: (x[:, :split], x[:, split:]) for pair, x in second_half.items()}
    far, rest = [both_cores({pair: x[i] for pair, x in pieces.items()}) for i in range(2)]
    sums = queries(far, "queries_forwarded_second", start=cuts[1], before=sums)
    q_far = queries(rest, "queries_forwarded_last", start=cuts[2], before=sums)
    far = places_of(far)
    late, block = attention(live, [q_far], [far], count, grad_out, k_gain, state, last=True)
    attended = assemble([places_of(near) + places_of(next_to), far], [early, late], grad_out)

    same_core = {(0, 0): block}
    same_core.update({distance(m): exchange(block, distance(m)) for m in reversed(masks)})
    swapped = {other_core(pair): swap(x) for pair, x in same_core.items()}
    before = None
    blocks = {**same_core, **swapped}
    if per_kv == 1:
        soon = {pair: blocks.pop(pair) for pair in [*same_core, (1, 1)]}
        before = feature_gradient(soon, w_key_value, per_kv, sections, last=False)
    pieces = feature_gradient(blocks, w_key_value, per_kv, sections, before)
    feature_grad, leaving = pieces[0], pieces[1:]
    arrived = []
    for k in range(1, sections):
        perm = [(i, (i + k) % sections) for i in range(sections)]
        arrived.append(lax.ppermute(leaving[k - 1], "section", perm))
    for x in arrived:
        feature_grad = feature_grad + x.astype(F32)
    return (attended, feature_grad)


def solution(mesh):
    return jax.shard_map(
        shards,
        mesh=mesh,
        in_specs=(
            P("section", "tensor", None),
            P(None, "tensor"),
            P("section", None),
            P("section", None, "tensor"),
            P("section", None),
            P("section", "tensor", None),
            P("section", None),
            P(),
            P(),
            P("section", None, "tensor"),
        ),
        out_specs=(P("section", None, "tensor"), P("section", "tensor")),
        check_vma=False,
    )
```

```python
import functools

import jax
import jax.numpy as jnp
from jax import lax
from jax.experimental import pallas as pl
from jax.experimental.pallas import tpu as pltpu
from jax.sharding import PartitionSpec as P

KV_HEADS = 8
HEAD_DIM = 128
TILES = 4
TILE_LEN = 24
TXT_TOK = 128
MB = 2
SLOTS = TILES * TILE_LEN

eps = 1e-05

F32 = jnp.float32
BF16 = jnp.bfloat16
MIB = 1 << 20


def whole(memory=pltpu.VMEM):
    return pl.BlockSpec(memory_space=memory)


def dot_nn(a, b):
    return jnp.dot(a, b, preferred_element_type=F32)


def dot_nt(a, b):
    return lax.dot_general(a, b, (((1,), (1,)), ((), ())), preferred_element_type=F32)


def dot_tn(a, b):
    return lax.dot_general(a, b, (((0,), (0,)), ((), ())), preferred_element_type=F32)


def params(mib):
    return pltpu.CompilerParams(vmem_limit_bytes=mib * MIB)


def cost(flops, size):
    return pl.CostEstimate(flops=flops, bytes_accessed=size, transcendentals=0)


def here():
    return lax.axis_index("tensor")


def of_core(pair):
    even, odd = pair
    return even if even == odd else even + lax.rem(here(), 2) * (odd - even)


def partner_at(pair):
    return lax.bitwise_xor(here(), of_core(pair))


def other_core(pair):
    return (1 ^ pair[1], 1 ^ pair[0])


def head_columns(head):
    return [
        pl.ds(pl.multiple_of((half * KV_HEADS + head) * HEAD_DIM, HEAD_DIM), HEAD_DIM)
        for half in range(2)
    ]


def kv_kernel(per_kv, pairs, feat_ref, weight_ref, *refs):
    features = feat_ref[...]
    for j, pair in enumerate(pairs):
        head = lax.div(partner_at(pair), per_kv)
        weight = jnp.concatenate([weight_ref[0, :, c] for c in head_columns(head)], axis=1)
        total = dot_nn(features, weight)
        out_ref = refs[j - len(pairs)]
        if len(refs) > len(pairs):
            total = total + refs[j][...]
        out_ref[...] = total.astype(out_ref.dtype)


def kv_partial(features, weight, per_kv, pairs, other=()):
    operands = (features, weight, *other)
    shape = (features.shape[0], 2 * HEAD_DIM)
    return pl.pallas_call(
        functools.partial(kv_kernel, per_kv, pairs),
        in_specs=[whole()] * len(operands),
        out_specs=[whole()] * len(pairs),
        out_shape=[
            jax.ShapeDtypeStruct(shape, BF16 if other and j % 2 else F32)
            for j in range(len(pairs))
        ],
        compiler_params=params(24),
        cost_estimate=cost(0, 0),
        name="kv_partial_own_core" if other else "kv_partial_other_core",
    )(*operands)


def kv_sum_kernel(*refs):
    size = len(refs) // 3
    for kept_ref, came_ref, out_ref in zip(refs, refs[size:], refs[2 * size :]):
        total = kept_ref[...] + came_ref[...].astype(F32)
        out_ref[...] = total.astype(out_ref.dtype)


def kv_sum(kept, came):
    return pl.pallas_call(
        kv_sum_kernel,
        in_specs=[whole()] * (2 * len(kept)),
        out_specs=[whole()] * len(kept),
        out_shape=[
            jax.ShapeDtypeStruct(x.shape, BF16 if i % 2 else F32) for i, x in enumerate(kept)
        ],
        compiler_params=params(24),
        cost_estimate=cost(0, 0),
        name="kv_sum",
    )(*kept, *came)


def live_masks(count_ref, start_ref, token_ref, slot_ref):
    for b in range(MB):
        token = lax.broadcasted_iota(jnp.int32, (TXT_TOK, HEAD_DIM), 0)
        token_ref[b * TXT_TOK : (b + 1) * TXT_TOK, :] = (token >= start_ref[b]).astype(F32)
        slot = lax.broadcasted_iota(jnp.int32, slot_ref.shape[1:], 1)
        slot_ref[b] = (slot < count_ref[b] * TILE_LEN).astype(F32)


def query_kernel(shape, slots, start, scalars, scratch, *refs):
    if scalars:
        end = len(refs) - scratch
        live_masks(refs[0], refs[1], refs[end - 2], refs[end - 1])
        refs = refs[2 : end - 2] + refs[end:]
    gain_ref, weight_ref, q_gain_ref, refs = refs[0], refs[1], refs[2], refs[3:]
    groups = []
    for parts in shape:
        groups.append(refs[:parts])
        refs = refs[parts:]
    depth, heads_width = weight_ref.shape[1:]
    width = sum(part.shape[1] for part in groups[0])
    last = start + width == depth
    span = 1024 if width % 1024 == 0 else 512

    def columns(parts, c):
        for part in parts:
            if c < part.shape[1]:
                return part[:, c : c + span].astype(F32)
            c -= part.shape[1]

    if start:
        raw, squares, refs = refs[0][...], refs[1][:, :1], refs[2:]
    else:
        raw, squares = 0.0, 0.0
    def rows_at(c):
        return jnp.concatenate([columns(parts, c) for parts in groups], axis=0)

    ahead = 1.0
    if not start and last:
        for c in range(0, width, span):
            squares = squares + jnp.sum(rows_at(c) ** 2, axis=-1, keepdims=True)
        ahead = lax.rsqrt(squares / depth + eps)
    for c in range(0, width, span):
        x = rows_at(c)
        if start or not last:
            squares = squares + jnp.sum(x * x, axis=-1, keepdims=True)
        cols = slice(start + c, start + c + span)
        scaled = (x * ahead * gain_ref[:, cols].astype(F32)).astype(BF16)
        raw = raw + dot_nn(scaled, weight_ref[0, cols, :])
    if not last:
        refs[0][...] = raw
        refs[1][...] = jnp.broadcast_to(squares, refs[1].shape)
        return
    out_ref = refs[-1]
    rows = groups[0][0].shape[0]
    inverse = lax.rsqrt(squares / depth + eps) if start else 1.0
    q_gain = q_gain_ref[...].astype(F32)
    for c in range(0, heads_width, HEAD_DIM):
        head = raw[:, c : c + HEAD_DIM] * inverse
        q_inverse = lax.rsqrt(jnp.mean(head * head, axis=-1, keepdims=True) + eps)
        head = head * q_inverse * q_gain
        for i, pair in enumerate(slots):
            at = of_core(pair) * rows
            if pair[0] != pair[1]:
                at = pl.multiple_of(at, rows)
            part = head[i * rows : (i + 1) * rows]
            out_ref[pl.ds(at, rows), c : c + HEAD_DIM] = part.astype(out_ref.dtype)
    if len(refs) > 1:
        refs[0][...] = out_ref[...].astype(BF16)


def queries_of(groups, slots, gain, weight, q_gain, name, start=0, before=(), scalars=()):
    arrays = [part for parts in groups for part in parts]
    rows = sum(parts[0].shape[0] for parts in groups)
    depth, heads_width = weight.shape[1:]
    last = start + sum(part.shape[1] for part in groups[0]) == depth
    scratch = []
    if last:
        out_shape = [jax.ShapeDtypeStruct((rows, heads_width), BF16)]
        if arrays[0].shape[0] % 16 != 0:
            scratch.append(pltpu.VMEM((rows, heads_width), F32))
        if scalars:
            out_shape.append(jax.ShapeDtypeStruct((MB * TXT_TOK, HEAD_DIM), F32))
            out_shape.append(jax.ShapeDtypeStruct((MB, 8, SLOTS), F32))
    else:
        out_shape = [jax.ShapeDtypeStruct((rows, w), F32) for w in (heads_width, HEAD_DIM)]
    out = pl.pallas_call(
        functools.partial(
            query_kernel,
            [len(parts) for parts in groups],
            slots,
            start,
            len(scalars),
            len(scratch),
        ),
        in_specs=[whole(pltpu.SMEM)] * len(scalars)
        + [whole()] * (3 + len(arrays) + len(before)),
        out_specs=[whole()] * len(out_shape),
        out_shape=out_shape,
        scratch_shapes=scratch,
        compiler_params=params(24),
        cost_estimate=cost(0, 0),
        name=name,
    )(*scalars, gain, weight, q_gain, *arrays, *before)
    return out[0] if last and not scalars else out


def attention_kernel(places, count, rows, last, sizes, project, *refs):
    token_ref, slot_ref, refs = refs[0], refs[1], refs[2:]
    queries_refs, refs = refs[:sizes], refs[sizes:]
    if last:
        held = 1 + (rows % 16 != 0)
        query_kernel(*project, 0, 0, *queries_refs, *refs[-held:])
        queries_refs, refs = refs[len(refs) - held : len(refs) - held + 1], refs[:-held]
    grad_ref, k_gain_ref, refs = refs[0], refs[1], refs[2:]
    narrow = rows % 16 != 0
    if narrow:
        refs, grad_rows = refs[:-1], refs[-1]
        grad_rows[...] = grad_ref[0].astype(F32)
    if last:
        d_keys_in, d_values_in, keys_ref, values_ref, hat_ref, inverse_ref = refs[:6]
        att_ref, block_ref, d_keys_ref, d_values_ref = refs[6:]
        d_keys_ref[...] = d_keys_in[...]
        d_values_ref[...] = d_values_in[...]
    else:
        parts = refs[:-7]
        att_ref, d_keys_ref, d_values_ref, keys_ref, values_ref, hat_ref, inverse_ref = refs[-7:]
        kv = sum(part[...].astype(F32) for part in parts)
        key_raw = kv[:, :HEAD_DIM]
        inverse = lax.rsqrt(jnp.mean(key_raw * key_raw, axis=-1, keepdims=True) + eps)
        hat_ref[...] = key_raw * inverse
        inverse_ref[...] = jnp.broadcast_to(inverse, key_raw.shape)
        keys_ref[...] = (key_raw * inverse * k_gain_ref[...].astype(F32)).astype(BF16)
        values_ref[...] = kv[:, HEAD_DIM:].astype(BF16)
        d_keys_ref[...] = jnp.zeros_like(d_keys_ref)
        d_values_ref[...] = jnp.zeros_like(d_values_ref)

    scale = HEAD_DIM ** (-0.5)
    heads = grad_ref.shape[2] // HEAD_DIM
    per_sample = count // MB
    mine = lax.div(here(), per_sample)
    blocks = [
        (p, ref, i * rows) for group, ref in zip(places, queries_refs) for i, p in enumerate(group)
    ]
    for far in range(MB):
        chosen = [block for block in blocks if block[0] // per_sample == far]
        if not chosen:
            continue
        sample = lax.bitwise_xor(mine, far)
        img = pl.ds(pl.multiple_of(sample * SLOTS, SLOTS), SLOTS)
        keys, values = keys_ref[img, :], values_ref[img, :]
        live = slot_ref[sample][:1, :] > 0
        spots = [
            pl.ds(pl.multiple_of(lax.bitwise_xor(here(), p) * rows, rows), rows)
            for p, _, _ in chosen
        ]
        masks = [token_ref[spot, :] for spot in spots]
        queries, upstream = [], []
        for h in range(heads):
            cols = slice(h * HEAD_DIM, (h + 1) * HEAD_DIM)
            for (p, ref, at), mask, spot in zip(chosen, masks, spots):
                queries.append(ref[at : at + rows, cols])
                grad = grad_rows[spot, cols] if narrow else grad_ref[0, spot, cols].astype(F32)
                upstream.append((grad * mask).astype(BF16))
        queries = jnp.concatenate(queries, axis=0)
        upstream = jnp.concatenate(upstream, axis=0)
        scores = dot_nt(queries, keys) * scale
        exponent = jnp.where(live, jnp.exp(scores), 0.0)
        probs = exponent * (1.0 / jnp.sum(exponent, axis=-1, keepdims=True))
        weights = probs.astype(BF16)
        head_out = dot_nn(weights, values)
        step = 0
        for h in range(heads):
            cols = slice(h * HEAD_DIM, (h + 1) * HEAD_DIM)
            for block, mask in zip(chosen, masks):
                at = blocks.index(block) * rows
                att_ref[at : at + rows, cols] = head_out[step : step + rows] * mask
                step += rows
        d_weights = dot_nt(upstream, values)
        inner = jnp.sum(probs * d_weights, axis=-1, keepdims=True)
        d_scores = (probs * (d_weights - inner) * scale).astype(BF16)
        d_keys_ref[img, :] += dot_tn(d_scores, queries)
        d_values_ref[img, :] += dot_tn(weights, upstream)
    if last:
        hat = hat_ref[...]
        scaled = d_keys_ref[...] * k_gain_ref[...].astype(F32)
        d_raw = inverse_ref[...] * (
            scaled - hat * jnp.mean(hat * scaled, axis=-1, keepdims=True)
        )
        block_ref[:, :HEAD_DIM] = d_raw.astype(BF16)
        block_ref[:, HEAD_DIM:] = d_values_ref[...].astype(BF16)


def attention(live, queries, places, count, grad_out, k_gain, state, last, project=()):
    rows, width = grad_out.shape[1] // count, grad_out.shape[2]
    image_rows = MB * SLOTS
    vector = jax.ShapeDtypeStruct((image_rows, HEAD_DIM), F32)
    rounded = jax.ShapeDtypeStruct((image_rows, HEAD_DIM), BF16)
    attended = jax.ShapeDtypeStruct((sum(map(len, places)) * rows, width), F32)
    scratch = []
    if last:
        out_shape = [attended, jax.ShapeDtypeStruct((image_rows, 2 * HEAD_DIM), BF16)]
        scratch += [pltpu.VMEM(vector.shape, F32)] * 2
    else:
        out_shape = [attended, vector, vector, rounded, rounded, vector, vector]
    if rows % 16 != 0:
        scratch += [pltpu.VMEM(grad_out.shape[1:], F32)]
    if last:
        scratch.append(pltpu.VMEM(attended.shape, BF16))
        if rows % 16 != 0:
            scratch.append(pltpu.VMEM(attended.shape, F32))
    operands = [*queries, grad_out, k_gain, *state]
    return pl.pallas_call(
        functools.partial(attention_kernel, places, count, rows, last, len(queries), project),
        in_specs=[whole()] * (2 + len(operands)),
        out_specs=[whole()] * len(out_shape),
        out_shape=out_shape,
        scratch_shapes=scratch,
        compiler_params=params(24),
        cost_estimate=cost(0, 0),
        name="attention_last" if last else "attention_first",
    )(*live, *operands)


def assemble_kernel(places, rows, *refs):
    refs, out_ref, held = refs[:-2], refs[-2], refs[-1]
    for group, ref in zip(places, refs):
        for i, p in enumerate(group):
            at = pl.multiple_of(lax.bitwise_xor(here(), p) * rows, rows)
            held[pl.ds(at, rows), :] = ref[i * rows : (i + 1) * rows, :]
    out_ref[0] = held[...].astype(BF16)


def assemble(places, arrays, like):
    rows = arrays[0].shape[0] // len(places[0])
    return pl.pallas_call(
        functools.partial(assemble_kernel, places, rows),
        in_specs=[whole()] * len(arrays),
        out_specs=whole(),
        out_shape=jax.ShapeDtypeStruct(like.shape, BF16),
        scratch_shapes=[pltpu.VMEM(like.shape[1:], F32)],
        compiler_params=params(24),
        cost_estimate=cost(0, 0),
        name="attended_rows",
    )(*arrays)


def grad_kernel(pairs, per_kv, sections, first, last, *refs):
    blocks, weight_ref, refs = refs[: len(pairs)], refs[len(pairs)], refs[len(pairs) + 1 :]
    if not first:
        before_ref, refs = refs[0], refs[1:]
    if per_kv > 1:
        refs, sums = refs[:-1], refs[-1]
        sums[...] = jnp.zeros_like(sums)
    total = refs[-1]
    image_rows, width = total.shape
    heads = []
    for block, pair in zip(blocks, pairs):
        columns = head_columns(lax.div(partner_at(pair), per_kv))
        if per_kv == 1:
            heads.append((columns, block[...]))
        else:
            for half, k in enumerate(columns):
                part = block[:, half * HEAD_DIM : (half + 1) * HEAD_DIM]
                sums[:, k] += part.astype(F32)
    if per_kv > 1:
        heads = [((slice(None),), sums[...].astype(BF16))]
    span = 256
    for c in range(0, width, span):
        cols = slice(c, c + span)
        part = 0.0 if first else before_ref[:, cols]
        for columns, block in heads:
            weight = jnp.concatenate([weight_ref[0, cols, k] for k in columns], axis=1)
            part = part + dot_nt(block, weight)
        total[:, cols] = part
    if last:
        rows = image_rows // sections
        for k in range(sections):
            to = lax.rem(lax.axis_index("section") + k, sections)
            piece = total[pl.ds(pl.multiple_of(to * rows, rows), rows), :]
            refs[k][...] = piece.astype(refs[k].dtype)


def feature_gradient(blocks, weight, per_kv, sections, before=None, last=True):
    pairs, arrays = list(blocks), list(blocks.values())
    image_rows = arrays[0].shape[0]
    width, depth = weight.shape[1:]
    rows = image_rows // sections
    if last:
        out_shape = [
            jax.ShapeDtypeStruct((rows, width), F32 if k == 0 else BF16) for k in range(sections)
        ]
        out_specs = [whole()] * sections
        scratch = [pltpu.VMEM((image_rows, width), F32)]
    else:
        out_shape = jax.ShapeDtypeStruct((image_rows, width), F32)
        out_specs = whole()
        scratch = []
    if per_kv > 1:
        scratch.append(pltpu.VMEM((image_rows, depth), F32))
    operands = [*arrays, weight] + ([] if before is None else [before])
    return pl.pallas_call(
        functools.partial(grad_kernel, pairs, per_kv, sections, before is None, last),
        in_specs=[whole()] * len(operands),
        out_specs=out_specs,
        out_shape=out_shape,
        scratch_shapes=scratch,
        compiler_params=params(24),
        cost_estimate=cost(0, 0),
        name="feature_grad_last" if last else "feature_grad_first",
    )(*operands)


def shards(
    text, features, in_gain, w_query, q_gain, w_key_value, k_gain, tile_count, image_start, grad_out
):
    count = lax.axis_size("tensor")
    sections = lax.axis_size("section")
    per_kv = count // KV_HEADS

    def exchange(x, pair):
        return lax.ppermute(x, "tensor", [(i, i ^ pair[i % 2]) for i in range(count)])

    def swap(x):
        return exchange(x, (1, 1))

    bits = [1 << b for b in range(1, count.bit_length() - 1)]
    steps = len(bits)

    def distance(mask):
        taken = [s for s in range(steps) if mask >> s & 1]
        return sum(bits[s] for s in taken), sum(bits[steps - 1 - s] for s in taken)

    masks = range(1, 1 << steps)

    own_text = text[0]
    depth = own_text.shape[1]
    cuts = (0, depth * 7 // 16, depth * 3 // 4, depth)
    direct = {1 << s: exchange(own_text, distance(1 << s)) for s in range(steps)}

    def both_cores(blocks):
        out = {}
        for pair, x in blocks.items():
            out[pair] = [x]
            out[other_core(pair)] = [swap(x)]
        return out

    def places_of(blocks):
        return sorted(even for even, _ in blocks)

    def queries(blocks, name, **more):
        order = places_of(blocks)
        slots = [(order.index(even), order.index(odd)) for even, odd in blocks]
        groups = list(blocks.values())
        return queries_of(groups, slots, in_gain, w_query, q_gain, name, **more)

    kv_pairs = [distance(mask) for mask in range(1 << steps)]
    other_heads = kv_partial(features, w_key_value, per_kv, [other_core(pair) for pair in kv_pairs])
    other_heads = [swap(x) for x in other_heads]
    sums = kv_partial(features, w_key_value, per_kv, kv_pairs, other_heads)
    for step in range(steps):
        kept, came = sums[::2], [exchange(x, distance(1 << step)) for x in sums[1::2]]
        if step == 0:
            direct, came = lax.optimization_barrier((direct, came))
        if step < steps - 1:
            sums = kv_sum(kept, came)
    parts = [kept[0], came[0]]
    near = both_cores({(0, 0): own_text})
    scalars = (tile_count, image_start)
    q_near, *live = queries(near, "queries_own_chip", scalars=scalars)
    forwarded = []
    for first, last in ((0, cuts[1]), (cuts[1], depth)):
        held = {mask: x[:, first:last] for mask, x in direct.items()}
        passed = {}
        for s in range(1, steps):
            for mask in range(1, 1 << s):
                more = mask | 1 << s
                held[more] = passed[distance(more)] = exchange(held[mask], distance(1 << s))
        forwarded.append(passed)

    next_to = both_cores({distance(mask): x for mask, x in direct.items()})
    q_next = queries(next_to, "queries_neighbours")

    first_half, parts, q_near, q_next = lax.optimization_barrier(
        (forwarded[0], parts, q_near, q_next)
    )
    far = both_cores(first_half)
    sums = queries(far, "queries_forwarded_first")
    early, *state = attention(
        live,
        [q_near, q_next],
        [places_of(near), places_of(next_to)],
        count,
        grad_out,
        k_gain,
        parts,
        last=False,
    )
    second_half, sums, state = lax.optimization_barrier((forwarded[1], sums, state))
    split = cuts[2] - cuts[1]
    pieces = {pair: (x[:, :split], x[:, split:]) for pair, x in second_half.items()}
    far, rest = [both_cores({pair: x[i] for pair, x in pieces.items()}) for i in range(2)]
    sums = queries(far, "queries_forwarded_second", start=cuts[1], before=sums)
    far = places_of(rest)
    groups = list(rest.values())
    slots = [(far.index(even), far.index(odd)) for even, odd in rest]
    project = ([len(group) for group in groups], slots, cuts[2])
    left = [in_gain, w_query, q_gain, *[x for group in groups for x in group], *sums]
    late, block = attention(
        live, left, [far], count, grad_out, k_gain, state, last=True, project=project
    )
    attended = assemble([places_of(near) + places_of(next_to), far], [early, late], grad_out)

    same_core = {(0, 0): block}
    same_core.update({distance(m): exchange(block, distance(m)) for m in reversed(masks)})
    swapped = {other_core(pair): swap(x) for pair, x in same_core.items()}
    before = None
    blocks = {**same_core, **swapped}
    if per_kv == 1:
        soon = {pair: blocks.pop(pair) for pair in [*same_core, (1, 1)]}
        before = feature_gradient(soon, w_key_value, per_kv, sections, last=False)
    pieces = feature_gradient(blocks, w_key_value, per_kv, sections, before)
    feature_grad, leaving = pieces[0], pieces[1:]
    arrived = []
    for k in range(1, sections):
        perm = [(i, (i + k) % sections) for i in range(sections)]
        arrived.append(lax.ppermute(leaving[k - 1], "section", perm))
    for x in arrived:
        feature_grad = feature_grad + x.astype(F32)
    return (attended, feature_grad)


def solution(mesh):
    return jax.shard_map(
        shards,
        mesh=mesh,
        in_specs=(
            P("section", "tensor", None),
            P(None, "tensor"),
            P("section", None),
            P("section", None, "tensor"),
            P("section", None),
            P("section", "tensor", None),
            P("section", None),
            P(),
            P(),
            P("section", None, "tensor"),
        ),
        out_specs=(P("section", None, "tensor"), P("section", "tensor")),
        check_vma=False,
    )
```

```python
import functools

import jax
import jax.numpy as jnp
from jax import lax
from jax.experimental import pallas as pl
from jax.experimental.pallas import tpu as pltpu
from jax.sharding import PartitionSpec as P

KV_HEADS = 8
HEAD_DIM = 128
TILES = 4
TILE_LEN = 24
TXT_TOK = 128
MB = 2
SLOTS = TILES * TILE_LEN

eps = 1e-05

F32 = jnp.float32
BF16 = jnp.bfloat16
MIB = 1 << 20


def whole(memory=pltpu.VMEM):
    return pl.BlockSpec(memory_space=memory)


def dot_nn(a, b):
    return jnp.dot(a, b, preferred_element_type=F32)


def dot_nt(a, b):
    return lax.dot_general(a, b, (((1,), (1,)), ((), ())), preferred_element_type=F32)


def dot_tn(a, b):
    return lax.dot_general(a, b, (((0,), (0,)), ((), ())), preferred_element_type=F32)


def params(mib):
    return pltpu.CompilerParams(vmem_limit_bytes=mib * MIB)


def cost(flops, size):
    return pl.CostEstimate(flops=flops, bytes_accessed=size, transcendentals=0)


def here():
    return lax.axis_index("tensor")


def of_core(pair):
    even, odd = pair
    return even if even == odd else even + lax.rem(here(), 2) * (odd - even)


def partner_at(pair):
    return lax.bitwise_xor(here(), of_core(pair))


def other_core(pair):
    return (1 ^ pair[1], 1 ^ pair[0])


def head_columns(head):
    return [
        pl.ds(pl.multiple_of((half * KV_HEADS + head) * HEAD_DIM, HEAD_DIM), HEAD_DIM)
        for half in range(2)
    ]


def kv_kernel(per_kv, pairs, feat_ref, weight_ref, *refs):
    features = feat_ref[...]
    for j, pair in enumerate(pairs):
        head = lax.div(partner_at(pair), per_kv)
        weight = jnp.concatenate([weight_ref[0, :, c] for c in head_columns(head)], axis=1)
        total = dot_nn(features, weight)
        out_ref = refs[j - len(pairs)]
        if len(refs) > len(pairs):
            total = total + refs[j][...]
        out_ref[...] = total.astype(out_ref.dtype)


def kv_partial(features, weight, per_kv, pairs, other=()):
    operands = (features, weight, *other)
    shape = (features.shape[0], 2 * HEAD_DIM)
    return pl.pallas_call(
        functools.partial(kv_kernel, per_kv, pairs),
        in_specs=[whole()] * len(operands),
        out_specs=[whole()] * len(pairs),
        out_shape=[
            jax.ShapeDtypeStruct(shape, BF16 if other and j % 2 else F32)
            for j in range(len(pairs))
        ],
        compiler_params=params(24),
        cost_estimate=cost(0, 0),
        name="kv_partial_own_core" if other else "kv_partial_other_core",
    )(*operands)


def kv_sum_kernel(*refs):
    size = len(refs) // 3
    for kept_ref, came_ref, out_ref in zip(refs, refs[size:], refs[2 * size :]):
        total = kept_ref[...] + came_ref[...].astype(F32)
        out_ref[...] = total.astype(out_ref.dtype)


def kv_sum(kept, came):
    return pl.pallas_call(
        kv_sum_kernel,
        in_specs=[whole()] * (2 * len(kept)),
        out_specs=[whole()] * len(kept),
        out_shape=[
            jax.ShapeDtypeStruct(x.shape, BF16 if i % 2 else F32) for i, x in enumerate(kept)
        ],
        compiler_params=params(24),
        cost_estimate=cost(0, 0),
        name="kv_sum",
    )(*kept, *came)


def live_masks(count_ref, start_ref, token_ref, slot_ref):
    for b in range(MB):
        token = lax.broadcasted_iota(jnp.int32, (TXT_TOK, HEAD_DIM), 0)
        token_ref[b * TXT_TOK : (b + 1) * TXT_TOK, :] = (token >= start_ref[b]).astype(F32)
        slot = lax.broadcasted_iota(jnp.int32, slot_ref.shape[1:], 1)
        slot_ref[b] = (slot < count_ref[b] * TILE_LEN).astype(F32)


def query_kernel(shape, slots, start, scalars, scratch, *refs):
    if scalars:
        end = len(refs) - scratch
        live_masks(refs[0], refs[1], refs[end - 2], refs[end - 1])
        refs = refs[2 : end - 2] + refs[end:]
    gain_ref, weight_ref, q_gain_ref, refs = refs[0], refs[1], refs[2], refs[3:]
    groups = []
    for parts in shape:
        groups.append(refs[:parts])
        refs = refs[parts:]
    depth, heads_width = weight_ref.shape[1:]
    width = sum(part.shape[1] for part in groups[0])
    last = start + width == depth
    span = 1024 if width % 1024 == 0 else 512

    def columns(parts, c):
        for part in parts:
            if c < part.shape[1]:
                return part[:, c : c + span].astype(F32)
            c -= part.shape[1]

    if start:
        raw, squares, refs = refs[0][...], refs[1][:, :1], refs[2:]
    else:
        raw, squares = 0.0, 0.0
    def rows_at(c):
        return jnp.concatenate([columns(parts, c) for parts in groups], axis=0)

    ahead = 1.0
    if not start and last:
        for c in range(0, width, span):
            squares = squares + jnp.sum(rows_at(c) ** 2, axis=-1, keepdims=True)
        ahead = lax.rsqrt(squares / depth + eps)
    for c in range(0, width, span):
        x = rows_at(c)
        if start or not last:
            squares = squares + jnp.sum(x * x, axis=-1, keepdims=True)
        cols = slice(start + c, start + c + span)
        scaled = (x * ahead * gain_ref[:, cols].astype(F32)).astype(BF16)
        raw = raw + dot_nn(scaled, weight_ref[0, cols, :])
    if not last:
        refs[0][...] = raw
        refs[1][...] = jnp.broadcast_to(squares, refs[1].shape)
        return
    out_ref = refs[-1]
    rows = groups[0][0].shape[0]
    inverse = lax.rsqrt(squares / depth + eps) if start else 1.0
    q_gain = q_gain_ref[...].astype(F32)
    for c in range(0, heads_width, HEAD_DIM):
        head = raw[:, c : c + HEAD_DIM] * inverse
        q_inverse = lax.rsqrt(jnp.mean(head * head, axis=-1, keepdims=True) + eps)
        head = head * q_inverse * q_gain
        for i, pair in enumerate(slots):
            at = of_core(pair) * rows
            if pair[0] != pair[1]:
                at = pl.multiple_of(at, rows)
            part = head[i * rows : (i + 1) * rows]
            out_ref[pl.ds(at, rows), c : c + HEAD_DIM] = part.astype(out_ref.dtype)
    if len(refs) > 1:
        refs[0][...] = out_ref[...].astype(BF16)


def queries_of(groups, slots, gain, weight, q_gain, name, start=0, before=(), scalars=()):
    arrays = [part for parts in groups for part in parts]
    rows = sum(parts[0].shape[0] for parts in groups)
    depth, heads_width = weight.shape[1:]
    last = start + sum(part.shape[1] for part in groups[0]) == depth
    scratch = []
    if last:
        out_shape = [jax.ShapeDtypeStruct((rows, heads_width), BF16)]
        if arrays[0].shape[0] % 16 != 0:
            scratch.append(pltpu.VMEM((rows, heads_width), F32))
        if scalars:
            out_shape.append(jax.ShapeDtypeStruct((MB * TXT_TOK, HEAD_DIM), F32))
            out_shape.append(jax.ShapeDtypeStruct((MB, 8, SLOTS), F32))
    else:
        out_shape = [jax.ShapeDtypeStruct((rows, w), F32) for w in (heads_width, HEAD_DIM)]
    out = pl.pallas_call(
        functools.partial(
            query_kernel,
            [len(parts) for parts in groups],
            slots,
            start,
            len(scalars),
            len(scratch),
        ),
        in_specs=[whole(pltpu.SMEM)] * len(scalars)
        + [whole()] * (3 + len(arrays) + len(before)),
        out_specs=[whole()] * len(out_shape),
        out_shape=out_shape,
        scratch_shapes=scratch,
        compiler_params=params(24),
        cost_estimate=cost(0, 0),
        name=name,
    )(*scalars, gain, weight, q_gain, *arrays, *before)
    return out[0] if last and not scalars else out


def attention_kernel(places, count, rows, last, sizes, project, *refs):
    token_ref, slot_ref, refs = refs[0], refs[1], refs[2:]
    queries_refs, refs = refs[:sizes], refs[sizes:]
    if last:
        held = 1 + (rows % 16 != 0)
        query_kernel(*project, 0, 0, *queries_refs, *refs[-held:])
        queries_refs, refs = refs[len(refs) - held : len(refs) - held + 1], refs[:-held]
    grad_ref, k_gain_ref, refs = refs[0], refs[1], refs[2:]
    narrow = rows % 16 != 0
    if narrow:
        refs, grad_rows = refs[:-1], refs[-1]
        grad_rows[...] = grad_ref[0].astype(F32)
    if last:
        d_keys_in, d_values_in, keys_ref, values_ref, hat_ref, inverse_ref = refs[:6]
        att_ref, block_ref, d_keys_ref, d_values_ref = refs[6:]
        d_keys_ref[...] = d_keys_in[...]
        d_values_ref[...] = d_values_in[...]
    else:
        parts = refs[:-7]
        att_ref, d_keys_ref, d_values_ref, keys_ref, values_ref, hat_ref, inverse_ref = refs[-7:]
        kv = sum(part[...].astype(F32) for part in parts)
        key_raw = kv[:, :HEAD_DIM]
        inverse = lax.rsqrt(jnp.mean(key_raw * key_raw, axis=-1, keepdims=True) + eps)
        hat_ref[...] = key_raw * inverse
        inverse_ref[...] = jnp.broadcast_to(inverse, key_raw.shape)
        keys_ref[...] = (key_raw * inverse * k_gain_ref[...].astype(F32)).astype(BF16)
        values_ref[...] = kv[:, HEAD_DIM:].astype(BF16)
        d_keys_ref[...] = jnp.zeros_like(d_keys_ref)
        d_values_ref[...] = jnp.zeros_like(d_values_ref)

    scale = HEAD_DIM ** (-0.5)
    heads = grad_ref.shape[2] // HEAD_DIM
    per_sample = count // MB
    mine = lax.div(here(), per_sample)
    blocks = [
        (p, ref, i * rows) for group, ref in zip(places, queries_refs) for i, p in enumerate(group)
    ]
    for far in range(MB):
        chosen = [block for block in blocks if block[0] // per_sample == far]
        if not chosen:
            continue
        sample = lax.bitwise_xor(mine, far)
        img = pl.ds(pl.multiple_of(sample * SLOTS, SLOTS), SLOTS)
        keys, values = keys_ref[img, :], values_ref[img, :]
        live = slot_ref[sample][:1, :] > 0
        spots = [
            pl.ds(pl.multiple_of(lax.bitwise_xor(here(), p) * rows, rows), rows)
            for p, _, _ in chosen
        ]
        masks = [token_ref[spot, :] for spot in spots]
        queries, upstream = [], []
        for h in range(heads):
            cols = slice(h * HEAD_DIM, (h + 1) * HEAD_DIM)
            for (p, ref, at), mask, spot in zip(chosen, masks, spots):
                queries.append(ref[at : at + rows, cols])
                grad = grad_rows[spot, cols] if narrow else grad_ref[0, spot, cols].astype(F32)
                upstream.append((grad * mask).astype(BF16))
        queries = jnp.concatenate(queries, axis=0)
        upstream = jnp.concatenate(upstream, axis=0)
        scores = dot_nt(queries, keys) * scale
        exponent = jnp.where(live, jnp.exp(scores), 0.0)
        probs = exponent * (1.0 / jnp.sum(exponent, axis=-1, keepdims=True))
        weights = probs.astype(BF16)
        head_out = dot_nn(weights, values)
        step = 0
        for h in range(heads):
            cols = slice(h * HEAD_DIM, (h + 1) * HEAD_DIM)
            for block, mask in zip(chosen, masks):
                at = blocks.index(block) * rows
                att_ref[at : at + rows, cols] = head_out[step : step + rows] * mask
                step += rows
        d_weights = dot_nt(upstream, values)
        inner = jnp.sum(probs * d_weights, axis=-1, keepdims=True)
        d_scores = (probs * (d_weights - inner) * scale).astype(BF16)
        d_keys_ref[img, :] += dot_tn(d_scores, queries)
        d_values_ref[img, :] += dot_tn(weights, upstream)
    if last:
        hat = hat_ref[...]
        scaled = d_keys_ref[...] * k_gain_ref[...].astype(F32)
        d_raw = inverse_ref[...] * (
            scaled - hat * jnp.mean(hat * scaled, axis=-1, keepdims=True)
        )
        block_ref[:, :HEAD_DIM] = d_raw.astype(BF16)
        block_ref[:, HEAD_DIM:] = d_values_ref[...].astype(BF16)


def attention(live, queries, places, count, grad_out, k_gain, state, last, project=()):
    rows, width = grad_out.shape[1] // count, grad_out.shape[2]
    image_rows = MB * SLOTS
    vector = jax.ShapeDtypeStruct((image_rows, HEAD_DIM), F32)
    rounded = jax.ShapeDtypeStruct((image_rows, HEAD_DIM), BF16)
    attended = jax.ShapeDtypeStruct((sum(map(len, places)) * rows, width), F32)
    scratch = []
    if last:
        out_shape = [attended, jax.ShapeDtypeStruct((image_rows, 2 * HEAD_DIM), BF16)]
        scratch += [pltpu.VMEM(vector.shape, F32)] * 2
    else:
        out_shape = [attended, vector, vector, rounded, rounded, vector, vector]
    if rows % 16 != 0:
        scratch += [pltpu.VMEM(grad_out.shape[1:], F32)]
    if last:
        scratch.append(pltpu.VMEM(attended.shape, BF16))
        if rows % 16 != 0:
            scratch.append(pltpu.VMEM(attended.shape, F32))
    operands = [*queries, grad_out, k_gain, *state]
    return pl.pallas_call(
        functools.partial(attention_kernel, places, count, rows, last, len(queries), project),
        in_specs=[whole()] * (2 + len(operands)),
        out_specs=[whole()] * len(out_shape),
        out_shape=out_shape,
        scratch_shapes=scratch,
        compiler_params=params(24),
        cost_estimate=cost(0, 0),
        name="attention_last" if last else "attention_first",
    )(*live, *operands)


def assemble_kernel(places, rows, *refs):
    refs, out_ref, held = refs[:-2], refs[-2], refs[-1]
    for group, ref in zip(places, refs):
        for i, p in enumerate(group):
            at = pl.multiple_of(lax.bitwise_xor(here(), p) * rows, rows)
            held[pl.ds(at, rows), :] = ref[i * rows : (i + 1) * rows, :]
    out_ref[0] = held[...].astype(BF16)


def assemble(places, arrays, like):
    rows = arrays[0].shape[0] // len(places[0])
    return pl.pallas_call(
        functools.partial(assemble_kernel, places, rows),
        in_specs=[whole()] * len(arrays),
        out_specs=whole(),
        out_shape=jax.ShapeDtypeStruct(like.shape, BF16),
        scratch_shapes=[pltpu.VMEM(like.shape[1:], F32)],
        compiler_params=params(24),
        cost_estimate=cost(0, 0),
        name="attended_rows",
    )(*arrays)


def grad_kernel(pairs, per_kv, sections, first, last, *refs):
    blocks, weight_ref, refs = refs[: len(pairs)], refs[len(pairs)], refs[len(pairs) + 1 :]
    if not first:
        before_ref, refs = refs[0], refs[1:]
    if per_kv > 1:
        refs, sums = refs[:-1], refs[-1]
        sums[...] = jnp.zeros_like(sums)
    total = refs[-1]
    image_rows, width = total.shape
    heads = []
    for block, pair in zip(blocks, pairs):
        columns = head_columns(lax.div(partner_at(pair), per_kv))
        if per_kv == 1:
            heads.append((columns, block[...]))
        else:
            for half, k in enumerate(columns):
                part = block[:, half * HEAD_DIM : (half + 1) * HEAD_DIM]
                sums[:, k] += part.astype(F32)
    if per_kv > 1:
        heads = [((slice(None),), sums[...].astype(BF16))]
    span = 256
    for c in range(0, width, span):
        cols = slice(c, c + span)
        part = 0.0 if first else before_ref[:, cols]
        for columns, block in heads:
            weight = jnp.concatenate([weight_ref[0, cols, k] for k in columns], axis=1)
            part = part + dot_nt(block, weight)
        total[:, cols] = part
    if last:
        rows = image_rows // sections
        for k in range(sections):
            to = lax.rem(lax.axis_index("section") + k, sections)
            piece = total[pl.ds(pl.multiple_of(to * rows, rows), rows), :]
            refs[k][...] = piece.astype(refs[k].dtype)


def feature_gradient(blocks, weight, per_kv, sections, before=None, last=True):
    pairs, arrays = list(blocks), list(blocks.values())
    image_rows = arrays[0].shape[0]
    width, depth = weight.shape[1:]
    rows = image_rows // sections
    if last:
        out_shape = [
            jax.ShapeDtypeStruct((rows, width), F32 if k == 0 else BF16) for k in range(sections)
        ]
        out_specs = [whole()] * sections
        scratch = [pltpu.VMEM((image_rows, width), F32)]
    else:
        out_shape = jax.ShapeDtypeStruct((image_rows, width), F32)
        out_specs = whole()
        scratch = []
    if per_kv > 1:
        scratch.append(pltpu.VMEM((image_rows, depth), F32))
    operands = [*arrays, weight] + ([] if before is None else [before])
    return pl.pallas_call(
        functools.partial(grad_kernel, pairs, per_kv, sections, before is None, last),
        in_specs=[whole()] * len(operands),
        out_specs=out_specs,
        out_shape=out_shape,
        scratch_shapes=scratch,
        compiler_params=params(24),
        cost_estimate=cost(0, 0),
        name="feature_grad_last" if last else "feature_grad_first",
    )(*operands)


def shards(
    text, features, in_gain, w_query, q_gain, w_key_value, k_gain, tile_count, image_start, grad_out
):
    count = lax.axis_size("tensor")
    sections = lax.axis_size("section")
    per_kv = count // KV_HEADS

    def exchange(x, pair):
        return lax.ppermute(x, "tensor", [(i, i ^ pair[i % 2]) for i in range(count)])

    def swap(x):
        return exchange(x, (1, 1))

    bits = [1 << b for b in range(1, count.bit_length() - 1)]
    steps = len(bits)

    def distance(mask):
        taken = [s for s in range(steps) if mask >> s & 1]
        return sum(bits[s] for s in taken), sum(bits[steps - 1 - s] for s in taken)

    masks = range(1, 1 << steps)

    own_text = text[0]
    depth = own_text.shape[1]
    cuts = (0, depth * 7 // 16, depth * 3 // 4, depth)
    direct = {1 << s: exchange(own_text, distance(1 << s)) for s in range(steps)}

    def both_cores(blocks):
        out = {}
        for pair, x in blocks.items():
            out[pair] = [x]
            out[other_core(pair)] = [swap(x)]
        return out

    def places_of(blocks):
        return sorted(even for even, _ in blocks)

    def queries(blocks, name, **more):
        order = places_of(blocks)
        slots = [(order.index(even), order.index(odd)) for even, odd in blocks]
        groups = list(blocks.values())
        return queries_of(groups, slots, in_gain, w_query, q_gain, name, **more)

    near = both_cores({(0, 0): own_text})
    scalars = (tile_count, image_start)
    q_near, *live = queries(near, "queries_own_chip", scalars=scalars)
    kv_pairs = [distance(mask) for mask in range(1 << steps)]
    other_heads = kv_partial(features, w_key_value, per_kv, [other_core(pair) for pair in kv_pairs])
    other_heads = [swap(x) for x in other_heads]
    sums = kv_partial(features, w_key_value, per_kv, kv_pairs, other_heads)
    for step in range(steps):
        kept, came = sums[::2], [exchange(x, distance(1 << step)) for x in sums[1::2]]
        if step == 0:
            direct, came, q_near = lax.optimization_barrier((direct, came, q_near))
        if step < steps - 1:
            sums = kv_sum(kept, came)
    parts = [kept[0], came[0]]
    forwarded = []
    for first, last in ((0, cuts[1]), (cuts[1], depth)):
        held = {mask: x[:, first:last] for mask, x in direct.items()}
        passed = {}
        for s in range(1, steps):
            for mask in range(1, 1 << s):
                more = mask | 1 << s
                held[more] = passed[distance(more)] = exchange(held[mask], distance(1 << s))
        forwarded.append(passed)

    next_to = both_cores({distance(mask): x for mask, x in direct.items()})
    q_next = queries(next_to, "queries_neighbours")

    first_half, parts, q_near, q_next = lax.optimization_barrier(
        (forwarded[0], parts, q_near, q_next)
    )
    far = both_cores(first_half)
    sums = queries(far, "queries_forwarded_first")
    early, *state = attention(
        live,
        [q_near, q_next],
        [places_of(near), places_of(next_to)],
        count,
        grad_out,
        k_gain,
        parts,
        last=False,
    )
    second_half, sums, state = lax.optimization_barrier((forwarded[1], sums, state))
    split = cuts[2] - cuts[1]
    pieces = {pair: (x[:, :split], x[:, split:]) for pair, x in second_half.items()}
    far, rest = [both_cores({pair: x[i] for pair, x in pieces.items()}) for i in range(2)]
    sums = queries(far, "queries_forwarded_second", start=cuts[1], before=sums)
    far = places_of(rest)
    groups = list(rest.values())
    slots = [(far.index(even), far.index(odd)) for even, odd in rest]
    project = ([len(group) for group in groups], slots, cuts[2])
    left = [in_gain, w_query, q_gain, *[x for group in groups for x in group], *sums]
    late, block = attention(
        live, left, [far], count, grad_out, k_gain, state, last=True, project=project
    )
    attended = assemble([places_of(near) + places_of(next_to), far], [early, late], grad_out)

    same_core = {(0, 0): block}
    same_core.update({distance(m): exchange(block, distance(m)) for m in reversed(masks)})
    swapped = {other_core(pair): swap(x) for pair, x in same_core.items()}
    before = None
    blocks = {**same_core, **swapped}
    if per_kv == 1:
        soon = {pair: blocks.pop(pair) for pair in [*same_core, (1, 1)]}
        before = feature_gradient(soon, w_key_value, per_kv, sections, last=False)
    pieces = feature_gradient(blocks, w_key_value, per_kv, sections, before)
    feature_grad, leaving = pieces[0], pieces[1:]
    arrived = []
    for k in range(1, sections):
        perm = [(i, (i + k) % sections) for i in range(sections)]
        arrived.append(lax.ppermute(leaving[k - 1], "section", perm))
    for x in arrived:
        feature_grad = feature_grad + x.astype(F32)
    return (attended, feature_grad)


def solution(mesh):
    return jax.shard_map(
        shards,
        mesh=mesh,
        in_specs=(
            P("section", "tensor", None),
            P(None, "tensor"),
            P("section", None),
            P("section", None, "tensor"),
            P("section", None),
            P("section", "tensor", None),
            P("section", None),
            P(),
            P(),
            P("section", None, "tensor"),
        ),
        out_specs=(P("section", None, "tensor"), P("section", "tensor")),
        check_vma=False,
    )
```

```python
import functools

import jax
import jax.numpy as jnp
from jax import lax
from jax.experimental import pallas as pl
from jax.experimental.pallas import tpu as pltpu
from jax.sharding import PartitionSpec as P

KV_HEADS = 8
HEAD_DIM = 128
TILES = 4
TILE_LEN = 24
TXT_TOK = 128
MB = 2
SLOTS = TILES * TILE_LEN

eps = 1e-05

F32 = jnp.float32
BF16 = jnp.bfloat16
MIB = 1 << 20


def whole(memory=pltpu.VMEM):
    return pl.BlockSpec(memory_space=memory)


def dot_nn(a, b):
    return jnp.dot(a, b, preferred_element_type=F32)


def dot_nt(a, b):
    return lax.dot_general(a, b, (((1,), (1,)), ((), ())), preferred_element_type=F32)


def dot_tn(a, b):
    return lax.dot_general(a, b, (((0,), (0,)), ((), ())), preferred_element_type=F32)


def params(mib):
    return pltpu.CompilerParams(vmem_limit_bytes=mib * MIB)


def cost(flops, size):
    return pl.CostEstimate(flops=flops, bytes_accessed=size, transcendentals=0)


def here():
    return lax.axis_index("tensor")


def of_core(pair):
    even, odd = pair
    return even if even == odd else even + lax.rem(here(), 2) * (odd - even)


def partner_at(pair):
    return lax.bitwise_xor(here(), of_core(pair))


def other_core(pair):
    return (1 ^ pair[1], 1 ^ pair[0])


def head_columns(head):
    return [
        pl.ds(pl.multiple_of((half * KV_HEADS + head) * HEAD_DIM, HEAD_DIM), HEAD_DIM)
        for half in range(2)
    ]


def kv_kernel(per_kv, pairs, feat_ref, weight_ref, *refs):
    features = feat_ref[...]
    for j, pair in enumerate(pairs):
        head = lax.div(partner_at(pair), per_kv)
        weight = jnp.concatenate([weight_ref[0, :, c] for c in head_columns(head)], axis=1)
        total = dot_nn(features, weight)
        out_ref = refs[j - len(pairs)]
        if len(refs) > len(pairs):
            total = total + refs[j][...]
        out_ref[...] = total.astype(out_ref.dtype)


def kv_partial(features, weight, per_kv, pairs, other=()):
    operands = (features, weight, *other)
    shape = (features.shape[0], 2 * HEAD_DIM)
    return pl.pallas_call(
        functools.partial(kv_kernel, per_kv, pairs),
        in_specs=[whole()] * len(operands),
        out_specs=[whole()] * len(pairs),
        out_shape=[
            jax.ShapeDtypeStruct(shape, BF16 if other and j % 2 else F32)
            for j in range(len(pairs))
        ],
        compiler_params=params(24),
        cost_estimate=cost(0, 0),
        name="kv_partial_own_core" if other else "kv_partial_other_core",
    )(*operands)


def kv_sum_kernel(*refs):
    size = len(refs) // 3
    for kept_ref, came_ref, out_ref in zip(refs, refs[size:], refs[2 * size :]):
        total = kept_ref[...] + came_ref[...].astype(F32)
        out_ref[...] = total.astype(out_ref.dtype)


def kv_sum(kept, came):
    return pl.pallas_call(
        kv_sum_kernel,
        in_specs=[whole()] * (2 * len(kept)),
        out_specs=[whole()] * len(kept),
        out_shape=[
            jax.ShapeDtypeStruct(x.shape, BF16 if i % 2 else F32) for i, x in enumerate(kept)
        ],
        compiler_params=params(24),
        cost_estimate=cost(0, 0),
        name="kv_sum",
    )(*kept, *came)


def live_masks(count_ref, start_ref, token_ref, slot_ref):
    for b in range(MB):
        token = lax.broadcasted_iota(jnp.int32, (TXT_TOK, HEAD_DIM), 0)
        token_ref[b * TXT_TOK : (b + 1) * TXT_TOK, :] = (token >= start_ref[b]).astype(F32)
        slot = lax.broadcasted_iota(jnp.int32, slot_ref.shape[1:], 1)
        slot_ref[b] = (slot < count_ref[b] * TILE_LEN).astype(F32)


def query_kernel(shape, slots, start, scalars, scratch, *refs):
    if scalars:
        end = len(refs) - scratch
        live_masks(refs[0], refs[1], refs[end - 2], refs[end - 1])
        refs = refs[2 : end - 2] + refs[end:]
    gain_ref, weight_ref, q_gain_ref, refs = refs[0], refs[1], refs[2], refs[3:]
    groups = []
    for parts in shape:
        groups.append(refs[:parts])
        refs = refs[parts:]
    depth, heads_width = weight_ref.shape[1:]
    width = sum(part.shape[1] for part in groups[0])
    last = start + width == depth
    span = 1024 if width % 1024 == 0 else 512

    def columns(parts, c):
        for part in parts:
            if c < part.shape[1]:
                return part[:, c : c + span].astype(F32)
            c -= part.shape[1]

    if start:
        raw, squares, refs = refs[0][...], refs[1][:, :1], refs[2:]
    else:
        raw, squares = 0.0, 0.0
    def rows_at(c):
        return jnp.concatenate([columns(parts, c) for parts in groups], axis=0)

    ahead = 1.0
    if not start and last:
        for c in range(0, width, span):
            squares = squares + jnp.sum(rows_at(c) ** 2, axis=-1, keepdims=True)
        ahead = lax.rsqrt(squares / depth + eps)
    for c in range(0, width, span):
        x = rows_at(c)
        if start or not last:
            squares = squares + jnp.sum(x * x, axis=-1, keepdims=True)
        cols = slice(start + c, start + c + span)
        scaled = (x * ahead * gain_ref[:, cols].astype(F32)).astype(BF16)
        raw = raw + dot_nn(scaled, weight_ref[0, cols, :])
    if not last:
        refs[0][...] = raw
        refs[1][...] = jnp.broadcast_to(squares, refs[1].shape)
        return
    out_ref = refs[-1]
    rows = groups[0][0].shape[0]
    inverse = lax.rsqrt(squares / depth + eps) if start else 1.0
    q_gain = q_gain_ref[...].astype(F32)
    for c in range(0, heads_width, HEAD_DIM):
        head = raw[:, c : c + HEAD_DIM] * inverse
        q_inverse = lax.rsqrt(jnp.mean(head * head, axis=-1, keepdims=True) + eps)
        head = head * q_inverse * q_gain
        for i, pair in enumerate(slots):
            at = of_core(pair) * rows
            if pair[0] != pair[1]:
                at = pl.multiple_of(at, rows)
            part = head[i * rows : (i + 1) * rows]
            out_ref[pl.ds(at, rows), c : c + HEAD_DIM] = part.astype(out_ref.dtype)
    if len(refs) > 1:
        refs[0][...] = out_ref[...].astype(BF16)


def queries_of(groups, slots, gain, weight, q_gain, name, start=0, before=(), scalars=()):
    arrays = [part for parts in groups for part in parts]
    rows = sum(parts[0].shape[0] for parts in groups)
    depth, heads_width = weight.shape[1:]
    last = start + sum(part.shape[1] for part in groups[0]) == depth
    scratch = []
    if last:
        out_shape = [jax.ShapeDtypeStruct((rows, heads_width), BF16)]
        if arrays[0].shape[0] % 16 != 0:
            scratch.append(pltpu.VMEM((rows, heads_width), F32))
        if scalars:
            out_shape.append(jax.ShapeDtypeStruct((MB * TXT_TOK, HEAD_DIM), F32))
            out_shape.append(jax.ShapeDtypeStruct((MB, 8, SLOTS), F32))
    else:
        out_shape = [jax.ShapeDtypeStruct((rows, w), F32) for w in (heads_width, HEAD_DIM)]
    out = pl.pallas_call(
        functools.partial(
            query_kernel,
            [len(parts) for parts in groups],
            slots,
            start,
            len(scalars),
            len(scratch),
        ),
        in_specs=[whole(pltpu.SMEM)] * len(scalars)
        + [whole()] * (3 + len(arrays) + len(before)),
        out_specs=[whole()] * len(out_shape),
        out_shape=out_shape,
        scratch_shapes=scratch,
        compiler_params=params(24),
        cost_estimate=cost(0, 0),
        name=name,
    )(*scalars, gain, weight, q_gain, *arrays, *before)
    return out[0] if last and not scalars else out


def attention_kernel(places, count, rows, last, sizes, project, *refs):
    token_ref, slot_ref, refs = refs[0], refs[1], refs[2:]
    queries_refs, refs = refs[:sizes], refs[sizes:]
    if last:
        held = 1 + (rows % 16 != 0)
        query_kernel(*project, 0, 0, *queries_refs, *refs[-held:])
        queries_refs, refs = refs[len(refs) - held : len(refs) - held + 1], refs[:-held]
    grad_ref, k_gain_ref, refs = refs[0], refs[1], refs[2:]
    narrow = rows % 16 != 0
    if narrow:
        refs, grad_rows = refs[:-1], refs[-1]
        grad_rows[...] = grad_ref[0].astype(F32)
    if last:
        d_keys_in, d_values_in, keys_ref, values_ref, hat_ref, inverse_ref = refs[:6]
        att_ref, block_ref, d_keys_ref, d_values_ref = refs[6:]
        d_keys_ref[...] = d_keys_in[...]
        d_values_ref[...] = d_values_in[...]
    else:
        parts = refs[:-7]
        att_ref, d_keys_ref, d_values_ref, keys_ref, values_ref, hat_ref, inverse_ref = refs[-7:]
        kv = sum(part[...].astype(F32) for part in parts)
        key_raw = kv[:, :HEAD_DIM]
        inverse = lax.rsqrt(jnp.mean(key_raw * key_raw, axis=-1, keepdims=True) + eps)
        hat_ref[...] = key_raw * inverse
        inverse_ref[...] = jnp.broadcast_to(inverse, key_raw.shape)
        keys_ref[...] = (key_raw * inverse * k_gain_ref[...].astype(F32)).astype(BF16)
        values_ref[...] = kv[:, HEAD_DIM:].astype(BF16)
        d_keys_ref[...] = jnp.zeros_like(d_keys_ref)
        d_values_ref[...] = jnp.zeros_like(d_values_ref)

    scale = HEAD_DIM ** (-0.5)
    heads = grad_ref.shape[2] // HEAD_DIM
    per_sample = count // MB
    mine = lax.div(here(), per_sample)
    blocks = [
        (p, ref, i * rows) for group, ref in zip(places, queries_refs) for i, p in enumerate(group)
    ]
    for far in range(MB):
        chosen = [block for block in blocks if block[0] // per_sample == far]
        if not chosen:
            continue
        sample = lax.bitwise_xor(mine, far)
        img = pl.ds(pl.multiple_of(sample * SLOTS, SLOTS), SLOTS)
        keys, values = keys_ref[img, :], values_ref[img, :]
        live = slot_ref[sample][:1, :] > 0
        spots = [
            pl.ds(pl.multiple_of(lax.bitwise_xor(here(), p) * rows, rows), rows)
            for p, _, _ in chosen
        ]
        masks = [token_ref[spot, :] for spot in spots]
        queries, upstream = [], []
        for h in range(heads):
            cols = slice(h * HEAD_DIM, (h + 1) * HEAD_DIM)
            for (p, ref, at), mask, spot in zip(chosen, masks, spots):
                queries.append(ref[at : at + rows, cols])
                grad = grad_rows[spot, cols] if narrow else grad_ref[0, spot, cols].astype(F32)
                upstream.append((grad * mask).astype(BF16))
        queries = jnp.concatenate(queries, axis=0)
        upstream = jnp.concatenate(upstream, axis=0)
        scores = dot_nt(queries, keys) * scale
        exponent = jnp.where(live, jnp.exp(scores), 0.0)
        probs = exponent * (1.0 / jnp.sum(exponent, axis=-1, keepdims=True))
        weights = probs.astype(BF16)
        head_out = dot_nn(weights, values)
        step = 0
        for h in range(heads):
            cols = slice(h * HEAD_DIM, (h + 1) * HEAD_DIM)
            for block, mask in zip(chosen, masks):
                at = blocks.index(block) * rows
                att_ref[at : at + rows, cols] = head_out[step : step + rows] * mask
                step += rows
        d_weights = dot_nt(upstream, values)
        inner = jnp.sum(probs * d_weights, axis=-1, keepdims=True)
        d_scores = (probs * (d_weights - inner) * scale).astype(BF16)
        d_keys_ref[img, :] += dot_tn(d_scores, queries)
        d_values_ref[img, :] += dot_tn(weights, upstream)
    if last:
        hat = hat_ref[...]
        scaled = d_keys_ref[...] * k_gain_ref[...].astype(F32)
        d_raw = inverse_ref[...] * (
            scaled - hat * jnp.mean(hat * scaled, axis=-1, keepdims=True)
        )
        block_ref[:, :HEAD_DIM] = d_raw.astype(BF16)
        block_ref[:, HEAD_DIM:] = d_values_ref[...].astype(BF16)


def attention(live, queries, places, count, grad_out, k_gain, state, last, project=()):
    rows, width = grad_out.shape[1] // count, grad_out.shape[2]
    image_rows = MB * SLOTS
    vector = jax.ShapeDtypeStruct((image_rows, HEAD_DIM), F32)
    rounded = jax.ShapeDtypeStruct((image_rows, HEAD_DIM), BF16)
    attended = jax.ShapeDtypeStruct((sum(map(len, places)) * rows, width), F32)
    scratch = []
    if last:
        out_shape = [attended, jax.ShapeDtypeStruct((image_rows, 2 * HEAD_DIM), BF16)]
        scratch += [pltpu.VMEM(vector.shape, F32)] * 2
    else:
        out_shape = [attended, vector, vector, rounded, rounded, vector, vector]
    if rows % 16 != 0:
        scratch += [pltpu.VMEM(grad_out.shape[1:], F32)]
    if last:
        scratch.append(pltpu.VMEM(attended.shape, BF16))
        if rows % 16 != 0:
            scratch.append(pltpu.VMEM(attended.shape, F32))
    operands = [*queries, grad_out, k_gain, *state]
    return pl.pallas_call(
        functools.partial(attention_kernel, places, count, rows, last, len(queries), project),
        in_specs=[whole()] * (2 + len(operands)),
        out_specs=[whole()] * len(out_shape),
        out_shape=out_shape,
        scratch_shapes=scratch,
        compiler_params=params(24),
        cost_estimate=cost(0, 0),
        name="attention_last" if last else "attention_first",
    )(*live, *operands)


def assemble_kernel(places, rows, *refs):
    refs, out_ref, held = refs[:-2], refs[-2], refs[-1]
    for group, ref in zip(places, refs):
        for i, p in enumerate(group):
            at = pl.multiple_of(lax.bitwise_xor(here(), p) * rows, rows)
            held[pl.ds(at, rows), :] = ref[i * rows : (i + 1) * rows, :]
    out_ref[0] = held[...].astype(BF16)


def assemble(places, arrays, like):
    rows = arrays[0].shape[0] // len(places[0])
    return pl.pallas_call(
        functools.partial(assemble_kernel, places, rows),
        in_specs=[whole()] * len(arrays),
        out_specs=whole(),
        out_shape=jax.ShapeDtypeStruct(like.shape, BF16),
        scratch_shapes=[pltpu.VMEM(like.shape[1:], F32)],
        compiler_params=params(24),
        cost_estimate=cost(0, 0),
        name="attended_rows",
    )(*arrays)


def grad_kernel(pairs, per_kv, sections, first, last, *refs):
    blocks, weight_ref, refs = refs[: len(pairs)], refs[len(pairs)], refs[len(pairs) + 1 :]
    if not first:
        before_ref, refs = refs[0], refs[1:]
    if per_kv > 1:
        refs, sums = refs[:-1], refs[-1]
        sums[...] = jnp.zeros_like(sums)
    total = refs[-1]
    image_rows, width = total.shape
    heads = []
    for block, pair in zip(blocks, pairs):
        columns = head_columns(lax.div(partner_at(pair), per_kv))
        if per_kv == 1:
            heads.append((columns, block[...]))
        else:
            for half, k in enumerate(columns):
                part = block[:, half * HEAD_DIM : (half + 1) * HEAD_DIM]
                sums[:, k] += part.astype(F32)
    if per_kv > 1:
        heads = [((slice(None),), sums[...].astype(BF16))]
    span = 256
    for c in range(0, width, span):
        cols = slice(c, c + span)
        part = 0.0 if first else before_ref[:, cols]
        for columns, block in heads:
            weight = jnp.concatenate([weight_ref[0, cols, k] for k in columns], axis=1)
            part = part + dot_nt(block, weight)
        total[:, cols] = part
    if last:
        rows = image_rows // sections
        for k in range(sections):
            to = lax.rem(lax.axis_index("section") + k, sections)
            piece = total[pl.ds(pl.multiple_of(to * rows, rows), rows), :]
            refs[k][...] = piece.astype(refs[k].dtype)


def feature_gradient(blocks, weight, per_kv, sections, before=None, last=True):
    pairs, arrays = list(blocks), list(blocks.values())
    image_rows = arrays[0].shape[0]
    width, depth = weight.shape[1:]
    rows = image_rows // sections
    if last:
        out_shape = [
            jax.ShapeDtypeStruct((rows, width), F32 if k == 0 else BF16) for k in range(sections)
        ]
        out_specs = [whole()] * sections
        scratch = [pltpu.VMEM((image_rows, width), F32)]
    else:
        out_shape = jax.ShapeDtypeStruct((image_rows, width), F32)
        out_specs = whole()
        scratch = []
    if per_kv > 1:
        scratch.append(pltpu.VMEM((image_rows, depth), F32))
    operands = [*arrays, weight] + ([] if before is None else [before])
    return pl.pallas_call(
        functools.partial(grad_kernel, pairs, per_kv, sections, before is None, last),
        in_specs=[whole()] * len(operands),
        out_specs=out_specs,
        out_shape=out_shape,
        scratch_shapes=scratch,
        compiler_params=params(24),
        cost_estimate=cost(0, 0),
        name="feature_grad_last" if last else "feature_grad_first",
    )(*operands)


def shards(
    text, features, in_gain, w_query, q_gain, w_key_value, k_gain, tile_count, image_start, grad_out
):
    count = lax.axis_size("tensor")
    sections = lax.axis_size("section")
    per_kv = count // KV_HEADS

    def exchange(x, pair):
        return lax.ppermute(x, "tensor", [(i, i ^ pair[i % 2]) for i in range(count)])

    def swap(x):
        return exchange(x, (1, 1))

    bits = [1 << b for b in range(1, count.bit_length() - 1)]
    steps = len(bits)

    def distance(mask):
        taken = [s for s in range(steps) if mask >> s & 1]
        return sum(bits[s] for s in taken), sum(bits[steps - 1 - s] for s in taken)

    masks = range(1, 1 << steps)

    own_text = text[0]
    depth = own_text.shape[1]
    cuts = (0, depth * 7 // 16, depth * 11 // 16, depth)
    direct = {1 << s: exchange(own_text, distance(1 << s)) for s in range(steps)}

    def both_cores(blocks):
        out = {}
        for pair, x in blocks.items():
            out[pair] = [x]
            out[other_core(pair)] = [swap(x)]
        return out

    def places_of(blocks):
        return sorted(even for even, _ in blocks)

    def queries(blocks, name, **more):
        order = places_of(blocks)
        slots = [(order.index(even), order.index(odd)) for even, odd in blocks]
        groups = list(blocks.values())
        return queries_of(groups, slots, in_gain, w_query, q_gain, name, **more)

    kv_pairs = [distance(mask) for mask in range(1 << steps)]
    other_heads = kv_partial(features, w_key_value, per_kv, [other_core(pair) for pair in kv_pairs])
    other_heads = [swap(x) for x in other_heads]
    sums = kv_partial(features, w_key_value, per_kv, kv_pairs, other_heads)
    for step in range(steps):
        kept, came = sums[::2], [exchange(x, distance(1 << step)) for x in sums[1::2]]
        if step == 0:
            direct, came = lax.optimization_barrier((direct, came))
        if step < steps - 1:
            sums = kv_sum(kept, came)
    parts = [kept[0], came[0]]
    near = both_cores({(0, 0): own_text})
    scalars = (tile_count, image_start)
    q_near, *live = queries(near, "queries_own_chip", scalars=scalars)
    forwarded = []
    for first, last in ((0, cuts[1]), (cuts[1], depth)):
        held = {mask: x[:, first:last] for mask, x in direct.items()}
        passed = {}
        for s in range(1, steps):
            for mask in range(1, 1 << s):
                more = mask | 1 << s
                held[more] = passed[distance(more)] = exchange(held[mask], distance(1 << s))
        forwarded.append(passed)

    next_to = both_cores({distance(mask): x for mask, x in direct.items()})
    q_next = queries(next_to, "queries_neighbours")

    first_half, parts, q_near, q_next = lax.optimization_barrier(
        (forwarded[0], parts, q_near, q_next)
    )
    far = both_cores(first_half)
    sums = queries(far, "queries_forwarded_first")
    early, *state = attention(
        live,
        [q_near, q_next],
        [places_of(near), places_of(next_to)],
        count,
        grad_out,
        k_gain,
        parts,
        last=False,
    )
    second_half, sums, state = lax.optimization_barrier((forwarded[1], sums, state))
    split = cuts[2] - cuts[1]
    pieces = {pair: (x[:, :split], x[:, split:]) for pair, x in second_half.items()}
    far, rest = [both_cores({pair: x[i] for pair, x in pieces.items()}) for i in range(2)]
    sums = queries(far, "queries_forwarded_second", start=cuts[1], before=sums)
    far = places_of(rest)
    groups = list(rest.values())
    slots = [(far.index(even), far.index(odd)) for even, odd in rest]
    project = ([len(group) for group in groups], slots, cuts[2])
    left = [in_gain, w_query, q_gain, *[x for group in groups for x in group], *sums]
    late, block = attention(
        live, left, [far], count, grad_out, k_gain, state, last=True, project=project
    )
    attended = assemble([places_of(near) + places_of(next_to), far], [early, late], grad_out)

    same_core = {(0, 0): block}
    same_core.update({distance(m): exchange(block, distance(m)) for m in reversed(masks)})
    swapped = {other_core(pair): swap(x) for pair, x in same_core.items()}
    before = None
    blocks = {**same_core, **swapped}
    if per_kv == 1:
        soon = {pair: blocks.pop(pair) for pair in [*same_core, (1, 1)]}
        before = feature_gradient(soon, w_key_value, per_kv, sections, last=False)
    pieces = feature_gradient(blocks, w_key_value, per_kv, sections, before)
    feature_grad, leaving = pieces[0], pieces[1:]
    arrived = []
    for k in range(1, sections):
        perm = [(i, (i + k) % sections) for i in range(sections)]
        arrived.append(lax.ppermute(leaving[k - 1], "section", perm))
    for x in arrived:
        feature_grad = feature_grad + x.astype(F32)
    return (attended, feature_grad)


def solution(mesh):
    return jax.shard_map(
        shards,
        mesh=mesh,
        in_specs=(
            P("section", "tensor", None),
            P(None, "tensor"),
            P("section", None),
            P("section", None, "tensor"),
            P("section", None),
            P("section", "tensor", None),
            P("section", None),
            P(),
            P(),
            P("section", None, "tensor"),
        ),
        out_specs=(P("section", None, "tensor"), P("section", "tensor")),
        check_vma=False,
    )
```
